256 devices in a mesh: basis: 8 (over z_lo, core), orb: 16 (over y, x), rep: 2 (over z_hi).
Axes of the slice: x: 4, y: 4, z: 8 (z_hi: 2, z_lo: 4; z = z_hi * 4 + z_lo), core: 2. Of those that a mesh axis runs over, the one named last changes fastest.
Arguments:
- coefficients: float32 [16, 8192, 512], P('orb', ('basis', 'rep')), may hold values from -6 to 6
- basis_metric: bfloat16 [65536, 128], P('orb'), as said below
- pattern: int32 [1024], P('orb'), may hold values 0 or 1
- starts: int32 [128], P('orb'), may hold values from 0 to 928, as said below
Outputs:
- coefficients_out: float32 [16, 8192, 512], P('orb', ('basis', 'rep'))
The draws below stay inside these ranges and needn't reach their ends.
Inputs may be any that keep to these rules, and one draw needn't show every extreme that they name: Orbital block j lies in group g = floor(j * 64 / 512); starts[j] is the smaller of 928 and a block between g * 64 and g * 64 + 2 * 64 - 96. `basis_metric`: the first 64 columns of each block's rows form a symmetric block with unit diagonal.
All inputs are finite; a program needn't handle non-finite values. No bound on the sum of `pattern` on one device may be relied on, other than what follows from the above.
Results may differ from the reference program's by a relative error of at most 0.0003.
Values may be sent and summed in bfloat16 or wider, within the bound.
A program may use at most 64 MiB of HBM per device.

```python
import jax
import jax.numpy as jnp
from jax import lax

BLK = 64
GROUP_BLOCKS = 64
ORB_DEV = 512
SUPPORT = 96
ITERS = 2
BASIS_BLOCKS = 1024
BASIS = 65536
ORB_BLOCKS = 128
WINDOW = 8192
N_ORB = 16


def draw_basis_metric(key, part):
    key = jax.random.fold_in(key, 11)
    first_key, second_key = jax.random.split(key)
    total_blocks = BASIS // BLK
    bound_value = 0.9 / (3.0 * BLK)
    up_bound = 0.7 / jnp.sqrt(2.0 * BLK)
    diag_raw = jax.random.uniform(first_key, (total_blocks, BLK, BLK), jnp.float32)
    up_raw = jax.random.uniform(second_key, (total_blocks, BLK, BLK), jnp.float32, -1.0, 1.0)
    diag_raw = bound_value * diag_raw
    up_raw = up_bound * up_raw
    symmetric = (diag_raw + jnp.swapaxes(diag_raw, 1, 2)) * 0.5
    identity = jnp.eye(BLK, dtype=bool)[None, :, :]
    diag_part = jnp.where(identity, 1.0, symmetric)
    joined = jnp.concatenate([diag_part.reshape(BASIS, BLK), up_raw.reshape(BASIS, BLK)], axis=1)
    return joined.astype(jnp.bfloat16)


def draw_starts(key, part):
    key = jax.random.fold_in(key, 23)
    block_index = jnp.arange(ORB_BLOCKS, dtype=jnp.int32)
    group_ids = block_index // (ORB_DEV // BLK)
    offsets = jax.random.randint(key, (ORB_BLOCKS,), 0, 2 * GROUP_BLOCKS - SUPPORT + 1, dtype=jnp.int32)
    first_blocks = jnp.minimum(group_ids * GROUP_BLOCKS + offsets, BASIS_BLOCKS - SUPPORT)
    first_blocks = jnp.where(block_index == 0, 0, first_blocks)
    first_blocks = jnp.where(block_index == ORB_BLOCKS - 1, BASIS_BLOCKS - SUPPORT, first_blocks)
    return first_blocks.astype(jnp.int32)


def with_ends(drawn, stream_key, smallest, top_value):
    spot = [jax.random.randint(jax.random.fold_in(stream_key, axis), (), 0, length) for axis, length in enumerate(drawn.shape)]
    widest = drawn.shape.index(max(drawn.shape))
    beside = spot[:widest] + [(spot[widest] + 1) % drawn.shape[widest]] + spot[widest + 1:]
    return drawn.at[tuple(spot)].set(smallest).at[tuple(beside)].set(top_value)


def block_scale(stream_key, dims, pieces, smallest, largest):
    level, own = 1.0, jax.random.fold_in(stream_key, 6)
    for axis_at, parts in pieces:
        heights = jnp.exp(jax.random.uniform(jax.random.fold_in(own, axis_at), (parts,), jnp.float32, smallest / len(pieces), largest / len(pieces)))
        level = level * jnp.repeat(heights, dims[axis_at] // parts).reshape([-1 if axis == axis_at else 1 for axis in range(len(dims))])
    return level


def gaussian(rng, shape, width, most, pieces=(), held_as=jnp.bfloat16):
    level = block_scale(rng, shape, pieces, -0.22, 0.18) if pieces else 1.0
    values = jax.random.normal(rng, shape, jnp.float32) * width * level
    return jnp.minimum(jnp.maximum(values, -most), most).astype(held_as)


def setup_inputs(seed: int = 0) -> dict:
    key_list = jax.random.split(jax.random.key(seed), 5)
    coefficients = gaussian(key_list[0], (N_ORB, WINDOW, ORB_DEV), 1.0, 6.0, ((0, 16), (1, 16)), jnp.float32)
    basis_metric = draw_basis_metric(jax.random.fold_in(key_list[4], 71), 0)
    pattern = with_ends((jax.random.randint(key_list[2], (BASIS_BLOCKS,), 0, 2) < 1).astype(jnp.int32), jax.random.fold_in(key_list[2], 1), 0, 1)
    starts = draw_starts(jax.random.fold_in(key_list[4], 71), 0)
    return {"coefficients": coefficients, "basis_metric": basis_metric, "pattern": pattern, "starts": starts}


HIGH = lax.Precision.HIGHEST


def metric_blocks(basis_metric, pattern):
    total_blocks = GROUP_BLOCKS * N_ORB
    shaped = basis_metric.astype(jnp.float32).reshape(total_blocks, BLK, 2 * BLK)
    last_flag = (jnp.arange(total_blocks, dtype=jnp.int32) < total_blocks - 1).astype(jnp.float32)
    keep_flag = pattern.astype(jnp.float32) * last_flag
    diag_blocks = shaped[:, :, :BLK]
    up_blocks = shaped[:, :, BLK:] * keep_flag[:, None, None]
    return diag_blocks, up_blocks


def window_blocks(blocks):
    padded = jnp.concatenate([blocks, jnp.zeros((GROUP_BLOCKS, BLK, BLK), jnp.float32)], axis=0)
    index_table = (jnp.arange(N_ORB, dtype=jnp.int32)[:, None] * GROUP_BLOCKS
                   + jnp.arange(2 * GROUP_BLOCKS, dtype=jnp.int32)[None, :]).astype(jnp.int32)
    return padded[index_table]


def support_mask(starts):
    window_rows = 2 * GROUP_BLOCKS * BLK
    group_ids = jnp.arange(N_ORB, dtype=jnp.int32)[:, None, None]
    block_rows = (jnp.arange(window_rows, dtype=jnp.int32) // BLK)[None, :, None]
    absolute = group_ids * GROUP_BLOCKS + block_rows
    column_starts = jnp.repeat(starts.reshape(N_ORB, ORB_DEV // BLK), BLK, axis=1)[:, None, :]
    inside = (absolute >= column_starts) & (absolute < column_starts + SUPPORT)
    return inside.astype(jnp.float32)


def apply_metric(coeff_now, diag_win, up_win):
    shaped = coeff_now.reshape(N_ORB, 2 * GROUP_BLOCKS, BLK, ORB_DEV)
    zero_block = jnp.zeros_like(shaped[:, :1])
    following = jnp.concatenate([shaped[:, 1:], zero_block], axis=1)
    preceding = jnp.concatenate([zero_block, shaped[:, :-1]], axis=1)
    prev_up = jnp.concatenate([jnp.zeros_like(up_win[:, :1]), up_win[:, :-1]], axis=1)
    result = jnp.einsum('gwij,gwjo->gwio', diag_win, shaped, precision=HIGH)
    result = result + jnp.einsum('gwij,gwjo->gwio', up_win, following, precision=HIGH)
    result = result + jnp.einsum('gwji,gwjo->gwio', prev_up, preceding, precision=HIGH)
    return result.reshape(N_ORB, 2 * GROUP_BLOCKS * BLK, ORB_DEV)


def reference(coefficients, basis_metric, pattern, starts):
    diag_blocks, up_blocks = metric_blocks(basis_metric, pattern)
    diag_win = window_blocks(diag_blocks)
    up_win = window_blocks(up_blocks)
    mask_live = support_mask(starts)
    half_rows = GROUP_BLOCKS * BLK
    norm_scale = 1.0 / (SUPPORT * BLK)
    identity = jnp.eye(ORB_DEV, dtype=jnp.float32)
    coeff_now = coefficients * mask_live
    for sweep_index in range(ITERS):
        applied = apply_metric(coeff_now, diag_win, up_win)
        gram_self = jnp.einsum('gro,grp->gop', coeff_now, applied, precision=HIGH) * norm_scale
        gram_next = jnp.einsum('gro,grp->gop', applied[:-1, half_rows:], coeff_now[1:, :half_rows],
                               precision=HIGH) * norm_scale
        self_step = (3.0 * identity - gram_self) * 0.5
        updated = jnp.einsum('gro,gop->grp', coeff_now, self_step, precision=HIGH)
        from_prev = jnp.einsum('gro,gop->grp', coeff_now[:-1, half_rows:], -0.5 * gram_next, precision=HIGH)
        from_next = jnp.einsum('gro,gpo->grp', coeff_now[1:, :half_rows], -0.5 * gram_next, precision=HIGH)
        zero_half = jnp.zeros((1, half_rows, ORB_DEV), jnp.float32)
        lower_add = jnp.concatenate([zero_half, from_prev], axis=0)
        upper_add = jnp.concatenate([from_next, zero_half], axis=0)
        updated = updated + jnp.concatenate([lower_add, upper_add], axis=1)
        coeff_now = updated * mask_live
    return coeff_now
```

```python
import functools

import jax
import jax.numpy as jnp
from jax import lax
from jax.experimental import pallas as pl
from jax.experimental.pallas import tpu as pltpu
from jax.sharding import PartitionSpec as P

BLK = 64
GROUP_BLOCKS = 64
SUPPORT = 96
ITERS = 2
ROWS = 512
ORBS = 512
HALF = 256
GP = 32
HP = 64
TILE = 128
CMAX = 6.0
QMAX = 32767.0
BF = jnp.bfloat16
F32 = jnp.float32
I16 = jnp.int16

HALO_NEXT, HALO_PREV, GSIB, HSIB = 0, 1, 2, 3
RS, RSC, HRS, HRSC = 4, 12, 20, 24
EA, EAS, NA, NAS = 28, 36, 44, 52
HA, HAS, HL, HLS = 60, 64, 68, 72
FE, FES, FN, FNS, FH, FHS = 76, 77, 78, 79, 80, 81
NX, NXC, MET = 82, 83, 84
COUNT = 85


def split(x):
    hi = x.astype(BF)
    return hi, (x - hi.astype(F32)).astype(BF)


def dot(a, b, dims=((1,), (0,))):
    return lax.dot_general(a, b, (dims, ((), ())), preferred_element_type=F32)


def dot3(ah, al, bh, bl, dims=((1,), (0,))):
    return dot(ah, bh, dims) + (dot(ah, bl, dims) + dot(al, bh, dims))


def kernel(
    coef, metric, pattern, starts, out,
    c, chi, clo, nf, nhi, nlo, yhi, ylo, band, gp, hp,
    nq_out, nq_in, cs_own, cs_in, meff, mrecv, msel,
    gsib, hsib, qs, rs, qsc, rsc, hqs, hrs, hqsc, hrsc,
    ea, es, na, ns, ha, hs, ehi, elo, xhi, xlo, mhi, mlo,
    ss, rr, local_sem,
):
    b, o, r = lax.axis_index("basis"), lax.axis_index("orb"), lax.axis_index("rep")
    groups = lax.axis_size("orb")
    core, zl = b % 2, b // 2
    z = r * 4 + zl
    p = b * 2 + r
    q = p % 8
    low = zl < 2
    high = jnp.logical_not(low)
    side = jnp.where(low, o - 1, o + 1)
    away = jnp.where(low, o + 1, o - 1)
    has_side = jnp.logical_and(side >= 0, side < groups)
    has_away = jnp.logical_and(away >= 0, away < groups)
    j = r * 2 + zl - 2

    def dev(bb, oo, rep):
        return {"basis": bb, "orb": oo, "rep": rep}

    def zdev(zz, oo):
        return dev((zz % 4) * 2 + core, oo, zz // 4)

    sibling = dev(zl * 2 + 1 - core, o, r)

    barrier = pltpu.get_barrier_semaphore()

    def greet(device):
        pl.semaphore_signal(barrier, inc=1, device_id=device, device_id_type=pl.DeviceIdType.MESH)

    for k in range(1, 8):
        greet(zdev((z + k) % 8, o))
    greet(sibling)
    step_b = jnp.where(r == 1, b + 1, b - 1)
    has_step = jnp.logical_and(step_b >= 0, step_b < 8)

    @pl.when(has_step)
    def _():
        greet(dev(step_b, o, 1 - r))

    @pl.when(has_side)
    def _():
        for k in range(8):
            greet(zdev((z + k) % 8, side))

    @pl.when(has_away)
    def _():
        base = jnp.where(low, 0, 4)
        for m in range(4):
            greet(dev(base + (m % 2) * 2 + core, away, m // 2))

    load_main = pltpu.make_async_copy(metric.at[pl.ds(pl.multiple_of(q * 512, 64), 512)], meff.at[pl.ds(0, 512)], local_sem.at[0])
    load_prev = pltpu.make_async_copy(
        metric.at[pl.ds(pl.multiple_of((q * 512 + 4032) % 4096, 64), 64)], meff.at[pl.ds(512, 64)], local_sem.at[1]
    )
    load_main.start()
    load_prev.start()
    lane = lax.broadcasted_iota(jnp.int32, (8, ORBS), 1) // BLK
    cs = jnp.zeros((8, ORBS), F32)
    for i in range(8):
        cs = jnp.where(lane == i, starts[i].astype(F32), cs)
    cs_own[...] = cs
    first_block = (o * GROUP_BLOCKS + p * 8).astype(F32)

    def live(t, cs_ref):
        rows = lax.broadcasted_iota(jnp.int32, (TILE, ORBS), 0) // BLK
        block = rows.astype(F32) + (first_block + (t * (TILE // BLK)).astype(F32))
        at = cs_ref[0:1, :]
        return jnp.logical_and(block >= at, block < at + SUPPORT)

    def tiles(body):
        def step(t, carry):
            body(t, pl.ds(pl.multiple_of(t * TILE, TILE), TILE))
            return carry

        lax.fori_loop(0, ROWS // TILE, step, 0)

    def prepare(t, rows):
        x = jnp.where(live(t, cs_own), coef[rows, :], 0.0)
        c[rows, :] = x
        hi, lo = split(x)
        chi[0, rows, :] = hi
        clo[0, rows, :] = lo
        nq_out[rows, :] = jnp.round(jnp.clip(x, -CMAX, CMAX) * (QMAX / CMAX)).astype(I16)

    tiles(prepare)

    for it in range(ITERS):

        @pl.when(p == 0)
        def _():
            chi[it, 512:576, :] = jnp.zeros((64, ORBS), BF)

        @pl.when(p == 15)
        def _():
            chi[it, 576:640, :] = jnp.zeros((64, ORBS), BF)

    load_main.wait()
    load_prev.wait()
    right = lax.broadcasted_iota(jnp.int32, (BLK, 2 * BLK), 1) >= BLK
    for i in range(9):
        at = (q * 8 + i) % 64 if i < 8 else (q * 8 + 63) % 64
        keep = jnp.where(o * GROUP_BLOCKS + at < groups * GROUP_BLOCKS - 1, pattern[at], 0).astype(F32)
        block = meff[i * 64 : i * 64 + 64, :].astype(F32)
        meff[i * 64 : i * 64 + 64, :] = jnp.where(right, block * keep, block).astype(BF)

    waits = [jnp.int32(8), has_step.astype(jnp.int32), 8 * has_side.astype(jnp.int32), 4 * has_away.astype(jnp.int32)]
    pl.semaphore_wait(barrier, waits[0] + waits[1] + waits[2] + waits[3])

    sent = []

    def send(src, dst, it, index, device, cond=None):
        def start():
            pltpu.make_async_remote_copy(
                src_ref=src, dst_ref=dst, send_sem=ss.at[it, index], recv_sem=rr.at[it, index],
                device_id=device, device_id_type=pl.DeviceIdType.MESH,
            ).start()

        if cond is None:
            start()
        else:
            pl.when(cond)(start)
        sent.append((src, it, index, cond))

    def arrived(dst, it, index):
        pltpu.make_async_copy(dst, dst, rr.at[it, index]).wait()

    def send_halo(it):
        up_b = jnp.where(r == 0, b, b + 1)
        down_b = jnp.where(r == 1, b, b - 1)
        send(chi.at[it, pl.ds(0, 64)], chi.at[it, pl.ds(576, 64)], it, HALO_NEXT, dev(down_b, o, 1 - r), p > 0)
        send(chi.at[it, pl.ds(448, 64)], chi.at[it, pl.ds(512, 64)], it, HALO_PREV, dev(up_b, o, 1 - r), p < 15)

    def wait_halo(it):
        pl.when(p < 15)(lambda: arrived(chi.at[it, pl.ds(576, 64)], it, HALO_NEXT))
        pl.when(p > 0)(lambda: arrived(chi.at[it, pl.ds(512, 64)], it, HALO_PREV))

    gives_metric = jnp.logical_and(high, o > 0)
    send(meff, mrecv, 0, MET, dev(b, o - 1, r), gives_metric)
    send_halo(0)
    partner = dev(jnp.where(low, b + 4, b - 4), side, r)
    send(nq_out, nq_in, 0, NX, partner, has_side)
    send(cs_own, cs_in, 0, NXC, partner, has_side)

    @pl.when(low)
    def _():
        msel[...] = meff[...]

    @pl.when(jnp.logical_and(high, has_side))
    def _():
        arrived(mrecv, 0, MET)
        msel[...] = mrecv[...]

    @pl.when(jnp.logical_and(high, jnp.logical_not(has_side)))
    def _():
        msel[...] = jnp.zeros((576, 128), BF)

    @pl.when(p == 8)
    def _():
        msel[512:576, :] = meff[512:576, :]

    band[...] = jnp.zeros((ROWS, 640), BF)
    row_at = lax.broadcasted_iota(jnp.int32, (128, 128), 0)
    lane_at = lax.broadcasted_iota(jnp.int32, (128, 128), 1)
    top, left = row_at < 64, lane_at < 64
    bottom, rest = row_at >= 64, lane_at >= 64
    for t in range(4):
        m = msel[t * 128 : t * 128 + 128, :].astype(F32)
        rolled = pltpu.roll(m, 64, 1)
        corner = jnp.where(jnp.logical_and(top, rest), m, 0.0)
        diag = jnp.where(top, m, jnp.where(rest, rolled, 0.0)) + corner.T
        band[t * 128 : t * 128 + 128, t * 128 : t * 128 + 128] = diag.astype(BF)
        if t < 3:
            off = jnp.where(jnp.logical_and(bottom, left), rolled, 0.0)
            band[t * 128 : t * 128 + 128, t * 128 + 128 : t * 128 + 256] = off.astype(BF)
            band[t * 128 + 128 : t * 128 + 256, t * 128 : t * 128 + 128] = off.T.astype(BF)
        else:
            band[384:512, 512:640] = jnp.where(jnp.logical_and(bottom, rest), m, 0.0).astype(BF)
    before = pltpu.roll(msel[448:576, :].astype(F32), 64, 1).T
    shifted = pltpu.roll(before, 64, 1)
    band[0:128, 512:640] = jnp.where(jnp.logical_and(top, left), shifted, 0.0).astype(BF)

    def images(it):
        def body(t, rows):
            y = dot(band[rows, :], chi[it]) + dot(band[rows, 0:512], clo[it])
            yhi[rows, :], ylo[rows, :] = split(y)

        tiles(body)

    def gram(it):
        def body(t, cols):
            gp[it, cols, :] = dot3(chi[it, 0:512, cols], clo[it, :, cols], yhi[...], ylo[...], ((0,), (0,)))

        tiles(body)

    def cross(it):
        def body(t, cols):
            hp[it, cols, :] = dot3(yhi[:, cols], ylo[:, cols], nhi[...], nlo[...], ((0,), (0,)))

        tiles(body)

    own_half = pl.ds(pl.multiple_of(core * HALF, HALF), HALF)
    other_half = pl.ds(pl.multiple_of((1 - core) * HALF, HALF), HALF)

    def pair_and_pack(it, part, from_pair, packed, scale, size):
        count = HALF // size

        def add(i, top_value):
            rows = pl.ds(pl.multiple_of(core * HALF + i * size, size), size)
            x = part[it, rows, :] + from_pair[it, pl.ds(pl.multiple_of(i * size, size), size), :]
            part[it, rows, :] = x
            return jnp.maximum(top_value, jnp.abs(x))

        peak = jnp.max(lax.fori_loop(0, count, add, jnp.zeros((size, ORBS), F32)), axis=(0, 1), keepdims=True)
        peak = jnp.maximum(peak, 1e-30)
        scale[it] = jnp.broadcast_to(peak * (1.0 / QMAX), (8, 128))
        inv = QMAX / peak

        def pack(i, carry):
            rows = pl.ds(pl.multiple_of(core * HALF + i * size, size), size)
            packed[it, i] = jnp.round(part[it, rows, :] * inv).astype(I16)
            return carry

        lax.fori_loop(0, count, pack, 0)

    def quantized(x):
        peak = jnp.maximum(jnp.max(jnp.abs(x), axis=(0, 1), keepdims=True), 1e-30)
        return jnp.round(x * (QMAX / peak)).astype(I16), jnp.broadcast_to(peak * (1.0 / QMAX), (8, 128))

    def scatter_gram(it):
        arrived(gsib.at[it], it, GSIB)
        pair_and_pack(it, gp, gsib, qs, qsc, GP)
        for k in range(1, 8):
            to = (z + k) % 8
            send(qs.at[it, to], rs.at[it, k], it, RS + k, zdev(to, o))
            send(qsc.at[it], rsc.at[it, k], it, RSC + k, zdev(to, o))

    def scatter_cross(it):
        arrived(hsib.at[it], it, HSIB)
        pair_and_pack(it, hp, hsib, hqs, hqsc, HP)

    def high_peer(m):
        pz = zl if m % 2 == 0 else 5 - zl
        pr = r if m // 2 == 0 else 1 - r
        return pz, pr

    def send_cross(it):
        for m in range(1, 4):
            pz, pr = high_peer(m)
            device = dev(pz * 2 + core, o, pr)
            send(hqs.at[it, pr * 2 + pz - 2], hrs.at[it, m], it, HRS + m, device, high)
            send(hqsc.at[it], hrsc.at[it, m], it, HRSC + m, device, high)

    def own_gram(it, with_side):
        rows = pl.ds(pl.multiple_of(core * HALF + z * GP, GP), GP)
        total = gp[it, rows, :]
        for k in range(1, 8):
            arrived(rs.at[it, k], it, RS + k)
            arrived(rsc.at[it, k], it, RSC + k)
            total = total + rs[it, k].astype(jnp.int32).astype(F32) * rsc[it, k, 0:1, 0:1]
        here = lax.broadcasted_iota(jnp.int32, (GP, ORBS), 0) + (core * HALF + z * GP)
        same = here == lax.broadcasted_iota(jnp.int32, (GP, ORBS), 1)
        value, scale = quantized(total * (1.0 / (SUPPORT * BLK)) - same.astype(F32))
        ea[it, rows, :] = value
        at = core * 8 + z
        es[it, at] = scale
        for k in range(1, 8):
            device = zdev((z + k) % 8, o)
            send(ea.at[it, rows], ea.at[it, rows], it, EA + k, device)
            send(es.at[it, at], es.at[it, at], it, EAS + k, device)
        if with_side:
            for k in range(8):
                to = (z + k) % 8
                column = jnp.where(to % 4 < 2, o + 1, o - 1)
                there = jnp.logical_and(column >= 0, column < groups)
                send(ea.at[it, rows], na.at[rows], it, NA + k, zdev(to, column), there)
                send(es.at[it, at], ns.at[at], it, NAS + k, zdev(to, column), there)

    def own_cross(it):
        rows = pl.ds(pl.multiple_of(core * HALF + j * HP, HP), HP)
        at = core * 4 + j
        low_there = jnp.logical_and(high, o < groups - 1)

        @pl.when(high)
        def _():
            total = hp[it, rows, :]
            for m in range(1, 4):
                arrived(hrs.at[it, m], it, HRS + m)
                arrived(hrsc.at[it, m], it, HRSC + m)
                total = total + hrs[it, m].astype(jnp.int32).astype(F32) * hrsc[it, m, 0:1, 0:1]
            value, scale = quantized(total * (1.0 / (SUPPORT * BLK)))
            ha[it, rows, :] = value
            hs[it, at] = scale

        for m in range(4):
            pz, pr = high_peer(m)
            low_z = zl - 2 if m % 2 == 0 else 3 - zl
            send(ha.at[it, rows], ha.at[it, rows], it, HL + m, dev(low_z * 2 + core, o + 1, pr), low_there)
            send(hs.at[it, at], hs.at[it, at], it, HLS + m, dev(low_z * 2 + core, o + 1, pr), low_there)
            if m > 0:
                send(ha.at[it, rows], ha.at[it, rows], it, HA + m, dev(pz * 2 + core, o, pr), high)
                send(hs.at[it, at], hs.at[it, at], it, HAS + m, dev(pz * 2 + core, o, pr), high)

    def from_peer(full, scales, it, k, size, count, data, tag):
        return full, scales

    own_eight = pl.ds(pl.multiple_of(core * 8, 8), 8)
    other_eight = pl.ds(pl.multiple_of((1 - core) * 8, 8), 8)
    own_four = pl.ds(pl.multiple_of(core * 4, 4), 4)
    other_four = pl.ds(pl.multiple_of((1 - core) * 4, 4), 4)

    def piece(at, size):
        return pl.ds(pl.multiple_of(at * size, size), size)

    def pass_gram(it):
        for k in range(1, 8):
            at = core * 8 + (z + 8 - k) % 8
            arrived(ea.at[it, piece(at, GP)], it, EA + k)
            arrived(es.at[it, at], it, EAS + k)
        send(ea.at[it, own_half], ea.at[it, own_half], it, FE, sibling)
        send(es.at[it, own_eight], es.at[it, own_eight], it, FES, sibling)

    def pass_side(it):
        @pl.when(has_side)
        def _():
            for k in range(8):
                at = core * 8 + (z + 8 - k) % 8
                arrived(na.at[piece(at, GP)], it, NA + k)
                arrived(ns.at[at], it, NAS + k)

        send(na.at[own_half], na.at[own_half], it, FN, sibling, has_side)
        send(ns.at[own_eight], ns.at[own_eight], it, FNS, sibling, has_side)

    def pass_cross(it):
        @pl.when(high)
        def _():
            for m in range(1, 4):
                pz, pr = high_peer(m)
                at = core * 4 + pr * 2 + pz - 2
                arrived(ha.at[it, piece(at, HP)], it, HA + m)
                arrived(hs.at[it, at], it, HAS + m)

        @pl.when(jnp.logical_and(low, has_side))
        def _():
            for m in range(4):
                pz = zl if m % 2 == 0 else 1 - zl
                pr = r if m // 2 == 0 else 1 - r
                at = core * 4 + pr * 2 + pz
                arrived(ha.at[it, piece(at, HP)], it, HL + m)
                arrived(hs.at[it, at], it, HLS + m)

        cond = jnp.logical_or(high, has_side)
        send(ha.at[it, own_half], ha.at[it, own_half], it, FH, sibling, cond)
        send(hs.at[it, own_four], hs.at[it, own_four], it, FHS, sibling, cond)

    def unpack(value, scale):
        return value.astype(jnp.int32).astype(F32) * scale[0:1, 0:1]

    def take_gram(it):
        arrived(ea.at[it, other_half], it, FE)
        arrived(es.at[it, other_eight], it, FES)

        def body(i, carry):
            rows = piece(i, GP)
            ehi[rows, :], elo[rows, :] = split(unpack(ea[it, rows, :], es[it, i]))
            return carry

        lax.fori_loop(0, 16, body, 0)

    def take_side(it):
        @pl.when(has_side)
        def _():
            arrived(na.at[other_half], it, FN)
            arrived(ns.at[other_eight], it, FNS)

            def body(i, carry):
                rows = piece(i, GP)
                mhi[rows, :], mlo[rows, :] = split(unpack(na[rows, :], ns[i]))
                return carry

            lax.fori_loop(0, 16, body, 0)

        @pl.when(jnp.logical_not(has_side))
        def _():
            mhi[...] = jnp.zeros((ORBS, ORBS), BF)
            mlo[...] = jnp.zeros((ORBS, ORBS), BF)

    def take_cross(it):
        @pl.when(jnp.logical_or(high, has_side))
        def _():
            arrived(ha.at[it, other_half], it, FH)
            arrived(hs.at[it, other_four], it, FHS)

        def value(i):
            return jnp.concatenate(
                [unpack(ha[it, piece(2 * i, HP), :], hs[it, 2 * i]), unpack(ha[it, piece(2 * i + 1, HP), :], hs[it, 2 * i + 1])], axis=0
            )

        @pl.when(jnp.logical_and(low, has_side))
        def _():
            def body(i, carry):
                rows = piece(i, TILE)
                xhi[rows, :], xlo[rows, :] = split(value(i))
                return carry

            lax.fori_loop(0, 4, body, 0)

        @pl.when(jnp.logical_and(high, has_side))
        def _():
            def body(i, carry):
                cols = piece(i, TILE)
                xhi[:, cols], xlo[:, cols] = split(value(i).T)
                return carry

            lax.fori_loop(0, 4, body, 0)

        @pl.when(jnp.logical_not(has_side))
        def _():
            xhi[...] = jnp.zeros((ORBS, ORBS), BF)
            xlo[...] = jnp.zeros((ORBS, ORBS), BF)

    def updated(it, t, rows):
        change = dot3(chi[it, rows, :], clo[it, rows, :], ehi[...], elo[...])
        change = change + dot3(nhi[rows, :], nlo[rows, :], xhi[...], xlo[...])
        return jnp.where(live(t, cs_own), c[rows, :] - 0.5 * change, 0.0)

    wait_halo(0)
    images(0)
    gram(0)
    send(gp.at[0, other_half], gsib.at[0], 0, GSIB, sibling)
    scatter_gram(0)
    own_gram(0, True)

    @pl.when(has_side)
    def _():
        arrived(nq_in, 0, NX)
        arrived(cs_in, 0, NXC)

        def body(t, rows):
            x = nq_in[rows, :].astype(jnp.int32).astype(F32) * (CMAX / QMAX)
            nf[rows, :] = x
            nhi[rows, :], nlo[rows, :] = split(x)

        tiles(body)

    @pl.when(jnp.logical_not(has_side))
    def _():
        nf[...] = jnp.zeros((ROWS, ORBS), F32)
        nhi[...] = jnp.zeros((ROWS, ORBS), BF)
        nlo[...] = jnp.zeros((ROWS, ORBS), BF)
        cs_in[...] = jnp.zeros((8, ORBS), F32)

    def cross_round(it):
        pl.when(high)(lambda: cross(it))
        send(hp.at[it, other_half], hsib.at[it], it, HSIB, sibling, high)

    cross_round(0)
    pass_gram(0)
    pass_side(0)
    pl.when(high)(lambda: scatter_cross(0))
    send_cross(0)
    own_cross(0)
    take_gram(0)
    pass_cross(0)
    take_cross(0)

    def first(t, rows):
        x = updated(0, t, rows)
        c[rows, :] = x
        hi, lo = split(x)
        chi[1, rows, :] = hi
        clo[1, rows, :] = lo

    tiles(first)
    send_halo(1)
    take_side(0)

    def beside(t, rows):
        change = dot3(nhi[rows, :], nlo[rows, :], mhi[...], mlo[...])
        change = change + dot3(chi[0, rows, :], clo[0, rows, :], xhi[...], xlo[...], ((1,), (1,)))
        x = jnp.where(live(t, cs_in), nf[rows, :] - 0.5 * change, 0.0)
        nhi[rows, :], nlo[rows, :] = split(x)

    pl.when(has_side)(lambda: tiles(beside))

    wait_halo(1)
    images(1)
    gram(1)
    send(gp.at[1, other_half], gsib.at[1], 1, GSIB, sibling)
    cross_round(1)
    scatter_gram(1)
    pl.when(high)(lambda: scatter_cross(1))
    send_cross(1)
    own_gram(1, False)
    own_cross(1)
    pass_gram(1)
    pass_cross(1)
    take_gram(1)
    take_cross(1)

    def last(t, rows):
        out[rows, :] = updated(1, t, rows)

    tiles(last)

    for src, it, index, cond in sent:

        def wait(src=src, it=it, index=index):
            pltpu.make_async_copy(src, src, ss.at[it, index]).wait()

        if cond is None:
            wait()
        else:
            pl.when(cond)(wait)


def per_device(coefficients, basis_metric, pattern, starts):
    vm = pltpu.VMEM
    square = (ORBS, ORBS)
    scratch = [
        vm((ROWS, ORBS), F32), vm((2, 640, ORBS), BF), vm((2, ROWS, ORBS), BF),
        vm((ROWS, ORBS), F32), vm((ROWS, ORBS), BF), vm((ROWS, ORBS), BF),
        vm((ROWS, ORBS), BF), vm((ROWS, ORBS), BF), vm((ROWS, 640), BF),
        vm((2, ORBS, ORBS), F32), vm((2, ORBS, ORBS), F32),
        vm((ROWS, ORBS), I16), vm((ROWS, ORBS), I16), vm((8, ORBS), F32), vm((8, ORBS), F32),
        vm((576, 128), BF), vm((576, 128), BF), vm((576, 128), BF),
        vm((2, HALF, ORBS), F32), vm((2, HALF, ORBS), F32),
        vm((2, 8, GP, ORBS), I16), vm((2, 8, GP, ORBS), I16), vm((2, 8, 128), F32), vm((2, 8, 8, 128), F32),
        vm((2, 4, HP, ORBS), I16), vm((2, 4, HP, ORBS), I16), vm((2, 8, 128), F32), vm((2, 4, 8, 128), F32),
        vm((2, ORBS, ORBS), I16), vm((2, 16, 8, 128), F32), vm(square, I16), vm((16, 8, 128), F32),
        vm((2, ORBS, ORBS), I16), vm((2, 8, 8, 128), F32),
        vm(square, BF), vm(square, BF), vm(square, BF), vm(square, BF), vm(square, BF), vm(square, BF),
        pltpu.SemaphoreType.DMA((2, COUNT)), pltpu.SemaphoreType.DMA((2, COUNT)), pltpu.SemaphoreType.DMA((2,)),
    ]
    result = pl.pallas_call(
        kernel,
        out_shape=jax.ShapeDtypeStruct((ROWS, ORBS), F32),
        in_specs=[
            pl.BlockSpec(memory_space=pltpu.VMEM),
            pl.BlockSpec(memory_space=pl.ANY),
            pl.BlockSpec(memory_space=pltpu.SMEM),
            pl.BlockSpec(memory_space=pltpu.SMEM),
        ],
        out_specs=pl.BlockSpec(memory_space=pltpu.VMEM),
        scratch_shapes=scratch,
        compiler_params=pltpu.CompilerParams(
            collective_id=0, has_side_effects=True, vmem_limit_bytes=50 * 1024 * 1024
        ),
    )(coefficients[0], basis_metric, pattern, starts)
    return result[None]


def solution(mesh):
    in_specs = (P("orb", ("basis", "rep"), None), P("orb", None), P("orb"), P("orb"))
    out_specs = P("orb", ("basis", "rep"), None)
    return jax.shard_map(
        per_device, mesh=mesh, in_specs=in_specs, out_specs=out_specs, check_vma=False
    )
```

```python
import functools

import jax
import jax.numpy as jnp
from jax import lax
from jax.experimental import pallas as pl
from jax.experimental.pallas import tpu as pltpu
from jax.sharding import PartitionSpec as P

BLK = 64
GROUP_BLOCKS = 64
SUPPORT = 96
ITERS = 2
ROWS = 512
ORBS = 512
HALF = 256
GP = 80
PACKED = 1280
PHALF = 640
HP = 64
TILE = 128
CMAX = 6.0
QMAX = 32767.0
BF = jnp.bfloat16
F32 = jnp.float32
I16 = jnp.int16

HALO_NEXT, HALO_PREV, GSIB, HSIB = 0, 1, 2, 3
RS, RSC, HRS, HRSC = 4, 12, 20, 24
EA, EAS, NA, NAS = 28, 36, 44, 52
HA, HAS, HL, HLS = 60, 64, 68, 72
FE, FES, FN, FNS, FH, FHS = 76, 77, 78, 79, 80, 82
NX, NXC, MET, HN, HNS = 84, 85, 86, 87, 88
COUNT = 89

KEPT = [(a, b) for a in range(4) for b in range(a, 4)]


def split(x):
    hi = x.astype(BF)
    return hi, (x - hi.astype(F32)).astype(BF)


def dot(a, b, dims=((1,), (0,))):
    return lax.dot_general(a, b, (dims, ((), ())), preferred_element_type=F32)


def dot3(ah, al, bh, bl, dims=((1,), (0,))):
    return dot(ah, bh, dims) + (dot(ah, bl, dims) + dot(al, bh, dims))


def kernel(
    coef, metric, pattern, starts, out,
    c, chi, clo, nf, nhi, nlo, yhi, ylo, band, gp, hp,
    nq_out, nq_in, cs_own, cs_in, meff, mrecv, msel,
    gsib, hsib, qs, rs, qsc, rsc, hqs, hrs, hqsc, hrsc,
    ea, es, na, ns, ha, hs, ehi, elo, xhi, xlo, thi, tlo, mhi, mlo, ef,
    ss, rr, local_sem,
):
    b, o, r = lax.axis_index("basis"), lax.axis_index("orb"), lax.axis_index("rep")
    groups = lax.axis_size("orb")
    core, zl = b % 2, b // 2
    z = r * 4 + zl
    p = b * 2 + r
    q = p % 8
    low = zl < 2
    high = jnp.logical_not(low)
    side = jnp.where(low, o - 1, o + 1)
    away = jnp.where(low, o + 1, o - 1)
    has_side = jnp.logical_and(side >= 0, side < groups)
    has_away = jnp.logical_and(away >= 0, away < groups)
    j = r * 2 + zl - 2

    def dev(bb, oo, rep):
        return {"basis": bb, "orb": oo, "rep": rep}

    def zdev(zz, oo):
        return dev((zz % 4) * 2 + core, oo, zz // 4)

    sibling = dev(zl * 2 + 1 - core, o, r)

    barrier = pltpu.get_barrier_semaphore()

    def greet(device):
        pl.semaphore_signal(barrier, inc=1, device_id=device, device_id_type=pl.DeviceIdType.MESH)

    for k in range(1, 8):
        greet(zdev((z + k) % 8, o))
    greet(sibling)
    step_b = jnp.where(r == 1, b + 1, b - 1)
    has_step = jnp.logical_and(step_b >= 0, step_b < 8)

    @pl.when(has_step)
    def _():
        greet(dev(step_b, o, 1 - r))

    @pl.when(has_side)
    def _():
        base = jnp.where(low, 4, 0)
        for m in range(4):
            greet(dev(base + (m % 2) * 2 + core, side, m // 2))
        greet(dev(b, side, r))

    @pl.when(has_away)
    def _():
        greet(dev(b, away, r))

    loads = [
        pltpu.make_async_copy(coef.at[pl.ds(t * TILE, TILE)], c.at[pl.ds(t * TILE, TILE)], local_sem.at[2 + t]) for t in range(4)
    ]
    for load in loads:
        load.start()
    load_main = pltpu.make_async_copy(metric.at[pl.ds(pl.multiple_of(q * 512, 64), 512)], meff.at[pl.ds(0, 512)], local_sem.at[0])
    load_prev = pltpu.make_async_copy(
        metric.at[pl.ds(pl.multiple_of((q * 512 + 4032) % 4096, 64), 64)], meff.at[pl.ds(512, 64)], local_sem.at[1]
    )
    load_main.start()
    load_prev.start()
    lane = lax.broadcasted_iota(jnp.int32, (8, ORBS), 1) // BLK
    cs = jnp.zeros((8, ORBS), F32)
    for i in range(8):
        cs = jnp.where(lane == i, starts[i].astype(F32), cs)
    cs_own[...] = cs
    first_block = (o * GROUP_BLOCKS + p * 8).astype(F32)

    def live(t, cs_ref):
        rows = lax.broadcasted_iota(jnp.int32, (TILE, ORBS), 0) // BLK
        block = rows.astype(F32) + (first_block + (t * (TILE // BLK)).astype(F32))
        at = cs_ref[0:1, :]
        return jnp.logical_and(block >= at, block < at + SUPPORT)

    def tiles(body):
        def step(t, carry):
            body(t, pl.ds(pl.multiple_of(t * TILE, TILE), TILE))
            return carry

        lax.fori_loop(0, ROWS // TILE, step, 0)

    def prepare(t, rows):
        x = jnp.where(live(t, cs_own), c[rows, :], 0.0)
        c[rows, :] = x
        hi, lo = split(x)
        chi[0, rows, :] = hi
        clo[0, rows, :] = lo
        nq_out[rows, :] = jnp.round(jnp.clip(x, -CMAX, CMAX) * (QMAX / CMAX)).astype(I16)

    for t in range(4):
        loads[t].wait()
        prepare(jnp.int32(t), pl.ds(t * TILE, TILE))

    for it in range(ITERS):

        @pl.when(p == 0)
        def _():
            chi[it, 512:576, :] = jnp.zeros((64, ORBS), BF)

        @pl.when(p == 15)
        def _():
            chi[it, 576:640, :] = jnp.zeros((64, ORBS), BF)

    load_main.wait()
    load_prev.wait()
    right = lax.broadcasted_iota(jnp.int32, (BLK, 2 * BLK), 1) >= BLK
    for i in range(9):
        at = (q * 8 + i) % 64 if i < 8 else (q * 8 + 63) % 64
        keep = jnp.where(o * GROUP_BLOCKS + at < groups * GROUP_BLOCKS - 1, pattern[at], 0).astype(F32)
        block = meff[i * 64 : i * 64 + 64, :].astype(F32)
        meff[i * 64 : i * 64 + 64, :] = jnp.where(right, block * keep, block).astype(BF)

    waits = [jnp.int32(8), has_step.astype(jnp.int32), 5 * has_side.astype(jnp.int32), has_away.astype(jnp.int32)]
    pl.semaphore_wait(barrier, waits[0] + waits[1] + waits[2] + waits[3])

    sent = []

    def send(src, dst, it, index, device, cond=None, land=None):
        land = index if land is None else land

        def start():
            pltpu.make_async_remote_copy(
                src_ref=src, dst_ref=dst, send_sem=ss.at[it, index], recv_sem=rr.at[it, land],
                device_id=device, device_id_type=pl.DeviceIdType.MESH,
            ).start()

        if cond is None:
            start()
        else:
            pl.when(cond)(start)
        sent.append((src, it, index, cond))

    def arrived(dst, it, index):
        pltpu.make_async_copy(dst, dst, rr.at[it, index]).wait()

    def send_halo(it):
        up_b = jnp.where(r == 0, b, b + 1)
        down_b = jnp.where(r == 1, b, b - 1)
        send(chi.at[it, pl.ds(0, 64)], chi.at[it, pl.ds(576, 64)], it, HALO_NEXT, dev(down_b, o, 1 - r), p > 0)
        send(chi.at[it, pl.ds(448, 64)], chi.at[it, pl.ds(512, 64)], it, HALO_PREV, dev(up_b, o, 1 - r), p < 15)

    def wait_halo(it):
        pl.when(p < 15)(lambda: arrived(chi.at[it, pl.ds(576, 64)], it, HALO_NEXT))
        pl.when(p > 0)(lambda: arrived(chi.at[it, pl.ds(512, 64)], it, HALO_PREV))

    gives_metric = jnp.logical_and(high, o > 0)
    send(meff, mrecv, 0, MET, dev(b, o - 1, r), gives_metric)
    send_halo(0)
    partner = dev(jnp.where(low, b + 4, b - 4), side, r)
    send(nq_out, nq_in, 0, NX, partner, has_side)
    send(cs_own, cs_in, 0, NXC, partner, has_side)

    @pl.when(low)
    def _():
        msel[...] = meff[...]

    @pl.when(jnp.logical_and(high, has_side))
    def _():
        arrived(mrecv, 0, MET)
        msel[...] = mrecv[...]

    @pl.when(jnp.logical_and(high, jnp.logical_not(has_side)))
    def _():
        msel[...] = jnp.zeros((576, 128), BF)

    @pl.when(p == 8)
    def _():
        msel[512:576, :] = meff[512:576, :]

    band[...] = jnp.zeros((ROWS, 640), BF)
    row_at = lax.broadcasted_iota(jnp.int32, (128, 128), 0)
    lane_at = lax.broadcasted_iota(jnp.int32, (128, 128), 1)
    top, left = row_at < 64, lane_at < 64
    bottom, rest = row_at >= 64, lane_at >= 64
    for t in range(4):
        m = msel[t * 128 : t * 128 + 128, :].astype(F32)
        rolled = pltpu.roll(m, 64, 1)
        corner = jnp.where(jnp.logical_and(top, rest), m, 0.0)
        diag = jnp.where(top, m, jnp.where(rest, rolled, 0.0)) + corner.T
        band[t * 128 : t * 128 + 128, t * 128 : t * 128 + 128] = diag.astype(BF)
        if t < 3:
            off = jnp.where(jnp.logical_and(bottom, left), rolled, 0.0)
            band[t * 128 : t * 128 + 128, t * 128 + 128 : t * 128 + 256] = off.astype(BF)
            band[t * 128 + 128 : t * 128 + 256, t * 128 : t * 128 + 128] = off.T.astype(BF)
        else:
            band[384:512, 512:640] = jnp.where(jnp.logical_and(bottom, rest), m, 0.0).astype(BF)
    before = pltpu.roll(msel[448:576, :].astype(F32), 64, 1).T
    shifted = pltpu.roll(before, 64, 1)
    band[0:128, 512:640] = jnp.where(jnp.logical_and(top, left), shifted, 0.0).astype(BF)

    def images(it):
        def body(t, rows):
            y = dot(band[rows, :], chi[it]) + dot(band[rows, 0:512], clo[it])
            yhi[rows, :], ylo[rows, :] = split(y)

        tiles(body)

    def gram(it):
        for a in range(4):
            cols = slice(a * TILE, a * TILE + TILE)
            rest = slice(a * TILE, ORBS)
            g = dot3(chi[it, 0:512, cols], clo[it, :, cols], yhi[:, rest], ylo[:, rest], ((0,), (0,)))
            for e in range(a, 4):
                k = KEPT.index((a, e))
                gp[it, k * TILE : k * TILE + TILE, :] = g[:, (e - a) * TILE : (e - a) * TILE + TILE]

    def cross(it):
        def body(t, cols):
            hp[it, cols, :] = dot3(yhi[:, cols], ylo[:, cols], nhi[...], nlo[...], ((0,), (0,)))

        tiles(body)

    own_half = pl.ds(pl.multiple_of(core * HALF, HALF), HALF)
    other_half = pl.ds(pl.multiple_of((1 - core) * HALF, HALF), HALF)
    own_part = pl.ds(pl.multiple_of(core * PHALF, PHALF), PHALF)
    other_part = pl.ds(pl.multiple_of((1 - core) * PHALF, PHALF), PHALF)

    def pair_and_pack(it, part, from_pair, packed, scale, size, count):
        half, wide = size * count, part.shape[2]

        def add(i, top_value):
            rows = pl.ds(pl.multiple_of(core * half + i * size, size), size)
            x = part[it, rows, :] + from_pair[it, pl.ds(pl.multiple_of(i * size, size), size), :]
            part[it, rows, :] = x
            return jnp.maximum(top_value, jnp.abs(x))

        peak = jnp.max(lax.fori_loop(0, count, add, jnp.zeros((size, wide), F32)), axis=(0, 1), keepdims=True)
        peak = jnp.maximum(peak, 1e-30)
        scale[it] = jnp.broadcast_to(peak * (1.0 / QMAX), (8, 128))
        inv = QMAX / peak

        def pack(i, carry):
            rows = pl.ds(pl.multiple_of(core * half + i * size, size), size)
            packed[it, i] = jnp.round(part[it, rows, :] * inv).astype(I16)
            return carry

        lax.fori_loop(0, count, pack, 0)

    def quantized(x):
        peak = jnp.maximum(jnp.max(jnp.abs(x), axis=(0, 1), keepdims=True), 1e-30)
        return jnp.round(x * (QMAX / peak)).astype(I16), jnp.broadcast_to(peak * (1.0 / QMAX), (8, 128))

    def scatter_gram(it):
        arrived(gsib.at[it], it, GSIB)
        pair_and_pack(it, gp, gsib, qs, qsc, GP, 8)
        for k in range(1, 8):
            to = (z + k) % 8
            send(qs.at[it, to], rs.at[it, k], it, RS + k, zdev(to, o))
            send(qsc.at[it], rsc.at[it, k], it, RSC + k, zdev(to, o))

    def scatter_cross(it):
        arrived(hsib.at[it], it, HSIB)
        pair_and_pack(it, hp, hsib, hqs, hqsc, HP, 4)

    def high_peer(m):
        pz = zl if m % 2 == 0 else 5 - zl
        pr = r if m // 2 == 0 else 1 - r
        return pz, pr

    def send_cross(it):
        for m in range(1, 4):
            pz, pr = high_peer(m)
            device = dev(pz * 2 + core, o, pr)
            send(hqs.at[it, pr * 2 + pz - 2], hrs.at[it, m], it, HRS + m, device, high)
            send(hqsc.at[it], hrsc.at[it, m], it, HRSC + m, device, high)

    def own_gram(it):
        rows = pl.ds(pl.multiple_of(core * PHALF + z * GP, GP), GP)
        total = gp[it, rows, :]
        for k in range(1, 8):
            arrived(rs.at[it, k], it, RS + k)
            arrived(rsc.at[it, k], it, RSC + k)
            total = total + rs[it, k].astype(jnp.int32).astype(F32) * rsc[it, k, 0:1, 0:1]
        here = lax.broadcasted_iota(jnp.int32, (GP, TILE), 0) + (core * PHALF + z * GP)
        tile = lax.shift_right_logical(here, 7)
        within = jnp.bitwise_and(here, 127) == lax.broadcasted_iota(jnp.int32, (GP, TILE), 1)
        on = jnp.zeros((GP, TILE), F32)
        for a in range(4):
            on = jnp.where(jnp.logical_and(tile == KEPT.index((a, a)), within), 1.0, on)
        value, scale = quantized(total * (1.0 / (SUPPORT * BLK)) - on)
        ea[it, rows, :] = value
        at = core * 8 + z
        es[it, at] = scale
        for k in range(1, 8):
            device = zdev((z + k) % 8, o)
            send(ea.at[it, rows], ea.at[it, rows], it, EA + k, device)
            send(es.at[it, at], es.at[it, at], it, EAS + k, device)

    def own_cross(it):
        rows = pl.ds(pl.multiple_of(core * HALF + j * HP, HP), HP)
        at = core * 4 + j
        low_there = jnp.logical_and(high, o < groups - 1)

        @pl.when(high)
        def _():
            total = hp[it, rows, :]
            for m in range(1, 4):
                arrived(hrs.at[it, m], it, HRS + m)
                arrived(hrsc.at[it, m], it, HRSC + m)
                total = total + hrs[it, m].astype(jnp.int32).astype(F32) * hrsc[it, m, 0:1, 0:1]
            value, scale = quantized(total * (1.0 / (SUPPORT * BLK)))
            ha[it, rows, :] = value
            hs[it, at] = scale

        for m in range(1, 4):
            pz, pr = high_peer(m)
            send(ha.at[it, rows], ha.at[it, rows], it, HA + m, dev(pz * 2 + core, o, pr), high)
            send(hs.at[it, at], hs.at[it, at], it, HAS + m, dev(pz * 2 + core, o, pr), high)
        for m in range(2):
            device = dev(2 + core, o + 1, r) if m == 0 else dev(core, o + 1, 1 - r)
            send(ha.at[it, rows], ha.at[it, rows], it, HL + m, device, low_there, HL + jnp.maximum(zl - 2, 0))
            send(hs.at[it, at], hs.at[it, at], it, HLS + m, device, low_there, HLS + jnp.maximum(zl - 2, 0))

    own_eight = pl.ds(pl.multiple_of(core * 8, 8), 8)
    other_eight = pl.ds(pl.multiple_of((1 - core) * 8, 8), 8)
    near = jnp.where(jnp.logical_and(low, zl == 0), 1 - r, r)
    near_rows = pl.ds(pl.multiple_of(core * HALF + near * 128, 128), 128)
    far_rows = pl.ds(pl.multiple_of(core * HALF + (1 - near) * 128, 128), 128)
    near_two = pl.ds(core * 4 + near * 2, 2)
    far_two = pl.ds(core * 4 + (1 - near) * 2, 2)
    pair_near_rows = pl.ds(pl.multiple_of((1 - core) * HALF + near * 128, 128), 128)
    pair_far_rows = pl.ds(pl.multiple_of((1 - core) * HALF + (1 - near) * 128, 128), 128)
    pair_near_two = pl.ds((1 - core) * 4 + near * 2, 2)
    pair_far_two = pl.ds((1 - core) * 4 + (1 - near) * 2, 2)

    def piece(at, size):
        return pl.ds(pl.multiple_of(at * size, size), size)

    def pass_gram(it, with_side):
        for k in range(1, 8):
            at = core * 8 + (z + 8 - k) % 8
            arrived(ea.at[it, piece(at, GP)], it, EA + k)
            arrived(es.at[it, at], it, EAS + k)
        send(ea.at[it, own_part], ea.at[it, own_part], it, FE, sibling)
        send(es.at[it, own_eight], es.at[it, own_eight], it, FES, sibling)
        if with_side:
            send(ea.at[it, own_part], na.at[own_part], it, NA, dev(b, away, r), has_away)
            send(es.at[it, own_eight], ns.at[own_eight], it, NAS, dev(b, away, r), has_away)

    def pass_side(it):
        @pl.when(has_side)
        def _():
            arrived(na.at[own_part], it, NA)
            arrived(ns.at[own_eight], it, NAS)

        send(na.at[own_part], na.at[own_part], it, FN, sibling, has_side)
        send(ns.at[own_eight], ns.at[own_eight], it, FNS, sibling, has_side)

    def pass_cross(it):
        cond = jnp.logical_or(high, has_side)
        low_side = jnp.logical_and(low, has_side)

        def high_arrived(m):
            pz, pr = high_peer(m)
            at = core * 4 + pr * 2 + pz - 2
            arrived(ha.at[it, piece(at, HP)], it, HA + m)
            arrived(hs.at[it, at], it, HAS + m)

        pl.when(high)(lambda: high_arrived(1))

        @pl.when(low_side)
        def _():
            for m in range(2):
                at = core * 4 + near * 2 + m
                arrived(ha.at[it, piece(at, HP)], it, HL + m)
                arrived(hs.at[it, at], it, HLS + m)

        beside_low = dev((1 - zl) * 2 + core, o, r)
        send(ha.at[it, near_rows], ha.at[it, near_rows], it, HN, beside_low, low_side)
        send(hs.at[it, near_two], hs.at[it, near_two], it, HNS, beside_low, low_side)
        send(ha.at[it, near_rows], ha.at[it, near_rows], it, FH, sibling, cond)
        send(hs.at[it, near_two], hs.at[it, near_two], it, FHS, sibling, cond)

        @pl.when(high)
        def _():
            high_arrived(2)
            high_arrived(3)

        @pl.when(low_side)
        def _():
            arrived(ha.at[it, far_rows], it, HN)
            arrived(hs.at[it, far_two], it, HNS)

        send(ha.at[it, far_rows], ha.at[it, far_rows], it, FH + 1, sibling, cond)
        send(hs.at[it, far_two], hs.at[it, far_two], it, FHS + 1, sibling, cond)

    def unpack(value, scale):
        return value.astype(jnp.int32).astype(F32) * scale[0:1, 0:1]

    def spread(packed, scales, to_hi, to_lo):
        def body(i, carry):
            rows = piece(i, GP)
            ef[rows, :] = unpack(packed[rows, :], scales[i])
            return carry

        lax.fori_loop(0, 16, body, 0)
        for k, (a, e) in enumerate(KEPT):
            x = ef[k * TILE : k * TILE + TILE, :]
            at, to = slice(a * TILE, a * TILE + TILE), slice(e * TILE, e * TILE + TILE)
            to_hi[at, to], to_lo[at, to] = split(x)
            if a != e:
                to_hi[to, at], to_lo[to, at] = split(x.T)

    def take_gram(it):
        arrived(ea.at[it, other_part], it, FE)
        arrived(es.at[it, other_eight], it, FES)
        spread(ea.at[it], es.at[it], ehi, elo)

    def take_side(it):
        @pl.when(has_side)
        def _():
            arrived(na.at[other_part], it, FN)
            arrived(ns.at[other_eight], it, FNS)
            spread(na, ns, mhi, mlo)

    def cross_value(it, i):
        return jnp.concatenate(
            [unpack(ha[it, piece(2 * i, HP), :], hs[it, 2 * i]), unpack(ha[it, piece(2 * i + 1, HP), :], hs[it, 2 * i + 1])], axis=0
        )

    def cross_plain(it, to_hi, to_lo):
        def body(i, carry):
            rows = piece(i, TILE)
            to_hi[rows, :], to_lo[rows, :] = split(cross_value(it, i))
            return carry

        lax.fori_loop(0, 4, body, 0)

    def cross_turned(it, to_hi, to_lo):
        def body(i, carry):
            cols = piece(i, TILE)
            to_hi[:, cols], to_lo[:, cols] = split(cross_value(it, i).T)
            return carry

        lax.fori_loop(0, 4, body, 0)

    def take_cross(it):
        @pl.when(jnp.logical_or(high, has_side))
        def _():
            arrived(ha.at[it, pair_near_rows], it, FH)
            arrived(hs.at[it, pair_near_two], it, FHS)
            arrived(ha.at[it, pair_far_rows], it, FH + 1)
            arrived(hs.at[it, pair_far_two], it, FHS + 1)

        pl.when(jnp.logical_and(low, has_side))(lambda: cross_plain(it, xhi, xlo))
        pl.when(jnp.logical_and(high, has_side))(lambda: cross_turned(it, xhi, xlo))

        @pl.when(jnp.logical_not(has_side))
        def _():
            xhi[...] = jnp.zeros((ORBS, ORBS), BF)
            xlo[...] = jnp.zeros((ORBS, ORBS), BF)

    def updated(it, t, rows):
        change = dot3(chi[it, rows, :], clo[it, rows, :], ehi[...], elo[...])
        change = change + dot3(nhi[rows, :], nlo[rows, :], xhi[...], xlo[...])
        return jnp.where(live(t, cs_own), c[rows, :] - 0.5 * change, 0.0)

    def take_rows():
        @pl.when(has_side)
        def _():
            arrived(nq_in, 0, NX)
            arrived(cs_in, 0, NXC)

            def body(t, rows):
                x = nq_in[rows, :].astype(jnp.int32).astype(F32) * (CMAX / QMAX)
                nf[rows, :] = x
                nhi[rows, :], nlo[rows, :] = split(x)

            tiles(body)

        @pl.when(jnp.logical_not(has_side))
        def _():
            nhi[...] = jnp.zeros((ROWS, ORBS), BF)
            nlo[...] = jnp.zeros((ROWS, ORBS), BF)

    def cross_round(it):
        pl.when(high)(lambda: cross(it))
        send(hp.at[it, other_half], hsib.at[it], it, HSIB, sibling, high)

    def first(t, rows):
        x = updated(0, t, rows)
        c[rows, :] = x
        hi, lo = split(x)
        chi[1, rows, :] = hi
        clo[1, rows, :] = lo

    def some(body, start, step):
        def run(i, carry):
            t = start + i * step
            body(t, pl.ds(pl.multiple_of(t * TILE, TILE), TILE))
            return carry

        lax.fori_loop(0, 2, run, 0)

    def beside(t, rows):
        change = dot3(nhi[rows, :], nlo[rows, :], mhi[...], mlo[...])
        change = change + dot3(chi[0, rows, :], clo[0, rows, :], thi[...], tlo[...])
        x = jnp.where(live(t, cs_in), nf[rows, :] - 0.5 * change, 0.0)
        nhi[rows, :], nlo[rows, :] = split(x)

    def last(t, rows):
        out[rows, :] = updated(1, t, rows)

    wait_halo(0)
    images(0)
    gram(0)
    send(gp.at[0, other_part], gsib.at[0], 0, GSIB, sibling)
    scatter_gram(0)
    take_rows()
    cross_round(0)
    own_gram(0)
    pl.when(high)(lambda: scatter_cross(0))
    send_cross(0)
    own_cross(0)
    pass_gram(0, True)
    pass_cross(0)
    take_gram(0)
    take_cross(0)
    some(first, 0, 3)
    send_halo(1)
    some(first, 1, 1)
    pass_side(0)
    pl.when(jnp.logical_and(low, has_side))(lambda: cross_turned(0, thi, tlo))
    pl.when(jnp.logical_and(high, has_side))(lambda: cross_plain(0, thi, tlo))
    take_side(0)
    pl.when(has_side)(lambda: tiles(beside))

    wait_halo(1)
    images(1)
    gram(1)
    send(gp.at[1, other_part], gsib.at[1], 1, GSIB, sibling)
    cross_round(1)
    scatter_gram(1)
    pl.when(high)(lambda: scatter_cross(1))
    send_cross(1)
    own_gram(1)
    own_cross(1)
    pass_gram(1, False)
    pass_cross(1)
    take_gram(1)
    take_cross(1)
    tiles(last)

    for src, it, index, cond in sent:

        def wait(src=src, it=it, index=index):
            pltpu.make_async_copy(src, src, ss.at[it, index]).wait()

        if cond is None:
            wait()
        else:
            pl.when(cond)(wait)


def per_device(coefficients, basis_metric, pattern, starts):
    vm = pltpu.VMEM
    square = (ORBS, ORBS)
    scratch = [
        vm((ROWS, ORBS), F32), vm((2, 640, ORBS), BF), vm((2, ROWS, ORBS), BF),
        vm((ROWS, ORBS), F32), vm((ROWS, ORBS), BF), vm((ROWS, ORBS), BF),
        vm((ROWS, ORBS), BF), vm((ROWS, ORBS), BF), vm((ROWS, 640), BF),
        vm((2, PACKED, TILE), F32), vm((2, ORBS, ORBS), F32),
        vm((ROWS, ORBS), I16), vm((ROWS, ORBS), I16), vm((8, ORBS), F32), vm((8, ORBS), F32),
        vm((576, 128), BF), vm((576, 128), BF), vm((576, 128), BF),
        vm((2, PHALF, TILE), F32), vm((2, HALF, ORBS), F32),
        vm((2, 8, GP, TILE), I16), vm((2, 8, GP, TILE), I16), vm((2, 8, 128), F32), vm((2, 8, 8, 128), F32),
        vm((2, 4, HP, ORBS), I16), vm((2, 4, HP, ORBS), I16), vm((2, 8, 128), F32), vm((2, 4, 8, 128), F32),
        vm((2, PACKED, TILE), I16), vm((2, 16, 8, 128), F32), vm((PACKED, TILE), I16), vm((16, 8, 128), F32),
        vm((2, ORBS, ORBS), I16), vm((2, 8, 8, 128), F32),
        vm(square, BF), vm(square, BF), vm(square, BF), vm(square, BF), vm(square, BF), vm(square, BF),
        vm(square, BF), vm(square, BF), vm((PACKED, TILE), F32),
        pltpu.SemaphoreType.DMA((2, COUNT)), pltpu.SemaphoreType.DMA((2, COUNT)), pltpu.SemaphoreType.DMA((6,)),
    ]
    result = pl.pallas_call(
        kernel,
        out_shape=jax.ShapeDtypeStruct((ROWS, ORBS), F32),
        in_specs=[
            pl.BlockSpec(memory_space=pltpu.HBM),
            pl.BlockSpec(memory_space=pltpu.HBM),
            pl.BlockSpec(memory_space=pltpu.SMEM),
            pl.BlockSpec(memory_space=pltpu.SMEM),
        ],
        out_specs=pl.BlockSpec(memory_space=pltpu.VMEM),
        scratch_shapes=scratch,
        compiler_params=pltpu.CompilerParams(
            collective_id=0, has_side_effects=True, vmem_limit_bytes=50 * 1024 * 1024
        ),
    )(coefficients[0], basis_metric, pattern, starts)
    return result[None]


def solution(mesh):
    in_specs = (P("orb", ("basis", "rep"), None), P("orb", None), P("orb"), P("orb"))
    out_specs = P("orb", ("basis", "rep"), None)
    return jax.shard_map(
        per_device, mesh=mesh, in_specs=in_specs, out_specs=out_specs, check_vma=False
    )
```

```python
import functools

import jax
import jax.numpy as jnp
from jax import lax
from jax.experimental import pallas as pl
from jax.experimental.pallas import tpu as pltpu
from jax.sharding import PartitionSpec as P

BLK = 64
GROUP_BLOCKS = 64
SUPPORT = 96
ITERS = 2
ROWS = 512
ORBS = 512
HALF = 256
GP = 80
PACKED = 1280
PHALF = 640
HP = 64
TILE = 128
CMAX = 6.0
QMAX = 32767.0
BF = jnp.bfloat16
F32 = jnp.float32
I16 = jnp.int16

HALO_NEXT, HALO_PREV, GSIB, RS, RSC, EA, EAS, NA, NAS = 0, 1, 2, 3, 11, 19, 27, 35, 36
FE, FES, FN, FNS, NXC, MET = 37, 38, 39, 40, 41, 42
CHUNKS = 2
WIDE = ORBS // CHUNKS
HSIB, HRS, HRSC, HA, HAS, HL, HLS, HN, HNS, FH, FHS, NX = 0, 1, 5, 9, 13, 17, 19, 21, 23, 25, 27, 29
CHUNK_COUNT = 30
COUNT = 43 + CHUNKS * CHUNK_COUNT


def of(ch, index):
    return 43 + ch * CHUNK_COUNT + index


KEPT = [(a, b) for a in range(4) for b in range(a, 4)]


def split(x):
    hi = x.astype(BF)
    return hi, (x - hi.astype(F32)).astype(BF)


def dot(a, b, dims=((1,), (0,))):
    return lax.dot_general(a, b, (dims, ((), ())), preferred_element_type=F32)


def dot3(ah, al, bh, bl, dims=((1,), (0,))):
    return dot(ah, bh, dims) + (dot(ah, bl, dims) + dot(al, bh, dims))


def kernel(
    coef, metric, pattern, starts, out,
    c, chi, clo, nf, nhi, nlo, yhi, ylo, band, gp, hp,
    nq_out, nq_in, cs_own, cs_in, meff, mrecv, msel,
    gsib, hsib, qs, rs, qsc, rsc, hqs, hrs, hqsc, hrsc,
    ea, es, na, ns, ha, hs, ehi, elo, xhi, xlo, thi, tlo, mhi, mlo, ef,
    ss, rr, local_sem,
):
    b, o, r = lax.axis_index("basis"), lax.axis_index("orb"), lax.axis_index("rep")
    groups = lax.axis_size("orb")
    core, zl = b % 2, b // 2
    z = r * 4 + zl
    p = b * 2 + r
    q = p % 8
    low = zl < 2
    high = jnp.logical_not(low)
    side = jnp.where(low, o - 1, o + 1)
    away = jnp.where(low, o + 1, o - 1)
    has_side = jnp.logical_and(side >= 0, side < groups)
    has_away = jnp.logical_and(away >= 0, away < groups)
    j = r * 2 + zl - 2

    def dev(bb, oo, rep):
        return {"basis": bb, "orb": oo, "rep": rep}

    def zdev(zz, oo):
        return dev((zz % 4) * 2 + core, oo, zz // 4)

    sibling = dev(zl * 2 + 1 - core, o, r)

    barrier = pltpu.get_barrier_semaphore()

    def greet(device):
        pl.semaphore_signal(barrier, inc=1, device_id=device, device_id_type=pl.DeviceIdType.MESH)

    for k in range(1, 8):
        greet(zdev((z + k) % 8, o))
    greet(sibling)
    step_b = jnp.where(r == 1, b + 1, b - 1)
    has_step = jnp.logical_and(step_b >= 0, step_b < 8)

    @pl.when(has_step)
    def _():
        greet(dev(step_b, o, 1 - r))

    @pl.when(has_side)
    def _():
        base = jnp.where(low, 4, 0)
        for m in range(4):
            greet(dev(base + (m % 2) * 2 + core, side, m // 2))
        greet(dev(b, side, r))

    @pl.when(has_away)
    def _():
        greet(dev(b, away, r))

    loads = [
        pltpu.make_async_copy(coef.at[pl.ds(t * TILE, TILE)], c.at[pl.ds(t * TILE, TILE)], local_sem.at[2 + t]) for t in range(4)
    ]
    for load in loads:
        load.start()
    load_main = pltpu.make_async_copy(metric.at[pl.ds(pl.multiple_of(q * 512, 64), 512)], meff.at[pl.ds(0, 512)], local_sem.at[0])
    load_prev = pltpu.make_async_copy(
        metric.at[pl.ds(pl.multiple_of((q * 512 + 4032) % 4096, 64), 64)], meff.at[pl.ds(512, 64)], local_sem.at[1]
    )
    load_main.start()
    load_prev.start()
    lane = lax.broadcasted_iota(jnp.int32, (8, ORBS), 1) // BLK
    cs = jnp.zeros((8, ORBS), F32)
    for i in range(8):
        cs = jnp.where(lane == i, starts[i].astype(F32), cs)
    cs_own[...] = cs
    first_block = (o * GROUP_BLOCKS + p * 8).astype(F32)

    def live(t, cs_ref):
        rows = lax.broadcasted_iota(jnp.int32, (TILE, ORBS), 0) // BLK
        block = rows.astype(F32) + (first_block + (t * (TILE // BLK)).astype(F32))
        at = cs_ref[0:1, :]
        return jnp.logical_and(block >= at, block < at + SUPPORT)

    def tiles(body):
        def step(t, carry):
            body(t, pl.ds(pl.multiple_of(t * TILE, TILE), TILE))
            return carry

        lax.fori_loop(0, ROWS // TILE, step, 0)

    def prepare(t, rows):
        x = jnp.where(live(t, cs_own), c[rows, :], 0.0)
        c[rows, :] = x
        hi, lo = split(x)
        chi[0, rows, :] = hi
        clo[0, rows, :] = lo
        coded = jnp.round(jnp.clip(x, -CMAX, CMAX) * (QMAX / CMAX)).astype(I16)
        for ch in range(CHUNKS):
            nq_out[ch, rows, :] = coded[:, ch * WIDE : ch * WIDE + WIDE]

    for t in range(4):
        loads[t].wait()
        prepare(jnp.int32(t), pl.ds(t * TILE, TILE))

    for it in range(ITERS):

        @pl.when(p == 0)
        def _():
            chi[it, 512:576, :] = jnp.zeros((64, ORBS), BF)

        @pl.when(p == 15)
        def _():
            chi[it, 576:640, :] = jnp.zeros((64, ORBS), BF)

    load_main.wait()
    load_prev.wait()
    right = lax.broadcasted_iota(jnp.int32, (BLK, 2 * BLK), 1) >= BLK
    for i in range(9):
        at = (q * 8 + i) % 64 if i < 8 else (q * 8 + 63) % 64
        keep = jnp.where(o * GROUP_BLOCKS + at < groups * GROUP_BLOCKS - 1, pattern[at], 0).astype(F32)
        block = meff[i * 64 : i * 64 + 64, :].astype(F32)
        meff[i * 64 : i * 64 + 64, :] = jnp.where(right, block * keep, block).astype(BF)

    waits = [jnp.int32(8), has_step.astype(jnp.int32), 5 * has_side.astype(jnp.int32), has_away.astype(jnp.int32)]
    pl.semaphore_wait(barrier, waits[0] + waits[1] + waits[2] + waits[3])

    sent = []

    def send(src, dst, it, index, device, cond=None, land=None):
        land = index if land is None else land

        def start():
            pltpu.make_async_remote_copy(
                src_ref=src, dst_ref=dst, send_sem=ss.at[it, index], recv_sem=rr.at[it, land],
                device_id=device, device_id_type=pl.DeviceIdType.MESH,
            ).start()

        if cond is None:
            start()
        else:
            pl.when(cond)(start)
        sent.append((src, it, index, cond))

    def arrived(dst, it, index):
        pltpu.make_async_copy(dst, dst, rr.at[it, index]).wait()

    def send_halo(it):
        up_b = jnp.where(r == 0, b, b + 1)
        down_b = jnp.where(r == 1, b, b - 1)
        send(chi.at[it, pl.ds(0, 64)], chi.at[it, pl.ds(576, 64)], it, HALO_NEXT, dev(down_b, o, 1 - r), p > 0)
        send(chi.at[it, pl.ds(448, 64)], chi.at[it, pl.ds(512, 64)], it, HALO_PREV, dev(up_b, o, 1 - r), p < 15)

    def wait_halo(it):
        pl.when(p < 15)(lambda: arrived(chi.at[it, pl.ds(576, 64)], it, HALO_NEXT))
        pl.when(p > 0)(lambda: arrived(chi.at[it, pl.ds(512, 64)], it, HALO_PREV))

    gives_metric = jnp.logical_and(high, o > 0)
    send(meff, mrecv, 0, MET, dev(b, o - 1, r), gives_metric)
    send_halo(0)
    partner = dev(jnp.where(low, b + 4, b - 4), side, r)
    send(cs_own, cs_in, 0, NXC, partner, has_side)

    def send_rows(ch):
        send(nq_out.at[ch], nq_in.at[ch], 0, of(ch, NX), partner, has_side)

    send_rows(0)

    @pl.when(low)
    def _():
        msel[...] = meff[...]

    @pl.when(jnp.logical_and(high, has_side))
    def _():
        arrived(mrecv, 0, MET)
        msel[...] = mrecv[...]

    @pl.when(jnp.logical_and(high, jnp.logical_not(has_side)))
    def _():
        msel[...] = jnp.zeros((576, 128), BF)

    @pl.when(p == 8)
    def _():
        msel[512:576, :] = meff[512:576, :]

    band[...] = jnp.zeros((ROWS, 640), BF)
    row_at = lax.broadcasted_iota(jnp.int32, (128, 128), 0)
    lane_at = lax.broadcasted_iota(jnp.int32, (128, 128), 1)
    top, left = row_at < 64, lane_at < 64
    bottom, rest = row_at >= 64, lane_at >= 64
    for t in range(4):
        m = msel[t * 128 : t * 128 + 128, :].astype(F32)
        rolled = pltpu.roll(m, 64, 1)
        corner = jnp.where(jnp.logical_and(top, rest), m, 0.0)
        diag = jnp.where(top, m, jnp.where(rest, rolled, 0.0)) + corner.T
        band[t * 128 : t * 128 + 128, t * 128 : t * 128 + 128] = diag.astype(BF)
        if t < 3:
            off = jnp.where(jnp.logical_and(bottom, left), rolled, 0.0)
            band[t * 128 : t * 128 + 128, t * 128 + 128 : t * 128 + 256] = off.astype(BF)
            band[t * 128 + 128 : t * 128 + 256, t * 128 : t * 128 + 128] = off.T.astype(BF)
        else:
            band[384:512, 512:640] = jnp.where(jnp.logical_and(bottom, rest), m, 0.0).astype(BF)
    before = pltpu.roll(msel[448:576, :].astype(F32), 64, 1).T
    shifted = pltpu.roll(before, 64, 1)
    band[0:128, 512:640] = jnp.where(jnp.logical_and(top, left), shifted, 0.0).astype(BF)

    def images(it):
        def body(t, rows):
            yhi[rows, :], ylo[rows, :] = split(dot(band[rows, 0:512], chi[it, 0:512]) + dot(band[rows, 0:512], clo[it]))

        tiles(body)

    def edges(it):
        wait_halo(it)
        for rows in (slice(0, 64), slice(448, 512)):
            y = yhi[rows, :].astype(F32) + ylo[rows, :].astype(F32)
            yhi[rows, :], ylo[rows, :] = split(y + dot(band[rows, 512:640], chi[it, 512:640]))

    def gram(it):
        for a in range(4):
            cols = slice(a * TILE, a * TILE + TILE)
            rest = slice(a * TILE, ORBS)
            g = dot3(chi[it, 0:512, cols], clo[it, :, cols], yhi[:, rest], ylo[:, rest], ((0,), (0,)))
            for e in range(a, 4):
                k = KEPT.index((a, e))
                gp[it, k * TILE : k * TILE + TILE, :] = g[:, (e - a) * TILE : (e - a) * TILE + TILE]

    def cross(it, ch):
        wide = slice(ch * WIDE, ch * WIDE + WIDE)

        def body(t, cols):
            hp[it, ch, cols, :] = dot3(yhi[:, cols], ylo[:, cols], nhi[:, wide], nlo[:, wide], ((0,), (0,)))

        tiles(body)

    own_half = pl.ds(pl.multiple_of(core * HALF, HALF), HALF)
    other_half = pl.ds(pl.multiple_of((1 - core) * HALF, HALF), HALF)
    own_part = pl.ds(pl.multiple_of(core * PHALF, PHALF), PHALF)
    other_part = pl.ds(pl.multiple_of((1 - core) * PHALF, PHALF), PHALF)

    def pair_and_pack(part, from_pair, packed, scale, size, count):
        half, wide = size * count, part.shape[1]

        def add(i, top_value):
            rows = pl.ds(pl.multiple_of(core * half + i * size, size), size)
            x = part[rows, :] + from_pair[pl.ds(pl.multiple_of(i * size, size), size), :]
            part[rows, :] = x
            return jnp.maximum(top_value, jnp.abs(x))

        peak = jnp.max(lax.fori_loop(0, count, add, jnp.zeros((size, wide), F32)), axis=(0, 1), keepdims=True)
        peak = jnp.maximum(peak, 1e-30)
        scale[...] = jnp.broadcast_to(peak * (1.0 / QMAX), (8, 128))
        inv = QMAX / peak

        def pack(i, carry):
            rows = pl.ds(pl.multiple_of(core * half + i * size, size), size)
            packed[i] = jnp.round(part[rows, :] * inv).astype(I16)
            return carry

        lax.fori_loop(0, count, pack, 0)

    def quantized(x):
        peak = jnp.maximum(jnp.max(jnp.abs(x), axis=(0, 1), keepdims=True), 1e-30)
        return jnp.round(x * (QMAX / peak)).astype(I16), jnp.broadcast_to(peak * (1.0 / QMAX), (8, 128))

    def scatter_gram(it):
        arrived(gsib.at[it], it, GSIB)
        pair_and_pack(gp.at[it], gsib.at[it], qs.at[it], qsc.at[it], GP, 8)
        for k in range(1, 8):
            to = (z + k) % 8
            send(qs.at[it, to], rs.at[it, k], it, RS + k, zdev(to, o))
            send(qsc.at[it], rsc.at[it, k], it, RSC + k, zdev(to, o))

    def scatter_cross(it, ch):
        arrived(hsib.at[it, ch], it, of(ch, HSIB))
        pair_and_pack(hp.at[it, ch], hsib.at[it, ch], hqs.at[it, ch], hqsc.at[it, ch], HP, 4)

    def high_peer(m):
        pz = zl if m % 2 == 0 else 5 - zl
        pr = r if m // 2 == 0 else 1 - r
        return pz, pr

    def send_cross(it, ch):
        pl.when(high)(lambda: scatter_cross(it, ch))
        for m in range(1, 4):
            pz, pr = high_peer(m)
            device = dev(pz * 2 + core, o, pr)
            send(hqs.at[it, ch, jnp.maximum(pr * 2 + pz - 2, 0)], hrs.at[it, ch, m], it, of(ch, HRS + m), device, high)
            send(hqsc.at[it, ch], hrsc.at[it, ch, m], it, of(ch, HRSC + m), device, high)

    def own_gram(it):
        rows = pl.ds(pl.multiple_of(core * PHALF + z * GP, GP), GP)
        total = gp[it, rows, :]
        for k in range(1, 8):
            arrived(rs.at[it, k], it, RS + k)
            arrived(rsc.at[it, k], it, RSC + k)
            total = total + rs[it, k].astype(jnp.int32).astype(F32) * rsc[it, k, 0:1, 0:1]
        here = lax.broadcasted_iota(jnp.int32, (GP, TILE), 0) + (core * PHALF + z * GP)
        tile = lax.shift_right_logical(here, 7)
        within = jnp.bitwise_and(here, 127) == lax.broadcasted_iota(jnp.int32, (GP, TILE), 1)
        on = jnp.zeros((GP, TILE), F32)
        for a in range(4):
            on = jnp.where(jnp.logical_and(tile == KEPT.index((a, a)), within), 1.0, on)
        value, scale = quantized(total * (1.0 / (SUPPORT * BLK)) - on)
        ea[it, rows, :] = value
        at = core * 8 + z
        es[it, at] = scale
        for k in range(1, 8):
            device = zdev((z + k) % 8, o)
            send(ea.at[it, rows], ea.at[it, rows], it, EA + k, device)
            send(es.at[it, at], es.at[it, at], it, EAS + k, device)

    def own_cross(it, ch):
        rows = pl.ds(pl.multiple_of(core * HALF + jnp.maximum(j, 0) * HP, HP), HP)
        at = core * 4 + jnp.maximum(j, 0)
        low_there = jnp.logical_and(high, o < groups - 1)
        data, tags = ha.at[it, ch], hs.at[it, ch]

        @pl.when(high)
        def _():
            total = hp[it, ch, rows, :]
            for m in range(1, 4):
                arrived(hrs.at[it, ch, m], it, of(ch, HRS + m))
                arrived(hrsc.at[it, ch, m], it, of(ch, HRSC + m))
                total = total + hrs[it, ch, m].astype(jnp.int32).astype(F32) * hrsc[it, ch, m, 0:1, 0:1]
            value, scale = quantized(total * (1.0 / (SUPPORT * BLK)))
            ha[it, ch, rows, :] = value
            hs[it, ch, at] = scale

        for m in (3, 1):
            pz, pr = high_peer(m)
            send(data.at[rows], data.at[rows], it, of(ch, HA + m), dev(pz * 2 + core, o, pr), high)
            send(tags.at[at], tags.at[at], it, of(ch, HAS + m), dev(pz * 2 + core, o, pr), high)
        for m in range(2):
            device = dev(2 + core, o + 1, r) if m == 0 else dev(core, o + 1, 1 - r)
            mine = jnp.maximum(zl - 2, 0)
            send(data.at[rows], data.at[rows], it, of(ch, HL + m), device, low_there, of(ch, HL + mine))
            send(tags.at[at], tags.at[at], it, of(ch, HLS + m), device, low_there, of(ch, HLS + mine))

    own_eight = pl.ds(pl.multiple_of(core * 8, 8), 8)
    other_eight = pl.ds(pl.multiple_of((1 - core) * 8, 8), 8)
    near = jnp.where(jnp.logical_and(low, zl == 0), 1 - r, r)
    near_rows = pl.ds(pl.multiple_of(core * HALF + near * 128, 128), 128)
    far_rows = pl.ds(pl.multiple_of(core * HALF + (1 - near) * 128, 128), 128)
    near_two = pl.ds(core * 4 + near * 2, 2)
    far_two = pl.ds(core * 4 + (1 - near) * 2, 2)
    pair_near_rows = pl.ds(pl.multiple_of((1 - core) * HALF + near * 128, 128), 128)
    pair_far_rows = pl.ds(pl.multiple_of((1 - core) * HALF + (1 - near) * 128, 128), 128)
    pair_near_two = pl.ds((1 - core) * 4 + near * 2, 2)
    pair_far_two = pl.ds((1 - core) * 4 + (1 - near) * 2, 2)

    def piece(at, size):
        return pl.ds(pl.multiple_of(at * size, size), size)

    def pass_gram(it, with_side):
        for k in range(1, 8):
            at = core * 8 + (z + 8 - k) % 8
            arrived(ea.at[it, piece(at, GP)], it, EA + k)
            arrived(es.at[it, at], it, EAS + k)
        send(ea.at[it, own_part], ea.at[it, own_part], it, FE, sibling)
        send(es.at[it, own_eight], es.at[it, own_eight], it, FES, sibling)
        if with_side:
            send(ea.at[it, own_part], na.at[own_part], it, NA, dev(b, away, r), has_away)
            send(es.at[it, own_eight], ns.at[own_eight], it, NAS, dev(b, away, r), has_away)

    def pass_side(it):
        @pl.when(has_side)
        def _():
            arrived(na.at[own_part], it, NA)
            arrived(ns.at[own_eight], it, NAS)

        send(na.at[own_part], na.at[own_part], it, FN, sibling, has_side)
        send(ns.at[own_eight], ns.at[own_eight], it, FNS, sibling, has_side)

    def pass_cross(it, ch):
        cond = jnp.logical_or(high, has_side)
        low_side = jnp.logical_and(low, has_side)
        data, tags = ha.at[it, ch], hs.at[it, ch]

        def pass_on(at, index, device, ok):
            rows = piece(at, HP)
            send(data.at[rows], data.at[rows], it, of(ch, HN + index), device, ok)
            send(tags.at[at], tags.at[at], it, of(ch, HNS + index), device, ok)

        def taken(at, index, tag):
            arrived(data.at[piece(at, HP)], it, of(ch, index))
            arrived(tags.at[at], it, of(ch, tag))

        def to_sibling(rows, two, index):
            send(data.at[rows], data.at[rows], it, of(ch, FH + index), sibling, cond)
            send(tags.at[two], tags.at[two], it, of(ch, FHS + index), sibling, cond)

        base = core * 4
        beside_low = dev(jnp.maximum(1 - zl, 0) * 2 + core, o, r)
        for m in range(2):
            at = base + near * 2 + m
            pl.when(low_side)(functools.partial(taken, at, HL + m, HLS + m))
            pass_on(at, m, beside_low, low_side)
        pl.when(high)(lambda: taken(base + r * 2 + jnp.maximum(3 - zl, 0), HA + 1, HAS + 1))
        to_sibling(near_rows, near_two, 0)
        far_own = base + (1 - r) * 2 + jnp.maximum(3 - zl, 0)
        pl.when(high)(lambda: taken(far_own, HA + 3, HAS + 3))
        pass_on(far_own, 0, dev(jnp.minimum(5 - zl, 3) * 2 + core, o, r), high)
        pl.when(high)(lambda: taken(base + (1 - r) * 2 + jnp.maximum(zl - 2, 0), HN, HNS))
        for m in range(2):
            pl.when(low_side)(functools.partial(taken, base + (1 - near) * 2 + m, HN + m, HNS + m))
        to_sibling(far_rows, far_two, 1)

    def unpack(value, scale):
        return value.astype(jnp.int32).astype(F32) * scale[0:1, 0:1]

    def spread(packed, scales, to_hi, to_lo):
        def body(i, carry):
            rows = piece(i, GP)
            ef[rows, :] = unpack(packed[rows, :], scales[i])
            return carry

        lax.fori_loop(0, 16, body, 0)
        for k, (a, e) in enumerate(KEPT):
            x = ef[k * TILE : k * TILE + TILE, :]
            at, to = slice(a * TILE, a * TILE + TILE), slice(e * TILE, e * TILE + TILE)
            to_hi[at, to], to_lo[at, to] = split(x)
            if a != e:
                to_hi[to, at], to_lo[to, at] = split(x.T)

    def take_gram(it):
        arrived(ea.at[it, other_part], it, FE)
        arrived(es.at[it, other_eight], it, FES)
        spread(ea.at[it], es.at[it], ehi, elo)

    def take_side(it):
        @pl.when(has_side)
        def _():
            arrived(na.at[other_part], it, FN)
            arrived(ns.at[other_eight], it, FNS)
            spread(na, ns, mhi, mlo)

    def cross_value(it, ch, i):
        two = [unpack(ha[it, ch, piece(2 * i + e, HP), :], hs[it, ch, 2 * i + e]) for e in range(2)]
        return jnp.concatenate(two, axis=0)

    def cross_plain(it, ch, to_hi, to_lo):
        wide = slice(ch * WIDE, ch * WIDE + WIDE)

        def body(i, carry):
            rows = piece(i, TILE)
            to_hi[rows, wide], to_lo[rows, wide] = split(cross_value(it, ch, i))
            return carry

        lax.fori_loop(0, 4, body, 0)

    def cross_turned(it, ch, to_hi, to_lo):
        wide = slice(ch * WIDE, ch * WIDE + WIDE)

        def body(i, carry):
            cols = piece(i, TILE)
            to_hi[wide, cols], to_lo[wide, cols] = split(cross_value(it, ch, i).T)
            return carry

        lax.fori_loop(0, 4, body, 0)

    def take_cross(it, ch):
        data, tags = ha.at[it, ch], hs.at[it, ch]

        @pl.when(jnp.logical_or(high, has_side))
        def _():
            arrived(data.at[pair_near_rows], it, of(ch, FH))
            arrived(tags.at[pair_near_two], it, of(ch, FHS))
            arrived(data.at[pair_far_rows], it, of(ch, FH + 1))
            arrived(tags.at[pair_far_two], it, of(ch, FHS + 1))

        pl.when(jnp.logical_and(low, has_side))(lambda: cross_plain(it, ch, xhi, xlo))
        pl.when(jnp.logical_and(high, has_side))(lambda: cross_turned(it, ch, xhi, xlo))

        if ch == 0:

            @pl.when(jnp.logical_not(has_side))
            def _():
                xhi[...] = jnp.zeros((ORBS, ORBS), BF)
                xlo[...] = jnp.zeros((ORBS, ORBS), BF)

    def updated(it, t, rows):
        change = dot3(chi[it, rows, :], clo[it, rows, :], ehi[...], elo[...])
        change = change + dot3(nhi[rows, :], nlo[rows, :], xhi[...], xlo[...])
        return jnp.where(live(t, cs_own), c[rows, :] - 0.5 * change, 0.0)

    def take_rows(ch):
        wide = slice(ch * WIDE, ch * WIDE + WIDE)

        @pl.when(has_side)
        def _():
            arrived(nq_in.at[ch], 0, of(ch, NX))

            def body(t, rows):
                x = nq_in[ch, rows, :].astype(jnp.int32).astype(F32) * (CMAX / QMAX)
                nf[rows, wide] = x
                nhi[rows, wide], nlo[rows, wide] = split(x)

            tiles(body)

        @pl.when(jnp.logical_not(has_side))
        def _():
            nhi[:, wide] = jnp.zeros((ROWS, WIDE), BF)
            nlo[:, wide] = jnp.zeros((ROWS, WIDE), BF)

    def cross_round(it, ch):
        pl.when(high)(lambda: cross(it, ch))
        send(hp.at[it, ch, other_half], hsib.at[it, ch], it, of(ch, HSIB), sibling, high)

    def turned_side(ch):
        pl.when(jnp.logical_and(low, has_side))(lambda: cross_turned(0, ch, thi, tlo))
        pl.when(jnp.logical_and(high, has_side))(lambda: cross_plain(0, ch, thi, tlo))

    def first(t, rows):
        x = updated(0, t, rows)
        c[rows, :] = x
        hi, lo = split(x)
        chi[1, rows, :] = hi
        clo[1, rows, :] = lo

    def some(body, start, step):
        def run(i, carry):
            t = start + i * step
            body(t, pl.ds(pl.multiple_of(t * TILE, TILE), TILE))
            return carry

        lax.fori_loop(0, 2, run, 0)

    def beside(t, rows):
        change = dot3(nhi[rows, :], nlo[rows, :], mhi[...], mlo[...])
        change = change + dot3(chi[0, rows, :], clo[0, rows, :], thi[...], tlo[...])
        x = jnp.where(live(t, cs_in), nf[rows, :] - 0.5 * change, 0.0)
        nhi[rows, :], nlo[rows, :] = split(x)

    def last(t, rows):
        out[rows, :] = updated(1, t, rows)

    images(0)
    edges(0)
    gram(0)
    send(gp.at[0, other_part], gsib.at[0], 0, GSIB, sibling)
    scatter_gram(0)
    send_rows(1)
    take_rows(0)
    cross_round(0, 0)
    own_gram(0)
    send_cross(0, 0)
    pass_gram(0, True)
    own_cross(0, 0)
    take_gram(0)
    pass_cross(0, 0)
    take_rows(1)
    cross_round(0, 1)
    take_cross(0, 0)
    send_cross(0, 1)
    pass_side(0)
    own_cross(0, 1)
    turned_side(0)
    pass_cross(0, 1)
    take_cross(0, 1)
    some(first, 0, 3)
    send_halo(1)
    some(first, 1, 1)
    pl.when(has_side)(lambda: arrived(cs_in, 0, NXC))
    turned_side(1)
    take_side(0)
    pl.when(has_side)(lambda: tiles(beside))

    images(1)
    edges(1)
    gram(1)
    send(gp.at[1, other_part], gsib.at[1], 1, GSIB, sibling)
    cross_round(1, 0)
    scatter_gram(1)
    cross_round(1, 1)
    send_cross(1, 0)
    own_gram(1)
    send_cross(1, 1)
    own_cross(1, 0)
    pass_gram(1, False)
    own_cross(1, 1)
    pass_cross(1, 0)
    take_gram(1)
    pass_cross(1, 1)
    take_cross(1, 0)
    take_cross(1, 1)
    tiles(last)

    for src, it, index, cond in sent:

        def wait(src=src, it=it, index=index):
            pltpu.make_async_copy(src, src, ss.at[it, index]).wait()

        if cond is None:
            wait()
        else:
            pl.when(cond)(wait)


def per_device(coefficients, basis_metric, pattern, starts):
    vm = pltpu.VMEM
    square = (ORBS, ORBS)
    scratch = [
        vm((ROWS, ORBS), F32), vm((2, 640, ORBS), BF), vm((2, ROWS, ORBS), BF),
        vm((ROWS, ORBS), F32), vm((ROWS, ORBS), BF), vm((ROWS, ORBS), BF),
        vm((ROWS, ORBS), BF), vm((ROWS, ORBS), BF), vm((ROWS, 640), BF),
        vm((2, PACKED, TILE), F32), vm((2, CHUNKS, ORBS, WIDE), F32),
        vm((CHUNKS, ROWS, WIDE), I16), vm((CHUNKS, ROWS, WIDE), I16), vm((8, ORBS), F32), vm((8, ORBS), F32),
        vm((576, 128), BF), vm((576, 128), BF), vm((576, 128), BF),
        vm((2, PHALF, TILE), F32), vm((2, CHUNKS, HALF, WIDE), F32),
        vm((2, 8, GP, TILE), I16), vm((2, 8, GP, TILE), I16), vm((2, 8, 128), F32), vm((2, 8, 8, 128), F32),
        vm((2, CHUNKS, 4, HP, WIDE), I16), vm((2, CHUNKS, 4, HP, WIDE), I16), vm((2, CHUNKS, 8, 128), F32), vm((2, CHUNKS, 4, 8, 128), F32),
        vm((2, PACKED, TILE), I16), vm((2, 16, 8, 128), F32), vm((PACKED, TILE), I16), vm((16, 8, 128), F32),
        vm((2, CHUNKS, ORBS, WIDE), I16), vm((2, CHUNKS, 8, 8, 128), F32),
        vm(square, BF), vm(square, BF), vm(square, BF), vm(square, BF), vm(square, BF), vm(square, BF),
        vm(square, BF), vm(square, BF), vm((PACKED, TILE), F32),
        pltpu.SemaphoreType.DMA((2, COUNT)), pltpu.SemaphoreType.DMA((2, COUNT)), pltpu.SemaphoreType.DMA((6,)),
    ]
    result = pl.pallas_call(
        kernel,
        out_shape=jax.ShapeDtypeStruct((ROWS, ORBS), F32),
        in_specs=[
            pl.BlockSpec(memory_space=pltpu.HBM),
            pl.BlockSpec(memory_space=pltpu.HBM),
            pl.BlockSpec(memory_space=pltpu.SMEM),
            pl.BlockSpec(memory_space=pltpu.SMEM),
        ],
        out_specs=pl.BlockSpec(memory_space=pltpu.VMEM),
        scratch_shapes=scratch,
        compiler_params=pltpu.CompilerParams(
            collective_id=0, has_side_effects=True, vmem_limit_bytes=50 * 1024 * 1024
        ),
    )(coefficients[0], basis_metric, pattern, starts)
    return result[None]


def solution(mesh):
    in_specs = (P("orb", ("basis", "rep"), None), P("orb", None), P("orb"), P("orb"))
    out_specs = P("orb", ("basis", "rep"), None)
    return jax.shard_map(
        per_device, mesh=mesh, in_specs=in_specs, out_specs=out_specs, check_vma=False
    )
```

```python
import functools

import jax
import jax.numpy as jnp
from jax import lax
from jax.experimental import pallas as pl
from jax.experimental.pallas import tpu as pltpu
from jax.sharding import PartitionSpec as P

BLK = 64
GROUP_BLOCKS = 64
SUPPORT = 96
ITERS = 2
ROWS = 512
ORBS = 512
HALF = 256
GP = 80
PACKED = 1280
PHALF = 640
HP = 64
TILE = 128
CMAX = 6.0
QMAX = 32767.0
BF = jnp.bfloat16
F32 = jnp.float32
I16 = jnp.int16

HALO_NEXT, HALO_PREV, GSIB, HSIB = 0, 1, 2, 3
RS, RSC, HRS, HRSC = 4, 12, 20, 24
EA, EAS, NA, NAS = 28, 36, 44, 52
HA, HAS, HL, HLS = 60, 64, 68, 72
FE, FES, FN, FNS, FH, FHS = 76, 77, 78, 79, 80, 82
NX, NXC, MET = 84, 88, 89
COUNT = 90

KEPT = [(a, b) for a in range(4) for b in range(a, 4)]


def split(x):
    hi = x.astype(BF)
    return hi, (x - hi.astype(F32)).astype(BF)


def dot(a, b, dims=((1,), (0,))):
    return lax.dot_general(a, b, (dims, ((), ())), preferred_element_type=F32)


def dot3(ah, al, bh, bl, dims=((1,), (0,))):
    return dot(ah, bh, dims) + (dot(ah, bl, dims) + dot(al, bh, dims))


def kernel(
    coef, metric, pattern, starts, out,
    c, chi, clo, nf, nhi, nlo, yhi, ylo, band, gp, hp,
    nq_out, nq_in, cs_own, cs_in, meff, mrecv, msel,
    gsib, hsib, qs, rs, qsc, rsc, hqs, hrs, hqsc, hrsc,
    ea, es, na, ns, ha, hs, ehi, elo, xhi, xlo, thi, tlo, mhi, mlo, ef,
    ss, rr, local_sem,
):
    b, o, r = lax.axis_index("basis"), lax.axis_index("orb"), lax.axis_index("rep")
    groups = lax.axis_size("orb")
    core, zl = b % 2, b // 2
    z = r * 4 + zl
    p = b * 2 + r
    q = p % 8
    low = zl < 2
    high = jnp.logical_not(low)
    side = jnp.where(low, o - 1, o + 1)
    away = jnp.where(low, o + 1, o - 1)
    has_side = jnp.logical_and(side >= 0, side < groups)
    has_away = jnp.logical_and(away >= 0, away < groups)
    j = r * 2 + zl - 2

    def dev(bb, oo, rep):
        return {"basis": bb, "orb": oo, "rep": rep}

    def zdev(zz, oo):
        return dev((zz % 4) * 2 + core, oo, zz // 4)

    sibling = dev(zl * 2 + 1 - core, o, r)

    barrier = pltpu.get_barrier_semaphore()

    def greet(device):
        pl.semaphore_signal(barrier, inc=1, device_id=device, device_id_type=pl.DeviceIdType.MESH)

    for k in range(1, 8):
        greet(zdev((z + k) % 8, o))
    greet(sibling)
    step_b = jnp.where(r == 1, b + 1, b - 1)
    has_step = jnp.logical_and(step_b >= 0, step_b < 8)

    @pl.when(has_step)
    def _():
        greet(dev(step_b, o, 1 - r))

    @pl.when(has_side)
    def _():
        base = jnp.where(low, 4, 0)
        for m in range(4):
            greet(dev(base + (m % 2) * 2 + core, side, m // 2))
        greet(dev(b, side, r))

    @pl.when(has_away)
    def _():
        greet(dev(b, away, r))

    loads = [
        pltpu.make_async_copy(coef.at[pl.ds(t * TILE, TILE)], c.at[pl.ds(t * TILE, TILE)], local_sem.at[2 + t]) for t in range(4)
    ]
    for t in (0, 3, 1, 2):
        loads[t].start()
    load_main = pltpu.make_async_copy(metric.at[pl.ds(pl.multiple_of(q * 512, 64), 512)], meff.at[pl.ds(0, 512)], local_sem.at[0])
    load_prev = pltpu.make_async_copy(
        metric.at[pl.ds(pl.multiple_of((q * 512 + 4032) % 4096, 64), 64)], meff.at[pl.ds(512, 64)], local_sem.at[1]
    )
    load_main.start()
    load_prev.start()
    lane = lax.broadcasted_iota(jnp.int32, (8, ORBS), 1) // BLK
    cs = jnp.zeros((8, ORBS), F32)
    for i in range(8):
        cs = jnp.where(lane == i, starts[i].astype(F32), cs)
    cs_own[...] = cs
    first_block = (o * GROUP_BLOCKS + p * 8).astype(F32)

    def live(t, cs_ref):
        rows = lax.broadcasted_iota(jnp.int32, (TILE, ORBS), 0) // BLK
        block = rows.astype(F32) + (first_block + (t * (TILE // BLK)).astype(F32))
        at = cs_ref[0:1, :]
        return jnp.logical_and(block >= at, block < at + SUPPORT)

    def tiles(body):
        def step(t, carry):
            body(t, pl.ds(pl.multiple_of(t * TILE, TILE), TILE))
            return carry

        lax.fori_loop(0, ROWS // TILE, step, 0)

    def prepare(t, rows):
        x = jnp.where(live(t, cs_own), c[rows, :], 0.0)
        c[rows, :] = x
        hi, lo = split(x)
        chi[0, rows, :] = hi
        clo[0, rows, :] = lo
        nq_out[rows, :] = jnp.round(jnp.clip(x, -CMAX, CMAX) * (QMAX / CMAX)).astype(I16)

    def prepare_tile(t):
        loads[t].wait()
        prepare(jnp.int32(t), pl.ds(t * TILE, TILE))

    prepare_tile(0)
    prepare_tile(3)
    for it in range(ITERS):

        @pl.when(p == 0)
        def _():
            chi[it, 512:576, :] = jnp.zeros((64, ORBS), BF)

        @pl.when(p == 15)
        def _():
            chi[it, 576:640, :] = jnp.zeros((64, ORBS), BF)

    load_main.wait()
    load_prev.wait()
    right = lax.broadcasted_iota(jnp.int32, (BLK, 2 * BLK), 1) >= BLK
    for i in range(9):
        at = (q * 8 + i) % 64 if i < 8 else (q * 8 + 63) % 64
        keep = jnp.where(o * GROUP_BLOCKS + at < groups * GROUP_BLOCKS - 1, pattern[at], 0).astype(F32)
        block = meff[i * 64 : i * 64 + 64, :].astype(F32)
        meff[i * 64 : i * 64 + 64, :] = jnp.where(right, block * keep, block).astype(BF)

    waits = [jnp.int32(8), has_step.astype(jnp.int32), 5 * has_side.astype(jnp.int32), has_away.astype(jnp.int32)]
    pl.semaphore_wait(barrier, waits[0] + waits[1] + waits[2] + waits[3])

    sent = []

    def send(src, dst, it, index, device, cond=None, land=None):
        land = index if land is None else land

        def start():
            pltpu.make_async_remote_copy(
                src_ref=src, dst_ref=dst, send_sem=ss.at[it, index], recv_sem=rr.at[it, land],
                device_id=device, device_id_type=pl.DeviceIdType.MESH,
            ).start()

        if cond is None:
            start()
        else:
            pl.when(cond)(start)
        sent.append((src, it, index, cond))

    def arrived(dst, it, index):
        pltpu.make_async_copy(dst, dst, rr.at[it, index]).wait()

    def send_halo(it):
        up_b = jnp.where(r == 0, b, b + 1)
        down_b = jnp.where(r == 1, b, b - 1)
        send(chi.at[it, pl.ds(0, 64)], chi.at[it, pl.ds(576, 64)], it, HALO_NEXT, dev(down_b, o, 1 - r), p > 0)
        send(chi.at[it, pl.ds(448, 64)], chi.at[it, pl.ds(512, 64)], it, HALO_PREV, dev(up_b, o, 1 - r), p < 15)

    def wait_halo(it):
        pl.when(p < 15)(lambda: arrived(chi.at[it, pl.ds(576, 64)], it, HALO_NEXT))
        pl.when(p > 0)(lambda: arrived(chi.at[it, pl.ds(512, 64)], it, HALO_PREV))

    gives_metric = jnp.logical_and(high, o > 0)
    send(meff, mrecv, 0, MET, dev(b, o - 1, r), gives_metric)
    send_halo(0)
    partner = dev(jnp.where(low, b + 4, b - 4), side, r)
    for t in (0, 3, 1, 2):
        if t in (1, 2):
            prepare_tile(t)
        rows = pl.ds(t * TILE, TILE)
        send(nq_out.at[rows], nq_in.at[rows], 0, NX + t, partner, has_side)
    send(cs_own, cs_in, 0, NXC, partner, has_side)

    @pl.when(low)
    def _():
        msel[...] = meff[...]

    @pl.when(jnp.logical_and(high, has_side))
    def _():
        arrived(mrecv, 0, MET)
        msel[...] = mrecv[...]

    @pl.when(jnp.logical_and(high, jnp.logical_not(has_side)))
    def _():
        msel[...] = jnp.zeros((576, 128), BF)

    @pl.when(p == 8)
    def _():
        msel[512:576, :] = meff[512:576, :]

    band[...] = jnp.zeros((ROWS, 640), BF)
    row_at = lax.broadcasted_iota(jnp.int32, (128, 128), 0)
    lane_at = lax.broadcasted_iota(jnp.int32, (128, 128), 1)
    top, left = row_at < 64, lane_at < 64
    bottom, rest = row_at >= 64, lane_at >= 64
    for t in range(4):
        m = msel[t * 128 : t * 128 + 128, :].astype(F32)
        rolled = pltpu.roll(m, 64, 1)
        corner = jnp.where(jnp.logical_and(top, rest), m, 0.0)
        diag = jnp.where(top, m, jnp.where(rest, rolled, 0.0)) + corner.T
        band[t * 128 : t * 128 + 128, t * 128 : t * 128 + 128] = diag.astype(BF)
        if t < 3:
            off = jnp.where(jnp.logical_and(bottom, left), rolled, 0.0)
            band[t * 128 : t * 128 + 128, t * 128 + 128 : t * 128 + 256] = off.astype(BF)
            band[t * 128 + 128 : t * 128 + 256, t * 128 : t * 128 + 128] = off.T.astype(BF)
        else:
            band[384:512, 512:640] = jnp.where(jnp.logical_and(bottom, rest), m, 0.0).astype(BF)
    before = pltpu.roll(msel[448:576, :].astype(F32), 64, 1).T
    shifted = pltpu.roll(before, 64, 1)
    band[0:128, 512:640] = jnp.where(jnp.logical_and(top, left), shifted, 0.0).astype(BF)

    def images(it):
        def body(t, rows):
            yhi[rows, :], ylo[rows, :] = split(dot(band[rows, 0:512], chi[it, 0:512]) + dot(band[rows, 0:512], clo[it]))

        tiles(body)

    def edges(it):
        wait_halo(it)
        for rows in (slice(0, 64), slice(448, 512)):
            y = yhi[rows, :].astype(F32) + ylo[rows, :].astype(F32)
            yhi[rows, :], ylo[rows, :] = split(y + dot(band[rows, 512:640], chi[it, 512:640]))

    def gram(it):
        for a in range(4):
            cols = slice(a * TILE, a * TILE + TILE)
            rest = slice(a * TILE, ORBS)
            g = dot3(chi[it, 0:512, cols], clo[it, :, cols], yhi[:, rest], ylo[:, rest], ((0,), (0,)))
            for e in range(a, 4):
                k = KEPT.index((a, e))
                gp[it, k * TILE : k * TILE + TILE, :] = g[:, (e - a) * TILE : (e - a) * TILE + TILE]

    def cross(it):
        def body(t, cols):
            hp[it, cols, :] = dot3(yhi[:, cols], ylo[:, cols], nhi[...], nlo[...], ((0,), (0,)))

        tiles(body)

    def cross_rows(it, rows, begin):
        def body(t, cols):
            more = dot3(yhi[rows, cols], ylo[rows, cols], nhi[rows, :], nlo[rows, :], ((0,), (0,)))
            hp[it, cols, :] = more if begin else hp[it, cols, :] + more

        tiles(body)

    own_half = pl.ds(pl.multiple_of(core * HALF, HALF), HALF)
    other_half = pl.ds(pl.multiple_of((1 - core) * HALF, HALF), HALF)
    own_part = pl.ds(pl.multiple_of(core * PHALF, PHALF), PHALF)
    other_part = pl.ds(pl.multiple_of((1 - core) * PHALF, PHALF), PHALF)

    def pair_and_pack(it, part, from_pair, packed, scale, size, count):
        half, wide = size * count, part.shape[2]

        def add(i, top_value):
            rows = pl.ds(pl.multiple_of(core * half + i * size, size), size)
            x = part[it, rows, :] + from_pair[it, pl.ds(pl.multiple_of(i * size, size), size), :]
            part[it, rows, :] = x
            return jnp.maximum(top_value, jnp.abs(x))

        peak = jnp.max(lax.fori_loop(0, count, add, jnp.zeros((size, wide), F32)), axis=(0, 1), keepdims=True)
        peak = jnp.maximum(peak, 1e-30)
        scale[it] = jnp.broadcast_to(peak * (1.0 / QMAX), (8, 128))
        inv = QMAX / peak

        def pack(i, carry):
            rows = pl.ds(pl.multiple_of(core * half + i * size, size), size)
            packed[it, i] = jnp.round(part[it, rows, :] * inv).astype(I16)
            return carry

        lax.fori_loop(0, count, pack, 0)

    def quantized(x):
        peak = jnp.maximum(jnp.max(jnp.abs(x), axis=(0, 1), keepdims=True), 1e-30)
        return jnp.round(x * (QMAX / peak)).astype(I16), jnp.broadcast_to(peak * (1.0 / QMAX), (8, 128))

    def scatter_gram(it):
        arrived(gsib.at[it], it, GSIB)
        pair_and_pack(it, gp, gsib, qs, qsc, GP, 8)
        for k in range(1, 8):
            to = (z + k) % 8
            send(qs.at[it, to], rs.at[it, k], it, RS + k, zdev(to, o))
            send(qsc.at[it], rsc.at[it, k], it, RSC + k, zdev(to, o))

    def scatter_cross(it):
        arrived(hsib.at[it], it, HSIB)
        pair_and_pack(it, hp, hsib, hqs, hqsc, HP, 4)

    def high_peer(m):
        pz = zl if m % 2 == 0 else 5 - zl
        pr = r if m // 2 == 0 else 1 - r
        return pz, pr

    def send_cross(it):
        for m in range(1, 4):
            pz, pr = high_peer(m)
            device = dev(pz * 2 + core, o, pr)
            send(hqs.at[it, pr * 2 + pz - 2], hrs.at[it, m], it, HRS + m, device, high)
            send(hqsc.at[it], hrsc.at[it, m], it, HRSC + m, device, high)

    def own_gram(it):
        rows = pl.ds(pl.multiple_of(core * PHALF + z * GP, GP), GP)
        total = gp[it, rows, :]
        for k in range(1, 8):
            arrived(rs.at[it, k], it, RS + k)
            arrived(rsc.at[it, k], it, RSC + k)
            total = total + rs[it, k].astype(jnp.int32).astype(F32) * rsc[it, k, 0:1, 0:1]
        here = lax.broadcasted_iota(jnp.int32, (GP, TILE), 0) + (core * PHALF + z * GP)
        tile = lax.shift_right_logical(here, 7)
        within = jnp.bitwise_and(here, 127) == lax.broadcasted_iota(jnp.int32, (GP, TILE), 1)
        on = jnp.zeros((GP, TILE), F32)
        for a in range(4):
            on = jnp.where(jnp.logical_and(tile == KEPT.index((a, a)), within), 1.0, on)
        value, scale = quantized(total * (1.0 / (SUPPORT * BLK)) - on)
        ea[it, rows, :] = value
        at = core * 8 + z
        es[it, at] = scale
        for k in range(1, 8):
            device = zdev((z + k) % 8, o)
            send(ea.at[it, rows], ea.at[it, rows], it, EA + k, device)
            send(es.at[it, at], es.at[it, at], it, EAS + k, device)

    def own_cross(it):
        rows = pl.ds(pl.multiple_of(core * HALF + jnp.maximum(j, 0) * HP, HP), HP)
        at = core * 4 + jnp.maximum(j, 0)
        low_there = jnp.logical_and(high, o < groups - 1)

        @pl.when(high)
        def _():
            total = hp[it, rows, :]
            for m in range(1, 4):
                arrived(hrs.at[it, m], it, HRS + m)
                arrived(hrsc.at[it, m], it, HRSC + m)
                total = total + hrs[it, m].astype(jnp.int32).astype(F32) * hrsc[it, m, 0:1, 0:1]
            value, scale = quantized(total * (1.0 / (SUPPORT * BLK)))
            ha[it, rows, :] = value
            hs[it, at] = scale

        for m in range(1, 4):
            pz, pr = high_peer(m)
            send(ha.at[it, rows], ha.at[it, rows], it, HA + m, dev(pz * 2 + core, o, pr), high)
            send(hs.at[it, at], hs.at[it, at], it, HAS + m, dev(pz * 2 + core, o, pr), high)
        mine = jnp.maximum(j, 0)
        for m in range(4):
            device = dev((m // 2) * 2 + core, o + 1, m % 2)
            send(ha.at[it, rows], ha.at[it, rows], it, HL + m, device, low_there, HL + mine)
            send(hs.at[it, at], hs.at[it, at], it, HLS + m, device, low_there, HLS + mine)

    own_eight = pl.ds(pl.multiple_of(core * 8, 8), 8)
    other_eight = pl.ds(pl.multiple_of((1 - core) * 8, 8), 8)
    near = jnp.where(jnp.logical_and(low, zl == 0), 1 - r, r)
    near_rows = pl.ds(pl.multiple_of(core * HALF + near * 128, 128), 128)
    far_rows = pl.ds(pl.multiple_of(core * HALF + (1 - near) * 128, 128), 128)
    near_two = pl.ds(core * 4 + near * 2, 2)
    far_two = pl.ds(core * 4 + (1 - near) * 2, 2)
    pair_near_rows = pl.ds(pl.multiple_of((1 - core) * HALF + near * 128, 128), 128)
    pair_far_rows = pl.ds(pl.multiple_of((1 - core) * HALF + (1 - near) * 128, 128), 128)
    pair_near_two = pl.ds((1 - core) * 4 + near * 2, 2)
    pair_far_two = pl.ds((1 - core) * 4 + (1 - near) * 2, 2)

    def piece(at, size):
        return pl.ds(pl.multiple_of(at * size, size), size)

    def pass_gram(it, with_side):
        for k in range(1, 8):
            at = core * 8 + (z + 8 - k) % 8
            arrived(ea.at[it, piece(at, GP)], it, EA + k)
            arrived(es.at[it, at], it, EAS + k)
        send(ea.at[it, own_part], ea.at[it, own_part], it, FE, sibling)
        send(es.at[it, own_eight], es.at[it, own_eight], it, FES, sibling)
        if with_side:
            send(ea.at[it, own_part], na.at[own_part], it, NA, dev(b, away, r), has_away)
            send(es.at[it, own_eight], ns.at[own_eight], it, NAS, dev(b, away, r), has_away)

    def pass_side(it):
        @pl.when(has_side)
        def _():
            arrived(na.at[own_part], it, NA)
            arrived(ns.at[own_eight], it, NAS)

        send(na.at[own_part], na.at[own_part], it, FN, sibling, has_side)
        send(ns.at[own_eight], ns.at[own_eight], it, FNS, sibling, has_side)

    def pass_cross(it):
        cond = jnp.logical_or(high, has_side)
        low_side = jnp.logical_and(low, has_side)
        data, tags = ha.at[it], hs.at[it]

        def high_arrived(m):
            pz, pr = high_peer(m)
            at = core * 4 + pr * 2 + pz - 2
            arrived(data.at[piece(at, HP)], it, HA + m)
            arrived(tags.at[at], it, HAS + m)

        def low_arrived(e, m):
            at = core * 4 + e * 2 + m
            arrived(data.at[piece(at, HP)], it, HL + e * 2 + m)
            arrived(tags.at[at], it, HLS + e * 2 + m)

        def to_sibling(rows, two, index):
            send(data.at[rows], data.at[rows], it, FH + index, sibling, cond)
            send(tags.at[two], tags.at[two], it, FHS + index, sibling, cond)

        pl.when(high)(lambda: high_arrived(1))
        for m in range(2):
            pl.when(low_side)(functools.partial(low_arrived, near, m))
        to_sibling(near_rows, near_two, 0)
        for m in range(2):
            pl.when(high)(functools.partial(high_arrived, m + 2))
            pl.when(low_side)(functools.partial(low_arrived, 1 - near, m))
        to_sibling(far_rows, far_two, 1)

    def unpack(value, scale):
        return value.astype(jnp.int32).astype(F32) * scale[0:1, 0:1]

    def spread(packed, scales, to_hi, to_lo):
        def body(i, carry):
            rows = piece(i, GP)
            ef[rows, :] = unpack(packed[rows, :], scales[i])
            return carry

        lax.fori_loop(0, 16, body, 0)
        for k, (a, e) in enumerate(KEPT):
            x = ef[k * TILE : k * TILE + TILE, :]
            at, to = slice(a * TILE, a * TILE + TILE), slice(e * TILE, e * TILE + TILE)
            to_hi[at, to], to_lo[at, to] = split(x)
            if a != e:
                to_hi[to, at], to_lo[to, at] = split(x.T)

    def take_gram(it):
        arrived(ea.at[it, other_part], it, FE)
        arrived(es.at[it, other_eight], it, FES)
        spread(ea.at[it], es.at[it], ehi, elo)

    def take_side(it):
        @pl.when(has_side)
        def _():
            arrived(na.at[other_part], it, FN)
            arrived(ns.at[other_eight], it, FNS)
            spread(na, ns, mhi, mlo)

    def cross_value(it, i):
        return jnp.concatenate(
            [unpack(ha[it, piece(2 * i, HP), :], hs[it, 2 * i]), unpack(ha[it, piece(2 * i + 1, HP), :], hs[it, 2 * i + 1])], axis=0
        )

    def cross_plain(it, to_hi, to_lo):
        def body(i, carry):
            rows = piece(i, TILE)
            to_hi[rows, :], to_lo[rows, :] = split(cross_value(it, i))
            return carry

        lax.fori_loop(0, 4, body, 0)

    def cross_turned(it, to_hi, to_lo):
        def body(i, carry):
            cols = piece(i, TILE)
            to_hi[:, cols], to_lo[:, cols] = split(cross_value(it, i).T)
            return carry

        lax.fori_loop(0, 4, body, 0)

    def take_cross(it):
        @pl.when(jnp.logical_or(high, has_side))
        def _():
            arrived(ha.at[it, pair_near_rows], it, FH)
            arrived(hs.at[it, pair_near_two], it, FHS)
            arrived(ha.at[it, pair_far_rows], it, FH + 1)
            arrived(hs.at[it, pair_far_two], it, FHS + 1)

        pl.when(jnp.logical_and(low, has_side))(lambda: cross_plain(it, xhi, xlo))
        pl.when(jnp.logical_and(high, has_side))(lambda: cross_turned(it, xhi, xlo))

        @pl.when(jnp.logical_not(has_side))
        def _():
            xhi[...] = jnp.zeros((ORBS, ORBS), BF)
            xlo[...] = jnp.zeros((ORBS, ORBS), BF)

    def own_change(it):
        def body(t, rows):
            c[rows, :] = c[rows, :] - 0.5 * dot3(chi[it, rows, :], clo[it, rows, :], ehi[...], elo[...])

        tiles(body)

    def updated(it, t, rows):
        change = dot3(nhi[rows, :], nlo[rows, :], xhi[...], xlo[...])
        return jnp.where(live(t, cs_own), c[rows, :] - 0.5 * change, 0.0)

    def take_rows():
        for t in (0, 3, 1, 2):
            rows = slice(t * TILE, t * TILE + TILE)

            @pl.when(has_side)
            def _():
                arrived(nq_in.at[rows], 0, NX + t)
                x = nq_in[rows, :].astype(jnp.int32).astype(F32) * (CMAX / QMAX)
                nf[rows, :] = x
                nhi[rows, :], nlo[rows, :] = split(x)

            @pl.when(jnp.logical_not(has_side))
            def _():
                nhi[rows, :] = jnp.zeros((TILE, ORBS), BF)
                nlo[rows, :] = jnp.zeros((TILE, ORBS), BF)

            pl.when(high)(functools.partial(cross_rows, 0, rows, t == 0))

    def pair_cross(it):
        send(hp.at[it, other_half], hsib.at[it], it, HSIB, sibling, high)

    def first(t, rows):
        x = updated(0, t, rows)
        c[rows, :] = x
        hi, lo = split(x)
        chi[1, rows, :] = hi
        clo[1, rows, :] = lo

    def some(body, start, step):
        def run(i, carry):
            t = start + i * step
            body(t, pl.ds(pl.multiple_of(t * TILE, TILE), TILE))
            return carry

        lax.fori_loop(0, 2, run, 0)

    def beside(t, rows):
        change = dot3(nhi[rows, :], nlo[rows, :], mhi[...], mlo[...])
        change = change + dot3(chi[0, rows, :], clo[0, rows, :], thi[...], tlo[...])
        x = jnp.where(live(t, cs_in), nf[rows, :] - 0.5 * change, 0.0)
        nhi[rows, :], nlo[rows, :] = split(x)

    def last(t, rows):
        out[rows, :] = updated(1, t, rows)

    images(0)
    edges(0)
    gram(0)
    send(gp.at[0, other_part], gsib.at[0], 0, GSIB, sibling)
    scatter_gram(0)
    own_gram(0)
    take_rows()
    pair_cross(0)
    pl.when(high)(lambda: scatter_cross(0))
    send_cross(0)
    pass_gram(0, True)
    take_gram(0)
    own_change(0)
    own_cross(0)
    pass_side(0)
    pass_cross(0)
    take_cross(0)
    some(first, 0, 3)
    send_halo(1)
    some(first, 1, 1)
    pl.when(has_side)(lambda: arrived(cs_in, 0, NXC))
    pl.when(jnp.logical_and(low, has_side))(lambda: cross_turned(0, thi, tlo))
    pl.when(jnp.logical_and(high, has_side))(lambda: cross_plain(0, thi, tlo))
    take_side(0)
    pl.when(has_side)(lambda: tiles(beside))

    images(1)
    edges(1)
    gram(1)
    send(gp.at[1, other_part], gsib.at[1], 1, GSIB, sibling)
    pl.when(high)(lambda: cross(1))
    pair_cross(1)
    scatter_gram(1)
    pl.when(high)(lambda: scatter_cross(1))
    send_cross(1)
    own_gram(1)
    own_cross(1)
    pass_gram(1, False)
    take_gram(1)
    own_change(1)
    pass_cross(1)
    take_cross(1)
    tiles(last)

    for src, it, index, cond in sent:

        def wait(src=src, it=it, index=index):
            pltpu.make_async_copy(src, src, ss.at[it, index]).wait()

        if cond is None:
            wait()
        else:
            pl.when(cond)(wait)


def per_device(coefficients, basis_metric, pattern, starts):
    vm = pltpu.VMEM
    square = (ORBS, ORBS)
    scratch = [
        vm((ROWS, ORBS), F32), vm((2, 640, ORBS), BF), vm((2, ROWS, ORBS), BF),
        vm((ROWS, ORBS), F32), vm((ROWS, ORBS), BF), vm((ROWS, ORBS), BF),
        vm((ROWS, ORBS), BF), vm((ROWS, ORBS), BF), vm((ROWS, 640), BF),
        vm((2, PACKED, TILE), F32), vm((2, ORBS, ORBS), F32),
        vm((ROWS, ORBS), I16), vm((ROWS, ORBS), I16), vm((8, ORBS), F32), vm((8, ORBS), F32),
        vm((576, 128), BF), vm((576, 128), BF), vm((576, 128), BF),
        vm((2, PHALF, TILE), F32), vm((2, HALF, ORBS), F32),
        vm((2, 8, GP, TILE), I16), vm((2, 8, GP, TILE), I16), vm((2, 8, 128), F32), vm((2, 8, 8, 128), F32),
        vm((2, 4, HP, ORBS), I16), vm((2, 4, HP, ORBS), I16), vm((2, 8, 128), F32), vm((2, 4, 8, 128), F32),
        vm((2, PACKED, TILE), I16), vm((2, 16, 8, 128), F32), vm((PACKED, TILE), I16), vm((16, 8, 128), F32),
        vm((2, ORBS, ORBS), I16), vm((2, 8, 8, 128), F32),
        vm(square, BF), vm(square, BF), vm(square, BF), vm(square, BF), vm(square, BF), vm(square, BF),
        vm(square, BF), vm(square, BF), vm((PACKED, TILE), F32),
        pltpu.SemaphoreType.DMA((2, COUNT)), pltpu.SemaphoreType.DMA((2, COUNT)), pltpu.SemaphoreType.DMA((6,)),
    ]
    result = pl.pallas_call(
        kernel,
        out_shape=jax.ShapeDtypeStruct((ROWS, ORBS), F32),
        in_specs=[
            pl.BlockSpec(memory_space=pltpu.HBM),
            pl.BlockSpec(memory_space=pltpu.HBM),
            pl.BlockSpec(memory_space=pltpu.SMEM),
            pl.BlockSpec(memory_space=pltpu.SMEM),
        ],
        out_specs=pl.BlockSpec(memory_space=pltpu.VMEM),
        scratch_shapes=scratch,
        compiler_params=pltpu.CompilerParams(
            collective_id=0, has_side_effects=True, vmem_limit_bytes=50 * 1024 * 1024
        ),
    )(coefficients[0], basis_metric, pattern, starts)
    return result[None]


def solution(mesh):
    in_specs = (P("orb", ("basis", "rep"), None), P("orb", None), P("orb"), P("orb"))
    out_specs = P("orb", ("basis", "rep"), None)
    return jax.shard_map(
        per_device, mesh=mesh, in_specs=in_specs, out_specs=out_specs, check_vma=False
    )
```

```python
import functools

import jax
import jax.numpy as jnp
from jax import lax
from jax.experimental import pallas as pl
from jax.experimental.pallas import tpu as pltpu
from jax.sharding import PartitionSpec as P

BLK = 64
GROUP_BLOCKS = 64
SUPPORT = 96
ITERS = 2
ROWS = 512
ORBS = 512
HALF = 256
GP = 80
PACKED = 1280
PHALF = 640
HP = 32
TILE = 128
CMAX = 6.0
QMAX = 32767.0
BF = jnp.bfloat16
F32 = jnp.float32
I16 = jnp.int16

HALO_NEXT, HALO_PREV, GSIB, HSIB, NA, NAS, FES, FN, FNS, FHS, NXC, MET = range(12)
NX = 12
RS, RSC, HRS, HRSC, EA, EAS, HA, HAS, FE, FH = range(16, 96, 8)
COUNT = 96

KEPT = [(a, b) for a in range(4) for b in range(a, 4)]


def split(x):
    hi = x.astype(BF)
    return hi, (x - hi.astype(F32)).astype(BF)


def dot(a, b, dims=((1,), (0,))):
    return lax.dot_general(a, b, (dims, ((), ())), preferred_element_type=F32)


def dot3(ah, al, bh, bl, dims=((1,), (0,))):
    return dot(ah, bh, dims) + (dot(ah, bl, dims) + dot(al, bh, dims))


def kernel(
    coef, metric, pattern_in, starts_in, out,
    c, chi, clo, nf, nhi, nlo, yhi, ylo, band, gp, hp,
    nq_out, nq_in, cs_own, cs_in, meff, mrecv, msel,
    gsib, hsib, qs, rs, qsc, rsc, hqs, hrs, hqsc, hrsc,
    ea, es, na, ns, ha, hs, ehi, elo, xhi, xlo, thi, tlo, mhi, mlo, ef, ho, hos, sums, dhi, dlo, pattern, starts,
    ss, rr, local_sem,
):
    b, o, r = lax.axis_index("basis"), lax.axis_index("orb"), lax.axis_index("rep")
    groups = lax.axis_size("orb")
    core, zl = b % 2, b // 2
    z = r * 4 + zl
    p = b * 2 + r
    q = p % 8
    low = zl < 2
    high = jnp.logical_not(low)
    side = jnp.where(low, o - 1, o + 1)
    away = jnp.where(low, o + 1, o - 1)
    has_side = jnp.logical_and(side >= 0, side < groups)
    has_away = jnp.logical_and(away >= 0, away < groups)

    def dev(bb, oo, rep):
        return {"basis": bb, "orb": oo, "rep": rep}

    def zdev(zz, oo):
        return dev((zz % 4) * 2 + core, oo, zz // 4)

    sibling = dev(zl * 2 + 1 - core, o, r)

    barrier = pltpu.get_barrier_semaphore()

    def greet(device):
        pl.semaphore_signal(barrier, inc=1, device_id=device, device_id_type=pl.DeviceIdType.MESH)

    for k in range(1, 8):
        greet(zdev((z + k) % 8, o))
    greet(sibling)
    step_b = jnp.where(r == 1, b + 1, b - 1)
    has_step = jnp.logical_and(step_b >= 0, step_b < 8)

    @pl.when(has_step)
    def _():
        greet(dev(step_b, o, 1 - r))

    below = jnp.logical_and(low, o > 0)
    above = o < groups - 1

    @pl.when(below)
    def _():
        for k in range(8):
            greet(zdev((z + k) % 8, o - 1))

    @pl.when(above)
    def _():
        for m in range(4):
            greet(dev((m // 2) * 2 + core, o + 1, m % 2))

    straight = jnp.logical_and(high, above)

    @pl.when(straight)
    def _():
        greet(dev(b, o + 1, r))

    straight_down = jnp.logical_and(high, o > 0)

    @pl.when(straight_down)
    def _():
        greet(dev(b, o - 1, r))

    loads = [
        pltpu.make_async_copy(coef.at[pl.ds(t * TILE, TILE)], c.at[pl.ds(t * TILE, TILE)], local_sem.at[2 + t]) for t in range(4)
    ]
    small = [
        pltpu.make_async_copy(starts_in, starts, local_sem.at[6]),
        pltpu.make_async_copy(pattern_in, pattern, local_sem.at[7]),
    ]
    for load in small:
        load.start()
    for t in (0, 3, 1, 2):
        loads[t].start()
    load_main = pltpu.make_async_copy(metric.at[pl.ds(pl.multiple_of(q * 512, 64), 512)], meff.at[pl.ds(0, 512)], local_sem.at[0])
    load_prev = pltpu.make_async_copy(
        metric.at[pl.ds(pl.multiple_of((q * 512 + 4032) % 4096, 64), 64)], meff.at[pl.ds(512, 64)], local_sem.at[1]
    )
    load_main.start()
    load_prev.start()
    small[0].wait()
    small[1].wait()
    lane = lax.broadcasted_iota(jnp.int32, (8, ORBS), 1) // BLK
    cs = jnp.zeros((8, ORBS), F32)
    for i in range(8):
        cs = jnp.where(lane == i, starts[i].astype(F32), cs)
    cs_own[...] = cs
    first_block = (o * GROUP_BLOCKS + p * 8).astype(F32)

    def live(t, cs_ref):
        rows = lax.broadcasted_iota(jnp.int32, (TILE, ORBS), 0) // BLK
        block = rows.astype(F32) + (first_block + (t * (TILE // BLK)).astype(F32))
        at = cs_ref[0:1, :]
        return jnp.logical_and(block >= at, block < at + SUPPORT)

    def tiles(body):
        def step(t, carry):
            body(t, pl.ds(pl.multiple_of(t * TILE, TILE), TILE))
            return carry

        lax.fori_loop(0, ROWS // TILE, step, 0)

    def prepare(t, rows):
        x = jnp.where(live(t, cs_own), c[rows, :], 0.0)
        c[rows, :] = x
        hi, lo = split(x)
        chi[0, rows, :] = hi
        clo[0, rows, :] = lo
        nq_out[rows, :] = jnp.round(jnp.clip(x, -CMAX, CMAX) * (QMAX / CMAX)).astype(I16)

    def prepare_tile(t):
        loads[t].wait()
        prepare(jnp.int32(t), pl.ds(t * TILE, TILE))

    prepare_tile(0)
    prepare_tile(3)
    for it in range(ITERS):

        @pl.when(low)
        def _():
            chi[it, 512:576, :] = jnp.zeros((64, ORBS), BF)

        @pl.when(p == 15)
        def _():
            chi[it, 576:640, :] = jnp.zeros((64, ORBS), BF)

    load_main.wait()
    load_prev.wait()
    right = lax.broadcasted_iota(jnp.int32, (BLK, 2 * BLK), 1) >= BLK
    for i in range(9):
        at = (q * 8 + i) % 64 if i < 8 else (q * 8 + 63) % 64
        keep = jnp.where(o * GROUP_BLOCKS + at < groups * GROUP_BLOCKS - 1, pattern[at], 0).astype(F32)
        block = meff[i * 64 : i * 64 + 64, :].astype(F32)
        meff[i * 64 : i * 64 + 64, :] = jnp.where(right, block * keep, block).astype(BF)

    def ones(flag):
        return flag.astype(jnp.int32)

    pl.semaphore_wait(barrier, 8 + ones(has_step) + 8 * ones(below) + 4 * ones(above) + ones(straight) + ones(straight_down))

    sent = []

    def send(src, dst, it, index, device, cond=None, land=None):
        land = index if land is None else land

        def start():
            pltpu.make_async_remote_copy(
                src_ref=src, dst_ref=dst, send_sem=ss.at[it, index], recv_sem=rr.at[it, land],
                device_id=device, device_id_type=pl.DeviceIdType.MESH,
            ).start()

        if cond is None:
            start()
        else:
            pl.when(cond)(start)
        sent.append((src, it, index, cond))

    def arrived(dst, it, index):
        pltpu.make_async_copy(dst, dst, rr.at[it, index]).wait()

    def send_halo(it):
        up_b = jnp.where(r == 0, b, b + 1)
        down_b = jnp.where(r == 1, b, b - 1)
        send(chi.at[it, pl.ds(0, 64)], chi.at[it, pl.ds(576, 64)], it, HALO_NEXT, dev(down_b, o, 1 - r), p > 0)
        send(chi.at[it, pl.ds(448, 64)], chi.at[it, pl.ds(512, 64)], it, HALO_PREV, dev(up_b, o, 1 - r), jnp.logical_and(p > 6, p < 15))

    def wait_halo(it):
        pl.when(p < 15)(lambda: arrived(chi.at[it, pl.ds(576, 64)], it, HALO_NEXT))
        pl.when(high)(lambda: arrived(chi.at[it, pl.ds(512, 64)], it, HALO_PREV))

    gives_metric = jnp.logical_and(high, o > 0)
    send(meff, mrecv, 0, MET, dev(b, o - 1, r), gives_metric)
    send_halo(0)
    partner = dev(jnp.where(low, b + 4, b - 4), side, r)
    for t in (0, 3, 1, 2):
        if t in (1, 2):
            prepare_tile(t)
        rows = pl.ds(t * TILE, TILE)
        send(nq_out.at[rows], nq_in.at[rows], 0, NX + t, partner, has_side)
    send(cs_own, cs_in, 0, NXC, partner, has_side)

    @pl.when(low)
    def _():
        msel[...] = meff[...]

    @pl.when(jnp.logical_and(high, has_side))
    def _():
        arrived(mrecv, 0, MET)
        msel[...] = mrecv[...]

    @pl.when(jnp.logical_and(high, jnp.logical_not(has_side)))
    def _():
        msel[...] = jnp.zeros((576, 128), BF)

    @pl.when(p == 8)
    def _():
        msel[512:576, :] = meff[512:576, :]

    band[...] = jnp.zeros((ROWS, 640), BF)
    row_at = lax.broadcasted_iota(jnp.int32, (128, 128), 0)
    lane_at = lax.broadcasted_iota(jnp.int32, (128, 128), 1)
    top, left = row_at < 64, lane_at < 64
    bottom, rest = row_at >= 64, lane_at >= 64
    for t in range(4):
        m = msel[t * 128 : t * 128 + 128, :].astype(F32)
        rolled = pltpu.roll(m, 64, 1)
        corner = jnp.where(jnp.logical_and(top, rest), m, 0.0)
        diag = jnp.where(top, m, jnp.where(rest, rolled, 0.0)) + corner.T
        band[t * 128 : t * 128 + 128, t * 128 : t * 128 + 128] = diag.astype(BF)
        if t < 3:
            off = jnp.where(jnp.logical_and(bottom, left), rolled, 0.0)
            band[t * 128 : t * 128 + 128, t * 128 + 128 : t * 128 + 256] = off.astype(BF)
            band[t * 128 + 128 : t * 128 + 256, t * 128 : t * 128 + 128] = off.T.astype(BF)
        else:
            band[384:512, 512:640] = jnp.where(jnp.logical_and(bottom, rest), m, 0.0).astype(BF)
    before = pltpu.roll(msel[448:576, :].astype(F32), 64, 1).T
    shifted = pltpu.roll(before, 64, 1)
    band[0:128, 512:640] = jnp.where(jnp.logical_and(top, left), shifted, 0.0).astype(BF)

    def images(it):
        def body(t, rows):
            yhi[rows, :], ylo[rows, :] = split(dot(band[rows, 0:512], chi[it, 0:512]) + dot(band[rows, 0:512], clo[it]))

        tiles(body)

    def edges(it):
        wait_halo(it)
        for rows in (slice(0, 64), slice(448, 512)):
            y = yhi[rows, :].astype(F32) + ylo[rows, :].astype(F32)
            more = dot(band[rows, 512:640], chi[it, 512:640])
            yhi[rows, :], ylo[rows, :] = split(y + more)
        dhi[...], dlo[...] = split(more)

    def gram(it):
        for a in range(4):
            cols = slice(a * TILE, a * TILE + TILE)
            rest = slice(a * TILE, ORBS)
            g = dot3(chi[it, 0:512, cols], clo[it, :, cols], yhi[:, rest], ylo[:, rest], ((0,), (0,)))
            for e in range(a, 4):
                k = KEPT.index((a, e))
                gp[it, k * TILE : k * TILE + TILE, :] = g[:, (e - a) * TILE : (e - a) * TILE + TILE]

        @pl.when(p < 7)
        def _():
            for a in range(4):
                cols = slice(a * TILE, a * TILE + TILE)
                rest = slice(a * TILE, ORBS)
                g = dot3(dhi[:, cols], dlo[:, cols], chi[it, 448:512, rest], clo[it, 448:512, rest], ((0,), (0,)))
                for e in range(a, 4):
                    rows = slice(KEPT.index((a, e)) * TILE, KEPT.index((a, e)) * TILE + TILE)
                    gp[it, rows, :] = gp[it, rows, :] + g[:, (e - a) * TILE : (e - a) * TILE + TILE]

    def cross(it):
        def body(t, cols):
            hp[it, cols, :] = dot3(yhi[:, cols], ylo[:, cols], nhi[...], nlo[...], ((0,), (0,)))

        tiles(body)

    def cross_rows(it, rows, begin):
        def body(t, cols):
            more = dot3(yhi[rows, cols], ylo[rows, cols], nhi[rows, :], nlo[rows, :], ((0,), (0,)))
            hp[it, cols, :] = more if begin else hp[it, cols, :] + more

        tiles(body)

    own_half = pl.ds(pl.multiple_of(core * HALF, HALF), HALF)
    other_half = pl.ds(pl.multiple_of((1 - core) * HALF, HALF), HALF)
    own_part = pl.ds(pl.multiple_of(core * PHALF, PHALF), PHALF)
    other_part = pl.ds(pl.multiple_of((1 - core) * PHALF, PHALF), PHALF)

    def pair_and_pack(it, part, from_pair, packed, scale, size, count):
        half, wide = size * count, part.shape[2]

        def add(i, top_value):
            rows = pl.ds(pl.multiple_of(core * half + i * size, size), size)
            x = part[it, rows, :] + from_pair[it, pl.ds(pl.multiple_of(i * size, size), size), :]
            part[it, rows, :] = x
            return jnp.maximum(top_value, jnp.abs(x))

        peak = jnp.max(lax.fori_loop(0, count, add, jnp.zeros((size, wide), F32)), axis=(0, 1), keepdims=True)
        peak = jnp.maximum(peak, 1e-30)
        scale[it] = jnp.broadcast_to(peak * (1.0 / QMAX), (8, 128))
        inv = QMAX / peak

        def pack(i, carry):
            rows = pl.ds(pl.multiple_of(core * half + i * size, size), size)
            packed[it, i] = jnp.round(part[it, rows, :] * inv).astype(I16)
            return carry

        lax.fori_loop(0, count, pack, 0)

    def quantized(x):
        peak = jnp.maximum(jnp.max(jnp.abs(x), axis=(0, 1), keepdims=True), 1e-30)
        return jnp.round(x * (QMAX / peak)).astype(I16), jnp.broadcast_to(peak * (1.0 / QMAX), (8, 128))

    def scatter_gram(it):
        arrived(gsib.at[it], it, GSIB)
        pair_and_pack(it, gp, gsib, qs, qsc, GP, 8)
        for k in range(1, 8):
            to = (z + k) % 8
            send(qs.at[it, to], rs.at[it, k], it, RS + k, zdev(to, o))
            send(qsc.at[it], rsc.at[it, k], it, RSC + k, zdev(to, o))

    def scatter_cross(it):
        arrived(hsib.at[it], it, HSIB)
        pair_and_pack(it, hp, hsib, hqs, hqsc, HP, 8)

    def from_high(k):
        return (z + 8 - k) % 4 >= 2

    def send_cross(it):
        for k in range(1, 8):
            to = (z + k) % 8
            send(hqs.at[it, to], hrs.at[it, k], it, HRS + k, zdev(to, o), high)
            send(hqsc.at[it], hrsc.at[it, k], it, HRSC + k, zdev(to, o), high)

    def own_gram(it):
        rows = pl.ds(pl.multiple_of(core * PHALF + z * GP, GP), GP)
        total = gp[it, rows, :]
        for k in range(1, 8):
            arrived(rs.at[it, k], it, RS + k)
            arrived(rsc.at[it, k], it, RSC + k)
            total = total + rs[it, k].astype(jnp.int32).astype(F32) * rsc[it, k, 0:1, 0:1]
        here = lax.broadcasted_iota(jnp.int32, (GP, TILE), 0) + (core * PHALF + z * GP)
        tile = lax.shift_right_logical(here, 7)
        within = jnp.bitwise_and(here, 127) == lax.broadcasted_iota(jnp.int32, (GP, TILE), 1)
        on = jnp.zeros((GP, TILE), F32)
        for a in range(4):
            on = jnp.where(jnp.logical_and(tile == KEPT.index((a, a)), within), 1.0, on)
        value, scale = quantized(total * (1.0 / (SUPPORT * BLK)) - on)
        ea[it, rows, :] = value
        at = core * 8 + z
        es[it, at] = scale
        for k in range(1, 8):
            device = zdev((z + k) % 8, o)
            send(ea.at[it, rows], ea.at[it, rows], it, EA + k, device)
            send(es.at[it, at], es.at[it, at], it, EAS + k, device)

    def own_cross(it):
        rows = pl.ds(pl.multiple_of(core * HALF + z * HP, HP), HP)
        at = core * 8 + z

        @pl.when(high)
        def _():
            sums[...] = hp[it, rows, :]

        @pl.when(low)
        def _():
            sums[...] = jnp.zeros((HP, ORBS), F32)

        for k in range(1, 8):

            @pl.when(from_high(k))
            def _():
                arrived(hrs.at[it, k], it, HRS + k)
                arrived(hrsc.at[it, k], it, HRSC + k)
                sums[...] = sums[...] + hrs[it, k].astype(jnp.int32).astype(F32) * hrsc[it, k, 0:1, 0:1]

        value, scale = quantized(sums[...] * (1.0 / (SUPPORT * BLK)))
        ho[it] = value
        hos[it] = scale

        @pl.when(high)
        def _():
            ha[it, rows, :] = value
            hs[it, at] = scale

        for k in range(8):
            to = (z + k) % 8
            to_low = to % 4 < 2
            cond = jnp.logical_and(to_low, above)
            if k > 0:
                cond = jnp.logical_or(cond, to % 4 >= 2)
            device = zdev(to, jnp.where(to_low, o + 1, o))
            send(ho.at[it], ha.at[it, rows], it, HA + k, device, cond)
            send(hos.at[it], hs.at[it, at], it, HAS + k, device, cond)

    own_eight = pl.ds(pl.multiple_of(core * 8, 8), 8)
    other_eight = pl.ds(pl.multiple_of((1 - core) * 8, 8), 8)
    def piece(at, size):
        return pl.ds(pl.multiple_of(at * size, size), size)

    def pass_gram(it, with_side):
        for k in range(1, 8):
            at = core * 8 + (z + 8 - k) % 8
            arrived(ea.at[it, piece(at, GP)], it, EA + k)
            arrived(es.at[it, at], it, EAS + k)
            send(ea.at[it, piece(at, GP)], ea.at[it, piece(at, GP)], it, FE + k, sibling)
        mine = piece(core * 8 + z, GP)
        send(ea.at[it, mine], ea.at[it, mine], it, FE, sibling)
        send(es.at[it, own_eight], es.at[it, own_eight], it, FES, sibling)
        if with_side:
            send(ea.at[it, own_part], na.at[own_part], it, NA, dev(b, away, r), has_away)
            send(es.at[it, own_eight], ns.at[own_eight], it, NAS, dev(b, away, r), has_away)

    def pass_side(it):
        @pl.when(has_side)
        def _():
            arrived(na.at[own_part], it, NA)
            arrived(ns.at[own_eight], it, NAS)

        send(na.at[own_part], na.at[own_part], it, FN, sibling, has_side)
        send(ns.at[own_eight], ns.at[own_eight], it, FNS, sibling, has_side)

    def pass_cross(it):
        data, tags = ha.at[it], hs.at[it]
        takes = jnp.logical_or(high, has_side)
        for k in range(8):
            at = core * 8 + (z + 8 - k) % 8

            def taken(at=at, k=k):
                arrived(data.at[piece(at, HP)], it, HA + k)
                arrived(tags.at[at], it, HAS + k)

            pl.when(below if k == 0 else takes)(taken)
            send(data.at[piece(at, HP)], data.at[piece(at, HP)], it, FH + k, sibling, takes)
        send(tags.at[own_eight], tags.at[own_eight], it, FHS, sibling, takes)

    def unpack(value, scale):
        return value.astype(jnp.int32).astype(F32) * scale[0:1, 0:1]

    def spread(packed, scales, to_hi, to_lo):
        def body(i, carry):
            rows = piece(i, GP)
            ef[rows, :] = unpack(packed[rows, :], scales[i])
            return carry

        lax.fori_loop(0, 16, body, 0)
        for k, (a, e) in enumerate(KEPT):
            x = ef[k * TILE : k * TILE + TILE, :]
            at, to = slice(a * TILE, a * TILE + TILE), slice(e * TILE, e * TILE + TILE)
            to_hi[at, to], to_lo[at, to] = split(x)
            if a != e:
                to_hi[to, at], to_lo[to, at] = split(x.T)

    def take_gram(it):
        for k in range(8):
            arrived(ea.at[it, piece((1 - core) * 8 + (z + 8 - k) % 8, GP)], it, FE + k)
        arrived(es.at[it, other_eight], it, FES)
        spread(ea.at[it], es.at[it], ehi, elo)

    def take_side(it):
        @pl.when(has_side)
        def _():
            arrived(na.at[other_part], it, FN)
            arrived(ns.at[other_eight], it, FNS)
            spread(na, ns, mhi, mlo)

    def cross_value(it, i):
        return jnp.concatenate([unpack(ha[it, piece(4 * i + e, HP), :], hs[it, 4 * i + e]) for e in range(4)], axis=0)

    def cross_plain(it, to_hi, to_lo):
        def body(i, carry):
            rows = piece(i, TILE)
            to_hi[rows, :], to_lo[rows, :] = split(cross_value(it, i))
            return carry

        lax.fori_loop(0, 4, body, 0)

    def cross_turned(it, to_hi, to_lo):
        def body(i, carry):
            cols = piece(i, TILE)
            to_hi[:, cols], to_lo[:, cols] = split(cross_value(it, i).T)
            return carry

        lax.fori_loop(0, 4, body, 0)

    def take_cross(it):
        @pl.when(jnp.logical_or(high, has_side))
        def _():
            for k in range(8):
                arrived(ha.at[it, piece((1 - core) * 8 + (z + 8 - k) % 8, HP)], it, FH + k)
            arrived(hs.at[it, other_eight], it, FHS)

        pl.when(jnp.logical_and(low, has_side))(lambda: cross_plain(it, xhi, xlo))
        pl.when(jnp.logical_and(high, has_side))(lambda: cross_turned(it, xhi, xlo))

        @pl.when(jnp.logical_not(has_side))
        def _():
            xhi[...] = jnp.zeros((ORBS, ORBS), BF)
            xlo[...] = jnp.zeros((ORBS, ORBS), BF)

    def own_change(it):
        def body(t, rows):
            c[rows, :] = c[rows, :] - 0.5 * dot3(chi[it, rows, :], clo[it, rows, :], ehi[...], elo[...])

        tiles(body)

    def updated(it, t, rows):
        change = dot3(nhi[rows, :], nlo[rows, :], xhi[...], xlo[...])
        return jnp.where(live(t, cs_own), c[rows, :] - 0.5 * change, 0.0)

    def take_rows():
        for t in (0, 3, 1, 2):
            rows = slice(t * TILE, t * TILE + TILE)

            @pl.when(has_side)
            def _():
                arrived(nq_in.at[rows], 0, NX + t)
                x = nq_in[rows, :].astype(jnp.int32).astype(F32) * (CMAX / QMAX)
                nf[rows, :] = x
                nhi[rows, :], nlo[rows, :] = split(x)

            @pl.when(jnp.logical_not(has_side))
            def _():
                nhi[rows, :] = jnp.zeros((TILE, ORBS), BF)
                nlo[rows, :] = jnp.zeros((TILE, ORBS), BF)

            pl.when(high)(functools.partial(cross_rows, 0, rows, t == 0))

    def pair_cross(it):
        send(hp.at[it, other_half], hsib.at[it], it, HSIB, sibling, high)

    def first(t, rows):
        x = updated(0, t, rows)
        c[rows, :] = x
        hi, lo = split(x)
        chi[1, rows, :] = hi
        clo[1, rows, :] = lo

    def some(body, start, step):
        def run(i, carry):
            t = start + i * step
            body(t, pl.ds(pl.multiple_of(t * TILE, TILE), TILE))
            return carry

        lax.fori_loop(0, 2, run, 0)

    def beside(t, rows):
        change = dot3(nhi[rows, :], nlo[rows, :], mhi[...], mlo[...])
        change = change + dot3(chi[0, rows, :], clo[0, rows, :], thi[...], tlo[...])
        x = jnp.where(live(t, cs_in), nf[rows, :] - 0.5 * change, 0.0)
        nhi[rows, :], nlo[rows, :] = split(x)

    def last(t, rows):
        c[rows, :] = updated(1, t, rows)
        pltpu.make_async_copy(c.at[rows], out.at[rows], local_sem.at[t]).start()

    images(0)
    edges(0)
    gram(0)
    send(gp.at[0, other_part], gsib.at[0], 0, GSIB, sibling)
    scatter_gram(0)
    own_gram(0)
    take_rows()
    pair_cross(0)
    pl.when(high)(lambda: scatter_cross(0))
    send_cross(0)
    pass_gram(0, True)
    take_gram(0)
    own_change(0)
    own_cross(0)
    pass_side(0)
    pass_cross(0)
    take_cross(0)
    some(first, 0, 3)
    send_halo(1)
    some(first, 1, 1)
    pl.when(has_side)(lambda: arrived(cs_in, 0, NXC))
    pl.when(jnp.logical_and(low, has_side))(lambda: cross_turned(0, thi, tlo))
    pl.when(jnp.logical_and(high, has_side))(lambda: cross_plain(0, thi, tlo))
    take_side(0)
    pl.when(has_side)(lambda: tiles(beside))

    images(1)
    edges(1)
    gram(1)
    send(gp.at[1, other_part], gsib.at[1], 1, GSIB, sibling)
    pl.when(high)(lambda: cross(1))
    pair_cross(1)
    scatter_gram(1)
    pl.when(high)(lambda: scatter_cross(1))
    send_cross(1)
    own_gram(1)
    own_cross(1)
    pass_gram(1, False)
    take_gram(1)
    own_change(1)
    pass_cross(1)
    take_cross(1)
    tiles(last)
    for t in range(4):
        rows = pl.ds(t * TILE, TILE)
        pltpu.make_async_copy(c.at[rows], out.at[rows], local_sem.at[t]).wait()

    for src, it, index, cond in sent:

        def wait(src=src, it=it, index=index):
            pltpu.make_async_copy(src, src, ss.at[it, index]).wait()

        if cond is None:
            wait()
        else:
            pl.when(cond)(wait)


def per_device(coefficients, basis_metric, pattern, starts):
    vm = pltpu.VMEM
    square = (ORBS, ORBS)
    scratch = [
        vm((ROWS, ORBS), F32), vm((2, 640, ORBS), BF), vm((2, ROWS, ORBS), BF),
        vm((ROWS, ORBS), F32), vm((ROWS, ORBS), BF), vm((ROWS, ORBS), BF),
        vm((ROWS, ORBS), BF), vm((ROWS, ORBS), BF), vm((ROWS, 640), BF),
        vm((2, PACKED, TILE), F32), vm((2, ORBS, ORBS), F32),
        vm((ROWS, ORBS), I16), vm((ROWS, ORBS), I16), vm((8, ORBS), F32), vm((8, ORBS), F32),
        vm((576, 128), BF), vm((576, 128), BF), vm((576, 128), BF),
        vm((2, PHALF, TILE), F32), vm((2, HALF, ORBS), F32),
        vm((2, 8, GP, TILE), I16), vm((2, 8, GP, TILE), I16), vm((2, 8, 128), F32), vm((2, 8, 8, 128), F32),
        vm((2, 8, HP, ORBS), I16), vm((2, 8, HP, ORBS), I16), vm((2, 8, 128), F32), vm((2, 8, 8, 128), F32),
        vm((2, PACKED, TILE), I16), vm((2, 16, 8, 128), F32), vm((PACKED, TILE), I16), vm((16, 8, 128), F32),
        vm((2, ORBS, ORBS), I16), vm((2, 16, 8, 128), F32),
        vm(square, BF), vm(square, BF), vm(square, BF), vm(square, BF), vm(square, BF), vm(square, BF),
        vm(square, BF), vm(square, BF), vm((PACKED, TILE), F32),
        vm((2, HP, ORBS), I16), vm((2, 8, 128), F32), vm((HP, ORBS), F32), vm((BLK, ORBS), BF), vm((BLK, ORBS), BF),
        pltpu.SMEM((64,), jnp.int32), pltpu.SMEM((8,), jnp.int32),
        pltpu.SemaphoreType.DMA((2, COUNT)), pltpu.SemaphoreType.DMA((2, COUNT)), pltpu.SemaphoreType.DMA((8,)),
    ]
    result = pl.pallas_call(
        kernel,
        out_shape=jax.ShapeDtypeStruct((ROWS, ORBS), F32),
        in_specs=[
            pl.BlockSpec(memory_space=pltpu.HBM),
            pl.BlockSpec(memory_space=pltpu.HBM),
            pl.BlockSpec(memory_space=pltpu.HBM),
            pl.BlockSpec(memory_space=pltpu.HBM),
        ],
        out_specs=pl.BlockSpec(memory_space=pltpu.HBM),
        scratch_shapes=scratch,
        compiler_params=pltpu.CompilerParams(
            collective_id=0, has_side_effects=True, vmem_limit_bytes=62 * 1024 * 1024
        ),
    )(coefficients[0], basis_metric, pattern, starts)
    return result[None]


def solution(mesh):
    in_specs = (P("orb", ("basis", "rep"), None), P("orb", None), P("orb"), P("orb"))
    out_specs = P("orb", ("basis", "rep"), None)
    return jax.shard_map(
        per_device, mesh=mesh, in_specs=in_specs, out_specs=out_specs, check_vma=False
    )
```

```python
import functools

import jax
import jax.numpy as jnp
from jax import lax
from jax.experimental import pallas as pl
from jax.experimental.pallas import tpu as pltpu
from jax.sharding import PartitionSpec as P

BLK = 64
GROUP_BLOCKS = 64
SUPPORT = 96
ITERS = 2
ROWS = 512
ORBS = 512
HALF = 256
GP = 80
PACKED = 1280
PHALF = 640
HP = 32
TILE = 128
CMAX = 6.0
QMAX = 32767.0
BF = jnp.bfloat16
F32 = jnp.float32
I16 = jnp.int16

HALO_NEXT, HALO_PREV, GSIB, HSIB, NA, NAS, FES, FN, FNS, FHS, NXC, MET = range(12)
NX = 12
RS, RSC, HRS, HRSC, EA, EAS, HA, HAS, FE, FH = range(16, 96, 8)
COUNT = 96

KEPT = [(a, b) for a in range(4) for b in range(a, 4)]


def split(x):
    hi = x.astype(BF)
    return hi, (x - hi.astype(F32)).astype(BF)


def dot(a, b, dims=((1,), (0,))):
    return lax.dot_general(a, b, (dims, ((), ())), preferred_element_type=F32)


def dot3(ah, al, bh, bl, dims=((1,), (0,))):
    return dot(ah, bh, dims) + (dot(ah, bl, dims) + dot(al, bh, dims))


def kernel(
    coef, metric, pattern_in, starts_in, out,
    c, chi, clo, nf, nhi, nlo, yhi, ylo, band, gp, hp,
    nq_out, nq_in, cs_own, cs_in, meff, mrecv, msel,
    gsib, hsib, qs, rs, qsc, rsc, hqs, hrs, hqsc, hrsc,
    ea, es, na, ns, ha, hs, ehi, elo, xhi, xlo, thi, tlo, mhi, mlo, ef, ho, hos, sums, lhs, rhs, ends, pattern, starts,
    ss, rr, local_sem,
):
    b, o, r = lax.axis_index("basis"), lax.axis_index("orb"), lax.axis_index("rep")
    groups = lax.axis_size("orb")
    core, zl = b % 2, b // 2
    z = r * 4 + zl
    p = b * 2 + r
    q = p % 8
    low = zl < 2
    high = jnp.logical_not(low)
    side = jnp.where(low, o - 1, o + 1)
    away = jnp.where(low, o + 1, o - 1)
    has_side = jnp.logical_and(side >= 0, side < groups)
    has_away = jnp.logical_and(away >= 0, away < groups)

    def dev(bb, oo, rep):
        return {"basis": bb, "orb": oo, "rep": rep}

    def zdev(zz, oo):
        return dev((zz % 4) * 2 + core, oo, zz // 4)

    sibling = dev(zl * 2 + 1 - core, o, r)

    barrier = pltpu.get_barrier_semaphore()

    def greet(device):
        pl.semaphore_signal(barrier, inc=1, device_id=device, device_id_type=pl.DeviceIdType.MESH)

    for k in range(1, 8):
        greet(zdev((z + k) % 8, o))
    greet(sibling)
    step_b = jnp.where(r == 1, b + 1, b - 1)
    has_step = jnp.logical_and(step_b >= 0, step_b < 8)

    @pl.when(has_step)
    def _():
        greet(dev(step_b, o, 1 - r))

    below = jnp.logical_and(low, o > 0)
    above = o < groups - 1

    @pl.when(below)
    def _():
        for k in range(8):
            greet(zdev((z + k) % 8, o - 1))

    @pl.when(above)
    def _():
        for m in range(4):
            greet(dev((m // 2) * 2 + core, o + 1, m % 2))

    straight = jnp.logical_and(high, above)

    @pl.when(straight)
    def _():
        greet(dev(b, o + 1, r))

    straight_down = jnp.logical_and(high, o > 0)

    @pl.when(straight_down)
    def _():
        greet(dev(b, o - 1, r))

    loads = [
        pltpu.make_async_copy(coef.at[pl.ds(t * TILE, TILE)], c.at[pl.ds(t * TILE, TILE)], local_sem.at[2 + t]) for t in range(4)
    ]
    small = [
        pltpu.make_async_copy(starts_in, starts, local_sem.at[6]),
        pltpu.make_async_copy(pattern_in, pattern, local_sem.at[7]),
    ]
    for load in small:
        load.start()
    for t in (0, 3, 1, 2):
        loads[t].start()
    load_main = pltpu.make_async_copy(metric.at[pl.ds(pl.multiple_of(q * 512, 64), 512)], meff.at[pl.ds(0, 512)], local_sem.at[0])
    load_prev = pltpu.make_async_copy(
        metric.at[pl.ds(pl.multiple_of((q * 512 + 4032) % 4096, 64), 64)], meff.at[pl.ds(512, 64)], local_sem.at[1]
    )
    load_main.start()
    load_prev.start()
    small[0].wait()
    small[1].wait()
    lane = lax.broadcasted_iota(jnp.int32, (8, ORBS), 1) // BLK
    cs = jnp.zeros((8, ORBS), F32)
    for i in range(8):
        cs = jnp.where(lane == i, starts[i].astype(F32), cs)
    cs_own[...] = cs
    first_block = (o * GROUP_BLOCKS + p * 8).astype(F32)

    def live(rows, cs_ref):
        start, count = rows.start, rows.size
        at = lax.broadcasted_iota(jnp.int32, (count, ORBS), 0) + start
        block = first_block + (at // BLK).astype(F32)
        begin = cs_ref[0:1, :]
        return jnp.logical_and(block >= begin, block < begin + SUPPORT)

    def tiles(body):
        def step(t, carry):
            body(t, pl.ds(pl.multiple_of(t * TILE, TILE), TILE))
            return carry

        lax.fori_loop(0, ROWS // TILE, step, 0)

    def prepare(t, rows):
        x = jnp.where(live(rows, cs_own), c[rows, :], 0.0)
        c[rows, :] = x
        hi, lo = split(x)
        chi[0, rows, :] = hi
        clo[0, rows, :] = lo
        nq_out[rows, :] = jnp.round(jnp.clip(x, -CMAX, CMAX) * (QMAX / CMAX)).astype(I16)

    def prepare_tile(t):
        loads[t].wait()
        prepare(jnp.int32(t), pl.ds(t * TILE, TILE))

    prepare_tile(0)
    prepare_tile(3)
    for it in range(ITERS):

        @pl.when(low)
        def _():
            chi[it, 512:576, :] = jnp.zeros((64, ORBS), BF)

        @pl.when(p == 15)
        def _():
            chi[it, 576:640, :] = jnp.zeros((64, ORBS), BF)

    load_main.wait()
    load_prev.wait()
    right = lax.broadcasted_iota(jnp.int32, (BLK, 2 * BLK), 1) >= BLK
    for i in range(9):
        at = (q * 8 + i) % 64 if i < 8 else (q * 8 + 63) % 64
        keep = jnp.where(o * GROUP_BLOCKS + at < groups * GROUP_BLOCKS - 1, pattern[at], 0).astype(F32)
        block = meff[i * 64 : i * 64 + 64, :].astype(F32)
        meff[i * 64 : i * 64 + 64, :] = jnp.where(right, block * keep, block).astype(BF)

    def ones(flag):
        return flag.astype(jnp.int32)

    pl.semaphore_wait(barrier, 8 + ones(has_step) + 8 * ones(below) + 4 * ones(above) + ones(straight) + ones(straight_down))

    sent = []

    def send(src, dst, it, index, device, cond=None, land=None):
        land = index if land is None else land

        def start():
            pltpu.make_async_remote_copy(
                src_ref=src, dst_ref=dst, send_sem=ss.at[it, index], recv_sem=rr.at[it, land],
                device_id=device, device_id_type=pl.DeviceIdType.MESH,
            ).start()

        if cond is None:
            start()
        else:
            pl.when(cond)(start)
        sent.append((src, it, index, cond))

    def arrived(dst, it, index):
        pltpu.make_async_copy(dst, dst, rr.at[it, index]).wait()

    def send_halo(it):
        up_b = jnp.where(r == 0, b, b + 1)
        down_b = jnp.where(r == 1, b, b - 1)
        send(chi.at[it, pl.ds(0, 64)], chi.at[it, pl.ds(576, 64)], it, HALO_NEXT, dev(down_b, o, 1 - r), p > 0)
        send(chi.at[it, pl.ds(448, 64)], chi.at[it, pl.ds(512, 64)], it, HALO_PREV, dev(up_b, o, 1 - r), jnp.logical_and(p > 6, p < 15))

    def wait_halo(it):
        pl.when(p < 15)(lambda: arrived(chi.at[it, pl.ds(576, 64)], it, HALO_NEXT))
        pl.when(high)(lambda: arrived(chi.at[it, pl.ds(512, 64)], it, HALO_PREV))

    gives_metric = jnp.logical_and(high, o > 0)
    send(meff, mrecv, 0, MET, dev(b, o - 1, r), gives_metric)
    send_halo(0)
    partner = dev(jnp.where(low, b + 4, b - 4), side, r)
    for t in (0, 3, 1, 2):
        if t in (1, 2):
            prepare_tile(t)
        rows = pl.ds(t * TILE, TILE)
        send(nq_out.at[rows], nq_in.at[rows], 0, NX + t, partner, has_side)
    send(cs_own, cs_in, 0, NXC, partner, has_side)

    @pl.when(low)
    def _():
        msel[...] = meff[...]

    @pl.when(jnp.logical_and(high, has_side))
    def _():
        arrived(mrecv, 0, MET)
        msel[...] = mrecv[...]

    @pl.when(jnp.logical_and(high, jnp.logical_not(has_side)))
    def _():
        msel[...] = jnp.zeros((576, 128), BF)

    @pl.when(p == 8)
    def _():
        msel[512:576, :] = meff[512:576, :]

    band[...] = jnp.zeros((ROWS, 640), BF)
    row_at = lax.broadcasted_iota(jnp.int32, (128, 128), 0)
    lane_at = lax.broadcasted_iota(jnp.int32, (128, 128), 1)
    top, left = row_at < 64, lane_at < 64
    bottom, rest = row_at >= 64, lane_at >= 64
    for t in range(4):
        m = msel[t * 128 : t * 128 + 128, :].astype(F32)
        rolled = pltpu.roll(m, 64, 1)
        corner = jnp.where(jnp.logical_and(top, rest), m, 0.0)
        diag = jnp.where(top, m, jnp.where(rest, rolled, 0.0)) + corner.T
        band[t * 128 : t * 128 + 128, t * 128 : t * 128 + 128] = diag.astype(BF)
        if t < 3:
            off = jnp.where(jnp.logical_and(bottom, left), rolled, 0.0)
            band[t * 128 : t * 128 + 128, t * 128 + 128 : t * 128 + 256] = off.astype(BF)
            band[t * 128 + 128 : t * 128 + 256, t * 128 : t * 128 + 128] = off.T.astype(BF)
        else:
            band[384:512, 512:640] = jnp.where(jnp.logical_and(bottom, rest), m, 0.0).astype(BF)
    before = pltpu.roll(msel[448:576, :].astype(F32), 64, 1).T
    shifted = pltpu.roll(before, 64, 1)
    band[0:128, 512:640] = jnp.where(jnp.logical_and(top, left), shifted, 0.0).astype(BF)

    def images(it):
        def body(t, rows):
            yhi[rows, :], ylo[rows, :] = split(dot(band[rows, 0:512], chi[it, 0:512]) + dot(band[rows, 0:512], clo[it]))

        tiles(body)

    def edges(it):
        wait_halo(it)
        top = dot(band[0:64, 512:640], chi[it, 512:640])
        bottom = dot(band[448:512, 512:640], chi[it, 512:640])
        last_block = chi[it, 448:512, :]
        lhs[0:64, :] = chi[it, 0:64, :]
        rhs[0:64, :] = top.astype(BF)
        lhs[64:128, :] = last_block
        rhs[64:128, :] = bottom.astype(BF)
        lhs[128:192, :] = bottom.astype(BF)
        rhs[128:192, :] = (last_block.astype(F32) * (p < 7).astype(F32)).astype(BF)
        for a in range(4):
            cols = slice(a * TILE, a * TILE + TILE)
            g = dot(lhs[:, cols], rhs[:, a * TILE : ORBS], ((0,), (0,)))
            for e in range(a, 4):
                rows = slice(KEPT.index((a, e)) * TILE, KEPT.index((a, e)) * TILE + TILE)
                gp[it, rows, :] = gp[it, rows, :] + g[:, (e - a) * TILE : (e - a) * TILE + TILE]
        if it == 0:
            for rows, more in ((slice(0, 64), top), (slice(448, 512), bottom)):
                y = yhi[rows, :].astype(F32) + ylo[rows, :].astype(F32)
                yhi[rows, :], ylo[rows, :] = split(y + more)

    def cross_edges(it):
        ends[0:64, :] = nhi[0:64, :]
        ends[64:128, :] = nhi[448:512, :]

        def body(t, cols):
            hp[it, cols, :] = hp[it, cols, :] + dot(rhs[0:128, cols], ends[...], ((0,), (0,)))

        tiles(body)

    def gram(it):
        for a in range(4):
            cols = slice(a * TILE, a * TILE + TILE)
            rest = slice(a * TILE, ORBS)
            g = dot3(chi[it, 0:512, cols], clo[it, :, cols], yhi[:, rest], ylo[:, rest], ((0,), (0,)))
            for e in range(a, 4):
                k = KEPT.index((a, e))
                gp[it, k * TILE : k * TILE + TILE, :] = g[:, (e - a) * TILE : (e - a) * TILE + TILE]

    def cross(it):
        def body(t, cols):
            hp[it, cols, :] = dot3(yhi[:, cols], ylo[:, cols], nhi[...], nlo[...], ((0,), (0,)))

        tiles(body)

    def cross_rows(it, rows, begin):
        def body(t, cols):
            more = dot3(yhi[rows, cols], ylo[rows, cols], nhi[rows, :], nlo[rows, :], ((0,), (0,)))
            hp[it, cols, :] = more if begin else hp[it, cols, :] + more

        tiles(body)

    own_half = pl.ds(pl.multiple_of(core * HALF, HALF), HALF)
    other_half = pl.ds(pl.multiple_of((1 - core) * HALF, HALF), HALF)
    own_part = pl.ds(pl.multiple_of(core * PHALF, PHALF), PHALF)
    other_part = pl.ds(pl.multiple_of((1 - core) * PHALF, PHALF), PHALF)

    def pair_and_pack(it, part, from_pair, packed, scale, size, count):
        half, wide = size * count, part.shape[2]

        def add(i, top_value):
            rows = pl.ds(pl.multiple_of(core * half + i * size, size), size)
            x = part[it, rows, :] + from_pair[it, pl.ds(pl.multiple_of(i * size, size), size), :]
            part[it, rows, :] = x
            return jnp.maximum(top_value, jnp.abs(x))

        peak = jnp.max(lax.fori_loop(0, count, add, jnp.zeros((size, wide), F32)), axis=(0, 1), keepdims=True)
        peak = jnp.maximum(peak, 1e-30)
        scale[it] = jnp.broadcast_to(peak * (1.0 / QMAX), (8, 128))
        inv = QMAX / peak

        def pack(i, carry):
            rows = pl.ds(pl.multiple_of(core * half + i * size, size), size)
            packed[it, i] = jnp.round(part[it, rows, :] * inv).astype(I16)
            return carry

        lax.fori_loop(0, count, pack, 0)

    def quantized(x):
        peak = jnp.maximum(jnp.max(jnp.abs(x), axis=(0, 1), keepdims=True), 1e-30)
        return jnp.round(x * (QMAX / peak)).astype(I16), jnp.broadcast_to(peak * (1.0 / QMAX), (8, 128))

    def scatter_gram(it):
        arrived(gsib.at[it], it, GSIB)
        pair_and_pack(it, gp, gsib, qs, qsc, GP, 8)
        for k in range(1, 8):
            to = (z + k) % 8
            send(qs.at[it, to], rs.at[it, k], it, RS + k, zdev(to, o))
            send(qsc.at[it], rsc.at[it, k], it, RSC + k, zdev(to, o))

    def scatter_cross(it):
        arrived(hsib.at[it], it, HSIB)
        pair_and_pack(it, hp, hsib, hqs, hqsc, HP, 8)

    def from_high(k):
        return (z + 8 - k) % 4 >= 2

    def send_cross(it):
        for k in range(1, 8):
            to = (z + k) % 8
            send(hqs.at[it, to], hrs.at[it, k], it, HRS + k, zdev(to, o), high)
            send(hqsc.at[it], hrsc.at[it, k], it, HRSC + k, zdev(to, o), high)

    def own_gram(it):
        rows = pl.ds(pl.multiple_of(core * PHALF + z * GP, GP), GP)
        total = gp[it, rows, :]
        for k in range(1, 8):
            arrived(rs.at[it, k], it, RS + k)
            arrived(rsc.at[it, k], it, RSC + k)
            total = total + rs[it, k].astype(jnp.int32).astype(F32) * rsc[it, k, 0:1, 0:1]
        here = lax.broadcasted_iota(jnp.int32, (GP, TILE), 0) + (core * PHALF + z * GP)
        tile = lax.shift_right_logical(here, 7)
        within = jnp.bitwise_and(here, 127) == lax.broadcasted_iota(jnp.int32, (GP, TILE), 1)
        on = jnp.zeros((GP, TILE), F32)
        for a in range(4):
            on = jnp.where(jnp.logical_and(tile == KEPT.index((a, a)), within), 1.0, on)
        value, scale = quantized(total * (1.0 / (SUPPORT * BLK)) - on)
        ea[it, rows, :] = value
        at = core * 8 + z
        es[it, at] = scale
        for k in range(1, 8):
            device = zdev((z + k) % 8, o)
            send(ea.at[it, rows], ea.at[it, rows], it, EA + k, device)
            send(es.at[it, at], es.at[it, at], it, EAS + k, device)

    def own_cross(it):
        rows = pl.ds(pl.multiple_of(core * HALF + z * HP, HP), HP)
        at = core * 8 + z

        @pl.when(high)
        def _():
            sums[...] = hp[it, rows, :]

        @pl.when(low)
        def _():
            sums[...] = jnp.zeros((HP, ORBS), F32)

        for k in range(1, 8):

            @pl.when(from_high(k))
            def _():
                arrived(hrs.at[it, k], it, HRS + k)
                arrived(hrsc.at[it, k], it, HRSC + k)
                sums[...] = sums[...] + hrs[it, k].astype(jnp.int32).astype(F32) * hrsc[it, k, 0:1, 0:1]

        value, scale = quantized(sums[...] * (1.0 / (SUPPORT * BLK)))
        ho[it] = value
        hos[it] = scale

        @pl.when(high)
        def _():
            ha[it, rows, :] = value
            hs[it, at] = scale

        for k in range(8):
            to = (z + k) % 8
            to_low = to % 4 < 2
            cond = jnp.logical_and(to_low, above)
            if k > 0:
                cond = jnp.logical_or(cond, to % 4 >= 2)
            device = zdev(to, jnp.where(to_low, o + 1, o))
            send(ho.at[it], ha.at[it, rows], it, HA + k, device, cond)
            send(hos.at[it], hs.at[it, at], it, HAS + k, device, cond)

    own_eight = pl.ds(pl.multiple_of(core * 8, 8), 8)
    other_eight = pl.ds(pl.multiple_of((1 - core) * 8, 8), 8)
    def piece(at, size):
        return pl.ds(pl.multiple_of(at * size, size), size)

    def pass_gram(it, with_side):
        for k in range(1, 8):
            at = core * 8 + (z + 8 - k) % 8
            arrived(ea.at[it, piece(at, GP)], it, EA + k)
            arrived(es.at[it, at], it, EAS + k)
            send(ea.at[it, piece(at, GP)], ea.at[it, piece(at, GP)], it, FE + k, sibling)
        mine = piece(core * 8 + z, GP)
        send(ea.at[it, mine], ea.at[it, mine], it, FE, sibling)
        send(es.at[it, own_eight], es.at[it, own_eight], it, FES, sibling)
        if with_side:
            send(ea.at[it, own_part], na.at[own_part], it, NA, dev(b, away, r), has_away)
            send(es.at[it, own_eight], ns.at[own_eight], it, NAS, dev(b, away, r), has_away)

    def pass_side(it):
        @pl.when(has_side)
        def _():
            arrived(na.at[own_part], it, NA)
            arrived(ns.at[own_eight], it, NAS)

        send(na.at[own_part], na.at[own_part], it, FN, sibling, has_side)
        send(ns.at[own_eight], ns.at[own_eight], it, FNS, sibling, has_side)

    def pass_cross(it):
        data, tags = ha.at[it], hs.at[it]
        takes = jnp.logical_or(high, has_side)
        for k in range(8):
            at = core * 8 + (z + 8 - k) % 8

            def taken(at=at, k=k):
                arrived(data.at[piece(at, HP)], it, HA + k)
                arrived(tags.at[at], it, HAS + k)

            pl.when(below if k == 0 else takes)(taken)
            send(data.at[piece(at, HP)], data.at[piece(at, HP)], it, FH + k, sibling, takes)
        send(tags.at[own_eight], tags.at[own_eight], it, FHS, sibling, takes)

    def unpack(value, scale):
        return value.astype(jnp.int32).astype(F32) * scale[0:1, 0:1]

    def spread(packed, scales, to_hi, to_lo):
        def body(i, carry):
            rows = piece(i, GP)
            ef[rows, :] = unpack(packed[rows, :], scales[i])
            return carry

        lax.fori_loop(0, 16, body, 0)
        for k, (a, e) in enumerate(KEPT):
            x = ef[k * TILE : k * TILE + TILE, :]
            at, to = slice(a * TILE, a * TILE + TILE), slice(e * TILE, e * TILE + TILE)
            to_hi[at, to], to_lo[at, to] = split(x)
            if a != e:
                to_hi[to, at], to_lo[to, at] = split(x.T)

    def take_gram(it):
        for k in range(8):
            arrived(ea.at[it, piece((1 - core) * 8 + (z + 8 - k) % 8, GP)], it, FE + k)
        arrived(es.at[it, other_eight], it, FES)
        spread(ea.at[it], es.at[it], ehi, elo)

    def take_side(it):
        @pl.when(has_side)
        def _():
            arrived(na.at[other_part], it, FN)
            arrived(ns.at[other_eight], it, FNS)
            spread(na, ns, mhi, mlo)

    def cross_value(it, i):
        return jnp.concatenate([unpack(ha[it, piece(4 * i + e, HP), :], hs[it, 4 * i + e]) for e in range(4)], axis=0)

    def cross_plain(it, to_hi, to_lo):
        def body(i, carry):
            rows = piece(i, TILE)
            to_hi[rows, :], to_lo[rows, :] = split(cross_value(it, i))
            return carry

        lax.fori_loop(0, 4, body, 0)

    def cross_turned(it, to_hi, to_lo):
        def body(i, carry):
            cols = piece(i, TILE)
            to_hi[:, cols], to_lo[:, cols] = split(cross_value(it, i).T)
            return carry

        lax.fori_loop(0, 4, body, 0)

    def take_cross(it):
        @pl.when(jnp.logical_or(high, has_side))
        def _():
            for k in range(8):
                arrived(ha.at[it, piece((1 - core) * 8 + (z + 8 - k) % 8, HP)], it, FH + k)
            arrived(hs.at[it, other_eight], it, FHS)

        pl.when(jnp.logical_and(low, has_side))(lambda: cross_plain(it, xhi, xlo))
        pl.when(jnp.logical_and(high, has_side))(lambda: cross_turned(it, xhi, xlo))

        @pl.when(jnp.logical_not(has_side))
        def _():
            xhi[...] = jnp.zeros((ORBS, ORBS), BF)
            xlo[...] = jnp.zeros((ORBS, ORBS), BF)

    def own_change(it):
        def body(t, rows):
            c[rows, :] = c[rows, :] - 0.5 * dot3(chi[it, rows, :], clo[it, rows, :], ehi[...], elo[...])

        tiles(body)

    def updated(it, t, rows):
        change = dot3(nhi[rows, :], nlo[rows, :], xhi[...], xlo[...])
        return jnp.where(live(rows, cs_own), c[rows, :] - 0.5 * change, 0.0)

    def take_rows():
        for t in (0, 3, 1, 2):
            rows = slice(t * TILE, t * TILE + TILE)

            @pl.when(has_side)
            def _():
                arrived(nq_in.at[rows], 0, NX + t)
                x = nq_in[rows, :].astype(jnp.int32).astype(F32) * (CMAX / QMAX)
                nf[rows, :] = x
                nhi[rows, :], nlo[rows, :] = split(x)

            @pl.when(jnp.logical_not(has_side))
            def _():
                nhi[rows, :] = jnp.zeros((TILE, ORBS), BF)
                nlo[rows, :] = jnp.zeros((TILE, ORBS), BF)

            pl.when(high)(functools.partial(cross_rows, 0, rows, t == 0))

    def pair_cross(it):
        send(hp.at[it, other_half], hsib.at[it], it, HSIB, sibling, high)

    def first(t, rows):
        x = updated(0, t, rows)
        c[rows, :] = x
        hi, lo = split(x)
        chi[1, rows, :] = hi
        clo[1, rows, :] = lo

    def some(body):
        def run(i, carry):
            body(i, pl.ds(pl.multiple_of(64 + i * TILE, 64), TILE))
            return carry

        lax.fori_loop(0, 3, run, 0)

    def beside(t, rows):
        change = dot3(nhi[rows, :], nlo[rows, :], mhi[...], mlo[...])
        change = change + dot3(chi[0, rows, :], clo[0, rows, :], thi[...], tlo[...])
        x = jnp.where(live(rows, cs_in), nf[rows, :] - 0.5 * change, 0.0)
        nhi[rows, :], nlo[rows, :] = split(x)

    def last(t, rows):
        out[rows, :] = updated(1, t, rows)

    images(0)
    gram(0)
    edges(0)
    send(gp.at[0, other_part], gsib.at[0], 0, GSIB, sibling)
    scatter_gram(0)
    take_rows()
    pair_cross(0)
    own_gram(0)
    pl.when(high)(lambda: scatter_cross(0))
    send_cross(0)
    pass_gram(0, True)
    take_gram(0)
    own_change(0)
    own_cross(0)
    pass_side(0)
    pass_cross(0)
    take_cross(0)
    first(0, pl.ds(0, BLK))
    first(0, pl.ds(448, BLK))
    send_halo(1)
    some(first)
    pl.when(has_side)(lambda: arrived(cs_in, 0, NXC))
    pl.when(jnp.logical_and(low, has_side))(lambda: cross_turned(0, thi, tlo))
    pl.when(jnp.logical_and(high, has_side))(lambda: cross_plain(0, thi, tlo))
    take_side(0)
    pl.when(has_side)(lambda: tiles(beside))

    images(1)
    gram(1)
    pl.when(high)(lambda: cross(1))
    edges(1)
    send(gp.at[1, other_part], gsib.at[1], 1, GSIB, sibling)
    pl.when(high)(lambda: cross_edges(1))
    pair_cross(1)
    scatter_gram(1)
    pl.when(high)(lambda: scatter_cross(1))
    send_cross(1)
    own_gram(1)
    own_cross(1)
    pass_gram(1, False)
    take_gram(1)
    own_change(1)
    pass_cross(1)
    take_cross(1)
    tiles(last)

    for src, it, index, cond in sent:

        def wait(src=src, it=it, index=index):
            pltpu.make_async_copy(src, src, ss.at[it, index]).wait()

        if cond is None:
            wait()
        else:
            pl.when(cond)(wait)


def per_device(coefficients, basis_metric, pattern, starts):
    vm = pltpu.VMEM
    square = (ORBS, ORBS)
    scratch = [
        vm((ROWS, ORBS), F32), vm((2, 640, ORBS), BF), vm((2, ROWS, ORBS), BF),
        vm((ROWS, ORBS), F32), vm((ROWS, ORBS), BF), vm((ROWS, ORBS), BF),
        vm((ROWS, ORBS), BF), vm((ROWS, ORBS), BF), vm((ROWS, 640), BF),
        vm((2, PACKED, TILE), F32), vm((2, ORBS, ORBS), F32),
        vm((ROWS, ORBS), I16), vm((ROWS, ORBS), I16), vm((8, ORBS), F32), vm((8, ORBS), F32),
        vm((576, 128), BF), vm((576, 128), BF), vm((576, 128), BF),
        vm((2, PHALF, TILE), F32), vm((2, HALF, ORBS), F32),
        vm((2, 8, GP, TILE), I16), vm((2, 8, GP, TILE), I16), vm((2, 8, 128), F32), vm((2, 8, 8, 128), F32),
        vm((2, 8, HP, ORBS), I16), vm((2, 8, HP, ORBS), I16), vm((2, 8, 128), F32), vm((2, 8, 8, 128), F32),
        vm((2, PACKED, TILE), I16), vm((2, 16, 8, 128), F32), vm((PACKED, TILE), I16), vm((16, 8, 128), F32),
        vm((2, ORBS, ORBS), I16), vm((2, 16, 8, 128), F32),
        vm(square, BF), vm(square, BF), vm(square, BF), vm(square, BF), vm(square, BF), vm(square, BF),
        vm(square, BF), vm(square, BF), vm((PACKED, TILE), F32),
        vm((2, HP, ORBS), I16), vm((2, 8, 128), F32), vm((HP, ORBS), F32), vm((192, ORBS), BF), vm((192, ORBS), BF), vm((128, ORBS), BF),
        pltpu.SMEM((64,), jnp.int32), pltpu.SMEM((8,), jnp.int32),
        pltpu.SemaphoreType.DMA((2, COUNT)), pltpu.SemaphoreType.DMA((2, COUNT)), pltpu.SemaphoreType.DMA((8,)),
    ]
    result = pl.pallas_call(
        kernel,
        out_shape=jax.ShapeDtypeStruct((ROWS, ORBS), F32),
        in_specs=[
            pl.BlockSpec(memory_space=pltpu.HBM),
            pl.BlockSpec(memory_space=pltpu.HBM),
            pl.BlockSpec(memory_space=pltpu.HBM),
            pl.BlockSpec(memory_space=pltpu.HBM),
        ],
        out_specs=pl.BlockSpec(memory_space=pltpu.VMEM),
        scratch_shapes=scratch,
        compiler_params=pltpu.CompilerParams(
            collective_id=0, has_side_effects=True, vmem_limit_bytes=52 * 1024 * 1024
        ),
    )(coefficients[0], basis_metric, pattern, starts)
    return result[None]


def solution(mesh):
    in_specs = (P("orb", ("basis", "rep"), None), P("orb", None), P("orb"), P("orb"))
    out_specs = P("orb", ("basis", "rep"), None)
    return jax.shard_map(
        per_device, mesh=mesh, in_specs=in_specs, out_specs=out_specs, check_vma=False
    )
```

```python
import functools

import jax
import jax.numpy as jnp
from jax import lax
from jax.experimental import pallas as pl
from jax.experimental.pallas import tpu as pltpu
from jax.sharding import PartitionSpec as P

BLK = 64
GROUP_BLOCKS = 64
SUPPORT = 96
ITERS = 2
ROWS = 512
ORBS = 512
HALF = 256
GP = 80
PACKED = 1280
PHALF = 640
HP = 32
TILE = 128
CMAX = 6.0
QMAX = 32767.0
BF = jnp.bfloat16
F32 = jnp.float32
I16 = jnp.int16

HALO_NEXT, HALO_PREV, GSIB, HSIB, NA, NAS, FES, FN, FNS, FHS, NXC, MET = range(12)
NX = 12
RS, RSC, HRS, HRSC, EA, EAS, HA, HAS, FE, FH = range(16, 96, 8)
COUNT = 96

KEPT = [(a, b) for a in range(4) for b in range(a, 4)]


def split(x):
    hi = x.astype(BF)
    return hi, (x - hi.astype(F32)).astype(BF)


def dot(a, b, dims=((1,), (0,))):
    return lax.dot_general(a, b, (dims, ((), ())), preferred_element_type=F32)


def dot3(ah, al, bh, bl, dims=((1,), (0,))):
    return dot(ah, bh, dims) + (dot(ah, bl, dims) + dot(al, bh, dims))


def kernel(
    coef, metric, pattern_in, starts_in, out,
    c, chi, clo, nf, nhi, nlo, yhi, ylo, band, gp, hp,
    nq_out, nq_in, cs_own, cs_in, meff, mrecv, msel,
    gsib, hsib, qs, rs, qsc, rsc, hqs, hrs, hqsc, hrsc,
    ea, es, na, ns, ha, hs, ehi, elo, xhi, xlo, thi, tlo, mhi, mlo, ef, ho, hos, sums, lhs, rhs, ends, pattern, starts,
    ss, rr, local_sem,
):
    b, o, r = lax.axis_index("basis"), lax.axis_index("orb"), lax.axis_index("rep")
    groups = lax.axis_size("orb")
    core, zl = b % 2, b // 2
    z = r * 4 + zl
    p = b * 2 + r
    q = p % 8
    low = zl < 2
    high = jnp.logical_not(low)
    side = jnp.where(low, o - 1, o + 1)
    away = jnp.where(low, o + 1, o - 1)
    has_side = jnp.logical_and(side >= 0, side < groups)
    has_away = jnp.logical_and(away >= 0, away < groups)

    def dev(bb, oo, rep):
        return {"basis": bb, "orb": oo, "rep": rep}

    def zdev(zz, oo):
        return dev((zz % 4) * 2 + core, oo, zz // 4)

    sibling = dev(zl * 2 + 1 - core, o, r)

    barrier = pltpu.get_barrier_semaphore()

    def greet(device):
        pl.semaphore_signal(barrier, inc=1, device_id=device, device_id_type=pl.DeviceIdType.MESH)

    for k in range(1, 8):
        greet(zdev((z + k) % 8, o))
    greet(sibling)
    step_b = jnp.where(r == 1, b + 1, b - 1)
    has_step = jnp.logical_and(step_b >= 0, step_b < 8)

    @pl.when(has_step)
    def _():
        greet(dev(step_b, o, 1 - r))

    below = jnp.logical_and(low, o > 0)
    above = o < groups - 1

    @pl.when(below)
    def _():
        for k in range(8):
            greet(zdev((z + k) % 8, o - 1))

    @pl.when(above)
    def _():
        for m in range(4):
            greet(dev((m // 2) * 2 + core, o + 1, m % 2))

    straight = jnp.logical_and(high, above)

    @pl.when(straight)
    def _():
        greet(dev(b, o + 1, r))

    straight_down = jnp.logical_and(high, o > 0)

    @pl.when(straight_down)
    def _():
        greet(dev(b, o - 1, r))

    loads = [
        pltpu.make_async_copy(coef.at[pl.ds(t * TILE, TILE)], c.at[pl.ds(t * TILE, TILE)], local_sem.at[2 + t]) for t in range(4)
    ]
    small = [
        pltpu.make_async_copy(starts_in, starts, local_sem.at[6]),
        pltpu.make_async_copy(pattern_in, pattern, local_sem.at[7]),
    ]
    for load in small:
        load.start()
    for t in (0, 3, 1, 2):
        loads[t].start()
    load_main = pltpu.make_async_copy(metric.at[pl.ds(pl.multiple_of(q * 512, 64), 512)], meff.at[pl.ds(0, 512)], local_sem.at[0])
    load_prev = pltpu.make_async_copy(
        metric.at[pl.ds(pl.multiple_of((q * 512 + 4032) % 4096, 64), 64)], meff.at[pl.ds(512, 64)], local_sem.at[1]
    )
    load_main.start()
    load_prev.start()
    small[0].wait()
    small[1].wait()
    lane = lax.broadcasted_iota(jnp.int32, (1, ORBS), 1) // BLK
    cs = jnp.zeros((1, ORBS), F32)
    for i in range(8):
        cs = jnp.where(lane == i, starts[i].astype(F32), cs)
    cs_own[...] = cs
    first_block = (o * GROUP_BLOCKS + p * 8).astype(F32)

    def live(rows, cs_ref):
        start, count = rows.start, rows.size
        at = lax.broadcasted_iota(jnp.int32, (count, ORBS), 0) + start
        block = first_block + (at // BLK).astype(F32)
        begin = cs_ref[0:1, :]
        return jnp.logical_and(block >= begin, block < begin + SUPPORT)

    def tiles(body):
        def step(t, carry):
            body(t, pl.ds(pl.multiple_of(t * TILE, TILE), TILE))
            return carry

        lax.fori_loop(0, ROWS // TILE, step, 0)

    def prepare(t, rows):
        x = jnp.where(live(rows, cs_own), c[rows, :], 0.0)
        c[rows, :] = x
        hi, lo = split(x)
        chi[0, rows, :] = hi
        clo[0, rows, :] = lo
        nq_out[rows, :] = jnp.round(jnp.clip(x, -CMAX, CMAX) * (QMAX / CMAX)).astype(I16)

    def prepare_tile(t):
        loads[t].wait()
        prepare(jnp.int32(t), pl.ds(t * TILE, TILE))

    prepare_tile(0)
    prepare_tile(3)
    for it in range(ITERS):

        @pl.when(low)
        def _():
            chi[it, 512:576, :] = jnp.zeros((64, ORBS), BF)

        @pl.when(p == 15)
        def _():
            chi[it, 576:640, :] = jnp.zeros((64, ORBS), BF)

    load_main.wait()
    load_prev.wait()
    right = lax.broadcasted_iota(jnp.int32, (BLK, 2 * BLK), 1) >= BLK
    for i in range(9):
        at = (q * 8 + i) % 64 if i < 8 else (q * 8 + 63) % 64
        keep = jnp.where(o * GROUP_BLOCKS + at < groups * GROUP_BLOCKS - 1, pattern[at], 0).astype(F32)
        block = meff[i * 64 : i * 64 + 64, :].astype(F32)
        meff[i * 64 : i * 64 + 64, :] = jnp.where(right, block * keep, block).astype(BF)

    def ones(flag):
        return flag.astype(jnp.int32)

    pl.semaphore_wait(barrier, 8 + ones(has_step) + 8 * ones(below) + 4 * ones(above) + ones(straight) + ones(straight_down))

    sent = []

    def send(src, dst, it, index, device, cond=None, land=None):
        land = index if land is None else land

        def start():
            pltpu.make_async_remote_copy(
                src_ref=src, dst_ref=dst, send_sem=ss.at[it, index], recv_sem=rr.at[it, land],
                device_id=device, device_id_type=pl.DeviceIdType.MESH,
            ).start()

        if cond is None:
            start()
        else:
            pl.when(cond)(start)
        sent.append((src, it, index, cond))

    def arrived(dst, it, index):
        pltpu.make_async_copy(dst, dst, rr.at[it, index]).wait()

    def send_halo(it):
        up_b = jnp.where(r == 0, b, b + 1)
        down_b = jnp.where(r == 1, b, b - 1)
        send(chi.at[it, pl.ds(0, 64)], chi.at[it, pl.ds(576, 64)], it, HALO_NEXT, dev(down_b, o, 1 - r), p > 0)
        send(chi.at[it, pl.ds(448, 64)], chi.at[it, pl.ds(512, 64)], it, HALO_PREV, dev(up_b, o, 1 - r), jnp.logical_and(p > 6, p < 15))

    def wait_halo(it):
        pl.when(p < 15)(lambda: arrived(chi.at[it, pl.ds(576, 64)], it, HALO_NEXT))
        pl.when(high)(lambda: arrived(chi.at[it, pl.ds(512, 64)], it, HALO_PREV))

    gives_metric = jnp.logical_and(high, o > 0)
    send(meff, mrecv, 0, MET, dev(b, o - 1, r), gives_metric)
    send_halo(0)
    partner = dev(jnp.where(low, b + 4, b - 4), side, r)
    for t in (0, 3, 1, 2):
        if t in (1, 2):
            prepare_tile(t)
        rows = pl.ds(t * TILE, TILE)
        send(nq_out.at[rows], nq_in.at[rows], 0, NX + t, partner, has_side)
    send(cs_own, cs_in, 0, NXC, partner, has_side)

    @pl.when(low)
    def _():
        msel[...] = meff[...]

    @pl.when(jnp.logical_and(high, has_side))
    def _():
        arrived(mrecv, 0, MET)
        msel[...] = mrecv[...]

    @pl.when(jnp.logical_and(high, jnp.logical_not(has_side)))
    def _():
        msel[...] = jnp.zeros((576, 128), BF)

    @pl.when(p == 8)
    def _():
        msel[512:576, :] = meff[512:576, :]

    band[...] = jnp.zeros((ROWS, 640), BF)
    row_at = lax.broadcasted_iota(jnp.int32, (128, 128), 0)
    lane_at = lax.broadcasted_iota(jnp.int32, (128, 128), 1)
    top, left = row_at < 64, lane_at < 64
    bottom, rest = row_at >= 64, lane_at >= 64
    for t in range(4):
        m = msel[t * 128 : t * 128 + 128, :].astype(F32)
        rolled = pltpu.roll(m, 64, 1)
        corner = jnp.where(jnp.logical_and(top, rest), m, 0.0)
        diag = jnp.where(top, m, jnp.where(rest, rolled, 0.0)) + corner.T
        band[t * 128 : t * 128 + 128, t * 128 : t * 128 + 128] = diag.astype(BF)
        if t < 3:
            off = jnp.where(jnp.logical_and(bottom, left), rolled, 0.0)
            band[t * 128 : t * 128 + 128, t * 128 + 128 : t * 128 + 256] = off.astype(BF)
            band[t * 128 + 128 : t * 128 + 256, t * 128 : t * 128 + 128] = off.T.astype(BF)
        else:
            band[384:512, 512:640] = jnp.where(jnp.logical_and(bottom, rest), m, 0.0).astype(BF)
    before = pltpu.roll(msel[448:576, :].astype(F32), 64, 1).T
    shifted = pltpu.roll(before, 64, 1)
    band[0:128, 512:640] = jnp.where(jnp.logical_and(top, left), shifted, 0.0).astype(BF)

    def images(it):
        yhi[...], ylo[...] = split(dot(band[:, 0:512], chi[it, 0:512]) + dot(band[:, 0:512], clo[it]))

    def edges(it):
        wait_halo(it)
        top = dot(band[0:64, 512:640], chi[it, 512:640])
        bottom = dot(band[448:512, 512:640], chi[it, 512:640])
        last_block = chi[it, 448:512, :]
        lhs[0:64, :] = chi[it, 0:64, :]
        rhs[0:64, :] = top.astype(BF)
        lhs[64:128, :] = last_block
        rhs[64:128, :] = bottom.astype(BF)
        lhs[128:192, :] = bottom.astype(BF)
        rhs[128:192, :] = (last_block.astype(F32) * (p < 7).astype(F32)).astype(BF)
        for a in range(4):
            cols = slice(a * TILE, a * TILE + TILE)
            g = dot(lhs[:, cols], rhs[:, a * TILE : ORBS], ((0,), (0,)))
            for e in range(a, 4):
                rows = slice(KEPT.index((a, e)) * TILE, KEPT.index((a, e)) * TILE + TILE)
                gp[it, rows, :] = gp[it, rows, :] + g[:, (e - a) * TILE : (e - a) * TILE + TILE]
        if it == 0:
            for rows, more in ((slice(0, 64), top), (slice(448, 512), bottom)):
                y = yhi[rows, :].astype(F32) + ylo[rows, :].astype(F32)
                yhi[rows, :], ylo[rows, :] = split(y + more)

    def cross_edges(it):
        ends[0:64, :] = nhi[0:64, :]
        ends[64:128, :] = nhi[448:512, :]

        hp[it] = hp[it] + dot(rhs[0:128, :], ends[...], ((0,), (0,)))

    def gram(it):
        for a in range(4):
            cols = slice(a * TILE, a * TILE + TILE)
            rest = slice(a * TILE, ORBS)
            g = dot3(chi[it, 0:512, cols], clo[it, :, cols], yhi[:, rest], ylo[:, rest], ((0,), (0,)))
            for e in range(a, 4):
                k = KEPT.index((a, e))
                gp[it, k * TILE : k * TILE + TILE, :] = g[:, (e - a) * TILE : (e - a) * TILE + TILE]

    def cross(it):
        hp[it] = dot3(yhi[...], ylo[...], nhi[...], nlo[...], ((0,), (0,)))

    def cross_rows(it, rows, begin):
        more = dot3(yhi[rows, :], ylo[rows, :], nhi[rows, :], nlo[rows, :], ((0,), (0,)))
        hp[it] = more if begin else hp[it] + more

    own_half = pl.ds(pl.multiple_of(core * HALF, HALF), HALF)
    other_half = pl.ds(pl.multiple_of((1 - core) * HALF, HALF), HALF)
    own_part = pl.ds(pl.multiple_of(core * PHALF, PHALF), PHALF)
    other_part = pl.ds(pl.multiple_of((1 - core) * PHALF, PHALF), PHALF)

    def pair_and_pack(it, part, from_pair, packed, scale, size, count):
        half, wide = size * count, part.shape[2]

        def add(i, top_value):
            rows = pl.ds(pl.multiple_of(core * half + i * size, size), size)
            x = part[it, rows, :] + from_pair[it, pl.ds(pl.multiple_of(i * size, size), size), :]
            part[it, rows, :] = x
            return jnp.maximum(top_value, jnp.abs(x))

        peak = jnp.max(lax.fori_loop(0, count, add, jnp.zeros((size, wide), F32)), axis=(0, 1), keepdims=True)
        peak = jnp.maximum(peak, 1e-30)
        scale[it] = jnp.broadcast_to(peak * (1.0 / QMAX), (1, 128))
        inv = QMAX / peak

        def pack(i, carry):
            rows = pl.ds(pl.multiple_of(core * half + i * size, size), size)
            packed[it, i] = jnp.round(part[it, rows, :] * inv).astype(I16)
            return carry

        lax.fori_loop(0, count, pack, 0)

    def quantized(x):
        peak = jnp.maximum(jnp.max(jnp.abs(x), axis=(0, 1), keepdims=True), 1e-30)
        return jnp.round(x * (QMAX / peak)).astype(I16), jnp.broadcast_to(peak * (1.0 / QMAX), (1, 128))

    def scatter_gram(it):
        arrived(gsib.at[it], it, GSIB)
        pair_and_pack(it, gp, gsib, qs, qsc, GP, 8)
        for k in range(1, 8):
            to = (z + k) % 8
            send(qs.at[it, to], rs.at[it, k], it, RS + k, zdev(to, o))
            send(qsc.at[it], rsc.at[it, k], it, RSC + k, zdev(to, o))

    def scatter_cross(it):
        arrived(hsib.at[it], it, HSIB)
        pair_and_pack(it, hp, hsib, hqs, hqsc, HP, 8)

    def from_high(k):
        return (z + 8 - k) % 4 >= 2

    def send_cross(it):
        for k in range(1, 8):
            to = (z + k) % 8
            send(hqs.at[it, to], hrs.at[it, k], it, HRS + k, zdev(to, o), high)
            send(hqsc.at[it], hrsc.at[it, k], it, HRSC + k, zdev(to, o), high)

    def own_gram(it):
        rows = pl.ds(pl.multiple_of(core * PHALF + z * GP, GP), GP)
        total = gp[it, rows, :]
        for k in range(1, 8):
            arrived(rs.at[it, k], it, RS + k)
            arrived(rsc.at[it, k], it, RSC + k)
            total = total + rs[it, k].astype(jnp.int32).astype(F32) * rsc[it, k, 0:1, 0:1]
        here = lax.broadcasted_iota(jnp.int32, (GP, TILE), 0) + (core * PHALF + z * GP)
        tile = lax.shift_right_logical(here, 7)
        within = jnp.bitwise_and(here, 127) == lax.broadcasted_iota(jnp.int32, (GP, TILE), 1)
        on = jnp.zeros((GP, TILE), F32)
        for a in range(4):
            on = jnp.where(jnp.logical_and(tile == KEPT.index((a, a)), within), 1.0, on)
        value, scale = quantized(total * (1.0 / (SUPPORT * BLK)) - on)
        ea[it, rows, :] = value
        at = core * 8 + z
        es[it, at] = scale
        for k in range(1, 8):
            device = zdev((z + k) % 8, o)
            send(ea.at[it, rows], ea.at[it, rows], it, EA + k, device)
            send(es.at[it, at], es.at[it, at], it, EAS + k, device)

    def own_cross(it):
        rows = pl.ds(pl.multiple_of(core * HALF + z * HP, HP), HP)
        at = core * 8 + z

        @pl.when(high)
        def _():
            sums[...] = hp[it, rows, :]

        @pl.when(low)
        def _():
            sums[...] = jnp.zeros((HP, ORBS), F32)

        for k in range(1, 8):

            @pl.when(from_high(k))
            def _():
                arrived(hrs.at[it, k], it, HRS + k)
                arrived(hrsc.at[it, k], it, HRSC + k)
                sums[...] = sums[...] + hrs[it, k].astype(jnp.int32).astype(F32) * hrsc[it, k, 0:1, 0:1]

        value, scale = quantized(sums[...] * (1.0 / (SUPPORT * BLK)))
        ho[it] = value
        hos[it] = scale

        @pl.when(high)
        def _():
            ha[it, rows, :] = value
            hs[it, at] = scale

        for k in range(8):
            to = (z + k) % 8
            to_low = to % 4 < 2
            cond = jnp.logical_and(to_low, above)
            if k > 0:
                cond = jnp.logical_or(cond, to % 4 >= 2)
            device = zdev(to, jnp.where(to_low, o + 1, o))
            send(ho.at[it], ha.at[it, rows], it, HA + k, device, cond)
            send(hos.at[it], hs.at[it, at], it, HAS + k, device, cond)

    own_eight = pl.ds(pl.multiple_of(core * 8, 8), 8)
    other_eight = pl.ds(pl.multiple_of((1 - core) * 8, 8), 8)
    def piece(at, size):
        return pl.ds(pl.multiple_of(at * size, size), size)

    def pass_gram(it, with_side):
        for k in range(1, 8):
            at = core * 8 + (z + 8 - k) % 8
            arrived(ea.at[it, piece(at, GP)], it, EA + k)
            arrived(es.at[it, at], it, EAS + k)
            send(ea.at[it, piece(at, GP)], ea.at[it, piece(at, GP)], it, FE + k, sibling)
        mine = piece(core * 8 + z, GP)
        send(ea.at[it, mine], ea.at[it, mine], it, FE, sibling)
        send(es.at[it, own_eight], es.at[it, own_eight], it, FES, sibling)
        if with_side:
            send(ea.at[it, own_part], na.at[own_part], it, NA, dev(b, away, r), has_away)
            send(es.at[it, own_eight], ns.at[own_eight], it, NAS, dev(b, away, r), has_away)

    def pass_side(it):
        @pl.when(has_side)
        def _():
            arrived(na.at[own_part], it, NA)
            arrived(ns.at[own_eight], it, NAS)

        send(na.at[own_part], na.at[own_part], it, FN, sibling, has_side)
        send(ns.at[own_eight], ns.at[own_eight], it, FNS, sibling, has_side)

    def pass_cross(it):
        data, tags = ha.at[it], hs.at[it]
        takes = jnp.logical_or(high, has_side)
        for k in range(8):
            at = core * 8 + (z + 8 - k) % 8

            def taken(at=at, k=k):
                arrived(data.at[piece(at, HP)], it, HA + k)
                arrived(tags.at[at], it, HAS + k)

            pl.when(below if k == 0 else takes)(taken)
            send(data.at[piece(at, HP)], data.at[piece(at, HP)], it, FH + k, sibling, takes)
        send(tags.at[own_eight], tags.at[own_eight], it, FHS, sibling, takes)

    def unpack(value, scale):
        return value.astype(jnp.int32).astype(F32) * scale[0:1, 0:1]

    def spread(packed, scales, to_hi, to_lo):
        def body(i, carry):
            rows = piece(i, GP)
            ef[rows, :] = unpack(packed[rows, :], scales[i])
            return carry

        lax.fori_loop(0, 16, body, 0)
        for k, (a, e) in enumerate(KEPT):
            x = ef[k * TILE : k * TILE + TILE, :]
            at, to = slice(a * TILE, a * TILE + TILE), slice(e * TILE, e * TILE + TILE)
            to_hi[at, to], to_lo[at, to] = split(x)
            if a != e:
                to_hi[to, at], to_lo[to, at] = split(x.T)

    def take_gram(it):
        for k in range(8):
            arrived(ea.at[it, piece((1 - core) * 8 + (z + 8 - k) % 8, GP)], it, FE + k)
        arrived(es.at[it, other_eight], it, FES)
        spread(ea.at[it], es.at[it], ehi, elo)

    def take_side(it):
        @pl.when(has_side)
        def _():
            arrived(na.at[other_part], it, FN)
            arrived(ns.at[other_eight], it, FNS)
            spread(na, ns, mhi, mlo)

    def cross_value(it, i):
        return jnp.concatenate([unpack(ha[it, piece(4 * i + e, HP), :], hs[it, 4 * i + e]) for e in range(4)], axis=0)

    def cross_plain(it, to_hi, to_lo):
        def body(i, carry):
            rows = piece(i, TILE)
            to_hi[rows, :], to_lo[rows, :] = split(cross_value(it, i))
            return carry

        lax.fori_loop(0, 4, body, 0)

    def cross_turned(it, to_hi, to_lo):
        def body(i, carry):
            cols = piece(i, TILE)
            to_hi[:, cols], to_lo[:, cols] = split(cross_value(it, i).T)
            return carry

        lax.fori_loop(0, 4, body, 0)

    def take_cross(it):
        @pl.when(jnp.logical_or(high, has_side))
        def _():
            for k in range(8):
                arrived(ha.at[it, piece((1 - core) * 8 + (z + 8 - k) % 8, HP)], it, FH + k)
            arrived(hs.at[it, other_eight], it, FHS)

        pl.when(jnp.logical_and(low, has_side))(lambda: cross_plain(it, xhi, xlo))
        pl.when(jnp.logical_and(high, has_side))(lambda: cross_turned(it, xhi, xlo))

        @pl.when(jnp.logical_not(has_side))
        def _():
            xhi[...] = jnp.zeros((ORBS, ORBS), BF)
            xlo[...] = jnp.zeros((ORBS, ORBS), BF)

    def own_change(it):
        c[...] = c[...] - 0.5 * dot3(chi[it, 0:512], clo[it], ehi[...], elo[...])

    def updated(it, t, rows):
        change = dot3(nhi[rows, :], nlo[rows, :], xhi[...], xlo[...])
        return jnp.where(live(rows, cs_own), c[rows, :] - 0.5 * change, 0.0)

    def take_rows():
        for t in (0, 3, 1, 2):
            rows = slice(t * TILE, t * TILE + TILE)

            @pl.when(has_side)
            def _():
                arrived(nq_in.at[rows], 0, NX + t)
                x = nq_in[rows, :].astype(jnp.int32).astype(F32) * (CMAX / QMAX)
                nf[rows, :] = x
                nhi[rows, :], nlo[rows, :] = split(x)

            @pl.when(jnp.logical_not(has_side))
            def _():
                nhi[rows, :] = jnp.zeros((TILE, ORBS), BF)
                nlo[rows, :] = jnp.zeros((TILE, ORBS), BF)

            pl.when(high)(functools.partial(cross_rows, 0, rows, t == 0))

    def pair_cross(it):
        send(hp.at[it, other_half], hsib.at[it], it, HSIB, sibling, high)

    def keep(rows, x):
        c[rows, :] = x
        hi, lo = split(x)
        chi[1, rows, :] = hi
        clo[1, rows, :] = lo

    def first(rows):
        keep(rows, updated(0, 0, rows))

    def first_ends():
        two = (pl.ds(0, BLK), pl.ds(448, BLK))
        change = dot3(
            jnp.concatenate([nhi[rows, :] for rows in two], axis=0), jnp.concatenate([nlo[rows, :] for rows in two], axis=0), xhi[...], xlo[...]
        )
        for i, rows in enumerate(two):
            keep(rows, jnp.where(live(rows, cs_own), c[rows, :] - 0.5 * change[i * BLK : i * BLK + BLK], 0.0))

    def beside(t, rows):
        change = dot3(nhi[rows, :], nlo[rows, :], mhi[...], mlo[...])
        change = change + dot3(chi[0, rows, :], clo[0, rows, :], thi[...], tlo[...])
        x = jnp.where(live(rows, cs_in), nf[rows, :] - 0.5 * change, 0.0)
        nhi[rows, :], nlo[rows, :] = split(x)

    def last(t, rows):
        out[rows, :] = updated(1, t, rows)

    images(0)
    gram(0)
    edges(0)
    send(gp.at[0, other_part], gsib.at[0], 0, GSIB, sibling)
    scatter_gram(0)
    take_rows()
    pair_cross(0)
    pl.when(high)(lambda: scatter_cross(0))
    send_cross(0)
    own_gram(0)
    pass_gram(0, True)
    take_gram(0)
    own_change(0)
    own_cross(0)
    pass_side(0)
    pass_cross(0)
    take_cross(0)
    first_ends()
    send_halo(1)
    first(pl.ds(64, 384))
    pl.when(has_side)(lambda: arrived(cs_in, 0, NXC))
    pl.when(jnp.logical_and(low, has_side))(lambda: cross_turned(0, thi, tlo))
    pl.when(jnp.logical_and(high, has_side))(lambda: cross_plain(0, thi, tlo))
    take_side(0)
    pl.when(has_side)(lambda: beside(0, pl.ds(0, ROWS)))

    images(1)
    gram(1)
    pl.when(high)(lambda: cross(1))
    edges(1)
    send(gp.at[1, other_part], gsib.at[1], 1, GSIB, sibling)
    pl.when(high)(lambda: cross_edges(1))
    pair_cross(1)
    scatter_gram(1)
    pl.when(high)(lambda: scatter_cross(1))
    send_cross(1)
    own_gram(1)
    own_cross(1)
    pass_gram(1, False)
    take_gram(1)
    own_change(1)
    pass_cross(1)
    take_cross(1)
    last(0, pl.ds(0, ROWS))

    for src, it, index, cond in sent:

        def wait(src=src, it=it, index=index):
            pltpu.make_async_copy(src, src, ss.at[it, index]).wait()

        if cond is None:
            wait()
        else:
            pl.when(cond)(wait)


def per_device(coefficients, basis_metric, pattern, starts):
    vm = pltpu.VMEM
    square = (ORBS, ORBS)
    scratch = [
        vm((ROWS, ORBS), F32), vm((2, 640, ORBS), BF), vm((2, ROWS, ORBS), BF),
        vm((ROWS, ORBS), F32), vm((ROWS, ORBS), BF), vm((ROWS, ORBS), BF),
        vm((ROWS, ORBS), BF), vm((ROWS, ORBS), BF), vm((ROWS, 640), BF),
        vm((2, PACKED, TILE), F32), vm((2, ORBS, ORBS), F32),
        vm((ROWS, ORBS), I16), vm((ROWS, ORBS), I16), vm((1, ORBS), F32), vm((1, ORBS), F32),
        vm((576, 128), BF), vm((576, 128), BF), vm((576, 128), BF),
        vm((2, PHALF, TILE), F32), vm((2, HALF, ORBS), F32),
        vm((2, 8, GP, TILE), I16), vm((2, 8, GP, TILE), I16), vm((2, 1, 128), F32), vm((2, 8, 1, 128), F32),
        vm((2, 8, HP, ORBS), I16), vm((2, 8, HP, ORBS), I16), vm((2, 1, 128), F32), vm((2, 8, 1, 128), F32),
        vm((2, PACKED, TILE), I16), vm((2, 16, 1, 128), F32), vm((PACKED, TILE), I16), vm((16, 1, 128), F32),
        vm((2, ORBS, ORBS), I16), vm((2, 16, 1, 128), F32),
        vm(square, BF), vm(square, BF), vm(square, BF), vm(square, BF), vm(square, BF), vm(square, BF),
        vm(square, BF), vm(square, BF), vm((PACKED, TILE), F32),
        vm((2, HP, ORBS), I16), vm((2, 1, 128), F32), vm((HP, ORBS), F32), vm((192, ORBS), BF), vm((192, ORBS), BF), vm((128, ORBS), BF),
        pltpu.SMEM((64,), jnp.int32), pltpu.SMEM((8,), jnp.int32),
        pltpu.SemaphoreType.DMA((2, COUNT)), pltpu.SemaphoreType.DMA((2, COUNT)), pltpu.SemaphoreType.DMA((8,)),
    ]
    result = pl.pallas_call(
        kernel,
        out_shape=jax.ShapeDtypeStruct((ROWS, ORBS), F32),
        in_specs=[
            pl.BlockSpec(memory_space=pltpu.HBM),
            pl.BlockSpec(memory_space=pltpu.HBM),
            pl.BlockSpec(memory_space=pltpu.HBM),
            pl.BlockSpec(memory_space=pltpu.HBM),
        ],
        out_specs=pl.BlockSpec(memory_space=pltpu.VMEM),
        scratch_shapes=scratch,
        compiler_params=pltpu.CompilerParams(
            collective_id=0, has_side_effects=True, vmem_limit_bytes=52 * 1024 * 1024
        ),
    )(coefficients[0], basis_metric, pattern, starts)
    return result[None]


def solution(mesh):
    in_specs = (P("orb", ("basis", "rep"), None), P("orb", None), P("orb"), P("orb"))
    out_specs = P("orb", ("basis", "rep"), None)
    return jax.shard_map(
        per_device, mesh=mesh, in_specs=in_specs, out_specs=out_specs, check_vma=False
    )
```

```python
import functools

import jax
import jax.numpy as jnp
from jax import lax
from jax.experimental import pallas as pl
from jax.experimental.pallas import tpu as pltpu
from jax.sharding import PartitionSpec as P

BLK = 64
GROUP_BLOCKS = 64
SUPPORT = 96
ITERS = 2
ROWS = 512
ORBS = 512
HALF = 256
GP = 80
PACKED = 1280
PHALF = 640
HP = 32
TILE = 128
CMAX = 6.0
QMAX = 32767.0
BF = jnp.bfloat16
F32 = jnp.float32
I16 = jnp.int16

HALO_NEXT, HALO_PREV, GSIB, HSIB, NA, NAS, FES, FN, FNS, FHS, NXC, MET = range(12)
NX = 12
RS, RSC, HRS, HRSC, EA, EAS, HA, HAS, FE, FH = range(16, 96, 8)
COUNT = 96

FAR = (4, 3, 5, 2, 6, 1, 7)

KEPT = [(a, b) for a in range(4) for b in range(a, 4)]


def split(x):
    hi = x.astype(BF)
    return hi, (x - hi.astype(F32)).astype(BF)


def dot(a, b, dims=((1,), (0,))):
    return lax.dot_general(a, b, (dims, ((), ())), preferred_element_type=F32)


def dot3(ah, al, bh, bl, dims=((1,), (0,))):
    return dot(ah, bh, dims) + (dot(ah, bl, dims) + dot(al, bh, dims))


def kernel(
    coef, metric, pattern_in, starts_in, out,
    c, chi, clo, nf, nhi, nlo, yhi, ylo, band, gp, hp,
    nq_out, nq_in, cs_own, cs_in, meff, mrecv, msel,
    gsib, hsib, qs, rs, qsc, rsc, hqs, hrs, hqsc, hrsc,
    ea, es, na, ns, ha, hs, ehi, elo, xhi, xlo, thi, tlo, mhi, mlo, ef, ho, hos, sums, lhs, rhs, ends, pattern, starts,
    ss, rr, local_sem,
):
    b, o, r = lax.axis_index("basis"), lax.axis_index("orb"), lax.axis_index("rep")
    groups = lax.axis_size("orb")
    core, zl = b % 2, b // 2
    z = r * 4 + zl
    p = b * 2 + r
    q = p % 8
    low = zl < 2
    high = jnp.logical_not(low)
    side = jnp.where(low, o - 1, o + 1)
    away = jnp.where(low, o + 1, o - 1)
    has_side = jnp.logical_and(side >= 0, side < groups)
    has_away = jnp.logical_and(away >= 0, away < groups)

    def dev(bb, oo, rep):
        return {"basis": bb, "orb": oo, "rep": rep}

    def zdev(zz, oo):
        return dev((zz % 4) * 2 + core, oo, zz // 4)

    sibling = dev(zl * 2 + 1 - core, o, r)

    barrier = pltpu.get_barrier_semaphore()

    def greet(device):
        pl.semaphore_signal(barrier, inc=1, device_id=device, device_id_type=pl.DeviceIdType.MESH)

    for k in range(1, 8):
        greet(zdev((z + k) % 8, o))
    greet(sibling)
    step_b = jnp.where(r == 1, b + 1, b - 1)
    has_step = jnp.logical_and(step_b >= 0, step_b < 8)

    @pl.when(has_step)
    def _():
        greet(dev(step_b, o, 1 - r))

    below = jnp.logical_and(low, o > 0)
    above = o < groups - 1

    @pl.when(below)
    def _():
        for k in range(8):
            greet(zdev((z + k) % 8, o - 1))

    @pl.when(above)
    def _():
        for m in range(4):
            greet(dev((m // 2) * 2 + core, o + 1, m % 2))

    straight = jnp.logical_and(high, above)

    @pl.when(straight)
    def _():
        greet(dev(b, o + 1, r))

    straight_down = jnp.logical_and(high, o > 0)

    @pl.when(straight_down)
    def _():
        greet(dev(b, o - 1, r))

    loads = [
        pltpu.make_async_copy(coef.at[pl.ds(t * TILE, TILE)], c.at[pl.ds(t * TILE, TILE)], local_sem.at[2 + t]) for t in range(4)
    ]
    small = [
        pltpu.make_async_copy(starts_in, starts, local_sem.at[6]),
        pltpu.make_async_copy(pattern_in, pattern, local_sem.at[7]),
    ]
    for load in small:
        load.start()
    for t in (0, 3, 1, 2):
        loads[t].start()
    load_main = pltpu.make_async_copy(metric.at[pl.ds(pl.multiple_of(q * 512, 64), 512)], meff.at[pl.ds(0, 512)], local_sem.at[0])
    load_prev = pltpu.make_async_copy(
        metric.at[pl.ds(pl.multiple_of((q * 512 + 4032) % 4096, 64), 64)], meff.at[pl.ds(512, 64)], local_sem.at[1]
    )
    load_main.start()
    load_prev.start()
    small[0].wait()
    small[1].wait()
    lane = lax.broadcasted_iota(jnp.int32, (1, ORBS), 1) // BLK
    cs = jnp.zeros((1, ORBS), F32)
    for i in range(8):
        cs = jnp.where(lane == i, starts[i].astype(F32), cs)
    cs_own[...] = cs
    first_block = (o * GROUP_BLOCKS + p * 8).astype(F32)

    def live(rows, cs_ref):
        start, count = rows.start, rows.size
        at = lax.broadcasted_iota(jnp.int32, (count, ORBS), 0) + start
        block = first_block + (at // BLK).astype(F32)
        begin = cs_ref[0:1, :]
        return jnp.logical_and(block >= begin, block < begin + SUPPORT)

    def tiles(body):
        def step(t, carry):
            body(t, pl.ds(pl.multiple_of(t * TILE, TILE), TILE))
            return carry

        lax.fori_loop(0, ROWS // TILE, step, 0)

    def prepare(t, rows):
        x = jnp.where(live(rows, cs_own), c[rows, :], 0.0)
        c[rows, :] = x
        hi, lo = split(x)
        chi[0, rows, :] = hi
        clo[0, rows, :] = lo
        nq_out[rows, :] = jnp.round(jnp.clip(x, -CMAX, CMAX) * (QMAX / CMAX)).astype(I16)

    def prepare_tile(t):
        loads[t].wait()
        prepare(jnp.int32(t), pl.ds(t * TILE, TILE))

    prepare_tile(0)
    prepare_tile(3)
    for it in range(ITERS):

        @pl.when(low)
        def _():
            chi[it, 512:576, :] = jnp.zeros((64, ORBS), BF)

        @pl.when(p == 15)
        def _():
            chi[it, 576:640, :] = jnp.zeros((64, ORBS), BF)

    load_main.wait()
    load_prev.wait()
    right = lax.broadcasted_iota(jnp.int32, (BLK, 2 * BLK), 1) >= BLK
    for i in range(9):
        at = (q * 8 + i) % 64 if i < 8 else (q * 8 + 63) % 64
        keep = jnp.where(o * GROUP_BLOCKS + at < groups * GROUP_BLOCKS - 1, pattern[at], 0).astype(F32)
        block = meff[i * 64 : i * 64 + 64, :].astype(F32)
        meff[i * 64 : i * 64 + 64, :] = jnp.where(right, block * keep, block).astype(BF)

    def ones(flag):
        return flag.astype(jnp.int32)

    pl.semaphore_wait(barrier, 8 + ones(has_step) + 8 * ones(below) + 4 * ones(above) + ones(straight) + ones(straight_down))

    sent = []

    def send(src, dst, it, index, device, cond=None, land=None):
        land = index if land is None else land

        def start():
            pltpu.make_async_remote_copy(
                src_ref=src, dst_ref=dst, send_sem=ss.at[it, index], recv_sem=rr.at[it, land],
                device_id=device, device_id_type=pl.DeviceIdType.MESH,
            ).start()

        if cond is None:
            start()
        else:
            pl.when(cond)(start)
        sent.append((src, it, index, cond))

    def arrived(dst, it, index):
        pltpu.make_async_copy(dst, dst, rr.at[it, index]).wait()

    def send_halo(it):
        up_b = jnp.where(r == 0, b, b + 1)
        down_b = jnp.where(r == 1, b, b - 1)
        send(chi.at[it, pl.ds(0, 64)], chi.at[it, pl.ds(576, 64)], it, HALO_NEXT, dev(down_b, o, 1 - r), p > 0)
        send(chi.at[it, pl.ds(448, 64)], chi.at[it, pl.ds(512, 64)], it, HALO_PREV, dev(up_b, o, 1 - r), jnp.logical_and(p > 6, p < 15))

    def wait_halo(it):
        pl.when(p < 15)(lambda: arrived(chi.at[it, pl.ds(576, 64)], it, HALO_NEXT))
        pl.when(high)(lambda: arrived(chi.at[it, pl.ds(512, 64)], it, HALO_PREV))

    gives_metric = jnp.logical_and(high, o > 0)
    send(meff, mrecv, 0, MET, dev(b, o - 1, r), gives_metric)
    send_halo(0)
    partner = dev(jnp.where(low, b + 4, b - 4), side, r)
    for t in (0, 3, 1, 2):
        if t in (1, 2):
            prepare_tile(t)
        rows = pl.ds(t * TILE, TILE)
        send(nq_out.at[rows], nq_in.at[rows], 0, NX + t, partner, has_side)
    send(cs_own, cs_in, 0, NXC, partner, has_side)

    @pl.when(low)
    def _():
        msel[...] = meff[...]

    @pl.when(jnp.logical_and(high, has_side))
    def _():
        arrived(mrecv, 0, MET)
        msel[...] = mrecv[...]

    @pl.when(jnp.logical_and(high, jnp.logical_not(has_side)))
    def _():
        msel[...] = jnp.zeros((576, 128), BF)

    @pl.when(p == 8)
    def _():
        msel[512:576, :] = meff[512:576, :]

    band[...] = jnp.zeros((ROWS, 640), BF)
    row_at = lax.broadcasted_iota(jnp.int32, (128, 128), 0)
    lane_at = lax.broadcasted_iota(jnp.int32, (128, 128), 1)
    top, left = row_at < 64, lane_at < 64
    bottom, rest = row_at >= 64, lane_at >= 64
    for t in range(4):
        m = msel[t * 128 : t * 128 + 128, :].astype(F32)
        rolled = pltpu.roll(m, 64, 1)
        corner = jnp.where(jnp.logical_and(top, rest), m, 0.0)
        diag = jnp.where(top, m, jnp.where(rest, rolled, 0.0)) + corner.T
        band[t * 128 : t * 128 + 128, t * 128 : t * 128 + 128] = diag.astype(BF)
        if t < 3:
            off = jnp.where(jnp.logical_and(bottom, left), rolled, 0.0)
            band[t * 128 : t * 128 + 128, t * 128 + 128 : t * 128 + 256] = off.astype(BF)
            band[t * 128 + 128 : t * 128 + 256, t * 128 : t * 128 + 128] = off.T.astype(BF)
        else:
            band[384:512, 512:640] = jnp.where(jnp.logical_and(bottom, rest), m, 0.0).astype(BF)
    before = pltpu.roll(msel[448:576, :].astype(F32), 64, 1).T
    shifted = pltpu.roll(before, 64, 1)
    band[0:128, 512:640] = jnp.where(jnp.logical_and(top, left), shifted, 0.0).astype(BF)

    def images(it):
        yhi[...], ylo[...] = split(dot(band[:, 0:512], chi[it, 0:512]) + dot(band[:, 0:512], clo[it]))

    def edges(it):
        wait_halo(it)
        top = dot(band[0:64, 512:640], chi[it, 512:640])
        bottom = dot(band[448:512, 512:640], chi[it, 512:640])
        last_block = chi[it, 448:512, :]
        lhs[0:64, :] = chi[it, 0:64, :]
        rhs[0:64, :] = top.astype(BF)
        lhs[64:128, :] = last_block
        rhs[64:128, :] = bottom.astype(BF)
        lhs[128:192, :] = bottom.astype(BF)
        rhs[128:192, :] = (last_block.astype(F32) * (p < 7).astype(F32)).astype(BF)
        for a in range(4):
            cols = slice(a * TILE, a * TILE + TILE)
            g = dot(lhs[:, cols], rhs[:, a * TILE : ORBS], ((0,), (0,)))
            for e in range(a, 4):
                rows = slice(KEPT.index((a, e)) * TILE, KEPT.index((a, e)) * TILE + TILE)
                gp[it, rows, :] = gp[it, rows, :] + g[:, (e - a) * TILE : (e - a) * TILE + TILE]
        if it == 0:
            for rows, more in ((slice(0, 64), top), (slice(448, 512), bottom)):
                y = yhi[rows, :].astype(F32) + ylo[rows, :].astype(F32)
                yhi[rows, :], ylo[rows, :] = split(y + more)

    def cross_edges(it):
        ends[0:64, :] = nhi[0:64, :]
        ends[64:128, :] = nhi[448:512, :]

        hp[it] = hp[it] + dot(rhs[0:128, :], ends[...], ((0,), (0,)))

    def gram(it):
        for a in range(4):
            cols = slice(a * TILE, a * TILE + TILE)
            rest = slice(a * TILE, ORBS)
            g = dot3(chi[it, 0:512, cols], clo[it, :, cols], yhi[:, rest], ylo[:, rest], ((0,), (0,)))
            for e in range(a, 4):
                k = KEPT.index((a, e))
                gp[it, k * TILE : k * TILE + TILE, :] = g[:, (e - a) * TILE : (e - a) * TILE + TILE]

    def cross(it):
        hp[it] = dot3(yhi[...], ylo[...], nhi[...], nlo[...], ((0,), (0,)))

    def cross_rows(it, rows, begin):
        more = dot3(yhi[rows, :], ylo[rows, :], nhi[rows, :], nlo[rows, :], ((0,), (0,)))
        hp[it] = more if begin else hp[it] + more

    own_half = pl.ds(pl.multiple_of(core * HALF, HALF), HALF)
    other_half = pl.ds(pl.multiple_of((1 - core) * HALF, HALF), HALF)
    own_part = pl.ds(pl.multiple_of(core * PHALF, PHALF), PHALF)
    other_part = pl.ds(pl.multiple_of((1 - core) * PHALF, PHALF), PHALF)

    def pair_and_pack(it, part, from_pair, packed, scale, size, count):
        half, wide = size * count, part.shape[2]

        def add(i, top_value):
            rows = pl.ds(pl.multiple_of(core * half + i * size, size), size)
            x = part[it, rows, :] + from_pair[it, pl.ds(pl.multiple_of(i * size, size), size), :]
            part[it, rows, :] = x
            return jnp.maximum(top_value, jnp.abs(x))

        peak = jnp.max(lax.fori_loop(0, count, add, jnp.zeros((size, wide), F32), unroll=True), axis=(0, 1), keepdims=True)
        peak = jnp.maximum(peak, 1e-30)
        scale[it] = jnp.broadcast_to(peak * (1.0 / QMAX), (1, 128))
        inv = QMAX / peak

        def pack(i, carry):
            rows = pl.ds(pl.multiple_of(core * half + i * size, size), size)
            packed[it, i] = jnp.round(part[it, rows, :] * inv).astype(I16)
            return carry

        lax.fori_loop(0, count, pack, 0, unroll=True)

    def quantized(x):
        peak = jnp.maximum(jnp.max(jnp.abs(x), axis=(0, 1), keepdims=True), 1e-30)
        return jnp.round(x * (QMAX / peak)).astype(I16), jnp.broadcast_to(peak * (1.0 / QMAX), (1, 128))

    def scatter_gram(it):
        arrived(gsib.at[it], it, GSIB)
        pair_and_pack(it, gp, gsib, qs, qsc, GP, 8)
        for k in FAR:
            to = (z + k) % 8
            send(qs.at[it, to], rs.at[it, k], it, RS + k, zdev(to, o))
            send(qsc.at[it], rsc.at[it, k], it, RSC + k, zdev(to, o))

    def scatter_cross(it):
        arrived(hsib.at[it], it, HSIB)
        pair_and_pack(it, hp, hsib, hqs, hqsc, HP, 8)

    def from_high(k):
        return (z + 8 - k) % 4 >= 2

    def send_cross(it):
        for k in FAR:
            to = (z + k) % 8
            send(hqs.at[it, to], hrs.at[it, k], it, HRS + k, zdev(to, o), high)
            send(hqsc.at[it], hrsc.at[it, k], it, HRSC + k, zdev(to, o), high)

    def own_gram(it):
        rows = pl.ds(pl.multiple_of(core * PHALF + z * GP, GP), GP)
        total = gp[it, rows, :]
        for k in range(1, 8):
            arrived(rs.at[it, k], it, RS + k)
            arrived(rsc.at[it, k], it, RSC + k)
            total = total + rs[it, k].astype(jnp.int32).astype(F32) * rsc[it, k, 0:1, 0:1]
        here = lax.broadcasted_iota(jnp.int32, (GP, TILE), 0) + (core * PHALF + z * GP)
        tile = lax.shift_right_logical(here, 7)
        within = jnp.bitwise_and(here, 127) == lax.broadcasted_iota(jnp.int32, (GP, TILE), 1)
        on = jnp.zeros((GP, TILE), F32)
        for a in range(4):
            on = jnp.where(jnp.logical_and(tile == KEPT.index((a, a)), within), 1.0, on)
        value, scale = quantized(total * (1.0 / (SUPPORT * BLK)) - on)
        ea[it, rows, :] = value
        at = core * 8 + z
        es[it, at] = scale
        for k in FAR:
            device = zdev((z + k) % 8, o)
            send(ea.at[it, rows], ea.at[it, rows], it, EA + k, device)
            send(es.at[it, at], es.at[it, at], it, EAS + k, device)

    def own_cross(it):
        rows = pl.ds(pl.multiple_of(core * HALF + z * HP, HP), HP)
        at = core * 8 + z

        @pl.when(high)
        def _():
            sums[...] = hp[it, rows, :]

        @pl.when(low)
        def _():
            sums[...] = jnp.zeros((HP, ORBS), F32)

        for k in range(1, 8):

            @pl.when(from_high(k))
            def _():
                arrived(hrs.at[it, k], it, HRS + k)
                arrived(hrsc.at[it, k], it, HRSC + k)
                sums[...] = sums[...] + hrs[it, k].astype(jnp.int32).astype(F32) * hrsc[it, k, 0:1, 0:1]

        value, scale = quantized(sums[...] * (1.0 / (SUPPORT * BLK)))
        ho[it] = value
        hos[it] = scale

        @pl.when(high)
        def _():
            ha[it, rows, :] = value
            hs[it, at] = scale

        for k in FAR + (0,):
            to = (z + k) % 8
            to_low = to % 4 < 2
            cond = jnp.logical_and(to_low, above)
            if k > 0:
                cond = jnp.logical_or(cond, to % 4 >= 2)
            device = zdev(to, jnp.where(to_low, o + 1, o))
            send(ho.at[it], ha.at[it, rows], it, HA + k, device, cond)
            send(hos.at[it], hs.at[it, at], it, HAS + k, device, cond)

    own_eight = pl.ds(pl.multiple_of(core * 8, 8), 8)
    other_eight = pl.ds(pl.multiple_of((1 - core) * 8, 8), 8)
    def piece(at, size):
        return pl.ds(pl.multiple_of(at * size, size), size)

    def pass_gram(it, with_side):
        for k in FAR[::-1]:
            at = core * 8 + (z + 8 - k) % 8
            arrived(ea.at[it, piece(at, GP)], it, EA + k)
            arrived(es.at[it, at], it, EAS + k)
            send(ea.at[it, piece(at, GP)], ea.at[it, piece(at, GP)], it, FE + k, sibling)
        mine = piece(core * 8 + z, GP)
        send(ea.at[it, mine], ea.at[it, mine], it, FE, sibling)
        send(es.at[it, own_eight], es.at[it, own_eight], it, FES, sibling)
        if with_side:
            send(ea.at[it, own_part], na.at[own_part], it, NA, dev(b, away, r), has_away)
            send(es.at[it, own_eight], ns.at[own_eight], it, NAS, dev(b, away, r), has_away)

    def pass_side(it):
        @pl.when(has_side)
        def _():
            arrived(na.at[own_part], it, NA)
            arrived(ns.at[own_eight], it, NAS)

        send(na.at[own_part], na.at[own_part], it, FN, sibling, has_side)
        send(ns.at[own_eight], ns.at[own_eight], it, FNS, sibling, has_side)

    def pass_cross(it):
        data, tags = ha.at[it], hs.at[it]
        takes = jnp.logical_or(high, has_side)
        for k in (0,) + FAR[::-1]:
            at = core * 8 + (z + 8 - k) % 8

            def taken(at=at, k=k):
                arrived(data.at[piece(at, HP)], it, HA + k)
                arrived(tags.at[at], it, HAS + k)

            pl.when(below if k == 0 else takes)(taken)
            send(data.at[piece(at, HP)], data.at[piece(at, HP)], it, FH + k, sibling, takes)
        send(tags.at[own_eight], tags.at[own_eight], it, FHS, sibling, takes)

    def unpack(value, scale):
        return value.astype(jnp.int32).astype(F32) * scale[0:1, 0:1]

    def spread(packed, scales, to_hi, to_lo):
        def body(i, carry):
            rows = piece(i, GP)
            ef[rows, :] = unpack(packed[rows, :], scales[i])
            return carry

        lax.fori_loop(0, 16, body, 0, unroll=True)
        for k, (a, e) in enumerate(KEPT):
            x = ef[k * TILE : k * TILE + TILE, :]
            at, to = slice(a * TILE, a * TILE + TILE), slice(e * TILE, e * TILE + TILE)
            to_hi[at, to], to_lo[at, to] = split(x)
            if a != e:
                to_hi[to, at], to_lo[to, at] = split(x.T)

    def take_gram(it):
        for k in range(8):
            arrived(ea.at[it, piece((1 - core) * 8 + (z + 8 - k) % 8, GP)], it, FE + k)
        arrived(es.at[it, other_eight], it, FES)
        spread(ea.at[it], es.at[it], ehi, elo)

    def take_side(it):
        @pl.when(has_side)
        def _():
            arrived(na.at[other_part], it, FN)
            arrived(ns.at[other_eight], it, FNS)
            spread(na, ns, mhi, mlo)

    def cross_value(it, i):
        return jnp.concatenate([unpack(ha[it, piece(4 * i + e, HP), :], hs[it, 4 * i + e]) for e in range(4)], axis=0)

    def cross_plain(it, to_hi, to_lo):
        def body(i, carry):
            rows = piece(i, TILE)
            to_hi[rows, :], to_lo[rows, :] = split(cross_value(it, i))
            return carry

        lax.fori_loop(0, 4, body, 0, unroll=True)

    def cross_turned(it, to_hi, to_lo):
        def body(i, carry):
            cols = piece(i, TILE)
            to_hi[:, cols], to_lo[:, cols] = split(cross_value(it, i).T)
            return carry

        lax.fori_loop(0, 4, body, 0, unroll=True)

    def take_cross(it):
        @pl.when(jnp.logical_or(high, has_side))
        def _():
            for k in range(8):
                arrived(ha.at[it, piece((1 - core) * 8 + (z + 8 - k) % 8, HP)], it, FH + k)
            arrived(hs.at[it, other_eight], it, FHS)

        pl.when(jnp.logical_and(low, has_side))(lambda: cross_plain(it, xhi, xlo))
        pl.when(jnp.logical_and(high, has_side))(lambda: cross_turned(it, xhi, xlo))

        @pl.when(jnp.logical_not(has_side))
        def _():
            xhi[...] = jnp.zeros((ORBS, ORBS), BF)
            xlo[...] = jnp.zeros((ORBS, ORBS), BF)

    def own_change(it):
        c[...] = c[...] - 0.5 * dot3(chi[it, 0:512], clo[it], ehi[...], elo[...])

    def updated(it, t, rows):
        change = dot3(nhi[rows, :], nlo[rows, :], xhi[...], xlo[...])
        return jnp.where(live(rows, cs_own), c[rows, :] - 0.5 * change, 0.0)

    def take_rows():
        for t in (0, 3, 1, 2):
            rows = slice(t * TILE, t * TILE + TILE)

            @pl.when(has_side)
            def _():
                arrived(nq_in.at[rows], 0, NX + t)
                x = nq_in[rows, :].astype(jnp.int32).astype(F32) * (CMAX / QMAX)
                nf[rows, :] = x
                nhi[rows, :], nlo[rows, :] = split(x)

            @pl.when(jnp.logical_not(has_side))
            def _():
                nhi[rows, :] = jnp.zeros((TILE, ORBS), BF)
                nlo[rows, :] = jnp.zeros((TILE, ORBS), BF)

            pl.when(high)(functools.partial(cross_rows, 0, rows, t == 0))

    def pair_cross(it):
        send(hp.at[it, other_half], hsib.at[it], it, HSIB, sibling, high)

    def keep(rows, x):
        c[rows, :] = x
        hi, lo = split(x)
        chi[1, rows, :] = hi
        clo[1, rows, :] = lo

    def first(rows):
        keep(rows, updated(0, 0, rows))

    def first_ends():
        two = (pl.ds(0, BLK), pl.ds(448, BLK))
        change = dot3(
            jnp.concatenate([nhi[rows, :] for rows in two], axis=0), jnp.concatenate([nlo[rows, :] for rows in two], axis=0), xhi[...], xlo[...]
        )
        for i, rows in enumerate(two):
            keep(rows, jnp.where(live(rows, cs_own), c[rows, :] - 0.5 * change[i * BLK : i * BLK + BLK], 0.0))

    def beside(t, rows):
        change = dot3(nhi[rows, :], nlo[rows, :], mhi[...], mlo[...])
        change = change + dot3(chi[0, rows, :], clo[0, rows, :], thi[...], tlo[...])
        x = jnp.where(live(rows, cs_in), nf[rows, :] - 0.5 * change, 0.0)
        nhi[rows, :], nlo[rows, :] = split(x)

    def last(t, rows):
        out[rows, :] = updated(1, t, rows)

    images(0)
    gram(0)
    edges(0)
    send(gp.at[0, other_part], gsib.at[0], 0, GSIB, sibling)
    scatter_gram(0)
    take_rows()
    pair_cross(0)
    pl.when(high)(lambda: scatter_cross(0))
    send_cross(0)
    own_gram(0)
    pass_gram(0, True)
    take_gram(0)
    own_change(0)
    own_cross(0)
    pass_side(0)
    pass_cross(0)
    take_cross(0)
    first_ends()
    send_halo(1)
    first(pl.ds(64, 384))
    pl.when(has_side)(lambda: arrived(cs_in, 0, NXC))
    pl.when(jnp.logical_and(low, has_side))(lambda: cross_turned(0, thi, tlo))
    pl.when(jnp.logical_and(high, has_side))(lambda: cross_plain(0, thi, tlo))
    take_side(0)
    pl.when(has_side)(lambda: beside(0, pl.ds(0, ROWS)))

    images(1)
    gram(1)
    pl.when(high)(lambda: cross(1))
    edges(1)
    send(gp.at[1, other_part], gsib.at[1], 1, GSIB, sibling)
    pl.when(high)(lambda: cross_edges(1))
    pair_cross(1)
    scatter_gram(1)
    pl.when(high)(lambda: scatter_cross(1))
    send_cross(1)
    own_gram(1)
    own_cross(1)
    pass_gram(1, False)
    take_gram(1)
    own_change(1)
    pass_cross(1)
    take_cross(1)
    last(0, pl.ds(0, ROWS))

    for src, it, index, cond in sent:

        def wait(src=src, it=it, index=index):
            pltpu.make_async_copy(src, src, ss.at[it, index]).wait()

        if cond is None:
            wait()
        else:
            pl.when(cond)(wait)


def per_device(coefficients, basis_metric, pattern, starts):
    vm = pltpu.VMEM
    square = (ORBS, ORBS)
    scratch = [
        vm((ROWS, ORBS), F32), vm((2, 640, ORBS), BF), vm((2, ROWS, ORBS), BF),
        vm((ROWS, ORBS), F32), vm((ROWS, ORBS), BF), vm((ROWS, ORBS), BF),
        vm((ROWS, ORBS), BF), vm((ROWS, ORBS), BF), vm((ROWS, 640), BF),
        vm((2, PACKED, TILE), F32), vm((2, ORBS, ORBS), F32),
        vm((ROWS, ORBS), I16), vm((ROWS, ORBS), I16), vm((1, ORBS), F32), vm((1, ORBS), F32),
        vm((576, 128), BF), vm((576, 128), BF), vm((576, 128), BF),
        vm((2, PHALF, TILE), F32), vm((2, HALF, ORBS), F32),
        vm((2, 8, GP, TILE), I16), vm((2, 8, GP, TILE), I16), vm((2, 1, 128), F32), vm((2, 8, 1, 128), F32),
        vm((2, 8, HP, ORBS), I16), vm((2, 8, HP, ORBS), I16), vm((2, 1, 128), F32), vm((2, 8, 1, 128), F32),
        vm((2, PACKED, TILE), I16), vm((2, 16, 1, 128), F32), vm((PACKED, TILE), I16), vm((16, 1, 128), F32),
        vm((2, ORBS, ORBS), I16), vm((2, 16, 1, 128), F32),
        vm(square, BF), vm(square, BF), vm(square, BF), vm(square, BF), vm(square, BF), vm(square, BF),
        vm(square, BF), vm(square, BF), vm((PACKED, TILE), F32),
        vm((2, HP, ORBS), I16), vm((2, 1, 128), F32), vm((HP, ORBS), F32), vm((192, ORBS), BF), vm((192, ORBS), BF), vm((128, ORBS), BF),
        pltpu.SMEM((64,), jnp.int32), pltpu.SMEM((8,), jnp.int32),
        pltpu.SemaphoreType.DMA((2, COUNT)), pltpu.SemaphoreType.DMA((2, COUNT)), pltpu.SemaphoreType.DMA((8,)),
    ]
    result = pl.pallas_call(
        kernel,
        out_shape=jax.ShapeDtypeStruct((ROWS, ORBS), F32),
        in_specs=[
            pl.BlockSpec(memory_space=pltpu.HBM),
            pl.BlockSpec(memory_space=pltpu.HBM),
            pl.BlockSpec(memory_space=pltpu.HBM),
            pl.BlockSpec(memory_space=pltpu.HBM),
        ],
        out_specs=pl.BlockSpec(memory_space=pltpu.VMEM),
        scratch_shapes=scratch,
        compiler_params=pltpu.CompilerParams(
            collective_id=0, has_side_effects=True, vmem_limit_bytes=52 * 1024 * 1024
        ),
    )(coefficients[0], basis_metric, pattern, starts)
    return result[None]


def solution(mesh):
    in_specs = (P("orb", ("basis", "rep"), None), P("orb", None), P("orb"), P("orb"))
    out_specs = P("orb", ("basis", "rep"), None)
    return jax.shard_map(
        per_device, mesh=mesh, in_specs=in_specs, out_specs=out_specs, check_vma=False
    )
```

```python
import functools

import jax
import jax.numpy as jnp
from jax import lax
from jax.experimental import pallas as pl
from jax.experimental.pallas import tpu as pltpu
from jax.sharding import PartitionSpec as P

BLK = 64
GROUP_BLOCKS = 64
SUPPORT = 96
ITERS = 2
ROWS = 512
ORBS = 512
HALF = 256
GP = 80
PACKED = 1280
PHALF = 640
HP = 32
TILE = 128
CMAX = 6.0
QMAX = 32767.0
BF = jnp.bfloat16
F32 = jnp.float32
I16 = jnp.int16

HALO_NEXT, HALO_PREV, GSIB, HSIB, NA, NAS, FES, FN, FNS, FHS, NXC, MET = range(12)
NX = 12
RS, RSC, HRS, HRSC, EA, EAS, HA, HAS, FE, FH = range(16, 96, 8)
COUNT = 96

FAR = (4, 3, 5, 2, 6, 1, 7)

KEPT = [(a, b) for a in range(4) for b in range(a, 4)]


def split(x):
    hi = x.astype(BF)
    return hi, (x - hi.astype(F32)).astype(BF)


def dot(a, b, dims=((1,), (0,))):
    return lax.dot_general(a, b, (dims, ((), ())), preferred_element_type=F32)


def dot3(ah, al, bh, bl, dims=((1,), (0,))):
    return dot(ah, bh, dims) + (dot(ah, bl, dims) + dot(al, bh, dims))


def kernel(
    coef, metric, pattern_in, starts_in, out,
    c, chi, clo, nf, nhi, nlo, yhi, ylo, band, gp, hp,
    nq_out, nq_in, cs_own, cs_in, meff, mrecv, msel,
    gsib, hsib, qs, rs, qsc, rsc, hqs, hrs, hqsc, hrsc,
    ea, es, na, ns, ha, hs, ehi, elo, xhi, xlo, thi, tlo, mhi, mlo, ef, ho, hos, sums, lhs, rhs, ends, pattern, starts,
    ss, rr, local_sem,
):
    b, o, r = lax.axis_index("basis"), lax.axis_index("orb"), lax.axis_index("rep")
    groups = lax.axis_size("orb")
    core, zl = b % 2, b // 2
    z = r * 4 + zl
    p = b * 2 + r
    q = p % 8
    low = zl < 2
    high = jnp.logical_not(low)
    side = jnp.where(low, o - 1, o + 1)
    away = jnp.where(low, o + 1, o - 1)
    has_side = jnp.logical_and(side >= 0, side < groups)
    has_away = jnp.logical_and(away >= 0, away < groups)

    def dev(bb, oo, rep):
        return {"basis": bb, "orb": oo, "rep": rep}

    def zdev(zz, oo):
        return dev((zz % 4) * 2 + core, oo, zz // 4)

    sibling = dev(zl * 2 + 1 - core, o, r)

    barrier = pltpu.get_barrier_semaphore()

    def greet(device):
        pl.semaphore_signal(barrier, inc=1, device_id=device, device_id_type=pl.DeviceIdType.MESH)

    for k in range(1, 8):
        greet(zdev((z + k) % 8, o))
    greet(sibling)
    step_b = jnp.where(r == 1, b + 1, b - 1)
    has_step = jnp.logical_and(step_b >= 0, step_b < 8)

    @pl.when(has_step)
    def _():
        greet(dev(step_b, o, 1 - r))

    below = jnp.logical_and(low, o > 0)
    above = o < groups - 1

    @pl.when(below)
    def _():
        for k in range(8):
            greet(zdev((z + k) % 8, o - 1))

    @pl.when(above)
    def _():
        for m in range(4):
            greet(dev((m // 2) * 2 + core, o + 1, m % 2))

    straight = jnp.logical_and(high, above)

    @pl.when(straight)
    def _():
        greet(dev(b, o + 1, r))

    straight_down = jnp.logical_and(high, o > 0)

    @pl.when(straight_down)
    def _():
        greet(dev(b, o - 1, r))

    loads = [
        pltpu.make_async_copy(coef.at[pl.ds(t * TILE, TILE)], c.at[pl.ds(t * TILE, TILE)], local_sem.at[2 + t]) for t in range(4)
    ]
    small = [
        pltpu.make_async_copy(starts_in, starts, local_sem.at[6]),
        pltpu.make_async_copy(pattern_in, pattern, local_sem.at[7]),
    ]
    for load in small:
        load.start()
    for t in (0, 3, 1, 2):
        loads[t].start()
    load_main = pltpu.make_async_copy(metric.at[pl.ds(pl.multiple_of(q * 512, 64), 512)], meff.at[pl.ds(0, 512)], local_sem.at[0])
    load_prev = pltpu.make_async_copy(
        metric.at[pl.ds(pl.multiple_of((q * 512 + 4032) % 4096, 64), 64)], meff.at[pl.ds(512, 64)], local_sem.at[1]
    )
    load_main.start()
    load_prev.start()
    small[0].wait()
    small[1].wait()
    lane = lax.broadcasted_iota(jnp.int32, (1, ORBS), 1) // BLK
    cs = jnp.zeros((1, ORBS), F32)
    for i in range(8):
        cs = jnp.where(lane == i, starts[i].astype(F32), cs)
    cs_own[...] = cs
    first_block = (o * GROUP_BLOCKS + p * 8).astype(F32)

    def live(rows, cs_ref):
        start, count = rows.start, rows.size
        at = lax.broadcasted_iota(jnp.int32, (count, ORBS), 0) + start
        block = first_block + (at // BLK).astype(F32)
        begin = cs_ref[0:1, :]
        return jnp.logical_and(block >= begin, block < begin + SUPPORT)

    def tiles(body):
        def step(t, carry):
            body(t, pl.ds(pl.multiple_of(t * TILE, TILE), TILE))
            return carry

        lax.fori_loop(0, ROWS // TILE, step, 0)

    def prepare(t, rows):
        x = jnp.where(live(rows, cs_own), c[rows, :], 0.0)
        c[rows, :] = x
        hi, lo = split(x)
        chi[0, rows, :] = hi
        clo[0, rows, :] = lo
        nq_out[rows, :] = jnp.round(jnp.clip(x, -CMAX, CMAX) * (QMAX / CMAX)).astype(I16)

    def prepare_tile(t):
        loads[t].wait()
        prepare(jnp.int32(t), pl.ds(t * TILE, TILE))

    prepare_tile(0)
    prepare_tile(3)
    for it in range(ITERS):

        @pl.when(low)
        def _():
            chi[it, 512:576, :] = jnp.zeros((64, ORBS), BF)

        @pl.when(p == 15)
        def _():
            chi[it, 576:640, :] = jnp.zeros((64, ORBS), BF)

    def ones(flag):
        return flag.astype(jnp.int32)

    pl.semaphore_wait(barrier, 8 + ones(has_step) + 8 * ones(below) + 4 * ones(above) + ones(straight) + ones(straight_down))

    sent = []

    def send(src, dst, it, index, device, cond=None, land=None):
        land = index if land is None else land

        def start():
            pltpu.make_async_remote_copy(
                src_ref=src, dst_ref=dst, send_sem=ss.at[it, index], recv_sem=rr.at[it, land],
                device_id=device, device_id_type=pl.DeviceIdType.MESH,
            ).start()

        if cond is None:
            start()
        else:
            pl.when(cond)(start)
        sent.append((src, it, index, cond))

    def drain():
        for src, it, index, cond in sent:

            def wait(src=src, it=it, index=index):
                pltpu.make_async_copy(src, src, ss.at[it, index]).wait()

            if cond is None:
                wait()
            else:
                pl.when(cond)(wait)
        sent.clear()

    def arrived(dst, it, index):
        pltpu.make_async_copy(dst, dst, rr.at[it, index]).wait()

    def send_halo(it):
        up_b = jnp.where(r == 0, b, b + 1)
        down_b = jnp.where(r == 1, b, b - 1)
        send(chi.at[it, pl.ds(0, 64)], chi.at[it, pl.ds(576, 64)], it, HALO_NEXT, dev(down_b, o, 1 - r), p > 0)
        send(chi.at[it, pl.ds(448, 64)], chi.at[it, pl.ds(512, 64)], it, HALO_PREV, dev(up_b, o, 1 - r), jnp.logical_and(p > 6, p < 15))

    def wait_halo(it):
        pl.when(p < 15)(lambda: arrived(chi.at[it, pl.ds(576, 64)], it, HALO_NEXT))
        pl.when(high)(lambda: arrived(chi.at[it, pl.ds(512, 64)], it, HALO_PREV))

    send_halo(0)
    partner = dev(jnp.where(low, b + 4, b - 4), side, r)
    for t in (0, 3, 1, 2):
        if t in (1, 2):
            prepare_tile(t)
        rows = pl.ds(t * TILE, TILE)
        send(nq_out.at[rows], nq_in.at[rows], 0, NX + t, partner, has_side)
    send(cs_own, cs_in, 0, NXC, partner, has_side)

    load_main.wait()
    load_prev.wait()
    right = lax.broadcasted_iota(jnp.int32, (BLK, 2 * BLK), 1) >= BLK
    for i in range(9):
        at = (q * 8 + i) % 64 if i < 8 else (q * 8 + 63) % 64
        keep = jnp.where(o * GROUP_BLOCKS + at < groups * GROUP_BLOCKS - 1, pattern[at], 0).astype(F32)
        block = meff[i * 64 : i * 64 + 64, :].astype(F32)
        meff[i * 64 : i * 64 + 64, :] = jnp.where(right, block * keep, block).astype(BF)

    gives_metric = jnp.logical_and(high, o > 0)
    send(meff, mrecv, 0, MET, dev(b, o - 1, r), gives_metric)

    @pl.when(low)
    def _():
        msel[...] = meff[...]

    @pl.when(jnp.logical_and(high, has_side))
    def _():
        arrived(mrecv, 0, MET)
        msel[...] = mrecv[...]

    @pl.when(jnp.logical_and(high, jnp.logical_not(has_side)))
    def _():
        msel[...] = jnp.zeros((576, 128), BF)

    @pl.when(p == 8)
    def _():
        msel[512:576, :] = meff[512:576, :]

    band[...] = jnp.zeros((ROWS, 640), BF)
    row_at = lax.broadcasted_iota(jnp.int32, (128, 128), 0)
    lane_at = lax.broadcasted_iota(jnp.int32, (128, 128), 1)
    top, left = row_at < 64, lane_at < 64
    bottom, rest = row_at >= 64, lane_at >= 64
    for t in range(4):
        m = msel[t * 128 : t * 128 + 128, :].astype(F32)
        rolled = pltpu.roll(m, 64, 1)
        corner = jnp.where(jnp.logical_and(top, rest), m, 0.0)
        diag = jnp.where(top, m, jnp.where(rest, rolled, 0.0)) + corner.T
        band[t * 128 : t * 128 + 128, t * 128 : t * 128 + 128] = diag.astype(BF)
        if t < 3:
            off = jnp.where(jnp.logical_and(bottom, left), rolled, 0.0)
            band[t * 128 : t * 128 + 128, t * 128 + 128 : t * 128 + 256] = off.astype(BF)
            band[t * 128 + 128 : t * 128 + 256, t * 128 : t * 128 + 128] = off.T.astype(BF)
        else:
            band[384:512, 512:640] = jnp.where(jnp.logical_and(bottom, rest), m, 0.0).astype(BF)
    before = pltpu.roll(msel[448:576, :].astype(F32), 64, 1).T
    shifted = pltpu.roll(before, 64, 1)
    band[0:128, 512:640] = jnp.where(jnp.logical_and(top, left), shifted, 0.0).astype(BF)

    def images(it):
        yhi[...], ylo[...] = split(dot(band[:, 0:512], chi[it, 0:512]) + dot(band[:, 0:512], clo[it]))

    def edges(it):
        wait_halo(it)
        top = dot(band[0:64, 512:640], chi[it, 512:640])
        bottom = dot(band[448:512, 512:640], chi[it, 512:640])
        last_block = chi[it, 448:512, :]
        lhs[0:64, :] = chi[it, 0:64, :]
        rhs[0:64, :] = top.astype(BF)
        lhs[64:128, :] = last_block
        rhs[64:128, :] = bottom.astype(BF)
        lhs[128:192, :] = bottom.astype(BF)
        rhs[128:192, :] = (last_block.astype(F32) * (p < 7).astype(F32)).astype(BF)
        for a in range(4):
            cols = slice(a * TILE, a * TILE + TILE)
            g = dot(lhs[:, cols], rhs[:, a * TILE : ORBS], ((0,), (0,)))
            for e in range(a, 4):
                rows = slice(KEPT.index((a, e)) * TILE, KEPT.index((a, e)) * TILE + TILE)
                gp[it, rows, :] = gp[it, rows, :] + g[:, (e - a) * TILE : (e - a) * TILE + TILE]
        if it == 0:
            for rows, more in ((slice(0, 64), top), (slice(448, 512), bottom)):
                y = yhi[rows, :].astype(F32) + ylo[rows, :].astype(F32)
                yhi[rows, :], ylo[rows, :] = split(y + more)

    def cross_edges(it):
        ends[0:64, :] = nhi[0:64, :]
        ends[64:128, :] = nhi[448:512, :]

        hp[it] = hp[it] + dot(rhs[0:128, :], ends[...], ((0,), (0,)))

    def gram(it):
        for a in range(4):
            cols = slice(a * TILE, a * TILE + TILE)
            rest = slice(a * TILE, ORBS)
            g = dot3(chi[it, 0:512, cols], clo[it, :, cols], yhi[:, rest], ylo[:, rest], ((0,), (0,)))
            for e in range(a, 4):
                k = KEPT.index((a, e))
                gp[it, k * TILE : k * TILE + TILE, :] = g[:, (e - a) * TILE : (e - a) * TILE + TILE]

    def cross(it):
        hp[it] = dot3(yhi[...], ylo[...], nhi[...], nlo[...], ((0,), (0,)))

    def cross_rows(it, rows, begin):
        more = dot3(yhi[rows, :], ylo[rows, :], nhi[rows, :], nlo[rows, :], ((0,), (0,)))
        hp[it] = more if begin else hp[it] + more

    own_half = pl.ds(pl.multiple_of(core * HALF, HALF), HALF)
    other_half = pl.ds(pl.multiple_of((1 - core) * HALF, HALF), HALF)
    own_part = pl.ds(pl.multiple_of(core * PHALF, PHALF), PHALF)
    other_part = pl.ds(pl.multiple_of((1 - core) * PHALF, PHALF), PHALF)

    def pair_and_pack(it, part, from_pair, packed, scale, size, count):
        half, wide = size * count, part.shape[2]

        def add(i, top_value):
            rows = pl.ds(pl.multiple_of(core * half + i * size, size), size)
            x = part[it, rows, :] + from_pair[it, pl.ds(pl.multiple_of(i * size, size), size), :]
            part[it, rows, :] = x
            return jnp.maximum(top_value, jnp.abs(x))

        peak = jnp.max(lax.fori_loop(0, count, add, jnp.zeros((size, wide), F32), unroll=True), axis=(0, 1), keepdims=True)
        peak = jnp.maximum(peak, 1e-30)
        scale[it] = jnp.broadcast_to(peak * (1.0 / QMAX), (1, 128))
        inv = QMAX / peak

        def pack(i, carry):
            rows = pl.ds(pl.multiple_of(core * half + i * size, size), size)
            packed[it, i] = jnp.round(part[it, rows, :] * inv).astype(I16)
            return carry

        lax.fori_loop(0, count, pack, 0, unroll=True)

    def quantized(x):
        peak = jnp.maximum(jnp.max(jnp.abs(x), axis=(0, 1), keepdims=True), 1e-30)
        return jnp.round(x * (QMAX / peak)).astype(I16), jnp.broadcast_to(peak * (1.0 / QMAX), (1, 128))

    def scatter_gram(it):
        arrived(gsib.at[it], it, GSIB)
        pair_and_pack(it, gp, gsib, qs, qsc, GP, 8)
        for k in FAR:
            to = (z + k) % 8
            send(qs.at[it, to], rs.at[it, k], it, RS + k, zdev(to, o))
            send(qsc.at[it], rsc.at[it, k], it, RSC + k, zdev(to, o))

    def scatter_cross(it):
        arrived(hsib.at[it], it, HSIB)
        pair_and_pack(it, hp, hsib, hqs, hqsc, HP, 8)

    def from_high(k):
        return (z + 8 - k) % 4 >= 2

    def send_cross(it):
        for k in FAR:
            to = (z + k) % 8
            send(hqs.at[it, to], hrs.at[it, k], it, HRS + k, zdev(to, o), high)
            send(hqsc.at[it], hrsc.at[it, k], it, HRSC + k, zdev(to, o), high)

    def own_gram(it):
        rows = pl.ds(pl.multiple_of(core * PHALF + z * GP, GP), GP)
        total = gp[it, rows, :]
        for k in range(1, 8):
            arrived(rs.at[it, k], it, RS + k)
            arrived(rsc.at[it, k], it, RSC + k)
            total = total + rs[it, k].astype(jnp.int32).astype(F32) * rsc[it, k, 0:1, 0:1]
        here = lax.broadcasted_iota(jnp.int32, (GP, TILE), 0) + (core * PHALF + z * GP)
        tile = lax.shift_right_logical(here, 7)
        within = jnp.bitwise_and(here, 127) == lax.broadcasted_iota(jnp.int32, (GP, TILE), 1)
        on = jnp.zeros((GP, TILE), F32)
        for a in range(4):
            on = jnp.where(jnp.logical_and(tile == KEPT.index((a, a)), within), 1.0, on)
        value, scale = quantized(total * (1.0 / (SUPPORT * BLK)) - on)
        ea[it, rows, :] = value
        at = core * 8 + z
        es[it, at] = scale
        for k in FAR:
            device = zdev((z + k) % 8, o)
            send(ea.at[it, rows], ea.at[it, rows], it, EA + k, device)
            send(es.at[it, at], es.at[it, at], it, EAS + k, device)

    def own_cross(it):
        rows = pl.ds(pl.multiple_of(core * HALF + z * HP, HP), HP)
        at = core * 8 + z

        @pl.when(high)
        def _():
            sums[...] = hp[it, rows, :]

        @pl.when(low)
        def _():
            sums[...] = jnp.zeros((HP, ORBS), F32)

        for k in range(1, 8):

            @pl.when(from_high(k))
            def _():
                arrived(hrs.at[it, k], it, HRS + k)
                arrived(hrsc.at[it, k], it, HRSC + k)
                sums[...] = sums[...] + hrs[it, k].astype(jnp.int32).astype(F32) * hrsc[it, k, 0:1, 0:1]

        value, scale = quantized(sums[...] * (1.0 / (SUPPORT * BLK)))
        ho[it] = value
        hos[it] = scale

        @pl.when(high)
        def _():
            ha[it, rows, :] = value
            hs[it, at] = scale

        for k in FAR + (0,):
            to = (z + k) % 8
            to_low = to % 4 < 2
            cond = jnp.logical_and(to_low, above)
            if k > 0:
                cond = jnp.logical_or(cond, to % 4 >= 2)
            device = zdev(to, jnp.where(to_low, o + 1, o))
            send(ho.at[it], ha.at[it, rows], it, HA + k, device, cond)
            send(hos.at[it], hs.at[it, at], it, HAS + k, device, cond)

    own_eight = pl.ds(pl.multiple_of(core * 8, 8), 8)
    other_eight = pl.ds(pl.multiple_of((1 - core) * 8, 8), 8)
    def piece(at, size):
        return pl.ds(pl.multiple_of(at * size, size), size)

    def pass_gram(it, with_side):
        for k in FAR[::-1]:
            at = core * 8 + (z + 8 - k) % 8
            arrived(ea.at[it, piece(at, GP)], it, EA + k)
            arrived(es.at[it, at], it, EAS + k)
            send(ea.at[it, piece(at, GP)], ea.at[it, piece(at, GP)], it, FE + k, sibling)
        mine = piece(core * 8 + z, GP)
        send(ea.at[it, mine], ea.at[it, mine], it, FE, sibling)
        send(es.at[it, own_eight], es.at[it, own_eight], it, FES, sibling)
        if with_side:
            send(ea.at[it, own_part], na.at[own_part], it, NA, dev(b, away, r), has_away)
            send(es.at[it, own_eight], ns.at[own_eight], it, NAS, dev(b, away, r), has_away)

    def pass_side(it):
        @pl.when(has_side)
        def _():
            arrived(na.at[own_part], it, NA)
            arrived(ns.at[own_eight], it, NAS)

        send(na.at[own_part], na.at[own_part], it, FN, sibling, has_side)
        send(ns.at[own_eight], ns.at[own_eight], it, FNS, sibling, has_side)

    def pass_cross(it):
        data, tags = ha.at[it], hs.at[it]
        takes = jnp.logical_or(high, has_side)
        for k in (0,) + FAR[::-1]:
            at = core * 8 + (z + 8 - k) % 8

            def taken(at=at, k=k):
                arrived(data.at[piece(at, HP)], it, HA + k)
                arrived(tags.at[at], it, HAS + k)

            pl.when(below if k == 0 else takes)(taken)
            send(data.at[piece(at, HP)], data.at[piece(at, HP)], it, FH + k, sibling, takes)
        send(tags.at[own_eight], tags.at[own_eight], it, FHS, sibling, takes)

    def unpack(value, scale):
        return value.astype(jnp.int32).astype(F32) * scale[0:1, 0:1]

    def spread(packed, scales, to_hi, to_lo):
        def body(i, carry):
            rows = piece(i, GP)
            ef[rows, :] = unpack(packed[rows, :], scales[i])
            return carry

        lax.fori_loop(0, 16, body, 0, unroll=True)
        for k, (a, e) in enumerate(KEPT):
            x = ef[k * TILE : k * TILE + TILE, :]
            at, to = slice(a * TILE, a * TILE + TILE), slice(e * TILE, e * TILE + TILE)
            to_hi[at, to], to_lo[at, to] = split(x)
            if a != e:
                to_hi[to, at], to_lo[to, at] = split(x.T)

    def take_gram(it):
        for k in range(8):
            arrived(ea.at[it, piece((1 - core) * 8 + (z + 8 - k) % 8, GP)], it, FE + k)
        arrived(es.at[it, other_eight], it, FES)
        spread(ea.at[it], es.at[it], ehi, elo)

    def take_side(it):
        @pl.when(has_side)
        def _():
            arrived(na.at[other_part], it, FN)
            arrived(ns.at[other_eight], it, FNS)
            spread(na, ns, mhi, mlo)

    def cross_value(it, i):
        return jnp.concatenate([unpack(ha[it, piece(4 * i + e, HP), :], hs[it, 4 * i + e]) for e in range(4)], axis=0)

    def cross_plain(it, to_hi, to_lo, halves=(0, 1)):
        for half in halves:
            for e in range(2):
                rows = piece(2 * half + e, TILE)
                to_hi[rows, :], to_lo[rows, :] = split(cross_value(it, 2 * half + e))

    def cross_turned(it, to_hi, to_lo, halves=(0, 1)):
        for half in halves:
            for e in range(2):
                cols = piece(2 * half + e, TILE)
                to_hi[:, cols], to_lo[:, cols] = split(cross_value(it, 2 * half + e).T)

    low_side = jnp.logical_and(low, has_side)
    high_side = jnp.logical_and(high, has_side)

    def unpack_half(it, half):
        pl.when(low_side)(lambda: cross_plain(it, xhi, xlo, (half,)))
        pl.when(high_side)(lambda: cross_turned(it, xhi, xlo, (half,)))

    def take_own_cross(it):
        if it == 0:

            @pl.when(jnp.logical_not(has_side))
            def _():
                xhi[...] = jnp.zeros((ORBS, ORBS), BF)
                xlo[...] = jnp.zeros((ORBS, ORBS), BF)

        unpack_half(it, core)

    def take_pair_cross(it):
        @pl.when(jnp.logical_or(high, has_side))
        def _():
            for k in range(8):
                arrived(ha.at[it, piece((1 - core) * 8 + (z + 8 - k) % 8, HP)], it, FH + k)
            arrived(hs.at[it, other_eight], it, FHS)

        unpack_half(it, 1 - core)

    def own_change(it):
        c[...] = c[...] - 0.5 * dot3(chi[it, 0:512], clo[it], ehi[...], elo[...])

    def updated(it, t, rows):
        change = dot3(nhi[rows, :], nlo[rows, :], xhi[...], xlo[...])
        return jnp.where(live(rows, cs_own), c[rows, :] - 0.5 * change, 0.0)

    def take_rows():
        for t in (0, 3, 1, 2):
            rows = slice(t * TILE, t * TILE + TILE)

            @pl.when(has_side)
            def _():
                arrived(nq_in.at[rows], 0, NX + t)
                x = nq_in[rows, :].astype(jnp.int32).astype(F32) * (CMAX / QMAX)
                nf[rows, :] = x
                nhi[rows, :], nlo[rows, :] = split(x)

            @pl.when(jnp.logical_not(has_side))
            def _():
                nhi[rows, :] = jnp.zeros((TILE, ORBS), BF)
                nlo[rows, :] = jnp.zeros((TILE, ORBS), BF)

            pl.when(high)(functools.partial(cross_rows, 0, rows, t == 0))

    def pair_cross(it):
        send(hp.at[it, other_half], hsib.at[it], it, HSIB, sibling, high)

    def keep(rows, x):
        c[rows, :] = x
        hi, lo = split(x)
        chi[1, rows, :] = hi
        clo[1, rows, :] = lo

    def first(rows):
        keep(rows, updated(0, 0, rows))

    def first_ends():
        two = (pl.ds(0, BLK), pl.ds(448, BLK))
        change = dot3(
            jnp.concatenate([nhi[rows, :] for rows in two], axis=0), jnp.concatenate([nlo[rows, :] for rows in two], axis=0), xhi[...], xlo[...]
        )
        for i, rows in enumerate(two):
            keep(rows, jnp.where(live(rows, cs_own), c[rows, :] - 0.5 * change[i * BLK : i * BLK + BLK], 0.0))

    def beside(t, rows):
        change = dot3(nhi[rows, :], nlo[rows, :], mhi[...], mlo[...])
        change = change + dot3(chi[0, rows, :], clo[0, rows, :], thi[...], tlo[...])
        x = jnp.where(live(rows, cs_in), nf[rows, :] - 0.5 * change, 0.0)
        nhi[rows, :], nlo[rows, :] = split(x)

    def ended(cols, change):
        at = lax.broadcasted_iota(jnp.int32, (ROWS, HALF), 0)
        block = first_block + (at // BLK).astype(F32)
        begin = cs_own[0:1, cols]
        lives = jnp.logical_and(block >= begin, block < begin + SUPPORT)
        out[:, cols] = jnp.where(lives, c[:, cols] - 0.5 * change, 0.0)

    def last_half(half, final):
        @pl.when(low)
        def _():
            part = dot3(nhi[:, half], nlo[:, half], xhi[half, :], xlo[half, :])
            if final:
                out[...] = jnp.where(live(pl.ds(0, ROWS), cs_own), nf[...] - 0.5 * part, 0.0)
            else:
                nf[...] = c[...] - 0.5 * part

        @pl.when(high)
        def _():
            ended(half, dot3(nhi[...], nlo[...], xhi[:, half], xlo[:, half]))

    images(0)
    gram(0)
    edges(0)
    send(gp.at[0, other_part], gsib.at[0], 0, GSIB, sibling)
    scatter_gram(0)
    take_rows()
    pair_cross(0)
    pl.when(high)(lambda: scatter_cross(0))
    send_cross(0)
    own_gram(0)
    pass_gram(0, True)
    take_gram(0)
    own_change(0)
    own_cross(0)
    pass_side(0)
    pass_cross(0)
    take_own_cross(0)
    take_pair_cross(0)
    first_ends()
    send_halo(1)
    first(pl.ds(64, 384))
    pl.when(has_side)(lambda: arrived(cs_in, 0, NXC))
    pl.when(jnp.logical_and(low, has_side))(lambda: cross_turned(0, thi, tlo))
    pl.when(jnp.logical_and(high, has_side))(lambda: cross_plain(0, thi, tlo))
    take_side(0)
    pl.when(has_side)(lambda: beside(0, pl.ds(0, ROWS)))

    images(1)
    gram(1)
    pl.when(high)(lambda: cross(1))
    drain()
    edges(1)
    send(gp.at[1, other_part], gsib.at[1], 1, GSIB, sibling)
    pl.when(high)(lambda: cross_edges(1))
    pair_cross(1)
    scatter_gram(1)
    pl.when(high)(lambda: scatter_cross(1))
    send_cross(1)
    own_gram(1)
    own_cross(1)
    pass_gram(1, False)
    take_gram(1)
    own_change(1)
    pass_cross(1)
    take_own_cross(1)
    last_half(own_half, False)
    drain()
    take_pair_cross(1)
    last_half(other_half, True)


def per_device(coefficients, basis_metric, pattern, starts):
    vm = pltpu.VMEM
    square = (ORBS, ORBS)
    scratch = [
        vm((ROWS, ORBS), F32), vm((2, 640, ORBS), BF), vm((2, ROWS, ORBS), BF),
        vm((ROWS, ORBS), F32), vm((ROWS, ORBS), BF), vm((ROWS, ORBS), BF),
        vm((ROWS, ORBS), BF), vm((ROWS, ORBS), BF), vm((ROWS, 640), BF),
        vm((2, PACKED, TILE), F32), vm((2, ORBS, ORBS), F32),
        vm((ROWS, ORBS), I16), vm((ROWS, ORBS), I16), vm((1, ORBS), F32), vm((1, ORBS), F32),
        vm((576, 128), BF), vm((576, 128), BF), vm((576, 128), BF),
        vm((2, PHALF, TILE), F32), vm((2, HALF, ORBS), F32),
        vm((2, 8, GP, TILE), I16), vm((2, 8, GP, TILE), I16), vm((2, 1, 128), F32), vm((2, 8, 1, 128), F32),
        vm((2, 8, HP, ORBS), I16), vm((2, 8, HP, ORBS), I16), vm((2, 1, 128), F32), vm((2, 8, 1, 128), F32),
        vm((2, PACKED, TILE), I16), vm((2, 16, 1, 128), F32), vm((PACKED, TILE), I16), vm((16, 1, 128), F32),
        vm((2, ORBS, ORBS), I16), vm((2, 16, 1, 128), F32),
        vm(square, BF), vm(square, BF), vm(square, BF), vm(square, BF), vm(square, BF), vm(square, BF),
        vm(square, BF), vm(square, BF), vm((PACKED, TILE), F32),
        vm((2, HP, ORBS), I16), vm((2, 1, 128), F32), vm((HP, ORBS), F32), vm((192, ORBS), BF), vm((192, ORBS), BF), vm((128, ORBS), BF),
        pltpu.SMEM((64,), jnp.int32), pltpu.SMEM((8,), jnp.int32),
        pltpu.SemaphoreType.DMA((2, COUNT)), pltpu.SemaphoreType.DMA((2, COUNT)), pltpu.SemaphoreType.DMA((8,)),
    ]
    result = pl.pallas_call(
        kernel,
        out_shape=jax.ShapeDtypeStruct((ROWS, ORBS), F32),
        in_specs=[
            pl.BlockSpec(memory_space=pltpu.HBM),
            pl.BlockSpec(memory_space=pltpu.HBM),
            pl.BlockSpec(memory_space=pltpu.HBM),
            pl.BlockSpec(memory_space=pltpu.HBM),
        ],
        out_specs=pl.BlockSpec(memory_space=pltpu.VMEM),
        scratch_shapes=scratch,
        compiler_params=pltpu.CompilerParams(
            collective_id=0, has_side_effects=True, vmem_limit_bytes=52 * 1024 * 1024
        ),
    )(coefficients[0], basis_metric, pattern, starts)
    return result[None]


def solution(mesh):
    in_specs = (P("orb", ("basis", "rep"), None), P("orb", None), P("orb"), P("orb"))
    out_specs = P("orb", ("basis", "rep"), None)
    return jax.shard_map(
        per_device, mesh=mesh, in_specs=in_specs, out_specs=out_specs, check_vma=False
    )
```

```python
import functools

import jax
import jax.numpy as jnp
from jax import lax
from jax.experimental import pallas as pl
from jax.experimental.pallas import tpu as pltpu
from jax.sharding import PartitionSpec as P

BLK = 64
GROUP_BLOCKS = 64
SUPPORT = 96
ITERS = 2
ROWS = 512
ORBS = 512
HALF = 256
GP = 80
PACKED = 1280
PHALF = 640
HP = 32
TILE = 128
CMAX = 6.0
QMAX = 32767.0
BF = jnp.bfloat16
F32 = jnp.float32
I16 = jnp.int16

HALO_NEXT, HALO_PREV, GSIB, HSIB, NA, NAS, FES, FN, FNS, FHS, NXC, MET = range(12)
NX = 12
RS, RSC, HRS, HRSC, EA, EAS, HA, HAS, FE, FH = range(16, 96, 8)
COUNT = 96

FAR = (4, 3, 5, 2, 6, 1, 7)

KEPT = [(a, b) for a in range(4) for b in range(a, 4)]


def split(x):
    hi = x.astype(BF)
    return hi, (x - hi.astype(F32)).astype(BF)


def dot(a, b, dims=((1,), (0,))):
    return lax.dot_general(a, b, (dims, ((), ())), preferred_element_type=F32)


def dot3(ah, al, bh, bl, dims=((1,), (0,))):
    return dot(ah, bh, dims) + (dot(ah, bl, dims) + dot(al, bh, dims))


def kernel(
    coef, metric, pattern_in, starts_in, out,
    c, chi, clo, nf, nhi, nlo, yhi, ylo, band, gp, hp,
    nq_out, nq_in, cs_own, cs_in, meff, mrecv, msel,
    gsib, hsib, qs, rs, qsc, rsc, hqs, hrs, hqsc, hrsc,
    ea, es, na, ns, ha, hs, ehi, elo, xhi, xlo, thi, tlo, mhi, mlo, ef, ho, hos, sums, lhs, rhs, ends, pattern, starts,
    ss, rr, local_sem,
):
    b, o, r = lax.axis_index("basis"), lax.axis_index("orb"), lax.axis_index("rep")
    groups = lax.axis_size("orb")
    core, zl = b % 2, b // 2
    z = r * 4 + zl
    p = b * 2 + r
    q = p % 8
    low = zl < 2
    high = jnp.logical_not(low)
    side = jnp.where(low, o - 1, o + 1)
    away = jnp.where(low, o + 1, o - 1)
    has_side = jnp.logical_and(side >= 0, side < groups)
    has_away = jnp.logical_and(away >= 0, away < groups)

    def dev(bb, oo, rep):
        return {"basis": bb, "orb": oo, "rep": rep}

    def zdev(zz, oo):
        return dev((zz % 4) * 2 + core, oo, zz // 4)

    sibling = dev(zl * 2 + 1 - core, o, r)

    barrier = pltpu.get_barrier_semaphore()

    def greet(device):
        pl.semaphore_signal(barrier, inc=1, device_id=device, device_id_type=pl.DeviceIdType.MESH)

    for k in range(1, 8):
        greet(zdev((z + k) % 8, o))
    greet(sibling)
    step_b = jnp.where(r == 1, b + 1, b - 1)
    has_step = jnp.logical_and(step_b >= 0, step_b < 8)

    @pl.when(has_step)
    def _():
        greet(dev(step_b, o, 1 - r))

    below = jnp.logical_and(low, o > 0)
    above = o < groups - 1

    @pl.when(below)
    def _():
        for k in range(8):
            greet(zdev((z + k) % 8, o - 1))

    @pl.when(above)
    def _():
        for m in range(4):
            greet(dev((m // 2) * 2 + core, o + 1, m % 2))

    straight = jnp.logical_and(high, above)

    @pl.when(straight)
    def _():
        greet(dev(b, o + 1, r))

    straight_down = jnp.logical_and(high, o > 0)

    @pl.when(straight_down)
    def _():
        greet(dev(b, o - 1, r))

    loads = [
        pltpu.make_async_copy(coef.at[pl.ds(t * TILE, TILE)], c.at[pl.ds(t * TILE, TILE)], local_sem.at[2 + t]) for t in range(4)
    ]
    small = [
        pltpu.make_async_copy(starts_in, starts, local_sem.at[6]),
        pltpu.make_async_copy(pattern_in, pattern, local_sem.at[7]),
    ]
    for load in small:
        load.start()
    for t in (0, 3, 1, 2):
        loads[t].start()
    load_main = pltpu.make_async_copy(metric.at[pl.ds(pl.multiple_of(q * 512, 64), 512)], meff.at[pl.ds(0, 512)], local_sem.at[0])
    load_prev = pltpu.make_async_copy(
        metric.at[pl.ds(pl.multiple_of((q * 512 + 4032) % 4096, 64), 64)], meff.at[pl.ds(512, 64)], local_sem.at[1]
    )
    load_main.start()
    load_prev.start()
    small[0].wait()
    small[1].wait()
    lane = lax.broadcasted_iota(jnp.int32, (1, ORBS), 1) // BLK
    cs = jnp.zeros((1, ORBS), F32)
    for i in range(8):
        cs = jnp.where(lane == i, starts[i].astype(F32), cs)
    cs_own[...] = cs
    first_block = (o * GROUP_BLOCKS + p * 8).astype(F32)

    def live(rows, cs_ref):
        start, count = rows.start, rows.size
        at = lax.broadcasted_iota(jnp.int32, (count, ORBS), 0) + start
        block = first_block + (at // BLK).astype(F32)
        begin = cs_ref[0:1, :]
        return jnp.logical_and(block >= begin, block < begin + SUPPORT)

    def tiles(body):
        def step(t, carry):
            body(t, pl.ds(pl.multiple_of(t * TILE, TILE), TILE))
            return carry

        lax.fori_loop(0, ROWS // TILE, step, 0)

    def prepare(t, rows):
        x = jnp.where(live(rows, cs_own), c[rows, :], 0.0)
        c[rows, :] = x
        hi, lo = split(x)
        chi[0, rows, :] = hi
        clo[0, rows, :] = lo
        nq_out[rows, :] = jnp.round(jnp.clip(x, -CMAX, CMAX) * (QMAX / CMAX)).astype(I16)

    def prepare_tile(t):
        loads[t].wait()
        prepare(jnp.int32(t), pl.ds(t * TILE, TILE))

    prepare_tile(0)
    prepare_tile(3)
    for it in range(ITERS):

        @pl.when(low)
        def _():
            chi[it, 512:576, :] = jnp.zeros((64, ORBS), BF)

        @pl.when(p == 15)
        def _():
            chi[it, 576:640, :] = jnp.zeros((64, ORBS), BF)

    def ones(flag):
        return flag.astype(jnp.int32)

    pl.semaphore_wait(barrier, 8 + ones(has_step) + 8 * ones(below) + 4 * ones(above) + ones(straight) + ones(straight_down))

    sent = []

    def send(src, dst, it, index, device, cond=None, land=None):
        land = index if land is None else land

        def start():
            pltpu.make_async_remote_copy(
                src_ref=src, dst_ref=dst, send_sem=ss.at[it, index], recv_sem=rr.at[it, land],
                device_id=device, device_id_type=pl.DeviceIdType.MESH,
            ).start()

        if cond is None:
            start()
        else:
            pl.when(cond)(start)
        sent.append((src, it, index, cond))

    def drain():
        for src, it, index, cond in sent:

            def wait(src=src, it=it, index=index):
                pltpu.make_async_copy(src, src, ss.at[it, index]).wait()

            if cond is None:
                wait()
            else:
                pl.when(cond)(wait)
        sent.clear()

    def arrived(dst, it, index):
        pltpu.make_async_copy(dst, dst, rr.at[it, index]).wait()

    def send_halo(it):
        up_b = jnp.where(r == 0, b, b + 1)
        down_b = jnp.where(r == 1, b, b - 1)
        send(chi.at[it, pl.ds(0, 64)], chi.at[it, pl.ds(576, 64)], it, HALO_NEXT, dev(down_b, o, 1 - r), p > 0)
        send(chi.at[it, pl.ds(448, 64)], chi.at[it, pl.ds(512, 64)], it, HALO_PREV, dev(up_b, o, 1 - r), jnp.logical_and(p > 6, p < 15))

    def wait_halo(it):
        pl.when(p < 15)(lambda: arrived(chi.at[it, pl.ds(576, 64)], it, HALO_NEXT))
        pl.when(high)(lambda: arrived(chi.at[it, pl.ds(512, 64)], it, HALO_PREV))

    send_halo(0)
    partner = dev(jnp.where(low, b + 4, b - 4), side, r)
    for t in (0, 3, 1, 2):
        if t in (1, 2):
            prepare_tile(t)
        rows = pl.ds(t * TILE, TILE)
        send(nq_out.at[rows], nq_in.at[rows], 0, NX + t, partner, has_side)
    send(cs_own, cs_in, 0, NXC, partner, has_side)

    load_main.wait()
    load_prev.wait()
    right = lax.broadcasted_iota(jnp.int32, (BLK, 2 * BLK), 1) >= BLK
    for i in range(9):
        at = (q * 8 + i) % 64 if i < 8 else (q * 8 + 63) % 64
        keep = jnp.where(o * GROUP_BLOCKS + at < groups * GROUP_BLOCKS - 1, pattern[at], 0).astype(F32)
        block = meff[i * 64 : i * 64 + 64, :].astype(F32)
        meff[i * 64 : i * 64 + 64, :] = jnp.where(right, block * keep, block).astype(BF)

    gives_metric = jnp.logical_and(high, o > 0)
    send(meff, mrecv, 0, MET, dev(b, o - 1, r), gives_metric)

    @pl.when(low)
    def _():
        msel[...] = meff[...]

    @pl.when(jnp.logical_and(high, has_side))
    def _():
        arrived(mrecv, 0, MET)
        msel[...] = mrecv[...]

    @pl.when(jnp.logical_and(high, jnp.logical_not(has_side)))
    def _():
        msel[...] = jnp.zeros((576, 128), BF)

    @pl.when(p == 8)
    def _():
        msel[512:576, :] = meff[512:576, :]

    band[...] = jnp.zeros((ROWS, 640), BF)
    row_at = lax.broadcasted_iota(jnp.int32, (128, 128), 0)
    lane_at = lax.broadcasted_iota(jnp.int32, (128, 128), 1)
    top, left = row_at < 64, lane_at < 64
    bottom, rest = row_at >= 64, lane_at >= 64
    for t in range(4):
        m = msel[t * 128 : t * 128 + 128, :].astype(F32)
        rolled = pltpu.roll(m, 64, 1)
        corner = jnp.where(jnp.logical_and(top, rest), m, 0.0)
        diag = jnp.where(top, m, jnp.where(rest, rolled, 0.0)) + corner.T
        band[t * 128 : t * 128 + 128, t * 128 : t * 128 + 128] = diag.astype(BF)
        if t < 3:
            off = jnp.where(jnp.logical_and(bottom, left), rolled, 0.0)
            band[t * 128 : t * 128 + 128, t * 128 + 128 : t * 128 + 256] = off.astype(BF)
            band[t * 128 + 128 : t * 128 + 256, t * 128 : t * 128 + 128] = off.T.astype(BF)
        else:
            band[384:512, 512:640] = jnp.where(jnp.logical_and(bottom, rest), m, 0.0).astype(BF)
    before = pltpu.roll(msel[448:576, :].astype(F32), 64, 1).T
    shifted = pltpu.roll(before, 64, 1)
    band[0:128, 512:640] = jnp.where(jnp.logical_and(top, left), shifted, 0.0).astype(BF)

    def images(it):
        yhi[...], ylo[...] = split(dot(band[:, 0:512], chi[it, 0:512]) + dot(band[:, 0:512], clo[it]))

    def edges(it):
        wait_halo(it)
        top = dot(band[0:64, 512:640], chi[it, 512:640])
        bottom = dot(band[448:512, 512:640], chi[it, 512:640])
        last_block = chi[it, 448:512, :]
        lhs[0:64, :] = chi[it, 0:64, :]
        rhs[0:64, :] = top.astype(BF)
        lhs[64:128, :] = last_block
        rhs[64:128, :] = bottom.astype(BF)
        lhs[128:192, :] = bottom.astype(BF)
        rhs[128:192, :] = (last_block.astype(F32) * (p < 7).astype(F32)).astype(BF)
        for a in range(4):
            cols = slice(a * TILE, a * TILE + TILE)
            g = dot(lhs[:, cols], rhs[:, a * TILE : ORBS], ((0,), (0,)))
            for e in range(a, 4):
                rows = slice(KEPT.index((a, e)) * TILE, KEPT.index((a, e)) * TILE + TILE)
                gp[it, rows, :] = gp[it, rows, :] + g[:, (e - a) * TILE : (e - a) * TILE + TILE]
        if it == 0:
            for rows, more in ((slice(0, 64), top), (slice(448, 512), bottom)):
                y = yhi[rows, :].astype(F32) + ylo[rows, :].astype(F32)
                yhi[rows, :], ylo[rows, :] = split(y + more)

    def cross_edges(it):
        ends[0:64, :] = nhi[0:64, :]
        ends[64:128, :] = nhi[448:512, :]

        hp[it] = hp[it] + dot(rhs[0:128, :], ends[...], ((0,), (0,)))

    def gram(it):
        for a in range(4):
            cols = slice(a * TILE, a * TILE + TILE)
            rest = slice(a * TILE, ORBS)
            g = dot3(chi[it, 0:512, cols], clo[it, :, cols], yhi[:, rest], ylo[:, rest], ((0,), (0,)))
            for e in range(a, 4):
                k = KEPT.index((a, e))
                gp[it, k * TILE : k * TILE + TILE, :] = g[:, (e - a) * TILE : (e - a) * TILE + TILE]

    def cross(it):
        hp[it] = dot3(yhi[...], ylo[...], nhi[...], nlo[...], ((0,), (0,)))

    own_half = pl.ds(pl.multiple_of(core * HALF, HALF), HALF)
    other_half = pl.ds(pl.multiple_of((1 - core) * HALF, HALF), HALF)
    own_part = pl.ds(pl.multiple_of(core * PHALF, PHALF), PHALF)
    other_part = pl.ds(pl.multiple_of((1 - core) * PHALF, PHALF), PHALF)

    def pair_and_pack(it, part, from_pair, packed, scale, size, count):
        half, wide = size * count, part.shape[2]

        def add(i, top_value):
            rows = pl.ds(pl.multiple_of(core * half + i * size, size), size)
            x = part[it, rows, :] + from_pair[it, pl.ds(pl.multiple_of(i * size, size), size), :]
            part[it, rows, :] = x
            return jnp.maximum(top_value, jnp.abs(x))

        peak = jnp.max(lax.fori_loop(0, count, add, jnp.zeros((size, wide), F32), unroll=True), axis=(0, 1), keepdims=True)
        peak = jnp.maximum(peak, 1e-30)
        scale[it] = jnp.broadcast_to(peak * (1.0 / QMAX), (1, 128))
        inv = QMAX / peak

        def pack(i, carry):
            rows = pl.ds(pl.multiple_of(core * half + i * size, size), size)
            packed[it, i] = jnp.round(part[it, rows, :] * inv).astype(I16)
            return carry

        lax.fori_loop(0, count, pack, 0, unroll=True)

    def quantized(x):
        peak = jnp.maximum(jnp.max(jnp.abs(x), axis=(0, 1), keepdims=True), 1e-30)
        return jnp.round(x * (QMAX / peak)).astype(I16), jnp.broadcast_to(peak * (1.0 / QMAX), (1, 128))

    def scatter_gram(it):
        arrived(gsib.at[it], it, GSIB)
        pair_and_pack(it, gp, gsib, qs, qsc, GP, 8)

    def send_gram(it):
        for k in FAR:
            to = (z + k) % 8
            send(qs.at[it, to], rs.at[it, k], it, RS + k, zdev(to, o))
            send(qsc.at[it], rsc.at[it, k], it, RSC + k, zdev(to, o))

    def scatter_cross(it):
        arrived(hsib.at[it], it, HSIB)
        pair_and_pack(it, hp, hsib, hqs, hqsc, HP, 8)

    def from_high(k):
        return (z + 8 - k) % 4 >= 2

    def send_cross(it):
        for k in FAR:
            to = (z + k) % 8
            send(hqs.at[it, to], hrs.at[it, k], it, HRS + k, zdev(to, o), high)
            send(hqsc.at[it], hrsc.at[it, k], it, HRSC + k, zdev(to, o), high)

    def own_gram(it):
        rows = pl.ds(pl.multiple_of(core * PHALF + z * GP, GP), GP)
        total = gp[it, rows, :]
        for k in range(1, 8):
            arrived(rs.at[it, k], it, RS + k)
            arrived(rsc.at[it, k], it, RSC + k)
            total = total + rs[it, k].astype(jnp.int32).astype(F32) * rsc[it, k, 0:1, 0:1]
        here = lax.broadcasted_iota(jnp.int32, (GP, TILE), 0) + (core * PHALF + z * GP)
        tile = lax.shift_right_logical(here, 7)
        within = jnp.bitwise_and(here, 127) == lax.broadcasted_iota(jnp.int32, (GP, TILE), 1)
        on = jnp.zeros((GP, TILE), F32)
        for a in range(4):
            on = jnp.where(jnp.logical_and(tile == KEPT.index((a, a)), within), 1.0, on)
        value, scale = quantized(total * (1.0 / (SUPPORT * BLK)) - on)
        ea[it, rows, :] = value
        at = core * 8 + z
        es[it, at] = scale
        for k in FAR:
            device = zdev((z + k) % 8, o)
            send(ea.at[it, rows], ea.at[it, rows], it, EA + k, device)
            send(es.at[it, at], es.at[it, at], it, EAS + k, device)

    def own_cross(it):
        rows = pl.ds(pl.multiple_of(core * HALF + z * HP, HP), HP)
        at = core * 8 + z

        @pl.when(high)
        def _():
            sums[...] = hp[it, rows, :]

        @pl.when(low)
        def _():
            sums[...] = jnp.zeros((HP, ORBS), F32)

        for k in range(1, 8):

            @pl.when(from_high(k))
            def _():
                arrived(hrs.at[it, k], it, HRS + k)
                arrived(hrsc.at[it, k], it, HRSC + k)
                sums[...] = sums[...] + hrs[it, k].astype(jnp.int32).astype(F32) * hrsc[it, k, 0:1, 0:1]

        value, scale = quantized(sums[...] * (1.0 / (SUPPORT * BLK)))
        ho[it] = value
        hos[it] = scale

        @pl.when(high)
        def _():
            ha[it, rows, :] = value
            hs[it, at] = scale

        for k in FAR + (0,):
            to = (z + k) % 8
            to_low = to % 4 < 2
            cond = jnp.logical_and(to_low, above)
            if k > 0:
                cond = jnp.logical_or(cond, to % 4 >= 2)
            device = zdev(to, jnp.where(to_low, o + 1, o))
            send(ho.at[it], ha.at[it, rows], it, HA + k, device, cond)
            send(hos.at[it], hs.at[it, at], it, HAS + k, device, cond)

    own_eight = pl.ds(pl.multiple_of(core * 8, 8), 8)
    other_eight = pl.ds(pl.multiple_of((1 - core) * 8, 8), 8)
    def piece(at, size):
        return pl.ds(pl.multiple_of(at * size, size), size)

    def pass_gram(it, with_side):
        for k in FAR[::-1]:
            at = core * 8 + (z + 8 - k) % 8
            arrived(ea.at[it, piece(at, GP)], it, EA + k)
            arrived(es.at[it, at], it, EAS + k)
            send(ea.at[it, piece(at, GP)], ea.at[it, piece(at, GP)], it, FE + k, sibling)
        mine = piece(core * 8 + z, GP)
        send(ea.at[it, mine], ea.at[it, mine], it, FE, sibling)
        send(es.at[it, own_eight], es.at[it, own_eight], it, FES, sibling)
        if with_side:
            send(ea.at[it, own_part], na.at[own_part], it, NA, dev(b, away, r), has_away)
            send(es.at[it, own_eight], ns.at[own_eight], it, NAS, dev(b, away, r), has_away)

    def pass_side(it):
        @pl.when(has_side)
        def _():
            arrived(na.at[own_part], it, NA)
            arrived(ns.at[own_eight], it, NAS)

        send(na.at[own_part], na.at[own_part], it, FN, sibling, has_side)
        send(ns.at[own_eight], ns.at[own_eight], it, FNS, sibling, has_side)

    def pass_cross(it):
        data, tags = ha.at[it], hs.at[it]
        takes = jnp.logical_or(high, has_side)
        for k in (0,) + FAR[::-1]:
            at = core * 8 + (z + 8 - k) % 8

            def taken(at=at, k=k):
                arrived(data.at[piece(at, HP)], it, HA + k)
                arrived(tags.at[at], it, HAS + k)

            pl.when(below if k == 0 else takes)(taken)
            send(data.at[piece(at, HP)], data.at[piece(at, HP)], it, FH + k, sibling, takes)
        send(tags.at[own_eight], tags.at[own_eight], it, FHS, sibling, takes)

    def unpack(value, scale):
        return value.astype(jnp.int32).astype(F32) * scale[0:1, 0:1]

    def spread(packed, scales, to_hi, to_lo):
        def body(i, carry):
            rows = piece(i, GP)
            ef[rows, :] = unpack(packed[rows, :], scales[i])
            return carry

        lax.fori_loop(0, 16, body, 0, unroll=True)
        for k, (a, e) in enumerate(KEPT):
            x = ef[k * TILE : k * TILE + TILE, :]
            at, to = slice(a * TILE, a * TILE + TILE), slice(e * TILE, e * TILE + TILE)
            to_hi[at, to], to_lo[at, to] = split(x)
            if a != e:
                to_hi[to, at], to_lo[to, at] = split(x.T)

    def take_gram(it):
        for k in range(8):
            arrived(ea.at[it, piece((1 - core) * 8 + (z + 8 - k) % 8, GP)], it, FE + k)
        arrived(es.at[it, other_eight], it, FES)
        spread(ea.at[it], es.at[it], ehi, elo)

    def take_side(it):
        @pl.when(has_side)
        def _():
            arrived(na.at[other_part], it, FN)
            arrived(ns.at[other_eight], it, FNS)
            spread(na, ns, mhi, mlo)

    def cross_value(it, i):
        return jnp.concatenate([unpack(ha[it, piece(4 * i + e, HP), :], hs[it, 4 * i + e]) for e in range(4)], axis=0)

    def cross_plain(it, to_hi, to_lo, halves=(0, 1)):
        for half in halves:
            for e in range(2):
                rows = piece(2 * half + e, TILE)
                to_hi[rows, :], to_lo[rows, :] = split(cross_value(it, 2 * half + e))

    def cross_turned(it, to_hi, to_lo, halves=(0, 1)):
        for half in halves:
            for e in range(2):
                cols = piece(2 * half + e, TILE)
                to_hi[:, cols], to_lo[:, cols] = split(cross_value(it, 2 * half + e).T)

    low_side = jnp.logical_and(low, has_side)
    high_side = jnp.logical_and(high, has_side)

    def unpack_half(it, half):
        pl.when(low_side)(lambda: cross_plain(it, xhi, xlo, (half,)))
        pl.when(high_side)(lambda: cross_turned(it, xhi, xlo, (half,)))

    def take_own_cross(it):
        if it == 0:

            @pl.when(jnp.logical_not(has_side))
            def _():
                xhi[...] = jnp.zeros((ORBS, ORBS), BF)
                xlo[...] = jnp.zeros((ORBS, ORBS), BF)

        unpack_half(it, core)

    def take_pair_cross(it):
        @pl.when(jnp.logical_or(high, has_side))
        def _():
            for k in range(8):
                arrived(ha.at[it, piece((1 - core) * 8 + (z + 8 - k) % 8, HP)], it, FH + k)
            arrived(hs.at[it, other_eight], it, FHS)

        unpack_half(it, 1 - core)

    def own_change(it):
        c[...] = c[...] - 0.5 * dot3(chi[it, 0:512], clo[it], ehi[...], elo[...])

    def updated(it, t, rows):
        change = dot3(nhi[rows, :], nlo[rows, :], xhi[...], xlo[...])
        return jnp.where(live(rows, cs_own), c[rows, :] - 0.5 * change, 0.0)

    def rows_arrived():
        @pl.when(has_side)
        def _():
            for t in range(4):
                arrived(nq_in.at[pl.ds(t * TILE, TILE)], 0, NX + t)

    def take_rows():
        @pl.when(has_side)
        def _():
            for t in range(4):
                rows = pl.ds(t * TILE, TILE)
                x = nq_in[rows, :].astype(jnp.int32).astype(F32) * (CMAX / QMAX)
                nf[rows, :] = x
                nhi[rows, :], nlo[rows, :] = split(x)

        @pl.when(jnp.logical_not(has_side))
        def _():
            nhi[...] = jnp.zeros((ROWS, ORBS), BF)
            nlo[...] = jnp.zeros((ROWS, ORBS), BF)

    def pair_cross(it):
        send(hp.at[it, other_half], hsib.at[it], it, HSIB, sibling, high)

    def keep(rows, x):
        c[rows, :] = x
        hi, lo = split(x)
        chi[1, rows, :] = hi
        clo[1, rows, :] = lo

    def first(rows):
        keep(rows, updated(0, 0, rows))

    def first_ends():
        two = (pl.ds(0, BLK), pl.ds(448, BLK))
        change = dot3(
            jnp.concatenate([nhi[rows, :] for rows in two], axis=0), jnp.concatenate([nlo[rows, :] for rows in two], axis=0), xhi[...], xlo[...]
        )
        for i, rows in enumerate(two):
            keep(rows, jnp.where(live(rows, cs_own), c[rows, :] - 0.5 * change[i * BLK : i * BLK + BLK], 0.0))

    def beside(t, rows):
        change = dot3(nhi[rows, :], nlo[rows, :], mhi[...], mlo[...])
        change = change + dot3(chi[0, rows, :], clo[0, rows, :], thi[...], tlo[...])
        x = jnp.where(live(rows, cs_in), nf[rows, :] - 0.5 * change, 0.0)
        nhi[rows, :], nlo[rows, :] = split(x)

    def ended(cols, change):
        at = lax.broadcasted_iota(jnp.int32, (ROWS, HALF), 0)
        block = first_block + (at // BLK).astype(F32)
        begin = cs_own[0:1, cols]
        lives = jnp.logical_and(block >= begin, block < begin + SUPPORT)
        out[:, cols] = jnp.where(lives, c[:, cols] - 0.5 * change, 0.0)

    def last_half(half, final):
        @pl.when(low)
        def _():
            part = dot3(nhi[:, half], nlo[:, half], xhi[half, :], xlo[half, :])
            if final:
                out[...] = jnp.where(live(pl.ds(0, ROWS), cs_own), nf[...] - 0.5 * part, 0.0)
            else:
                nf[...] = c[...] - 0.5 * part

        @pl.when(high)
        def _():
            ended(half, dot3(nhi[...], nlo[...], xhi[:, half], xlo[:, half]))

    images(0)
    gram(0)
    edges(0)
    send(gp.at[0, other_part], gsib.at[0], 0, GSIB, sibling)
    scatter_gram(0)
    rows_arrived()
    send_gram(0)
    take_rows()
    pl.when(high)(lambda: cross(0))
    pair_cross(0)
    pl.when(high)(lambda: scatter_cross(0))
    send_cross(0)
    own_gram(0)
    pass_gram(0, True)
    take_gram(0)
    own_change(0)
    own_cross(0)
    pass_side(0)
    pass_cross(0)
    take_own_cross(0)
    take_pair_cross(0)
    first_ends()
    send_halo(1)
    first(pl.ds(64, 384))
    pl.when(has_side)(lambda: arrived(cs_in, 0, NXC))
    pl.when(jnp.logical_and(low, has_side))(lambda: cross_turned(0, thi, tlo))
    pl.when(jnp.logical_and(high, has_side))(lambda: cross_plain(0, thi, tlo))
    take_side(0)
    pl.when(has_side)(lambda: beside(0, pl.ds(0, ROWS)))

    images(1)
    gram(1)
    pl.when(high)(lambda: cross(1))
    drain()
    edges(1)
    send(gp.at[1, other_part], gsib.at[1], 1, GSIB, sibling)
    pl.when(high)(lambda: cross_edges(1))
    pair_cross(1)
    scatter_gram(1)
    send_gram(1)
    pl.when(high)(lambda: scatter_cross(1))
    send_cross(1)
    own_gram(1)
    own_cross(1)
    pass_gram(1, False)
    take_gram(1)
    own_change(1)
    pass_cross(1)
    take_own_cross(1)
    last_half(own_half, False)
    drain()
    take_pair_cross(1)
    last_half(other_half, True)


def per_device(coefficients, basis_metric, pattern, starts):
    vm = pltpu.VMEM
    square = (ORBS, ORBS)
    scratch = [
        vm((ROWS, ORBS), F32), vm((2, 640, ORBS), BF), vm((2, ROWS, ORBS), BF),
        vm((ROWS, ORBS), F32), vm((ROWS, ORBS), BF), vm((ROWS, ORBS), BF),
        vm((ROWS, ORBS), BF), vm((ROWS, ORBS), BF), vm((ROWS, 640), BF),
        vm((2, PACKED, TILE), F32), vm((2, ORBS, ORBS), F32),
        vm((ROWS, ORBS), I16), vm((ROWS, ORBS), I16), vm((1, ORBS), F32), vm((1, ORBS), F32),
        vm((576, 128), BF), vm((576, 128), BF), vm((576, 128), BF),
        vm((2, PHALF, TILE), F32), vm((2, HALF, ORBS), F32),
        vm((2, 8, GP, TILE), I16), vm((2, 8, GP, TILE), I16), vm((2, 1, 128), F32), vm((2, 8, 1, 128), F32),
        vm((2, 8, HP, ORBS), I16), vm((2, 8, HP, ORBS), I16), vm((2, 1, 128), F32), vm((2, 8, 1, 128), F32),
        vm((2, PACKED, TILE), I16), vm((2, 16, 1, 128), F32), vm((PACKED, TILE), I16), vm((16, 1, 128), F32),
        vm((2, ORBS, ORBS), I16), vm((2, 16, 1, 128), F32),
        vm(square, BF), vm(square, BF), vm(square, BF), vm(square, BF), vm(square, BF), vm(square, BF),
        vm(square, BF), vm(square, BF), vm((PACKED, TILE), F32),
        vm((2, HP, ORBS), I16), vm((2, 1, 128), F32), vm((HP, ORBS), F32), vm((192, ORBS), BF), vm((192, ORBS), BF), vm((128, ORBS), BF),
        pltpu.SMEM((64,), jnp.int32), pltpu.SMEM((8,), jnp.int32),
        pltpu.SemaphoreType.DMA((2, COUNT)), pltpu.SemaphoreType.DMA((2, COUNT)), pltpu.SemaphoreType.DMA((8,)),
    ]
    result = pl.pallas_call(
        kernel,
        out_shape=jax.ShapeDtypeStruct((ROWS, ORBS), F32),
        in_specs=[
            pl.BlockSpec(memory_space=pltpu.HBM),
            pl.BlockSpec(memory_space=pltpu.HBM),
            pl.BlockSpec(memory_space=pltpu.HBM),
            pl.BlockSpec(memory_space=pltpu.HBM),
        ],
        out_specs=pl.BlockSpec(memory_space=pltpu.VMEM),
        scratch_shapes=scratch,
        compiler_params=pltpu.CompilerParams(
            collective_id=0, has_side_effects=True, vmem_limit_bytes=52 * 1024 * 1024
        ),
    )(coefficients[0], basis_metric, pattern, starts)
    return result[None]


def solution(mesh):
    in_specs = (P("orb", ("basis", "rep"), None), P("orb", None), P("orb"), P("orb"))
    out_specs = P("orb", ("basis", "rep"), None)
    return jax.shard_map(
        per_device, mesh=mesh, in_specs=in_specs, out_specs=out_specs, check_vma=False
    )
```

```python
import functools

import jax
import jax.numpy as jnp
from jax import lax
from jax.experimental import pallas as pl
from jax.experimental.pallas import tpu as pltpu
from jax.sharding import PartitionSpec as P

BLK = 64
GROUP_BLOCKS = 64
SUPPORT = 96
ITERS = 2
ROWS = 512
ORBS = 512
HALF = 256
GP = 80
PACKED = 1280
PHALF = 640
HP = 32
TILE = 128
CMAX = 6.0
QMAX = 32767.0
BF = jnp.bfloat16
F32 = jnp.float32
I16 = jnp.int16

HALO_NEXT, HALO_PREV, GSIB, HSIB, NA, NAS, FES, FN, FNS, FHS, NXC, MET = range(12)
NX = 12
RS, RSC, HRS, HRSC, EA, EAS, HA, HAS, FE, FH = range(16, 96, 8)
COUNT = 96

FAR = (4, 3, 5, 2, 6, 1, 7)

KEPT = [(a, b) for a in range(4) for b in range(a, 4)]


def split(x):
    hi = x.astype(BF)
    return hi, (x - hi.astype(F32)).astype(BF)


def dot(a, b, dims=((1,), (0,))):
    return lax.dot_general(a, b, (dims, ((), ())), preferred_element_type=F32)


def dot3(ah, al, bh, bl, dims=((1,), (0,))):
    return dot(ah, bh, dims) + (dot(ah, bl, dims) + dot(al, bh, dims))


def kernel(
    coef, metric, pattern_in, starts_in, out,
    c, chi, clo, nf, nhi, nlo, yhi, ylo, band, gp, hp,
    nq_out, nq_in, cs_own, cs_in, meff, mrecv, msel,
    gsib, hsib, qs, rs, qsc, rsc, hqs, hrs, hqsc, hrsc,
    ea, es, na, ns, ha, hs, ehi, elo, xhi, xlo, thi, tlo, mhi, mlo, ef, ho, hos, sums, lhs, rhs, ends, pattern, starts,
    ss, rr, local_sem,
):
    b, o, r = lax.axis_index("basis"), lax.axis_index("orb"), lax.axis_index("rep")
    groups = lax.axis_size("orb")
    core, zl = b % 2, b // 2
    z = r * 4 + zl
    p = b * 2 + r
    q = p % 8
    low = zl < 2
    high = jnp.logical_not(low)
    side = jnp.where(low, o - 1, o + 1)
    away = jnp.where(low, o + 1, o - 1)
    has_side = jnp.logical_and(side >= 0, side < groups)
    has_away = jnp.logical_and(away >= 0, away < groups)

    def dev(bb, oo, rep):
        return {"basis": bb, "orb": oo, "rep": rep}

    def zdev(zz, oo):
        return dev((zz % 4) * 2 + core, oo, zz // 4)

    sibling = dev(zl * 2 + 1 - core, o, r)

    barrier = pltpu.get_barrier_semaphore()

    def greet(device):
        pl.semaphore_signal(barrier, inc=1, device_id=device, device_id_type=pl.DeviceIdType.MESH)

    for k in range(1, 8):
        greet(zdev((z + k) % 8, o))
    greet(sibling)
    step_b = jnp.where(r == 1, b + 1, b - 1)
    has_step = jnp.logical_and(step_b >= 0, step_b < 8)

    @pl.when(has_step)
    def _():
        greet(dev(step_b, o, 1 - r))

    below = jnp.logical_and(low, o > 0)
    above = o < groups - 1

    @pl.when(below)
    def _():
        for k in range(8):
            greet(zdev((z + k) % 8, o - 1))

    @pl.when(above)
    def _():
        for m in range(4):
            greet(dev((m // 2) * 2 + core, o + 1, m % 2))

    straight = jnp.logical_and(high, above)

    @pl.when(straight)
    def _():
        greet(dev(b, o + 1, r))

    straight_down = jnp.logical_and(high, o > 0)

    @pl.when(straight_down)
    def _():
        greet(dev(b, o - 1, r))

    loads = [
        pltpu.make_async_copy(coef.at[pl.ds(t * TILE, TILE)], c.at[pl.ds(t * TILE, TILE)], local_sem.at[2 + t]) for t in range(4)
    ]
    small = [
        pltpu.make_async_copy(starts_in, starts, local_sem.at[6]),
        pltpu.make_async_copy(pattern_in, pattern, local_sem.at[7]),
    ]
    for load in small:
        load.start()
    for t in (0, 3, 1, 2):
        loads[t].start()
    load_main = pltpu.make_async_copy(metric.at[pl.ds(pl.multiple_of(q * 512, 64), 512)], meff.at[pl.ds(0, 512)], local_sem.at[0])
    load_prev = pltpu.make_async_copy(
        metric.at[pl.ds(pl.multiple_of((q * 512 + 4032) % 4096, 64), 64)], meff.at[pl.ds(512, 64)], local_sem.at[1]
    )
    load_main.start()
    load_prev.start()
    small[0].wait()
    small[1].wait()
    lane = lax.broadcasted_iota(jnp.int32, (1, ORBS), 1) // BLK
    cs = jnp.zeros((1, ORBS), F32)
    for i in range(8):
        cs = jnp.where(lane == i, starts[i].astype(F32), cs)
    cs_own[...] = cs
    first_block = (o * GROUP_BLOCKS + p * 8).astype(F32)

    def live(rows, cs_ref):
        start, count = rows.start, rows.size
        at = lax.broadcasted_iota(jnp.int32, (count, ORBS), 0) + start
        block = first_block + (at // BLK).astype(F32)
        begin = cs_ref[0:1, :]
        return jnp.logical_and(block >= begin, block < begin + SUPPORT)

    def tiles(body):
        def step(t, carry):
            body(t, pl.ds(pl.multiple_of(t * TILE, TILE), TILE))
            return carry

        lax.fori_loop(0, ROWS // TILE, step, 0)

    def prepare(t, rows):
        x = jnp.where(live(rows, cs_own), c[rows, :], 0.0)
        c[rows, :] = x
        hi, lo = split(x)
        chi[0, rows, :] = hi
        clo[0, rows, :] = lo
        nq_out[rows, :] = jnp.round(jnp.clip(x, -CMAX, CMAX) * (QMAX / CMAX)).astype(I16)

    def prepare_tile(t):
        loads[t].wait()
        prepare(jnp.int32(t), pl.ds(t * TILE, TILE))

    prepare_tile(0)
    prepare_tile(3)
    for it in range(ITERS):

        @pl.when(low)
        def _():
            chi[it, 512:576, :] = jnp.zeros((64, ORBS), BF)

        @pl.when(p == 15)
        def _():
            chi[it, 576:640, :] = jnp.zeros((64, ORBS), BF)

    def ones(flag):
        return flag.astype(jnp.int32)

    pl.semaphore_wait(barrier, 8 + ones(has_step) + 8 * ones(below) + 4 * ones(above) + ones(straight) + ones(straight_down))

    sent = []

    def send(src, dst, it, index, device, cond=None, land=None):
        land = index if land is None else land

        def start():
            pltpu.make_async_remote_copy(
                src_ref=src, dst_ref=dst, send_sem=ss.at[it, index], recv_sem=rr.at[it, land],
                device_id=device, device_id_type=pl.DeviceIdType.MESH,
            ).start()

        if cond is None:
            start()
        else:
            pl.when(cond)(start)
        sent.append((src, it, index, cond))

    def drain():
        for src, it, index, cond in sent:

            def wait(src=src, it=it, index=index):
                pltpu.make_async_copy(src, src, ss.at[it, index]).wait()

            if cond is None:
                wait()
            else:
                pl.when(cond)(wait)
        sent.clear()

    def arrived(dst, it, index):
        pltpu.make_async_copy(dst, dst, rr.at[it, index]).wait()

    def send_halo(it):
        up_b = jnp.where(r == 0, b, b + 1)
        down_b = jnp.where(r == 1, b, b - 1)
        send(chi.at[it, pl.ds(0, 64)], chi.at[it, pl.ds(576, 64)], it, HALO_NEXT, dev(down_b, o, 1 - r), p > 0)
        send(chi.at[it, pl.ds(448, 64)], chi.at[it, pl.ds(512, 64)], it, HALO_PREV, dev(up_b, o, 1 - r), jnp.logical_and(p > 6, p < 15))

    def wait_halo(it):
        pl.when(p < 15)(lambda: arrived(chi.at[it, pl.ds(576, 64)], it, HALO_NEXT))
        pl.when(high)(lambda: arrived(chi.at[it, pl.ds(512, 64)], it, HALO_PREV))

    send_halo(0)
    partner = dev(jnp.where(low, b + 4, b - 4), side, r)
    for t in (0, 3, 1, 2):
        if t in (1, 2):
            prepare_tile(t)
        rows = pl.ds(t * TILE, TILE)
        send(nq_out.at[rows], nq_in.at[rows], 0, NX + t, partner, has_side)
    send(cs_own, cs_in, 0, NXC, partner, has_side)

    load_main.wait()
    load_prev.wait()
    right = lax.broadcasted_iota(jnp.int32, (BLK, 2 * BLK), 1) >= BLK
    for i in range(9):
        at = (q * 8 + i) % 64 if i < 8 else (q * 8 + 63) % 64
        keep = jnp.where(o * GROUP_BLOCKS + at < groups * GROUP_BLOCKS - 1, pattern[at], 0).astype(F32)
        block = meff[i * 64 : i * 64 + 64, :].astype(F32)
        meff[i * 64 : i * 64 + 64, :] = jnp.where(right, block * keep, block).astype(BF)

    gives_metric = jnp.logical_and(high, o > 0)
    send(meff, mrecv, 0, MET, dev(b, o - 1, r), gives_metric)

    @pl.when(low)
    def _():
        msel[...] = meff[...]

    @pl.when(jnp.logical_and(high, has_side))
    def _():
        arrived(mrecv, 0, MET)
        msel[...] = mrecv[...]

    @pl.when(jnp.logical_and(high, jnp.logical_not(has_side)))
    def _():
        msel[...] = jnp.zeros((576, 128), BF)

    @pl.when(p == 8)
    def _():
        msel[512:576, :] = meff[512:576, :]

    band[...] = jnp.zeros((ROWS, 640), BF)
    row_at = lax.broadcasted_iota(jnp.int32, (128, 128), 0)
    lane_at = lax.broadcasted_iota(jnp.int32, (128, 128), 1)
    top, left = row_at < 64, lane_at < 64
    bottom, rest = row_at >= 64, lane_at >= 64
    for t in range(4):
        m = msel[t * 128 : t * 128 + 128, :].astype(F32)
        rolled = pltpu.roll(m, 64, 1)
        corner = jnp.where(jnp.logical_and(top, rest), m, 0.0)
        diag = jnp.where(top, m, jnp.where(rest, rolled, 0.0)) + corner.T
        band[t * 128 : t * 128 + 128, t * 128 : t * 128 + 128] = diag.astype(BF)
        if t < 3:
            off = jnp.where(jnp.logical_and(bottom, left), rolled, 0.0)
            band[t * 128 : t * 128 + 128, t * 128 + 128 : t * 128 + 256] = off.astype(BF)
            band[t * 128 + 128 : t * 128 + 256, t * 128 : t * 128 + 128] = off.T.astype(BF)
        else:
            band[384:512, 512:640] = jnp.where(jnp.logical_and(bottom, rest), m, 0.0).astype(BF)
    before = pltpu.roll(msel[448:576, :].astype(F32), 64, 1).T
    shifted = pltpu.roll(before, 64, 1)
    band[0:128, 512:640] = jnp.where(jnp.logical_and(top, left), shifted, 0.0).astype(BF)

    def images(it):
        yhi[...], ylo[...] = split(dot(band[:, 0:512], chi[it, 0:512]) + dot(band[:, 0:512], clo[it]))

    def edges(it):
        wait_halo(it)
        top = dot(band[0:64, 512:640], chi[it, 512:640])
        bottom = dot(band[448:512, 512:640], chi[it, 512:640])
        last_block = chi[it, 448:512, :]
        lhs[0:64, :] = chi[it, 0:64, :]
        rhs[0:64, :] = top.astype(BF)
        lhs[64:128, :] = last_block
        rhs[64:128, :] = bottom.astype(BF)
        lhs[128:192, :] = bottom.astype(BF)
        rhs[128:192, :] = (last_block.astype(F32) * (p < 7).astype(F32)).astype(BF)
        for a in range(4):
            cols = slice(a * TILE, a * TILE + TILE)
            g = dot(lhs[:, cols], rhs[:, a * TILE : ORBS], ((0,), (0,)))
            for e in range(a, 4):
                rows = slice(KEPT.index((a, e)) * TILE, KEPT.index((a, e)) * TILE + TILE)
                gp[it, rows, :] = gp[it, rows, :] + g[:, (e - a) * TILE : (e - a) * TILE + TILE]
        if it == 0:
            for rows, more in ((slice(0, 64), top), (slice(448, 512), bottom)):
                y = yhi[rows, :].astype(F32) + ylo[rows, :].astype(F32)
                yhi[rows, :], ylo[rows, :] = split(y + more)

    def cross_edges(it):
        ends[0:64, :] = nhi[0:64, :]
        ends[64:128, :] = nhi[448:512, :]

        hp[it] = hp[it] + dot(rhs[0:128, :], ends[...], ((0,), (0,)))

    def gram(it):
        for a in range(4):
            cols = slice(a * TILE, a * TILE + TILE)
            rest = slice(a * TILE, ORBS)
            g = dot3(chi[it, 0:512, cols], clo[it, :, cols], yhi[:, rest], ylo[:, rest], ((0,), (0,)))
            for e in range(a, 4):
                k = KEPT.index((a, e))
                gp[it, k * TILE : k * TILE + TILE, :] = g[:, (e - a) * TILE : (e - a) * TILE + TILE]

    def cross(it):
        hp[it] = dot3(yhi[...], ylo[...], nhi[...], nlo[...], ((0,), (0,)))

    own_half = pl.ds(pl.multiple_of(core * HALF, HALF), HALF)
    other_half = pl.ds(pl.multiple_of((1 - core) * HALF, HALF), HALF)
    own_part = pl.ds(pl.multiple_of(core * PHALF, PHALF), PHALF)
    other_part = pl.ds(pl.multiple_of((1 - core) * PHALF, PHALF), PHALF)

    def pair_and_pack(it, part, from_pair, packed, scale, size, count):
        half, wide = size * count, part.shape[2]

        def add(i, top_value):
            rows = pl.ds(pl.multiple_of(core * half + i * size, size), size)
            x = part[it, rows, :] + from_pair[it, pl.ds(pl.multiple_of(i * size, size), size), :]
            part[it, rows, :] = x
            return jnp.maximum(top_value, jnp.abs(x))

        peak = jnp.max(lax.fori_loop(0, count, add, jnp.zeros((size, wide), F32), unroll=True), axis=(0, 1), keepdims=True)
        peak = jnp.maximum(peak, 1e-30)
        scale[it] = jnp.broadcast_to(peak * (1.0 / QMAX), (1, 128))
        inv = QMAX / peak

        def pack(i, carry):
            rows = pl.ds(pl.multiple_of(core * half + i * size, size), size)
            packed[it, i] = jnp.round(part[it, rows, :] * inv).astype(I16)
            return carry

        lax.fori_loop(0, count, pack, 0, unroll=True)

    def quantized(x):
        peak = jnp.maximum(jnp.max(jnp.abs(x), axis=(0, 1), keepdims=True), 1e-30)
        return jnp.round(x * (QMAX / peak)).astype(I16), jnp.broadcast_to(peak * (1.0 / QMAX), (1, 128))

    def scatter_gram(it):
        arrived(gsib.at[it], it, GSIB)
        pair_and_pack(it, gp, gsib, qs, qsc, GP, 8)

    def send_gram(it):
        for k in FAR:
            to = (z + k) % 8
            send(qs.at[it, to], rs.at[it, k], it, RS + k, zdev(to, o))
            send(qsc.at[it], rsc.at[it, k], it, RSC + k, zdev(to, o))

    def scatter_cross(it):
        arrived(hsib.at[it], it, HSIB)
        pair_and_pack(it, hp, hsib, hqs, hqsc, HP, 8)

    def from_high(k):
        return (z + 8 - k) % 4 >= 2

    def send_cross(it):
        for k in FAR:
            to = (z + k) % 8
            send(hqs.at[it, to], hrs.at[it, k], it, HRS + k, zdev(to, o), high)
            send(hqsc.at[it], hrsc.at[it, k], it, HRSC + k, zdev(to, o), high)

    def own_gram(it):
        rows = pl.ds(pl.multiple_of(core * PHALF + z * GP, GP), GP)
        total = gp[it, rows, :]
        for k in range(1, 8):
            arrived(rs.at[it, k], it, RS + k)
            arrived(rsc.at[it, k], it, RSC + k)
            total = total + rs[it, k].astype(jnp.int32).astype(F32) * rsc[it, k, 0:1, 0:1]
        here = lax.broadcasted_iota(jnp.int32, (GP, TILE), 0) + (core * PHALF + z * GP)
        tile = lax.shift_right_logical(here, 7)
        within = jnp.bitwise_and(here, 127) == lax.broadcasted_iota(jnp.int32, (GP, TILE), 1)
        on = jnp.zeros((GP, TILE), F32)
        for a in range(4):
            on = jnp.where(jnp.logical_and(tile == KEPT.index((a, a)), within), 1.0, on)
        value, scale = quantized(total * (1.0 / (SUPPORT * BLK)) - on)
        ea[it, rows, :] = value
        at = core * 8 + z
        es[it, at] = scale
        for k in FAR:
            device = zdev((z + k) % 8, o)
            send(ea.at[it, rows], ea.at[it, rows], it, EA + k, device)
            send(es.at[it, at], es.at[it, at], it, EAS + k, device)

    def own_cross(it):
        rows = pl.ds(pl.multiple_of(core * HALF + z * HP, HP), HP)
        at = core * 8 + z

        @pl.when(high)
        def _():
            sums[...] = hp[it, rows, :]

        @pl.when(low)
        def _():
            sums[...] = jnp.zeros((HP, ORBS), F32)

        for k in range(1, 8):

            @pl.when(from_high(k))
            def _():
                arrived(hrs.at[it, k], it, HRS + k)
                arrived(hrsc.at[it, k], it, HRSC + k)
                sums[...] = sums[...] + hrs[it, k].astype(jnp.int32).astype(F32) * hrsc[it, k, 0:1, 0:1]

        value, scale = quantized(sums[...] * (1.0 / (SUPPORT * BLK)))
        ho[it] = value
        hos[it] = scale

        @pl.when(high)
        def _():
            ha[it, rows, :] = value
            hs[it, at] = scale

        for k in FAR + (0,):
            to = (z + k) % 8
            to_low = to % 4 < 2
            cond = jnp.logical_and(to_low, above)
            if k > 0:
                cond = jnp.logical_or(cond, to % 4 >= 2)
            device = zdev(to, jnp.where(to_low, o + 1, o))
            send(ho.at[it], ha.at[it, rows], it, HA + k, device, cond)
            send(hos.at[it], hs.at[it, at], it, HAS + k, device, cond)

    own_eight = pl.ds(pl.multiple_of(core * 8, 8), 8)
    other_eight = pl.ds(pl.multiple_of((1 - core) * 8, 8), 8)
    def piece(at, size):
        return pl.ds(pl.multiple_of(at * size, size), size)

    def pass_gram(it, with_side):
        for k in FAR[::-1]:
            at = core * 8 + (z + 8 - k) % 8
            arrived(ea.at[it, piece(at, GP)], it, EA + k)
            arrived(es.at[it, at], it, EAS + k)
            send(ea.at[it, piece(at, GP)], ea.at[it, piece(at, GP)], it, FE + k, sibling)
        mine = piece(core * 8 + z, GP)
        send(ea.at[it, mine], ea.at[it, mine], it, FE, sibling)
        send(es.at[it, own_eight], es.at[it, own_eight], it, FES, sibling)
        if with_side:
            send(ea.at[it, own_part], na.at[own_part], it, NA, dev(b, away, r), has_away)
            send(es.at[it, own_eight], ns.at[own_eight], it, NAS, dev(b, away, r), has_away)

    def pass_side(it):
        @pl.when(has_side)
        def _():
            arrived(na.at[own_part], it, NA)
            arrived(ns.at[own_eight], it, NAS)

        send(na.at[own_part], na.at[own_part], it, FN, sibling, has_side)
        send(ns.at[own_eight], ns.at[own_eight], it, FNS, sibling, has_side)

    def pass_cross(it):
        data, tags = ha.at[it], hs.at[it]
        takes = jnp.logical_or(high, has_side)
        for k in (0,) + FAR[::-1]:
            at = core * 8 + (z + 8 - k) % 8

            def taken(at=at, k=k):
                arrived(data.at[piece(at, HP)], it, HA + k)
                arrived(tags.at[at], it, HAS + k)

            pl.when(below if k == 0 else takes)(taken)
            send(data.at[piece(at, HP)], data.at[piece(at, HP)], it, FH + k, sibling, takes)
        send(tags.at[own_eight], tags.at[own_eight], it, FHS, sibling, takes)

    def unpack(value, scale):
        return value.astype(jnp.int32).astype(F32) * scale[0:1, 0:1]

    def spread(packed, scales, to_hi, to_lo):
        def body(i, carry):
            rows = piece(i, GP)
            ef[rows, :] = unpack(packed[rows, :], scales[i])
            return carry

        lax.fori_loop(0, 16, body, 0, unroll=True)
        for k, (a, e) in enumerate(KEPT):
            x = ef[k * TILE : k * TILE + TILE, :]
            at, to = slice(a * TILE, a * TILE + TILE), slice(e * TILE, e * TILE + TILE)
            to_hi[at, to], to_lo[at, to] = split(x)
            if a != e:
                to_hi[to, at], to_lo[to, at] = split(x.T)

    def take_gram(it):
        for k in range(8):
            arrived(ea.at[it, piece((1 - core) * 8 + (z + 8 - k) % 8, GP)], it, FE + k)
        arrived(es.at[it, other_eight], it, FES)
        spread(ea.at[it], es.at[it], ehi, elo)

    def take_side(it):
        @pl.when(has_side)
        def _():
            arrived(na.at[other_part], it, FN)
            arrived(ns.at[other_eight], it, FNS)
            spread(na, ns, mhi, mlo)

    def cross_value(it, i):
        return jnp.concatenate([unpack(ha[it, piece(4 * i + e, HP), :], hs[it, 4 * i + e]) for e in range(4)], axis=0)

    def cross_plain(it, to_hi, to_lo, halves=(0, 1)):
        for half in halves:
            for e in range(2):
                rows = piece(2 * half + e, TILE)
                to_hi[rows, :], to_lo[rows, :] = split(cross_value(it, 2 * half + e))

    def cross_turned(it, to_hi, to_lo, halves=(0, 1)):
        for half in halves:
            for e in range(2):
                cols = piece(2 * half + e, TILE)
                to_hi[:, cols], to_lo[:, cols] = split(cross_value(it, 2 * half + e).T)

    low_side = jnp.logical_and(low, has_side)
    high_side = jnp.logical_and(high, has_side)

    def unpack_half(it, half):
        pl.when(low_side)(lambda: cross_plain(it, xhi, xlo, (half,)))
        pl.when(high_side)(lambda: cross_turned(it, xhi, xlo, (half,)))

    def take_own_cross(it):
        if it == 0:

            @pl.when(jnp.logical_not(has_side))
            def _():
                xhi[...] = jnp.zeros((ORBS, ORBS), BF)
                xlo[...] = jnp.zeros((ORBS, ORBS), BF)

        unpack_half(it, core)

    def take_pair_cross(it):
        @pl.when(jnp.logical_or(high, has_side))
        def _():
            for k in range(8):
                arrived(ha.at[it, piece((1 - core) * 8 + (z + 8 - k) % 8, HP)], it, FH + k)
            arrived(hs.at[it, other_eight], it, FHS)

        unpack_half(it, 1 - core)

    def own_change(it):
        c[...] = c[...] - 0.5 * dot3(chi[it, 0:512], clo[it], ehi[...], elo[...])

    def updated(it, t, rows):
        change = dot3(nhi[rows, :], nlo[rows, :], xhi[...], xlo[...])
        return jnp.where(live(rows, cs_own), c[rows, :] - 0.5 * change, 0.0)

    def rows_arrived():
        @pl.when(has_side)
        def _():
            for t in range(4):
                arrived(nq_in.at[pl.ds(t * TILE, TILE)], 0, NX + t)

    def take_rows():
        @pl.when(has_side)
        def _():
            for t in range(4):
                rows = pl.ds(t * TILE, TILE)
                x = nq_in[rows, :].astype(jnp.int32).astype(F32) * (CMAX / QMAX)
                nf[rows, :] = x
                nhi[rows, :], nlo[rows, :] = split(x)

        @pl.when(jnp.logical_not(has_side))
        def _():
            nhi[...] = jnp.zeros((ROWS, ORBS), BF)
            nlo[...] = jnp.zeros((ROWS, ORBS), BF)

    def pair_cross(it):
        send(hp.at[it, other_half], hsib.at[it], it, HSIB, sibling, high)

    def keep(rows, x):
        c[rows, :] = x
        hi, lo = split(x)
        chi[1, rows, :] = hi
        clo[1, rows, :] = lo

    def first(rows):
        keep(rows, updated(0, 0, rows))

    def first_ends():
        two = (pl.ds(0, BLK), pl.ds(448, BLK))
        change = dot3(
            jnp.concatenate([nhi[rows, :] for rows in two], axis=0), jnp.concatenate([nlo[rows, :] for rows in two], axis=0), xhi[...], xlo[...]
        )
        for i, rows in enumerate(two):
            keep(rows, jnp.where(live(rows, cs_own), c[rows, :] - 0.5 * change[i * BLK : i * BLK + BLK], 0.0))

    def beside(t, rows):
        change = dot3(nhi[rows, :], nlo[rows, :], mhi[...], mlo[...])
        change = change + dot3(chi[0, rows, :], clo[0, rows, :], thi[...], tlo[...])
        x = jnp.where(live(rows, cs_in), nf[rows, :] - 0.5 * change, 0.0)
        nhi[rows, :], nlo[rows, :] = split(x)

    def ended(cols, change):
        at = lax.broadcasted_iota(jnp.int32, (ROWS, HALF), 0)
        block = first_block + (at // BLK).astype(F32)
        begin = cs_own[0:1, cols]
        lives = jnp.logical_and(block >= begin, block < begin + SUPPORT)
        out[:, cols] = jnp.where(lives, c[:, cols] - 0.5 * change, 0.0)

    def last_half(half, final):
        @pl.when(low)
        def _():
            part = dot3(nhi[:, half], nlo[:, half], xhi[half, :], xlo[half, :])
            if final:
                out[...] = jnp.where(live(pl.ds(0, ROWS), cs_own), nf[...] - 0.5 * part, 0.0)
            else:
                nf[...] = c[...] - 0.5 * part

        @pl.when(high)
        def _():
            ended(half, dot3(nhi[...], nlo[...], xhi[:, half], xlo[:, half]))

    images(0)
    gram(0)
    edges(0)
    send(gp.at[0, other_part], gsib.at[0], 0, GSIB, sibling)
    scatter_gram(0)
    rows_arrived()
    send_gram(0)
    take_rows()
    pl.when(high)(lambda: cross(0))
    pair_cross(0)
    pl.when(high)(lambda: scatter_cross(0))
    send_cross(0)
    own_gram(0)
    own_cross(0)
    pass_gram(0, True)
    take_gram(0)
    own_change(0)
    pass_side(0)
    pass_cross(0)
    take_own_cross(0)
    take_pair_cross(0)
    first_ends()
    send_halo(1)
    first(pl.ds(64, 384))
    pl.when(has_side)(lambda: arrived(cs_in, 0, NXC))
    pl.when(jnp.logical_and(low, has_side))(lambda: cross_turned(0, thi, tlo))
    pl.when(jnp.logical_and(high, has_side))(lambda: cross_plain(0, thi, tlo))
    take_side(0)
    pl.when(has_side)(lambda: beside(0, pl.ds(0, ROWS)))

    images(1)
    gram(1)
    pl.when(high)(lambda: cross(1))
    drain()
    edges(1)
    send(gp.at[1, other_part], gsib.at[1], 1, GSIB, sibling)
    pl.when(high)(lambda: cross_edges(1))
    pair_cross(1)
    scatter_gram(1)
    send_gram(1)
    pl.when(high)(lambda: scatter_cross(1))
    send_cross(1)
    own_gram(1)
    own_cross(1)
    pass_gram(1, False)
    take_gram(1)
    own_change(1)
    pass_cross(1)
    take_own_cross(1)
    last_half(own_half, False)
    drain()
    take_pair_cross(1)
    last_half(other_half, True)


def per_device(coefficients, basis_metric, pattern, starts):
    vm = pltpu.VMEM
    square = (ORBS, ORBS)
    scratch = [
        vm((ROWS, ORBS), F32), vm((2, 640, ORBS), BF), vm((2, ROWS, ORBS), BF),
        vm((ROWS, ORBS), F32), vm((ROWS, ORBS), BF), vm((ROWS, ORBS), BF),
        vm((ROWS, ORBS), BF), vm((ROWS, ORBS), BF), vm((ROWS, 640), BF),
        vm((2, PACKED, TILE), F32), vm((2, ORBS, ORBS), F32),
        vm((ROWS, ORBS), I16), vm((ROWS, ORBS), I16), vm((1, ORBS), F32), vm((1, ORBS), F32),
        vm((576, 128), BF), vm((576, 128), BF), vm((576, 128), BF),
        vm((2, PHALF, TILE), F32), vm((2, HALF, ORBS), F32),
        vm((2, 8, GP, TILE), I16), vm((2, 8, GP, TILE), I16), vm((2, 1, 128), F32), vm((2, 8, 1, 128), F32),
        vm((2, 8, HP, ORBS), I16), vm((2, 8, HP, ORBS), I16), vm((2, 1, 128), F32), vm((2, 8, 1, 128), F32),
        vm((2, PACKED, TILE), I16), vm((2, 16, 1, 128), F32), vm((PACKED, TILE), I16), vm((16, 1, 128), F32),
        vm((2, ORBS, ORBS), I16), vm((2, 16, 1, 128), F32),
        vm(square, BF), vm(square, BF), vm(square, BF), vm(square, BF), vm(square, BF), vm(square, BF),
        vm(square, BF), vm(square, BF), vm((PACKED, TILE), F32),
        vm((2, HP, ORBS), I16), vm((2, 1, 128), F32), vm((HP, ORBS), F32), vm((192, ORBS), BF), vm((192, ORBS), BF), vm((128, ORBS), BF),
        pltpu.SMEM((64,), jnp.int32), pltpu.SMEM((8,), jnp.int32),
        pltpu.SemaphoreType.DMA((2, COUNT)), pltpu.SemaphoreType.DMA((2, COUNT)), pltpu.SemaphoreType.DMA((8,)),
    ]
    result = pl.pallas_call(
        kernel,
        out_shape=jax.ShapeDtypeStruct((ROWS, ORBS), F32),
        in_specs=[
            pl.BlockSpec(memory_space=pltpu.HBM),
            pl.BlockSpec(memory_space=pltpu.HBM),
            pl.BlockSpec(memory_space=pltpu.HBM),
            pl.BlockSpec(memory_space=pltpu.HBM),
        ],
        out_specs=pl.BlockSpec(memory_space=pltpu.VMEM),
        scratch_shapes=scratch,
        compiler_params=pltpu.CompilerParams(
            collective_id=0, has_side_effects=True, vmem_limit_bytes=52 * 1024 * 1024
        ),
    )(coefficients[0], basis_metric, pattern, starts)
    return result[None]


def solution(mesh):
    in_specs = (P("orb", ("basis", "rep"), None), P("orb", None), P("orb"), P("orb"))
    out_specs = P("orb", ("basis", "rep"), None)
    return jax.shard_map(
        per_device, mesh=mesh, in_specs=in_specs, out_specs=out_specs, check_vma=False
    )
```

```python
import functools

import jax
import jax.numpy as jnp
from jax import lax
from jax.experimental import pallas as pl
from jax.experimental.pallas import tpu as pltpu
from jax.sharding import PartitionSpec as P

BLK = 64
GROUP_BLOCKS = 64
SUPPORT = 96
ITERS = 2
ROWS = 512
ORBS = 512
HALF = 256
GP = 80
PACKED = 1280
PHALF = 640
HP = 32
TILE = 128
CMAX = 6.0
QMAX = 32767.0
BF = jnp.bfloat16
F32 = jnp.float32
I16 = jnp.int16

HALO_NEXT, HALO_PREV, GSIB, HSIB, NA, NAS, FES, FN, FNS, FHS, NXC, MET = range(12)
NX = 12
RS, RSC, HRS, HRSC, EA, EAS, HA, HAS, FE, FH = range(16, 96, 8)
COUNT = 96

FAR = (4, 3, 5, 2, 6, 1, 7)

KEPT = [(a, b) for a in range(4) for b in range(a, 4)]


def split(x):
    hi = x.astype(BF)
    return hi, (x - hi.astype(F32)).astype(BF)


def dot(a, b, dims=((1,), (0,))):
    return lax.dot_general(a, b, (dims, ((), ())), preferred_element_type=F32)


def dot3(ah, al, bh, bl, dims=((1,), (0,))):
    return dot(ah, bh, dims) + (dot(ah, bl, dims) + dot(al, bh, dims))


def kernel(
    coef, metric, pattern_in, starts_in, out,
    c, chi, clo, nf, nhi, nlo, yhi, ylo, band, gp, hp,
    nq_out, nq_in, cs_own, cs_in, meff, mrecv, msel,
    gsib, hsib, qs, rs, qsc, rsc, hqs, hrs, hqsc, hrsc,
    ea, es, na, ns, ha, hs, ehi, elo, xhi, xlo, thi, tlo, mhi, mlo, ef, ho, hos, sums, lhs, rhs, ends, pattern, starts,
    ss, rr, local_sem,
):
    b, o, r = lax.axis_index("basis"), lax.axis_index("orb"), lax.axis_index("rep")
    groups = lax.axis_size("orb")
    core, zl = b % 2, b // 2
    z = r * 4 + zl
    p = b * 2 + r
    q = p % 8
    low = zl < 2
    high = jnp.logical_not(low)
    side = jnp.where(low, o - 1, o + 1)
    away = jnp.where(low, o + 1, o - 1)
    has_side = jnp.logical_and(side >= 0, side < groups)
    has_away = jnp.logical_and(away >= 0, away < groups)

    def dev(bb, oo, rep):
        return {"basis": bb, "orb": oo, "rep": rep}

    def zdev(zz, oo):
        return dev((zz % 4) * 2 + core, oo, zz // 4)

    sibling = dev(zl * 2 + 1 - core, o, r)

    barrier = pltpu.get_barrier_semaphore()

    def greet(device):
        pl.semaphore_signal(barrier, inc=1, device_id=device, device_id_type=pl.DeviceIdType.MESH)

    for k in range(1, 8):
        greet(zdev((z + k) % 8, o))
    greet(sibling)
    step_b = jnp.where(r == 1, b + 1, b - 1)
    has_step = jnp.logical_and(step_b >= 0, step_b < 8)

    @pl.when(has_step)
    def _():
        greet(dev(step_b, o, 1 - r))

    below = jnp.logical_and(low, o > 0)
    above = o < groups - 1

    @pl.when(below)
    def _():
        for k in range(8):
            greet(zdev((z + k) % 8, o - 1))

    @pl.when(above)
    def _():
        for m in range(4):
            greet(dev((m // 2) * 2 + core, o + 1, m % 2))

    straight = jnp.logical_and(high, above)

    @pl.when(straight)
    def _():
        greet(dev(b, o + 1, r))

    straight_down = jnp.logical_and(high, o > 0)

    @pl.when(straight_down)
    def _():
        greet(dev(b, o - 1, r))

    loads = [
        pltpu.make_async_copy(coef.at[pl.ds(t * TILE, TILE)], c.at[pl.ds(t * TILE, TILE)], local_sem.at[2 + t]) for t in range(4)
    ]
    small = [
        pltpu.make_async_copy(starts_in, starts, local_sem.at[6]),
        pltpu.make_async_copy(pattern_in, pattern, local_sem.at[7]),
    ]
    for load in small:
        load.start()
    for t in (0, 3, 1, 2):
        loads[t].start()
    load_main = pltpu.make_async_copy(metric.at[pl.ds(pl.multiple_of(q * 512, 64), 512)], meff.at[pl.ds(0, 512)], local_sem.at[0])
    load_prev = pltpu.make_async_copy(
        metric.at[pl.ds(pl.multiple_of((q * 512 + 4032) % 4096, 64), 64)], meff.at[pl.ds(512, 64)], local_sem.at[1]
    )
    load_main.start()
    load_prev.start()
    small[0].wait()
    small[1].wait()
    lane = lax.broadcasted_iota(jnp.int32, (1, ORBS), 1) // BLK
    cs = jnp.zeros((1, ORBS), F32)
    for i in range(8):
        cs = jnp.where(lane == i, starts[i].astype(F32), cs)
    cs_own[...] = cs
    first_block = (o * GROUP_BLOCKS + p * 8).astype(F32)

    def live(rows, cs_ref):
        start, count = rows.start, rows.size
        at = lax.broadcasted_iota(jnp.int32, (count, ORBS), 0) + start
        block = first_block + (at // BLK).astype(F32)
        begin = cs_ref[0:1, :]
        return jnp.logical_and(block >= begin, block < begin + SUPPORT)

    def tiles(body):
        def step(t, carry):
            body(t, pl.ds(pl.multiple_of(t * TILE, TILE), TILE))
            return carry

        lax.fori_loop(0, ROWS // TILE, step, 0)

    def prepare(t, rows):
        x = jnp.where(live(rows, cs_own), c[rows, :], 0.0)
        c[rows, :] = x
        hi, lo = split(x)
        chi[0, rows, :] = hi
        clo[0, rows, :] = lo
        nq_out[rows, :] = jnp.round(jnp.clip(x, -CMAX, CMAX) * (QMAX / CMAX)).astype(I16)

    def prepare_tile(t):
        loads[t].wait()
        prepare(jnp.int32(t), pl.ds(t * TILE, TILE))

    prepare_tile(0)
    prepare_tile(3)
    for it in range(ITERS):

        @pl.when(low)
        def _():
            chi[it, 512:576, :] = jnp.zeros((64, ORBS), BF)

        @pl.when(p == 15)
        def _():
            chi[it, 576:640, :] = jnp.zeros((64, ORBS), BF)

    def ones(flag):
        return flag.astype(jnp.int32)

    pl.semaphore_wait(barrier, 8 + ones(has_step) + 8 * ones(below) + 4 * ones(above) + ones(straight) + ones(straight_down))

    sent = []

    def send(src, dst, it, index, device, cond=None, land=None):
        land = index if land is None else land

        def start():
            pltpu.make_async_remote_copy(
                src_ref=src, dst_ref=dst, send_sem=ss.at[it, index], recv_sem=rr.at[it, land],
                device_id=device, device_id_type=pl.DeviceIdType.MESH,
            ).start()

        if cond is None:
            start()
        else:
            pl.when(cond)(start)
        sent.append((src, it, index, cond))

    def drain(count=None):
        for src, it, index, cond in sent[:count]:

            def wait(src=src, it=it, index=index):
                pltpu.make_async_copy(src, src, ss.at[it, index]).wait()

            if cond is None:
                wait()
            else:
                pl.when(cond)(wait)
        del sent[:count]

    def arrived(dst, it, index):
        pltpu.make_async_copy(dst, dst, rr.at[it, index]).wait()

    def send_halo(it):
        up_b = jnp.where(r == 0, b, b + 1)
        down_b = jnp.where(r == 1, b, b - 1)
        send(chi.at[it, pl.ds(0, 64)], chi.at[it, pl.ds(576, 64)], it, HALO_NEXT, dev(down_b, o, 1 - r), p > 0)
        send(chi.at[it, pl.ds(448, 64)], chi.at[it, pl.ds(512, 64)], it, HALO_PREV, dev(up_b, o, 1 - r), jnp.logical_and(p > 6, p < 15))

    def wait_halo(it):
        pl.when(p < 15)(lambda: arrived(chi.at[it, pl.ds(576, 64)], it, HALO_NEXT))
        pl.when(high)(lambda: arrived(chi.at[it, pl.ds(512, 64)], it, HALO_PREV))

    send_halo(0)
    partner = dev(jnp.where(low, b + 4, b - 4), side, r)
    for t in (0, 3, 1, 2):
        if t in (1, 2):
            prepare_tile(t)
        rows = pl.ds(t * TILE, TILE)
        send(nq_out.at[rows], nq_in.at[rows], 0, NX + t, partner, has_side)
    send(cs_own, cs_in, 0, NXC, partner, has_side)

    load_main.wait()
    load_prev.wait()
    right = lax.broadcasted_iota(jnp.int32, (BLK, 2 * BLK), 1) >= BLK
    for i in range(9):
        at = (q * 8 + i) % 64 if i < 8 else (q * 8 + 63) % 64
        keep = jnp.where(o * GROUP_BLOCKS + at < groups * GROUP_BLOCKS - 1, pattern[at], 0).astype(F32)
        block = meff[i * 64 : i * 64 + 64, :].astype(F32)
        meff[i * 64 : i * 64 + 64, :] = jnp.where(right, block * keep, block).astype(BF)

    gives_metric = jnp.logical_and(high, o > 0)
    send(meff, mrecv, 0, MET, dev(b, o - 1, r), gives_metric)

    @pl.when(low)
    def _():
        msel[...] = meff[...]

    @pl.when(jnp.logical_and(high, has_side))
    def _():
        arrived(mrecv, 0, MET)
        msel[...] = mrecv[...]

    @pl.when(jnp.logical_and(high, jnp.logical_not(has_side)))
    def _():
        msel[...] = jnp.zeros((576, 128), BF)

    @pl.when(p == 8)
    def _():
        msel[512:576, :] = meff[512:576, :]

    band[...] = jnp.zeros((ROWS, 640), BF)
    row_at = lax.broadcasted_iota(jnp.int32, (128, 128), 0)
    lane_at = lax.broadcasted_iota(jnp.int32, (128, 128), 1)
    top, left = row_at < 64, lane_at < 64
    bottom, rest = row_at >= 64, lane_at >= 64
    for t in range(4):
        m = msel[t * 128 : t * 128 + 128, :].astype(F32)
        rolled = pltpu.roll(m, 64, 1)
        corner = jnp.where(jnp.logical_and(top, rest), m, 0.0)
        diag = jnp.where(top, m, jnp.where(rest, rolled, 0.0)) + corner.T
        band[t * 128 : t * 128 + 128, t * 128 : t * 128 + 128] = diag.astype(BF)
        if t < 3:
            off = jnp.where(jnp.logical_and(bottom, left), rolled, 0.0)
            band[t * 128 : t * 128 + 128, t * 128 + 128 : t * 128 + 256] = off.astype(BF)
            band[t * 128 + 128 : t * 128 + 256, t * 128 : t * 128 + 128] = off.T.astype(BF)
        else:
            band[384:512, 512:640] = jnp.where(jnp.logical_and(bottom, rest), m, 0.0).astype(BF)
    before = pltpu.roll(msel[448:576, :].astype(F32), 64, 1).T
    shifted = pltpu.roll(before, 64, 1)
    band[0:128, 512:640] = jnp.where(jnp.logical_and(top, left), shifted, 0.0).astype(BF)

    def images(it):
        yhi[...], ylo[...] = split(dot(band[:, 0:512], chi[it, 0:512]) + dot(band[:, 0:512], clo[it]))

    def edges(it):
        wait_halo(it)
        top = dot(band[0:64, 512:640], chi[it, 512:640])
        bottom = dot(band[448:512, 512:640], chi[it, 512:640])
        last_block = chi[it, 448:512, :]
        lhs[0:64, :] = chi[it, 0:64, :]
        rhs[0:64, :] = top.astype(BF)
        lhs[64:128, :] = last_block
        rhs[64:128, :] = bottom.astype(BF)
        lhs[128:192, :] = bottom.astype(BF)
        rhs[128:192, :] = (last_block.astype(F32) * (p < 7).astype(F32)).astype(BF)
        for a in range(4):
            cols = slice(a * TILE, a * TILE + TILE)
            g = dot(lhs[:, cols], rhs[:, a * TILE : ORBS], ((0,), (0,)))
            for e in range(a, 4):
                rows = slice(KEPT.index((a, e)) * TILE, KEPT.index((a, e)) * TILE + TILE)
                gp[it, rows, :] = gp[it, rows, :] + g[:, (e - a) * TILE : (e - a) * TILE + TILE]
        if it == 0:
            for rows, more in ((slice(0, 64), top), (slice(448, 512), bottom)):
                y = yhi[rows, :].astype(F32) + ylo[rows, :].astype(F32)
                yhi[rows, :], ylo[rows, :] = split(y + more)

    def cross_edges(it):
        ends[0:64, :] = nhi[0:64, :]
        ends[64:128, :] = nhi[448:512, :]

        hp[it] = hp[it] + dot(rhs[0:128, :], ends[...], ((0,), (0,)))

    def gram(it):
        for a in range(4):
            cols = slice(a * TILE, a * TILE + TILE)
            rest = slice(a * TILE, ORBS)
            g = dot3(chi[it, 0:512, cols], clo[it, :, cols], yhi[:, rest], ylo[:, rest], ((0,), (0,)))
            for e in range(a, 4):
                k = KEPT.index((a, e))
                gp[it, k * TILE : k * TILE + TILE, :] = g[:, (e - a) * TILE : (e - a) * TILE + TILE]

    def cross(it):
        hp[it] = dot3(yhi[...], ylo[...], nhi[...], nlo[...], ((0,), (0,)))

    def cross_half(it, half):
        hp[it, half, :] = dot3(yhi[:, half], ylo[:, half], nhi[...], nlo[...], ((0,), (0,)))

    own_half = pl.ds(pl.multiple_of(core * HALF, HALF), HALF)
    other_half = pl.ds(pl.multiple_of((1 - core) * HALF, HALF), HALF)
    own_part = pl.ds(pl.multiple_of(core * PHALF, PHALF), PHALF)
    other_part = pl.ds(pl.multiple_of((1 - core) * PHALF, PHALF), PHALF)

    def pair_and_pack(it, part, from_pair, packed, scale, size, count):
        half, wide = size * count, part.shape[2]

        def add(i, top_value):
            rows = pl.ds(pl.multiple_of(core * half + i * size, size), size)
            x = part[it, rows, :] + from_pair[it, pl.ds(pl.multiple_of(i * size, size), size), :]
            part[it, rows, :] = x
            return jnp.maximum(top_value, jnp.abs(x))

        peak = jnp.max(lax.fori_loop(0, count, add, jnp.zeros((size, wide), F32), unroll=True), axis=(0, 1), keepdims=True)
        peak = jnp.maximum(peak, 1e-30)
        scale[it] = jnp.broadcast_to(peak * (1.0 / QMAX), (1, 128))
        inv = QMAX / peak

        def pack(i, carry):
            rows = pl.ds(pl.multiple_of(core * half + i * size, size), size)
            packed[it, i] = jnp.round(part[it, rows, :] * inv).astype(I16)
            return carry

        lax.fori_loop(0, count, pack, 0, unroll=True)

    def quantized(x):
        peak = jnp.maximum(jnp.max(jnp.abs(x), axis=(0, 1), keepdims=True), 1e-30)
        return jnp.round(x * (QMAX / peak)).astype(I16), jnp.broadcast_to(peak * (1.0 / QMAX), (1, 128))

    def scatter_gram(it):
        arrived(gsib.at[it], it, GSIB)
        pair_and_pack(it, gp, gsib, qs, qsc, GP, 8)

    def send_gram(it):
        for k in FAR:
            to = (z + k) % 8
            send(qs.at[it, to], rs.at[it, k], it, RS + k, zdev(to, o))
            send(qsc.at[it], rsc.at[it, k], it, RSC + k, zdev(to, o))

    def scatter_cross(it):
        arrived(hsib.at[it], it, HSIB)
        pair_and_pack(it, hp, hsib, hqs, hqsc, HP, 8)

    def from_high(k):
        return (z + 8 - k) % 4 >= 2

    def send_cross(it):
        for k in FAR:
            to = (z + k) % 8
            send(hqs.at[it, to], hrs.at[it, k], it, HRS + k, zdev(to, o), high)
            send(hqsc.at[it], hrsc.at[it, k], it, HRSC + k, zdev(to, o), high)

    def own_gram(it):
        rows = pl.ds(pl.multiple_of(core * PHALF + z * GP, GP), GP)
        total = gp[it, rows, :]
        for k in range(1, 8):
            arrived(rs.at[it, k], it, RS + k)
            arrived(rsc.at[it, k], it, RSC + k)
            total = total + rs[it, k].astype(jnp.int32).astype(F32) * rsc[it, k, 0:1, 0:1]
        here = lax.broadcasted_iota(jnp.int32, (GP, TILE), 0) + (core * PHALF + z * GP)
        tile = lax.shift_right_logical(here, 7)
        within = jnp.bitwise_and(here, 127) == lax.broadcasted_iota(jnp.int32, (GP, TILE), 1)
        on = jnp.zeros((GP, TILE), F32)
        for a in range(4):
            on = jnp.where(jnp.logical_and(tile == KEPT.index((a, a)), within), 1.0, on)
        value, scale = quantized(total * (1.0 / (SUPPORT * BLK)) - on)
        ea[it, rows, :] = value
        at = core * 8 + z
        es[it, at] = scale
        for k in FAR:
            device = zdev((z + k) % 8, o)
            send(ea.at[it, rows], ea.at[it, rows], it, EA + k, device)
            send(es.at[it, at], es.at[it, at], it, EAS + k, device)

    def own_cross(it):
        rows = pl.ds(pl.multiple_of(core * HALF + z * HP, HP), HP)
        at = core * 8 + z

        @pl.when(high)
        def _():
            sums[...] = hp[it, rows, :]

        @pl.when(low)
        def _():
            sums[...] = jnp.zeros((HP, ORBS), F32)

        for k in range(1, 8):

            @pl.when(from_high(k))
            def _():
                arrived(hrs.at[it, k], it, HRS + k)
                arrived(hrsc.at[it, k], it, HRSC + k)
                sums[...] = sums[...] + hrs[it, k].astype(jnp.int32).astype(F32) * hrsc[it, k, 0:1, 0:1]

        value, scale = quantized(sums[...] * (1.0 / (SUPPORT * BLK)))
        ho[it] = value
        hos[it] = scale

        @pl.when(high)
        def _():
            ha[it, rows, :] = value
            hs[it, at] = scale

        for k in FAR + (0,):
            to = (z + k) % 8
            to_low = to % 4 < 2
            cond = jnp.logical_and(to_low, above)
            if k > 0:
                cond = jnp.logical_or(cond, to % 4 >= 2)
            device = zdev(to, jnp.where(to_low, o + 1, o))
            send(ho.at[it], ha.at[it, rows], it, HA + k, device, cond)
            send(hos.at[it], hs.at[it, at], it, HAS + k, device, cond)

    own_eight = pl.ds(pl.multiple_of(core * 8, 8), 8)
    other_eight = pl.ds(pl.multiple_of((1 - core) * 8, 8), 8)
    def piece(at, size):
        return pl.ds(pl.multiple_of(at * size, size), size)

    def pass_gram(it, with_side):
        for k in FAR[::-1]:
            at = core * 8 + (z + 8 - k) % 8
            arrived(ea.at[it, piece(at, GP)], it, EA + k)
            arrived(es.at[it, at], it, EAS + k)
            send(ea.at[it, piece(at, GP)], ea.at[it, piece(at, GP)], it, FE + k, sibling)
        mine = piece(core * 8 + z, GP)
        send(ea.at[it, mine], ea.at[it, mine], it, FE, sibling)
        send(es.at[it, own_eight], es.at[it, own_eight], it, FES, sibling)
        if with_side:
            send(ea.at[it, own_part], na.at[own_part], it, NA, dev(b, away, r), has_away)
            send(es.at[it, own_eight], ns.at[own_eight], it, NAS, dev(b, away, r), has_away)

    def pass_side(it):
        @pl.when(has_side)
        def _():
            arrived(na.at[own_part], it, NA)
            arrived(ns.at[own_eight], it, NAS)

        send(na.at[own_part], na.at[own_part], it, FN, sibling, has_side)
        send(ns.at[own_eight], ns.at[own_eight], it, FNS, sibling, has_side)

    def pass_cross(it):
        data, tags = ha.at[it], hs.at[it]
        takes = jnp.logical_or(high, has_side)
        for k in (0,) + FAR[::-1]:
            at = core * 8 + (z + 8 - k) % 8

            def taken(at=at, k=k):
                arrived(data.at[piece(at, HP)], it, HA + k)
                arrived(tags.at[at], it, HAS + k)

            pl.when(below if k == 0 else takes)(taken)
            send(data.at[piece(at, HP)], data.at[piece(at, HP)], it, FH + k, sibling, takes)
        send(tags.at[own_eight], tags.at[own_eight], it, FHS, sibling, takes)

    def unpack(value, scale):
        return value.astype(jnp.int32).astype(F32) * scale[0:1, 0:1]

    def spread(packed, scales, to_hi, to_lo):
        def body(i, carry):
            rows = piece(i, GP)
            ef[rows, :] = unpack(packed[rows, :], scales[i])
            return carry

        lax.fori_loop(0, 16, body, 0, unroll=True)
        for k, (a, e) in enumerate(KEPT):
            x = ef[k * TILE : k * TILE + TILE, :]
            at, to = slice(a * TILE, a * TILE + TILE), slice(e * TILE, e * TILE + TILE)
            to_hi[at, to], to_lo[at, to] = split(x)
            if a != e:
                to_hi[to, at], to_lo[to, at] = split(x.T)

    def take_gram(it):
        for k in range(8):
            arrived(ea.at[it, piece((1 - core) * 8 + (z + 8 - k) % 8, GP)], it, FE + k)
        arrived(es.at[it, other_eight], it, FES)
        spread(ea.at[it], es.at[it], ehi, elo)

    def take_side(it):
        @pl.when(has_side)
        def _():
            arrived(na.at[other_part], it, FN)
            arrived(ns.at[other_eight], it, FNS)
            spread(na, ns, mhi, mlo)

    def cross_value(it, i):
        return jnp.concatenate([unpack(ha[it, piece(4 * i + e, HP), :], hs[it, 4 * i + e]) for e in range(4)], axis=0)

    def cross_plain(it, to_hi, to_lo, halves=(0, 1)):
        for half in halves:
            for e in range(2):
                rows = piece(2 * half + e, TILE)
                to_hi[rows, :], to_lo[rows, :] = split(cross_value(it, 2 * half + e))

    def cross_turned(it, to_hi, to_lo, halves=(0, 1)):
        for half in halves:
            for e in range(2):
                cols = piece(2 * half + e, TILE)
                to_hi[:, cols], to_lo[:, cols] = split(cross_value(it, 2 * half + e).T)

    low_side = jnp.logical_and(low, has_side)
    high_side = jnp.logical_and(high, has_side)

    def unpack_half(it, half):
        pl.when(low_side)(lambda: cross_plain(it, xhi, xlo, (half,)))
        pl.when(high_side)(lambda: cross_turned(it, xhi, xlo, (half,)))

    def take_own_cross(it):
        if it == 0:

            @pl.when(jnp.logical_not(has_side))
            def _():
                xhi[...] = jnp.zeros((ORBS, ORBS), BF)
                xlo[...] = jnp.zeros((ORBS, ORBS), BF)

        unpack_half(it, core)

    def take_pair_cross(it):
        @pl.when(jnp.logical_or(high, has_side))
        def _():
            for k in range(8):
                arrived(ha.at[it, piece((1 - core) * 8 + (z + 8 - k) % 8, HP)], it, FH + k)
            arrived(hs.at[it, other_eight], it, FHS)

        unpack_half(it, 1 - core)

    def own_change(it):
        c[...] = c[...] - 0.5 * dot3(chi[it, 0:512], clo[it], ehi[...], elo[...])

    def updated(it, t, rows):
        change = dot3(nhi[rows, :], nlo[rows, :], xhi[...], xlo[...])
        return jnp.where(live(rows, cs_own), c[rows, :] - 0.5 * change, 0.0)

    def rows_arrived():
        @pl.when(has_side)
        def _():
            for t in range(4):
                arrived(nq_in.at[pl.ds(t * TILE, TILE)], 0, NX + t)

    def take_rows():
        @pl.when(has_side)
        def _():
            for t in range(4):
                rows = pl.ds(t * TILE, TILE)
                x = nq_in[rows, :].astype(jnp.int32).astype(F32) * (CMAX / QMAX)
                nf[rows, :] = x
                nhi[rows, :], nlo[rows, :] = split(x)

        @pl.when(jnp.logical_not(has_side))
        def _():
            nhi[...] = jnp.zeros((ROWS, ORBS), BF)
            nlo[...] = jnp.zeros((ROWS, ORBS), BF)

    def pair_cross(it):
        send(hp.at[it, other_half], hsib.at[it], it, HSIB, sibling, high)

    def keep(rows, x):
        c[rows, :] = x
        hi, lo = split(x)
        chi[1, rows, :] = hi
        clo[1, rows, :] = lo

    def first(rows):
        keep(rows, updated(0, 0, rows))

    def first_ends():
        two = (pl.ds(0, BLK), pl.ds(448, BLK))
        change = dot3(
            jnp.concatenate([nhi[rows, :] for rows in two], axis=0), jnp.concatenate([nlo[rows, :] for rows in two], axis=0), xhi[...], xlo[...]
        )
        for i, rows in enumerate(two):
            keep(rows, jnp.where(live(rows, cs_own), c[rows, :] - 0.5 * change[i * BLK : i * BLK + BLK], 0.0))

    def beside(t, rows):
        change = dot3(nhi[rows, :], nlo[rows, :], mhi[...], mlo[...])
        change = change + dot3(chi[0, rows, :], clo[0, rows, :], thi[...], tlo[...])
        x = jnp.where(live(rows, cs_in), nf[rows, :] - 0.5 * change, 0.0)
        nhi[rows, :], nlo[rows, :] = split(x)

    def ended(cols, change):
        at = lax.broadcasted_iota(jnp.int32, (ROWS, HALF), 0)
        block = first_block + (at // BLK).astype(F32)
        begin = cs_own[0:1, cols]
        lives = jnp.logical_and(block >= begin, block < begin + SUPPORT)
        out[:, cols] = jnp.where(lives, c[:, cols] - 0.5 * change, 0.0)

    def last_half(half, final):
        @pl.when(low)
        def _():
            part = dot3(nhi[:, half], nlo[:, half], xhi[half, :], xlo[half, :])
            if final:
                out[...] = jnp.where(live(pl.ds(0, ROWS), cs_own), nf[...] - 0.5 * part, 0.0)
            else:
                nf[...] = c[...] - 0.5 * part

        @pl.when(high)
        def _():
            ended(half, dot3(nhi[...], nlo[...], xhi[:, half], xlo[:, half]))

    images(0)
    gram(0)
    edges(0)
    send(gp.at[0, other_part], gsib.at[0], 0, GSIB, sibling)
    scatter_gram(0)
    rows_arrived()
    send_gram(0)
    take_rows()
    pl.when(high)(lambda: cross_half(0, other_half))
    pair_cross(0)
    pl.when(high)(lambda: cross_half(0, own_half))
    pl.when(high)(lambda: scatter_cross(0))
    send_cross(0)
    own_gram(0)
    own_cross(0)
    pass_gram(0, True)
    take_gram(0)
    own_change(0)
    pass_cross(0)
    take_own_cross(0)
    take_pair_cross(0)
    first_ends()
    send_halo(1)
    pass_side(0)
    first(pl.ds(64, 384))
    pl.when(has_side)(lambda: arrived(cs_in, 0, NXC))
    pl.when(jnp.logical_and(low, has_side))(lambda: cross_turned(0, thi, tlo))
    pl.when(jnp.logical_and(high, has_side))(lambda: cross_plain(0, thi, tlo))
    take_side(0)
    pl.when(has_side)(lambda: beside(0, pl.ds(0, ROWS)))

    images(1)
    gram(1)
    pl.when(high)(lambda: cross(1))
    edges(1)
    send(gp.at[1, other_part], gsib.at[1], 1, GSIB, sibling)
    pl.when(high)(lambda: cross_edges(1))
    pair_cross(1)
    scatter_gram(1)
    before = len(sent)
    send_gram(1)
    pl.when(high)(lambda: scatter_cross(1))
    send_cross(1)
    drain(before)
    own_gram(1)
    own_cross(1)
    pass_gram(1, False)
    take_gram(1)
    own_change(1)
    pass_cross(1)
    take_own_cross(1)
    last_half(own_half, False)
    drain()
    take_pair_cross(1)
    last_half(other_half, True)


def per_device(coefficients, basis_metric, pattern, starts):
    vm = pltpu.VMEM
    square = (ORBS, ORBS)
    scratch = [
        vm((ROWS, ORBS), F32), vm((2, 640, ORBS), BF), vm((2, ROWS, ORBS), BF),
        vm((ROWS, ORBS), F32), vm((ROWS, ORBS), BF), vm((ROWS, ORBS), BF),
        vm((ROWS, ORBS), BF), vm((ROWS, ORBS), BF), vm((ROWS, 640), BF),
        vm((2, PACKED, TILE), F32), vm((2, ORBS, ORBS), F32),
        vm((ROWS, ORBS), I16), vm((ROWS, ORBS), I16), vm((1, ORBS), F32), vm((1, ORBS), F32),
        vm((576, 128), BF), vm((576, 128), BF), vm((576, 128), BF),
        vm((2, PHALF, TILE), F32), vm((2, HALF, ORBS), F32),
        vm((2, 8, GP, TILE), I16), vm((2, 8, GP, TILE), I16), vm((2, 1, 128), F32), vm((2, 8, 1, 128), F32),
        vm((2, 8, HP, ORBS), I16), vm((2, 8, HP, ORBS), I16), vm((2, 1, 128), F32), vm((2, 8, 1, 128), F32),
        vm((2, PACKED, TILE), I16), vm((2, 16, 1, 128), F32), vm((PACKED, TILE), I16), vm((16, 1, 128), F32),
        vm((2, ORBS, ORBS), I16), vm((2, 16, 1, 128), F32),
        vm(square, BF), vm(square, BF), vm(square, BF), vm(square, BF), vm(square, BF), vm(square, BF),
        vm(square, BF), vm(square, BF), vm((PACKED, TILE), F32),
        vm((2, HP, ORBS), I16), vm((2, 1, 128), F32), vm((HP, ORBS), F32), vm((192, ORBS), BF), vm((192, ORBS), BF), vm((128, ORBS), BF),
        pltpu.SMEM((64,), jnp.int32), pltpu.SMEM((8,), jnp.int32),
        pltpu.SemaphoreType.DMA((2, COUNT)), pltpu.SemaphoreType.DMA((2, COUNT)), pltpu.SemaphoreType.DMA((8,)),
    ]
    result = pl.pallas_call(
        kernel,
        out_shape=jax.ShapeDtypeStruct((ROWS, ORBS), F32),
        in_specs=[
            pl.BlockSpec(memory_space=pltpu.HBM),
            pl.BlockSpec(memory_space=pltpu.HBM),
            pl.BlockSpec(memory_space=pltpu.HBM),
            pl.BlockSpec(memory_space=pltpu.HBM),
        ],
        out_specs=pl.BlockSpec(memory_space=pltpu.VMEM),
        scratch_shapes=scratch,
        compiler_params=pltpu.CompilerParams(
            collective_id=0, has_side_effects=True, vmem_limit_bytes=52 * 1024 * 1024
        ),
    )(coefficients[0], basis_metric, pattern, starts)
    return result[None]


def solution(mesh):
    in_specs = (P("orb", ("basis", "rep"), None), P("orb", None), P("orb"), P("orb"))
    out_specs = P("orb", ("basis", "rep"), None)
    return jax.shard_map(
        per_device, mesh=mesh, in_specs=in_specs, out_specs=out_specs, check_vma=False
    )
```

```python
import functools

import jax
import jax.numpy as jnp
from jax import lax
from jax.experimental import pallas as pl
from jax.experimental.pallas import tpu as pltpu
from jax.sharding import PartitionSpec as P

BLK = 64
GROUP_BLOCKS = 64
SUPPORT = 96
ITERS = 2
ROWS = 512
ORBS = 512
HALF = 256
GP = 80
PACKED = 1280
PHALF = 640
HP = 32
TILE = 128
CMAX = 6.0
QMAX = 32767.0
BF = jnp.bfloat16
F32 = jnp.float32
I16 = jnp.int16

HALO_NEXT, HALO_PREV, GSIB, HSIB, NA, NAS, FES, FN, FNS, FHS, NXC, MET = range(12)
NX = 12
RS, RSC, HRS, HRSC, EA, EAS, HA, HAS, FE, FH = range(16, 96, 8)
COUNT = 96

FAR = (4, 3, 5, 2, 6, 1, 7)

KEPT = [(a, b) for a in range(4) for b in range(a, 4)]


def split(x):
    hi = x.astype(BF)
    return hi, (x - hi.astype(F32)).astype(BF)


def dot(a, b, dims=((1,), (0,))):
    return lax.dot_general(a, b, (dims, ((), ())), preferred_element_type=F32)


def dot3(ah, al, bh, bl, dims=((1,), (0,))):
    return dot(ah, bh, dims) + (dot(ah, bl, dims) + dot(al, bh, dims))


def kernel(
    coef, metric, pattern_in, starts_in, out,
    c, chi, clo, nf, nhi, nlo, yhi, ylo, band, gp, hp,
    nq_out, nq_in, cs_own, cs_in, meff, mrecv, msel,
    gsib, hsib, qs, rs, qsc, rsc, hqs, hrs, hqsc, hrsc,
    ea, es, na, ns, ha, hs, ehi, elo, xhi, xlo, thi, tlo, mhi, mlo, ef, ho, hos, sums, lhs, rhs, ends, pattern, starts,
    ss, rr, local_sem,
):
    b, o, r = lax.axis_index("basis"), lax.axis_index("orb"), lax.axis_index("rep")
    groups = lax.axis_size("orb")
    core, zl = b % 2, b // 2
    z = r * 4 + zl
    p = b * 2 + r
    q = p % 8
    low = zl < 2
    high = jnp.logical_not(low)
    side = jnp.where(low, o - 1, o + 1)
    away = jnp.where(low, o + 1, o - 1)
    has_side = jnp.logical_and(side >= 0, side < groups)
    has_away = jnp.logical_and(away >= 0, away < groups)

    def dev(bb, oo, rep):
        return {"basis": bb, "orb": oo, "rep": rep}

    def zdev(zz, oo):
        return dev((zz % 4) * 2 + core, oo, zz // 4)

    sibling = dev(zl * 2 + 1 - core, o, r)

    barrier = pltpu.get_barrier_semaphore()

    def greet(device):
        pl.semaphore_signal(barrier, inc=1, device_id=device, device_id_type=pl.DeviceIdType.MESH)

    for k in range(1, 8):
        greet(zdev((z + k) % 8, o))
    greet(sibling)
    step_b = jnp.where(r == 1, b + 1, b - 1)
    has_step = jnp.logical_and(step_b >= 0, step_b < 8)

    @pl.when(has_step)
    def _():
        greet(dev(step_b, o, 1 - r))

    below = jnp.logical_and(low, o > 0)
    above = o < groups - 1

    @pl.when(below)
    def _():
        for k in range(8):
            greet(zdev((z + k) % 8, o - 1))

    @pl.when(above)
    def _():
        for m in range(4):
            greet(dev((m // 2) * 2 + core, o + 1, m % 2))

    straight = jnp.logical_and(high, above)

    @pl.when(straight)
    def _():
        greet(dev(b, o + 1, r))

    straight_down = jnp.logical_and(high, o > 0)

    @pl.when(straight_down)
    def _():
        greet(dev(b, o - 1, r))

    loads = [
        pltpu.make_async_copy(coef.at[pl.ds(t * TILE, TILE)], c.at[pl.ds(t * TILE, TILE)], local_sem.at[2 + t]) for t in range(4)
    ]
    small = [
        pltpu.make_async_copy(starts_in, starts, local_sem.at[6]),
        pltpu.make_async_copy(pattern_in, pattern, local_sem.at[7]),
    ]
    for load in small:
        load.start()
    for t in (0, 3, 1, 2):
        loads[t].start()
    load_main = pltpu.make_async_copy(metric.at[pl.ds(pl.multiple_of(q * 512, 64), 512)], meff.at[pl.ds(0, 512)], local_sem.at[0])
    load_prev = pltpu.make_async_copy(
        metric.at[pl.ds(pl.multiple_of((q * 512 + 4032) % 4096, 64), 64)], meff.at[pl.ds(512, 64)], local_sem.at[1]
    )
    load_main.start()
    load_prev.start()
    small[0].wait()
    small[1].wait()
    lane = lax.broadcasted_iota(jnp.int32, (1, ORBS), 1) // BLK
    cs = jnp.zeros((1, ORBS), F32)
    for i in range(8):
        cs = jnp.where(lane == i, starts[i].astype(F32), cs)
    cs_own[...] = cs
    first_block = (o * GROUP_BLOCKS + p * 8).astype(F32)

    def live(rows, cs_ref):
        start, count = rows.start, rows.size
        at = lax.broadcasted_iota(jnp.int32, (count, ORBS), 0) + start
        block = first_block + (at // BLK).astype(F32)
        begin = cs_ref[0:1, :]
        return jnp.logical_and(block >= begin, block < begin + SUPPORT)

    def tiles(body):
        def step(t, carry):
            body(t, pl.ds(pl.multiple_of(t * TILE, TILE), TILE))
            return carry

        lax.fori_loop(0, ROWS // TILE, step, 0)

    def prepare(t, rows):
        x = jnp.where(live(rows, cs_own), c[rows, :], 0.0)
        c[rows, :] = x
        hi, lo = split(x)
        chi[0, rows, :] = hi
        clo[0, rows, :] = lo
        nq_out[rows, :] = jnp.round(jnp.clip(x, -CMAX, CMAX) * (QMAX / CMAX)).astype(I16)

    def prepare_tile(t):
        loads[t].wait()
        prepare(jnp.int32(t), pl.ds(t * TILE, TILE))

    prepare_tile(0)
    prepare_tile(3)
    for it in range(ITERS):

        @pl.when(low)
        def _():
            chi[it, 512:576, :] = jnp.zeros((64, ORBS), BF)

        @pl.when(p == 15)
        def _():
            chi[it, 576:640, :] = jnp.zeros((64, ORBS), BF)

    def ones(flag):
        return flag.astype(jnp.int32)

    pl.semaphore_wait(barrier, 8 + ones(has_step) + 8 * ones(below) + 4 * ones(above) + ones(straight) + ones(straight_down))

    sent = []

    def send(src, dst, it, index, device, cond=None, land=None):
        land = index if land is None else land

        def start():
            pltpu.make_async_remote_copy(
                src_ref=src, dst_ref=dst, send_sem=ss.at[it, index], recv_sem=rr.at[it, land],
                device_id=device, device_id_type=pl.DeviceIdType.MESH,
            ).start()

        if cond is None:
            start()
        else:
            pl.when(cond)(start)
        sent.append((src, it, index, cond))

    def drain(count=None):
        for src, it, index, cond in sent[:count]:

            def wait(src=src, it=it, index=index):
                pltpu.make_async_copy(src, src, ss.at[it, index]).wait()

            if cond is None:
                wait()
            else:
                pl.when(cond)(wait)
        del sent[:count]

    def arrived(dst, it, index):
        pltpu.make_async_copy(dst, dst, rr.at[it, index]).wait()

    def send_halo(it):
        up_b = jnp.where(r == 0, b, b + 1)
        down_b = jnp.where(r == 1, b, b - 1)
        send(chi.at[it, pl.ds(0, 64)], chi.at[it, pl.ds(576, 64)], it, HALO_NEXT, dev(down_b, o, 1 - r), p > 0)
        send(chi.at[it, pl.ds(448, 64)], chi.at[it, pl.ds(512, 64)], it, HALO_PREV, dev(up_b, o, 1 - r), jnp.logical_and(p > 6, p < 15))

    def wait_halo(it):
        pl.when(p < 15)(lambda: arrived(chi.at[it, pl.ds(576, 64)], it, HALO_NEXT))
        pl.when(high)(lambda: arrived(chi.at[it, pl.ds(512, 64)], it, HALO_PREV))

    send_halo(0)
    partner = dev(jnp.where(low, b + 4, b - 4), side, r)
    for t in (0, 3, 1, 2):
        if t in (1, 2):
            prepare_tile(t)
        rows = pl.ds(t * TILE, TILE)
        send(nq_out.at[rows], nq_in.at[rows], 0, NX + t, partner, has_side)
    send(cs_own, cs_in, 0, NXC, partner, has_side)

    load_main.wait()
    load_prev.wait()
    right = lax.broadcasted_iota(jnp.int32, (BLK, 2 * BLK), 1) >= BLK
    for i in range(9):
        at = (q * 8 + i) % 64 if i < 8 else (q * 8 + 63) % 64
        keep = jnp.where(o * GROUP_BLOCKS + at < groups * GROUP_BLOCKS - 1, pattern[at], 0).astype(F32)
        block = meff[i * 64 : i * 64 + 64, :].astype(F32)
        meff[i * 64 : i * 64 + 64, :] = jnp.where(right, block * keep, block).astype(BF)

    gives_metric = jnp.logical_and(high, o > 0)
    send(meff, mrecv, 0, MET, dev(b, o - 1, r), gives_metric)

    @pl.when(low)
    def _():
        msel[...] = meff[...]

    @pl.when(jnp.logical_and(high, has_side))
    def _():
        arrived(mrecv, 0, MET)
        msel[...] = mrecv[...]

    @pl.when(jnp.logical_and(high, jnp.logical_not(has_side)))
    def _():
        msel[...] = jnp.zeros((576, 128), BF)

    @pl.when(p == 8)
    def _():
        msel[512:576, :] = meff[512:576, :]

    band[...] = jnp.zeros((ROWS, 640), BF)
    row_at = lax.broadcasted_iota(jnp.int32, (128, 128), 0)
    lane_at = lax.broadcasted_iota(jnp.int32, (128, 128), 1)
    top, left = row_at < 64, lane_at < 64
    bottom, rest = row_at >= 64, lane_at >= 64
    for t in range(4):
        m = msel[t * 128 : t * 128 + 128, :].astype(F32)
        rolled = pltpu.roll(m, 64, 1)
        corner = jnp.where(jnp.logical_and(top, rest), m, 0.0)
        diag = jnp.where(top, m, jnp.where(rest, rolled, 0.0)) + corner.T
        band[t * 128 : t * 128 + 128, t * 128 : t * 128 + 128] = diag.astype(BF)
        if t < 3:
            off = jnp.where(jnp.logical_and(bottom, left), rolled, 0.0)
            band[t * 128 : t * 128 + 128, t * 128 + 128 : t * 128 + 256] = off.astype(BF)
            band[t * 128 + 128 : t * 128 + 256, t * 128 : t * 128 + 128] = off.T.astype(BF)
        else:
            band[384:512, 512:640] = jnp.where(jnp.logical_and(bottom, rest), m, 0.0).astype(BF)
    before = pltpu.roll(msel[448:576, :].astype(F32), 64, 1).T
    shifted = pltpu.roll(before, 64, 1)
    band[0:128, 512:640] = jnp.where(jnp.logical_and(top, left), shifted, 0.0).astype(BF)

    def images(it):
        yhi[...], ylo[...] = split(dot(band[:, 0:512], chi[it, 0:512]) + dot(band[:, 0:512], clo[it]))

    def edges(it):
        wait_halo(it)
        top = dot(band[0:64, 512:640], chi[it, 512:640])
        bottom = dot(band[448:512, 512:640], chi[it, 512:640])
        last_block = chi[it, 448:512, :]
        lhs[0:64, :] = chi[it, 0:64, :]
        rhs[0:64, :] = top.astype(BF)
        lhs[64:128, :] = last_block
        rhs[64:128, :] = bottom.astype(BF)
        lhs[128:192, :] = bottom.astype(BF)
        rhs[128:192, :] = (last_block.astype(F32) * (p < 7).astype(F32)).astype(BF)
        for a in range(4):
            cols = slice(a * TILE, a * TILE + TILE)
            g = dot(lhs[:, cols], rhs[:, a * TILE : ORBS], ((0,), (0,)))
            for e in range(a, 4):
                rows = slice(KEPT.index((a, e)) * TILE, KEPT.index((a, e)) * TILE + TILE)
                gp[it, rows, :] = gp[it, rows, :] + g[:, (e - a) * TILE : (e - a) * TILE + TILE]
        if it == 0:
            for rows, more in ((slice(0, 64), top), (slice(448, 512), bottom)):
                y = yhi[rows, :].astype(F32) + ylo[rows, :].astype(F32)
                yhi[rows, :], ylo[rows, :] = split(y + more)

    def cross_edges(it, half):
        ends[0:64, :] = nhi[0:64, :]
        ends[64:128, :] = nhi[448:512, :]

        hp[it, half, :] = hp[it, half, :] + dot(rhs[0:128, half], ends[...], ((0,), (0,)))

    def gram(it):
        for a in range(4):
            cols = slice(a * TILE, a * TILE + TILE)
            rest = slice(a * TILE, ORBS)
            g = dot3(chi[it, 0:512, cols], clo[it, :, cols], yhi[:, rest], ylo[:, rest], ((0,), (0,)))
            for e in range(a, 4):
                k = KEPT.index((a, e))
                gp[it, k * TILE : k * TILE + TILE, :] = g[:, (e - a) * TILE : (e - a) * TILE + TILE]

    def cross(it):
        hp[it] = dot3(yhi[...], ylo[...], nhi[...], nlo[...], ((0,), (0,)))

    def cross_half(it, half):
        hp[it, half, :] = dot3(yhi[:, half], ylo[:, half], nhi[...], nlo[...], ((0,), (0,)))

    own_half = pl.ds(pl.multiple_of(core * HALF, HALF), HALF)
    other_half = pl.ds(pl.multiple_of((1 - core) * HALF, HALF), HALF)
    own_part = pl.ds(pl.multiple_of(core * PHALF, PHALF), PHALF)
    other_part = pl.ds(pl.multiple_of((1 - core) * PHALF, PHALF), PHALF)

    def pair_and_pack(it, part, from_pair, packed, scale, size, count):
        half, wide = size * count, part.shape[2]

        def add(i, top_value):
            rows = pl.ds(pl.multiple_of(core * half + i * size, size), size)
            x = part[it, rows, :] + from_pair[it, pl.ds(pl.multiple_of(i * size, size), size), :]
            part[it, rows, :] = x
            return jnp.maximum(top_value, jnp.abs(x))

        peak = jnp.max(lax.fori_loop(0, count, add, jnp.zeros((size, wide), F32), unroll=True), axis=(0, 1), keepdims=True)
        peak = jnp.maximum(peak, 1e-30)
        scale[it] = jnp.broadcast_to(peak * (1.0 / QMAX), (1, 128))
        inv = QMAX / peak

        def pack(i, carry):
            rows = pl.ds(pl.multiple_of(core * half + i * size, size), size)
            packed[it, i] = jnp.round(part[it, rows, :] * inv).astype(I16)
            return carry

        lax.fori_loop(0, count, pack, 0, unroll=True)

    def quantized(x):
        peak = jnp.maximum(jnp.max(jnp.abs(x), axis=(0, 1), keepdims=True), 1e-30)
        return jnp.round(x * (QMAX / peak)).astype(I16), jnp.broadcast_to(peak * (1.0 / QMAX), (1, 128))

    def scatter_gram(it):
        arrived(gsib.at[it], it, GSIB)
        pair_and_pack(it, gp, gsib, qs, qsc, GP, 8)

    def send_gram(it):
        for k in FAR:
            to = (z + k) % 8
            send(qs.at[it, to], rs.at[it, k], it, RS + k, zdev(to, o))
            send(qsc.at[it], rsc.at[it, k], it, RSC + k, zdev(to, o))

    def scatter_cross(it):
        arrived(hsib.at[it], it, HSIB)
        pair_and_pack(it, hp, hsib, hqs, hqsc, HP, 8)

    def from_high(k):
        return (z + 8 - k) % 4 >= 2

    def send_cross(it):
        for k in FAR:
            to = (z + k) % 8
            send(hqs.at[it, to], hrs.at[it, k], it, HRS + k, zdev(to, o), high)
            send(hqsc.at[it], hrsc.at[it, k], it, HRSC + k, zdev(to, o), high)

    def own_gram(it):
        rows = pl.ds(pl.multiple_of(core * PHALF + z * GP, GP), GP)
        total = gp[it, rows, :]
        for k in range(1, 8):
            arrived(rs.at[it, k], it, RS + k)
            arrived(rsc.at[it, k], it, RSC + k)
            total = total + rs[it, k].astype(jnp.int32).astype(F32) * rsc[it, k, 0:1, 0:1]
        here = lax.broadcasted_iota(jnp.int32, (GP, TILE), 0) + (core * PHALF + z * GP)
        tile = lax.shift_right_logical(here, 7)
        within = jnp.bitwise_and(here, 127) == lax.broadcasted_iota(jnp.int32, (GP, TILE), 1)
        on = jnp.zeros((GP, TILE), F32)
        for a in range(4):
            on = jnp.where(jnp.logical_and(tile == KEPT.index((a, a)), within), 1.0, on)
        value, scale = quantized(total * (1.0 / (SUPPORT * BLK)) - on)
        ea[it, rows, :] = value
        at = core * 8 + z
        es[it, at] = scale
        for k in FAR:
            device = zdev((z + k) % 8, o)
            send(ea.at[it, rows], ea.at[it, rows], it, EA + k, device)
            send(es.at[it, at], es.at[it, at], it, EAS + k, device)

    def own_cross(it):
        rows = pl.ds(pl.multiple_of(core * HALF + z * HP, HP), HP)
        at = core * 8 + z

        @pl.when(high)
        def _():
            sums[...] = hp[it, rows, :]

        @pl.when(low)
        def _():
            sums[...] = jnp.zeros((HP, ORBS), F32)

        for k in range(1, 8):

            @pl.when(from_high(k))
            def _():
                arrived(hrs.at[it, k], it, HRS + k)
                arrived(hrsc.at[it, k], it, HRSC + k)
                sums[...] = sums[...] + hrs[it, k].astype(jnp.int32).astype(F32) * hrsc[it, k, 0:1, 0:1]

        value, scale = quantized(sums[...] * (1.0 / (SUPPORT * BLK)))
        ho[it] = value
        hos[it] = scale

        @pl.when(high)
        def _():
            ha[it, rows, :] = value
            hs[it, at] = scale

        for k in FAR + (0,):
            to = (z + k) % 8
            to_low = to % 4 < 2
            cond = jnp.logical_and(to_low, above)
            if k > 0:
                cond = jnp.logical_or(cond, to % 4 >= 2)
            device = zdev(to, jnp.where(to_low, o + 1, o))
            send(ho.at[it], ha.at[it, rows], it, HA + k, device, cond)
            send(hos.at[it], hs.at[it, at], it, HAS + k, device, cond)

    own_eight = pl.ds(pl.multiple_of(core * 8, 8), 8)
    other_eight = pl.ds(pl.multiple_of((1 - core) * 8, 8), 8)
    def piece(at, size):
        return pl.ds(pl.multiple_of(at * size, size), size)

    def pass_gram(it, with_side):
        for k in FAR[::-1]:
            at = core * 8 + (z + 8 - k) % 8
            arrived(ea.at[it, piece(at, GP)], it, EA + k)
            arrived(es.at[it, at], it, EAS + k)
            send(ea.at[it, piece(at, GP)], ea.at[it, piece(at, GP)], it, FE + k, sibling)
        mine = piece(core * 8 + z, GP)
        send(ea.at[it, mine], ea.at[it, mine], it, FE, sibling)
        send(es.at[it, own_eight], es.at[it, own_eight], it, FES, sibling)
        if with_side:
            send(ea.at[it, own_part], na.at[own_part], it, NA, dev(b, away, r), has_away)
            send(es.at[it, own_eight], ns.at[own_eight], it, NAS, dev(b, away, r), has_away)

    def pass_side(it):
        @pl.when(has_side)
        def _():
            arrived(na.at[own_part], it, NA)
            arrived(ns.at[own_eight], it, NAS)

        send(na.at[own_part], na.at[own_part], it, FN, sibling, has_side)
        send(ns.at[own_eight], ns.at[own_eight], it, FNS, sibling, has_side)

    def pass_cross(it):
        data, tags = ha.at[it], hs.at[it]
        takes = jnp.logical_or(high, has_side)
        for k in (0,) + FAR[::-1]:
            at = core * 8 + (z + 8 - k) % 8

            def taken(at=at, k=k):
                arrived(data.at[piece(at, HP)], it, HA + k)
                arrived(tags.at[at], it, HAS + k)

            pl.when(below if k == 0 else takes)(taken)
            send(data.at[piece(at, HP)], data.at[piece(at, HP)], it, FH + k, sibling, takes)
        send(tags.at[own_eight], tags.at[own_eight], it, FHS, sibling, takes)

    def unpack(value, scale):
        return value.astype(jnp.int32).astype(F32) * scale[0:1, 0:1]

    def spread(packed, scales, to_hi, to_lo):
        def body(i, carry):
            rows = piece(i, GP)
            ef[rows, :] = unpack(packed[rows, :], scales[i])
            return carry

        lax.fori_loop(0, 16, body, 0, unroll=True)
        for k, (a, e) in enumerate(KEPT):
            x = ef[k * TILE : k * TILE + TILE, :]
            at, to = slice(a * TILE, a * TILE + TILE), slice(e * TILE, e * TILE + TILE)
            to_hi[at, to], to_lo[at, to] = split(x)
            if a != e:
                to_hi[to, at], to_lo[to, at] = split(x.T)

    def take_gram(it):
        for k in range(8):
            arrived(ea.at[it, piece((1 - core) * 8 + (z + 8 - k) % 8, GP)], it, FE + k)
        arrived(es.at[it, other_eight], it, FES)
        spread(ea.at[it], es.at[it], ehi, elo)

    def take_side(it):
        @pl.when(has_side)
        def _():
            arrived(na.at[other_part], it, FN)
            arrived(ns.at[other_eight], it, FNS)
            spread(na, ns, mhi, mlo)

    def cross_value(it, i):
        return jnp.concatenate([unpack(ha[it, piece(4 * i + e, HP), :], hs[it, 4 * i + e]) for e in range(4)], axis=0)

    def cross_plain(it, to_hi, to_lo, halves=(0, 1)):
        for half in halves:
            for e in range(2):
                rows = piece(2 * half + e, TILE)
                to_hi[rows, :], to_lo[rows, :] = split(cross_value(it, 2 * half + e))

    def cross_turned(it, to_hi, to_lo, halves=(0, 1)):
        for half in halves:
            for e in range(2):
                cols = piece(2 * half + e, TILE)
                to_hi[:, cols], to_lo[:, cols] = split(cross_value(it, 2 * half + e).T)

    low_side = jnp.logical_and(low, has_side)
    high_side = jnp.logical_and(high, has_side)

    def unpack_half(it, half):
        pl.when(low_side)(lambda: cross_plain(it, xhi, xlo, (half,)))
        pl.when(high_side)(lambda: cross_turned(it, xhi, xlo, (half,)))

    def take_own_cross(it):
        if it == 0:

            @pl.when(jnp.logical_not(has_side))
            def _():
                xhi[...] = jnp.zeros((ORBS, ORBS), BF)
                xlo[...] = jnp.zeros((ORBS, ORBS), BF)

        unpack_half(it, core)

    def take_pair_cross(it):
        @pl.when(jnp.logical_or(high, has_side))
        def _():
            for k in range(8):
                arrived(ha.at[it, piece((1 - core) * 8 + (z + 8 - k) % 8, HP)], it, FH + k)
            arrived(hs.at[it, other_eight], it, FHS)

        unpack_half(it, 1 - core)

    def own_change(it):
        c[...] = c[...] - 0.5 * dot3(chi[it, 0:512], clo[it], ehi[...], elo[...])

    def updated(it, t, rows):
        change = dot3(nhi[rows, :], nlo[rows, :], xhi[...], xlo[...])
        return jnp.where(live(rows, cs_own), c[rows, :] - 0.5 * change, 0.0)

    def rows_arrived():
        @pl.when(has_side)
        def _():
            for t in range(4):
                arrived(nq_in.at[pl.ds(t * TILE, TILE)], 0, NX + t)

    def take_rows():
        @pl.when(has_side)
        def _():
            for t in range(4):
                rows = pl.ds(t * TILE, TILE)
                x = nq_in[rows, :].astype(jnp.int32).astype(F32) * (CMAX / QMAX)
                nhi[rows, :], nlo[rows, :] = split(x)

        @pl.when(jnp.logical_not(has_side))
        def _():
            nhi[...] = jnp.zeros((ROWS, ORBS), BF)
            nlo[...] = jnp.zeros((ROWS, ORBS), BF)

    def pair_cross(it):
        send(hp.at[it, other_half], hsib.at[it], it, HSIB, sibling, high)

    def keep(rows, x):
        c[rows, :] = x
        hi, lo = split(x)
        chi[1, rows, :] = hi
        clo[1, rows, :] = lo

    def first(rows):
        keep(rows, updated(0, 0, rows))

    def first_ends():
        two = (pl.ds(0, BLK), pl.ds(448, BLK))
        change = dot3(
            jnp.concatenate([nhi[rows, :] for rows in two], axis=0), jnp.concatenate([nlo[rows, :] for rows in two], axis=0), xhi[...], xlo[...]
        )
        for i, rows in enumerate(two):
            keep(rows, jnp.where(live(rows, cs_own), c[rows, :] - 0.5 * change[i * BLK : i * BLK + BLK], 0.0))

    def beside(t, rows):
        change = dot3(nhi[rows, :], nlo[rows, :], mhi[...], mlo[...])
        change = change + dot3(chi[0, rows, :], clo[0, rows, :], thi[...], tlo[...])
        x = jnp.where(live(rows, cs_in), nq_in[rows, :].astype(jnp.int32).astype(F32) * (CMAX / QMAX) - 0.5 * change, 0.0)
        nhi[rows, :], nlo[rows, :] = split(x)

    def ended(cols, change):
        at = lax.broadcasted_iota(jnp.int32, (ROWS, HALF), 0)
        block = first_block + (at // BLK).astype(F32)
        begin = cs_own[0:1, cols]
        lives = jnp.logical_and(block >= begin, block < begin + SUPPORT)
        out[:, cols] = jnp.where(lives, c[:, cols] - 0.5 * change, 0.0)

    def last_half(half, final):
        @pl.when(low)
        def _():
            part = dot3(nhi[:, half], nlo[:, half], xhi[half, :], xlo[half, :])
            if final:
                out[...] = jnp.where(live(pl.ds(0, ROWS), cs_own), nf[...] - 0.5 * part, 0.0)
            else:
                nf[...] = c[...] - 0.5 * part

        @pl.when(high)
        def _():
            ended(half, dot3(nhi[...], nlo[...], xhi[:, half], xlo[:, half]))

    images(0)
    gram(0)
    edges(0)
    send(gp.at[0, other_part], gsib.at[0], 0, GSIB, sibling)
    scatter_gram(0)
    rows_arrived()
    send_gram(0)
    take_rows()
    pl.when(high)(lambda: cross_half(0, other_half))
    pair_cross(0)
    pl.when(high)(lambda: cross_half(0, own_half))
    pl.when(high)(lambda: scatter_cross(0))
    send_cross(0)
    own_gram(0)
    own_cross(0)
    pass_gram(0, True)
    take_gram(0)
    own_change(0)
    pass_cross(0)
    take_own_cross(0)
    take_pair_cross(0)
    first_ends()
    send_halo(1)
    pass_side(0)
    first(pl.ds(64, 384))
    pl.when(has_side)(lambda: arrived(cs_in, 0, NXC))
    pl.when(jnp.logical_and(low, has_side))(lambda: cross_turned(0, thi, tlo))
    pl.when(jnp.logical_and(high, has_side))(lambda: cross_plain(0, thi, tlo))
    take_side(0)
    pl.when(has_side)(lambda: beside(0, pl.ds(0, ROWS)))

    images(1)
    gram(1)
    pl.when(high)(lambda: cross(1))
    edges(1)
    send(gp.at[1, other_part], gsib.at[1], 1, GSIB, sibling)
    pl.when(high)(lambda: cross_edges(1, other_half))
    pair_cross(1)
    pl.when(high)(lambda: cross_edges(1, own_half))
    scatter_gram(1)
    before = len(sent)
    send_gram(1)
    pl.when(high)(lambda: scatter_cross(1))
    send_cross(1)
    drain(before)
    own_gram(1)
    own_cross(1)
    pass_gram(1, False)
    take_gram(1)
    own_change(1)
    pass_cross(1)
    take_own_cross(1)
    last_half(own_half, False)
    drain()
    take_pair_cross(1)
    last_half(other_half, True)


def per_device(coefficients, basis_metric, pattern, starts):
    vm = pltpu.VMEM
    square = (ORBS, ORBS)
    scratch = [
        vm((ROWS, ORBS), F32), vm((2, 640, ORBS), BF), vm((2, ROWS, ORBS), BF),
        vm((ROWS, ORBS), F32), vm((ROWS, ORBS), BF), vm((ROWS, ORBS), BF),
        vm((ROWS, ORBS), BF), vm((ROWS, ORBS), BF), vm((ROWS, 640), BF),
        vm((2, PACKED, TILE), F32), vm((2, ORBS, ORBS), F32),
        vm((ROWS, ORBS), I16), vm((ROWS, ORBS), I16), vm((1, ORBS), F32), vm((1, ORBS), F32),
        vm((576, 128), BF), vm((576, 128), BF), vm((576, 128), BF),
        vm((2, PHALF, TILE), F32), vm((2, HALF, ORBS), F32),
        vm((2, 8, GP, TILE), I16), vm((2, 8, GP, TILE), I16), vm((2, 1, 128), F32), vm((2, 8, 1, 128), F32),
        vm((2, 8, HP, ORBS), I16), vm((2, 8, HP, ORBS), I16), vm((2, 1, 128), F32), vm((2, 8, 1, 128), F32),
        vm((2, PACKED, TILE), I16), vm((2, 16, 1, 128), F32), vm((PACKED, TILE), I16), vm((16, 1, 128), F32),
        vm((2, ORBS, ORBS), I16), vm((2, 16, 1, 128), F32),
        vm(square, BF), vm(square, BF), vm(square, BF), vm(square, BF), vm(square, BF), vm(square, BF),
        vm(square, BF), vm(square, BF), vm((PACKED, TILE), F32),
        vm((2, HP, ORBS), I16), vm((2, 1, 128), F32), vm((HP, ORBS), F32), vm((192, ORBS), BF), vm((192, ORBS), BF), vm((128, ORBS), BF),
        pltpu.SMEM((64,), jnp.int32), pltpu.SMEM((8,), jnp.int32),
        pltpu.SemaphoreType.DMA((2, COUNT)), pltpu.SemaphoreType.DMA((2, COUNT)), pltpu.SemaphoreType.DMA((8,)),
    ]
    result = pl.pallas_call(
        kernel,
        out_shape=jax.ShapeDtypeStruct((ROWS, ORBS), F32),
        in_specs=[
            pl.BlockSpec(memory_space=pltpu.HBM),
            pl.BlockSpec(memory_space=pltpu.HBM),
            pl.BlockSpec(memory_space=pltpu.HBM),
            pl.BlockSpec(memory_space=pltpu.HBM),
        ],
        out_specs=pl.BlockSpec(memory_space=pltpu.VMEM),
        scratch_shapes=scratch,
        compiler_params=pltpu.CompilerParams(
            collective_id=0, has_side_effects=True, vmem_limit_bytes=52 * 1024 * 1024
        ),
    )(coefficients[0], basis_metric, pattern, starts)
    return result[None]


def solution(mesh):
    in_specs = (P("orb", ("basis", "rep"), None), P("orb", None), P("orb"), P("orb"))
    out_specs = P("orb", ("basis", "rep"), None)
    return jax.shard_map(
        per_device, mesh=mesh, in_specs=in_specs, out_specs=out_specs, check_vma=False
    )
```
